32 devices in a mesh: groups: 1, subtree: 32 (over z, y, x, core).
Axes of the slice: x: 2, y: 2, z: 4, core: 2. Of those that a mesh axis runs over, the one named last changes fastest.
Arguments:
- composition: bfloat16 [196608, 128], P(('groups', 'subtree')), may hold values from -6 to 6
- leaf_basis: bfloat16 [384, 64, 512], P('subtree'), may hold values from -0.25 to 0.25
- transfer: bfloat16 [384, 64, 64], P('subtree'), may hold values from -0.21875 to 0.21875
- coupling: bfloat16 [384, 16, 64, 64], P('subtree'), may hold values from -0.375 to 0.375
- top_coupling: bfloat16 [32, 32, 64, 64], P('subtree'), may hold values from -0.75 to 0.75
- admissible_owner: int32 [384, 16], P(('groups', 'subtree')), may hold values from 0 to 31, all different within a row; in each aligned block of 12 rows (0 to 11, 12 to 23, ...) at most 12 rows name the same one
- admissible_leaf: int32 [384, 16], P(('groups', 'subtree')), may hold values from 0 to 11
- near_list: int32 [384, 2], P(('groups', 'subtree')), may hold values 0 or 1
- leaf_order: int32 [384, 512], P(('groups', 'subtree')), may hold values from 0 to 511, each once within a row
Outputs:
- potential: bfloat16 [196608, 128], P(('groups', 'subtree'))
The draws below stay inside these ranges and needn't reach their ends.
Inputs may be any that keep to these rules, and one draw needn't show every extreme that they name: `admissible_owner`: each row names 16 different owners; among the rows of one device no owner is named more than 12 times, a bound that some block reaches. `leaf_order`: each row holds every number of 0 to 511 once.
All inputs are finite; a program needn't handle non-finite values. No bound on the sum of `near_list` on one device may be relied on, other than what follows from the above.
Results may differ from the reference program's by a relative error of at most 0.0053.
Values may be sent and summed in bfloat16 or wider, within the bound.
No kernel may reach another device: no remote copies, remote signals or barrier semaphores. Data moves between devices by JAX's collectives and lax.ppermute only.
A program may use at most 128 MiB of HBM per device.

```python
import math
import jax
import jax.numpy as jnp
import numpy as np
from jax import lax

LEAF = 512
R = 64
NV = 128
LEAF_DEV = 12
ADM = 16
CAP = 12
LEAVES = 384
CELLS = 196608
N_SUBTREE = 32


def place_ends(values, own_key, low, top_value):
    dims = values.shape
    index_at = [jax.random.randint(jax.random.fold_in(own_key, axis), (), 0, dims[axis]) for axis in range(len(dims))]
    values = values.at[tuple(index_at)].set(low)
    longest = dims.index(max(dims))
    index_at[longest] = (index_at[longest] + 1) % dims[longest]
    return values.at[tuple(index_at)].set(top_value)


def raised(drawn, rng, source, target, shards_of, factor):
    def block_of(axis_at):
        return (jnp.arange(drawn.shape[axis_at]) // (drawn.shape[axis_at] // shards_of)).reshape((-1,) + (1,) * (drawn.ndim - 1 - axis_at))

    first = jax.random.permutation(rng, shards_of)[block_of(target)]
    second = (block_of(target) + shards_of // 2) % shards_of
    return jnp.where((block_of(source) == first) | (block_of(source) == second), factor * drawn, drawn)


def shard_levels(own_key, dims, shards, smallest, high):
    level = 1.0
    for axis_at, blocks in shards:
        heights = jax.random.uniform(jax.random.fold_in(jax.random.fold_in(own_key, 6), axis_at), (blocks,), jnp.float32, smallest / len(shards), high / len(shards))
        level = level * jnp.repeat(jnp.exp(heights), dims[axis_at] // blocks).reshape((-1,) + (1,) * (len(dims) - 1 - axis_at))
    return level


def assign_block(rng, own, number, rows, count, top, most, skew):
    order = jax.random.permutation(rng, count)
    crowded, usual = shares(count, rows * top, most, skew, True), shares(count, rows * top, most, skew, False)
    places = jnp.arange(count)

    def named(sizes, offset_by):
        used = int((sizes > 0).sum())
        fixed = max(1, used // 4)
        passed = fixed + (places - fixed + offset_by * (used - fixed)) % max(1, count - fixed)
        return jnp.zeros((count,), jnp.int32).at[order[jnp.where(places < fixed, places, passed)]].set(jnp.asarray(sizes, jnp.int32))

    sizes = jnp.where(number % 4 == 0, named(crowded, number // 4), named(usual, number - number // 4 - 1))
    mixed = jax.random.permutation(jax.random.fold_in(own, 3), count)
    giver, receiver = mixed[0:count // 2 * 2:2], mixed[1:count // 2 * 2:2]
    slack = jnp.minimum(sizes[giver] - 1, most - sizes[receiver]) // 2
    slack = jnp.where((giver == order[0]) | (receiver == order[0]) | (sizes[receiver] == 0), 0, jnp.maximum(slack, 0))
    passed = jax.random.randint(jax.random.fold_in(own, 4), (count // 2,), 0, 1 << 20) % (slack + 1)
    sizes = sizes.at[giver].add(-passed).at[receiver].add(passed)
    labels = jnp.searchsorted(jnp.cumsum(sizes), jnp.arange(rows * top), side="right").astype(jnp.int32)
    grid = labels.reshape(top, rows).T
    grid = grid[jax.random.permutation(jax.random.fold_in(own, 1), rows)]
    offset_by = jax.random.randint(jax.random.fold_in(own, 2), (rows, 1), 0, top)
    return jnp.take_along_axis(grid, (jnp.arange(top)[None, :] + offset_by) % top, axis=1)


def shares(count, total, limit, lean, full):
    weights = [(1 << 20) // math.isqrt(grade ** lean) + 1 for grade in range(1, count + 1)]
    largest = limit if full else min(limit, max(-(-total // count), total * weights[0] // sum(weights)))
    least = 1 if total - largest >= count - 1 else 0
    counts, spare = [largest] + [least] * (count - 1), total - largest - least * (count - 1)
    while spare > 0:
        candidates = [i for i in range(1, count) if counts[i] < largest] or [i for i in range(1, count) if counts[i] < limit]
        pool, left = sum([weights[i] for i in candidates]), spare
        for i in candidates:
            more = min(limit - counts[i], max(1, left * weights[i] // pool), spare)
            counts[i] = counts[i] + more
            spare = spare - more
    return np.array(counts)


def normal_values(own_key, shape, width, reach, split=(), held_as=jnp.bfloat16):
    values = jax.random.normal(own_key, shape, jnp.float32) * width
    if len(split) > 0:
        values = shard_levels(own_key, shape, split, -0.22, 0.18) * values
    return jnp.clip(values, min=-reach, max=reach).astype(held_as)


def gaussian_with(stream_key, dims, deviation, limit, split, heavy, held_as=jnp.bfloat16):
    values = deviation * jax.random.normal(stream_key, dims, jnp.float32)
    if split:
        values = values * shard_levels(stream_key, dims, split, -0.22, 0.18)
    return jnp.clip(raised(values, jax.random.fold_in(stream_key, 3), *heavy), -limit, limit).astype(held_as)


def setup_inputs(seed: int = 0, part: int = 0) -> dict:
    keys = jax.random.split(jax.random.key(seed), 10)
    own_keys = jax.random.split(jax.random.fold_in(keys[9], part), 10)
    composition = normal_values(own_keys[0], (CELLS, NV), 1.0, 6.0, ((0, 32),))
    leaf_basis = normal_values(keys[1], (LEAVES, R, LEAF), LEAF ** -0.5, 0.25, ((0, 32),))
    transfer = normal_values(keys[2], (LEAVES, R, R), (R * LEAF_DEV) ** -0.5, 0.21875, ((0, 32),))
    coupling = normal_values(keys[3], (LEAVES, ADM, R, R), (R * ADM // 4) ** -0.5, 0.375, ((0, 32),))
    top_coupling = gaussian_with(keys[4], (N_SUBTREE, N_SUBTREE, R, R), (R * N_SUBTREE // 8) ** -0.5, 0.75, ((0, 32),), (1, 0, 32, 2.75))
    admissible_owner_keys = jax.random.split(jax.random.fold_in(own_keys[5], 1), LEAVES // LEAF_DEV)
    admissible_owner_turns = jax.random.permutation(jax.random.fold_in(own_keys[5], 3), LEAVES // LEAF_DEV)
    admissible_owner = jax.vmap(lambda own, number: assign_block(jax.random.fold_in(own_keys[5], 2), own, number, LEAF_DEV, N_SUBTREE, ADM, CAP, 2))(admissible_owner_keys, admissible_owner_turns).reshape((LEAVES, ADM))
    admissible_leaf = place_ends(jax.random.randint(own_keys[6], (LEAVES, ADM), 0, LEAF_DEV), jax.random.fold_in(own_keys[6], 1), 0, LEAF_DEV - 1).astype(jnp.int32)
    near_list = place_ends((jax.random.randint(own_keys[7], (LEAVES, 2), 0, 4) < 3).astype(jnp.int32), jax.random.fold_in(own_keys[7], 1), 0, 1)
    leaf_order = jax.vmap(lambda own: jax.random.permutation(own, LEAF))(jax.random.split(own_keys[8], LEAVES)).reshape((LEAVES, LEAF)).astype(jnp.int32)
    return {"composition": composition, "leaf_basis": leaf_basis, "transfer": transfer, "coupling": coupling, "top_coupling": top_coupling, "admissible_owner": admissible_owner, "admissible_leaf": admissible_leaf, "near_list": near_list, "leaf_order": leaf_order}


COULOMB_SCALE = 0.15
SOFTENING = 0.25

def near_tables(leaf_len):
    cells = jnp.arange(leaf_len)
    along = (cells // 64).astype(jnp.float32)
    across = (cells // 8 % 8).astype(jnp.float32)
    height = (cells % 8).astype(jnp.float32)
    extent = leaf_len // 64
    tables = []
    for offset in (-1, 0, 1):
        delta_x = along[:, None] - along[None, :] - float(offset * extent)
        delta_y = across[:, None] - across[None, :]
        delta_z = height[:, None] - height[None, :]
        square = delta_x * delta_x + delta_y * delta_y + delta_z * delta_z
        tables.append((COULOMB_SCALE / jnp.sqrt(square + SOFTENING)).astype(jnp.bfloat16))
    return jnp.stack(tables)

def reference(composition, leaf_basis, transfer, coupling, top_coupling, admissible_owner, admissible_leaf, near_list, leaf_order):
    highest = lax.Precision.HIGHEST
    on_grid = composition.reshape(LEAVES, LEAF, NV)
    ordered = jnp.take_along_axis(on_grid, leaf_order[:, :, None], axis=1)

    def leaf_skeleton(paired):
        return jnp.dot(paired[0], paired[1], preferred_element_type=jnp.float32).astype(jnp.bfloat16)
    skeleton = lax.map(leaf_skeleton, (leaf_basis, ordered))
    transfer_dev = transfer.reshape(N_SUBTREE, LEAF_DEV, R, R)
    skeleton_dev = skeleton.reshape(N_SUBTREE, LEAF_DEV, R, NV)

    def device_root(paired):
        return jnp.einsum('lab,lbv->av', paired[0].astype(jnp.float32), paired[1].astype(jnp.float32), precision=highest).astype(jnp.bfloat16)
    roots = lax.map(device_root, (transfer_dev, skeleton_dev))
    indices = jnp.arange(N_SUBTREE, dtype=jnp.int32)

    def root_field(target):
        blocks = top_coupling[target].astype(jnp.float32)
        distant = jnp.abs(indices - target) >= 2
        blocks = jnp.where(distant[:, None, None], blocks, jnp.zeros_like(blocks))
        return jnp.einsum('jab,jbv->av', blocks, roots.astype(jnp.float32), precision=highest)
    root_local = lax.map(root_field, indices)
    zero_leaf = jnp.zeros((1, LEAF, NV), jnp.bfloat16)
    padded = jnp.concatenate([zero_leaf, ordered, zero_leaf], axis=0)
    tables = near_tables(LEAF).astype(jnp.float32)

    def device_out(device):
        first_leaf = device * LEAF_DEV

        def slice_rows(array):
            return lax.dynamic_slice_in_dim(array, first_leaf, LEAF_DEV, 0)
        owners = slice_rows(admissible_owner)
        leaf_index = slice_rows(admissible_leaf)
        chosen = skeleton[(owners * LEAF_DEV + leaf_index).astype(jnp.int32)]
        far_part = jnp.einsum('lkab,lkbv->lav', slice_rows(coupling).astype(jnp.float32), chosen.astype(jnp.float32), precision=highest)
        far_part = far_part + jnp.einsum('lba,bv->lav', slice_rows(transfer).astype(jnp.float32), root_local[device], precision=highest)
        leaf_local = far_part.astype(jnp.bfloat16)
        window = lax.dynamic_slice_in_dim(padded, first_leaf, LEAF_DEV + 2, 0).astype(jnp.float32)
        masks = slice_rows(near_list).astype(jnp.float32)
        near = jnp.einsum('ij,ljv->liv', tables[1], window[1:-1], precision=highest)
        near = near + masks[:, 0][:, None, None] * jnp.einsum('ij,ljv->liv', tables[0], window[:-2], precision=highest)
        near = near + masks[:, 1][:, None, None] * jnp.einsum('ij,ljv->liv', tables[2], window[2:], precision=highest)
        field = near + jnp.einsum('lrc,lrv->lcv', slice_rows(leaf_basis).astype(jnp.float32), leaf_local.astype(jnp.float32), precision=highest)
        order_rows = slice_rows(leaf_order)
        placed = jnp.zeros((LEAF_DEV, LEAF, NV), jnp.float32).at[jnp.arange(LEAF_DEV)[:, None], order_rows].set(field)
        return placed.astype(jnp.bfloat16).reshape(LEAF_DEV * LEAF, NV)
    result = lax.map(device_out, indices)
    return result.reshape(CELLS, NV)
```

```python
import jax
import jax.numpy as jnp
from jax import lax
from jax.sharding import PartitionSpec as P

COULOMB_SCALE = 0.15
SOFTENING = 0.25


def near_tables(leaf_len):
    cells = jnp.arange(leaf_len)
    along = (cells // 64).astype(jnp.float32)
    across = (cells // 8 % 8).astype(jnp.float32)
    height = (cells % 8).astype(jnp.float32)
    extent = leaf_len // 64
    tables = []
    for offset in (-1, 0, 1):
        delta_x = along[:, None] - along[None, :] - float(offset * extent)
        delta_y = across[:, None] - across[None, :]
        delta_z = height[:, None] - height[None, :]
        square = delta_x * delta_x + delta_y * delta_y + delta_z * delta_z
        tables.append((COULOMB_SCALE / jnp.sqrt(square + SOFTENING)).astype(jnp.bfloat16))
    return jnp.stack(tables)


def ring_order(layers):
    return [0] + list(range(1, layers, 2)) + list(range(layers - 2, 0, -2))


def send(block, target):
    count = lax.axis_size("subtree")
    return lax.ppermute(block, "subtree", [(d, target(d)) for d in range(count)])


def plane_gather(mine):
    half = mine.shape[0] // 2
    from_x = send(mine, lambda d: d ^ 2)
    from_y = send(mine, lambda d: d ^ 4)
    low = send(from_y[:half], lambda d: d ^ 2)
    high = send(from_x[half:], lambda d: d ^ 4)
    return [mine, from_x, from_y, jnp.concatenate([low, high], axis=0)]


def line_gather(mine, layers):
    order = ring_order(layers)
    following = {order[i]: order[(i + 1) % layers] for i in range(layers)}
    parts = [mine]
    for _ in range(layers - 1):
        parts.append(send(parts[-1], lambda d: following[d // 8] * 8 + d % 8))
    return parts


def both_cores(parts):
    return parts + [send(part, lambda d: d ^ 1) for part in parts]


def on_device(
    composition,
    leaf_basis,
    transfer,
    coupling,
    top_coupling,
    admissible_owner,
    admissible_leaf,
    near_list,
    leaf_order,
):
    highest = lax.Precision.HIGHEST
    leaf_dev = leaf_basis.shape[0]
    rank_dim = leaf_basis.shape[1]
    leaf_len = leaf_basis.shape[2]
    fields = composition.shape[1]
    adm_count = coupling.shape[1]
    count = lax.axis_size("subtree")
    layers = count // 8
    my_index = lax.axis_index("subtree")
    on_grid = composition.reshape(leaf_dev, leaf_len, fields)
    leaf_hot = (
        leaf_order[:, :, None] == jnp.arange(leaf_len, dtype=jnp.int32)[None, None, :]
    ).astype(jnp.bfloat16)
    ordered = jnp.einsum(
        "lij,ljv->liv", leaf_hot, on_grid, preferred_element_type=jnp.float32
    ).astype(jnp.bfloat16)
    skeleton = jnp.einsum(
        "lrc,lcv->lrv", leaf_basis, ordered, preferred_element_type=jnp.float32
    ).astype(jnp.bfloat16)
    root_part = jnp.einsum(
        "lab,lbv->av", transfer, skeleton, preferred_element_type=jnp.float32
    ).astype(jnp.bfloat16)

    shared = jnp.concatenate([root_part[None], skeleton], axis=0)
    first = leaf_dev // 3
    second = leaf_dev + 1 - first
    plane = plane_gather(shared[:first])
    line = line_gather(jnp.concatenate(plane, axis=0), layers)
    tall = line_gather(shared[first:], layers)
    wide = plane_gather(jnp.concatenate(tall, axis=0))
    low_blocks = jnp.concatenate(both_cores(line), axis=0)
    high_blocks = jnp.concatenate(both_cores(wide), axis=0)
    every = jnp.concatenate([low_blocks, high_blocks], axis=0)

    order = ring_order(layers)
    position = jnp.zeros((layers,), jnp.int32).at[jnp.array(order)].set(
        jnp.arange(layers, dtype=jnp.int32)
    )

    def place_of(owner, block):
        layer = (position[my_index // 8] - position[owner // 8]) % layers
        chip = (owner // 2 % 4) ^ (my_index // 2 % 4)
        core = (owner % 2) ^ (my_index % 2)
        low = ((core * layers + layer) * 4 + chip) * first + block
        high = count * first + ((core * 4 + chip) * layers + layer) * second + block - first
        return jnp.where(block < first, low, high)

    sources = jnp.arange(count, dtype=jnp.int32)
    segment = every[place_of(sources, jnp.zeros_like(sources))]
    blocks = top_coupling[0]
    distant = jnp.abs(sources - my_index) >= 2
    blocks = jnp.where(distant[:, None, None], blocks, jnp.zeros_like(blocks))
    root_local = jnp.einsum("jab,jbv->av", blocks, segment, preferred_element_type=jnp.float32)
    wanted = place_of(admissible_owner.reshape(-1), admissible_leaf.reshape(-1) + 1)
    chosen = every[wanted].reshape(leaf_dev, adm_count, rank_dim, fields)
    far_part = jnp.einsum("lkab,lkbv->lav", coupling, chosen, preferred_element_type=jnp.float32)
    far_part = far_part + jnp.einsum(
        "lba,bv->lav", transfer.astype(jnp.float32), root_local, precision=highest
    )
    leaf_local = far_part.astype(jnp.bfloat16)
    before = lax.ppermute(ordered[-1:], "subtree", [(d, d + 1) for d in range(count - 1)])
    after = lax.ppermute(ordered[:1], "subtree", [(d + 1, d) for d in range(count - 1)])
    padded = jnp.concatenate([before, ordered, after], axis=0)
    tables = near_tables(leaf_len)
    masks = near_list.astype(jnp.float32)
    near = jnp.einsum("ij,ljv->liv", tables[1], ordered, preferred_element_type=jnp.float32)
    near = near + masks[:, 0][:, None, None] * jnp.einsum(
        "ij,ljv->liv", tables[0], padded[:-2], preferred_element_type=jnp.float32
    )
    near = near + masks[:, 1][:, None, None] * jnp.einsum(
        "ij,ljv->liv", tables[2], padded[2:], preferred_element_type=jnp.float32
    )
    field = near + jnp.einsum(
        "lrc,lrv->lcv", leaf_basis, leaf_local, preferred_element_type=jnp.float32
    )
    rounded = field.astype(jnp.bfloat16)
    placed = jnp.einsum("lij,liv->ljv", leaf_hot, rounded, preferred_element_type=jnp.float32)
    return placed.astype(jnp.bfloat16).reshape(leaf_dev * leaf_len, fields)


def solution(mesh):
    placed = (
        P(("groups", "subtree"), None),
        P("subtree", None, None),
        P("subtree", None, None),
        P("subtree", None, None, None),
        P("subtree", None, None, None),
        P(("groups", "subtree"), None),
        P(("groups", "subtree"), None),
        P(("groups", "subtree"), None),
        P(("groups", "subtree"), None),
    )
    return jax.shard_map(
        on_device,
        mesh=mesh,
        in_specs=placed,
        out_specs=P(("groups", "subtree"), None),
        check_vma=False,
    )
```

```python
import functools

import jax
import jax.numpy as jnp
import ml_dtypes
import numpy as np
from jax import lax
from jax.experimental import pallas as pl
from jax.experimental.pallas import tpu as pltpu
from jax.sharding import PartitionSpec as P

COULOMB_SCALE = 0.15
SOFTENING = 0.25
BF = jnp.bfloat16
F32 = jnp.float32
VMEM_LIMIT = 48 * 1024 * 1024


def near_tables(leaf_len):
    cells = np.arange(leaf_len)
    along = (cells // 64).astype(np.float32)
    across = (cells // 8 % 8).astype(np.float32)
    height = (cells % 8).astype(np.float32)
    extent = leaf_len // 64
    tables = []
    for offset in (-1, 0, 1):
        delta_x = along[:, None] - along[None, :] - np.float32(offset * extent)
        delta_y = across[:, None] - across[None, :]
        delta_z = height[:, None] - height[None, :]
        square = delta_x * delta_x + delta_y * delta_y + delta_z * delta_z
        value = np.float32(COULOMB_SCALE) / np.sqrt(square + np.float32(SOFTENING))
        tables.append(value.astype(ml_dtypes.bfloat16))
    return np.concatenate(tables, axis=1)


def ring_order(layers):
    return [0] + list(range(1, layers, 2)) + list(range(layers - 2, 0, -2))


def owner_table(count):
    layers = count // 8
    order = ring_order(layers)
    position = {layer: at for at, layer in enumerate(order)}
    table = np.zeros((count, 2, layers * 4), np.int32)
    for device in range(count):
        layer, chip, core = device // 8, device // 2 % 4, device % 2
        for plane in range(2):
            for step in range(layers):
                source = order[(position[layer] - step) % layers]
                for side in range(4):
                    table[device, plane, step * 4 + side] = (
                        source * 8 + (chip ^ side) * 2 + (core ^ plane)
                    )
    return table


def send(block, target):
    count = lax.axis_size("subtree")
    return lax.ppermute(block, "subtree", [(d, target(d)) for d in range(count)])


def over_core(block):
    return send(block, lambda d: d ^ 1)


def over_x(block):
    return send(block, lambda d: d ^ 2)


def over_y(block):
    return send(block, lambda d: d ^ 4)


def along_z(block):
    layers = lax.axis_size("subtree") // 8
    order = ring_order(layers)
    following = {order[i]: order[(i + 1) % layers] for i in range(layers)}
    return send(block, lambda d: following[d // 8] * 8 + d % 8)


def params():
    return pltpu.CompilerParams(vmem_limit_bytes=VMEM_LIMIT)


def cost(flops, moved):
    return pl.CostEstimate(flops=flops, bytes_accessed=moved, transcendentals=0)


def whole():
    return pl.BlockSpec(memory_space=pltpu.VMEM)


def scalars():
    return pl.BlockSpec(memory_space=pltpu.SMEM)


def dot(a, b):
    return jnp.dot(a, b, preferred_element_type=F32)


def skeleton_kernel(per, order_ref, comp_ref, basis_ref, transfer_ref,
                    ordered_ref, shared_ref, first_ref, last_ref, root_ref):
    step = pl.program_id(0)
    leaf_len = basis_ref.shape[2]

    @pl.when(step == 0)
    def _():
        root_ref[...] = jnp.zeros_like(root_ref)

    for i in range(per):
        leaf = step * per + i
        row = order_ref[pl.ds(leaf, 1), :]
        column = jnp.broadcast_to(row, (128, leaf_len)).T
        lanes = lax.broadcasted_iota(jnp.int32, (leaf_len, 128), 1)
        hot = jnp.concatenate(
            [
                jnp.where(column == lanes + 128 * t, 1.0, 0.0).astype(BF)
                for t in range(leaf_len // 128)
            ],
            axis=1,
        )
        ordered = dot(hot, comp_ref[pl.ds(i * leaf_len, leaf_len), :]).astype(BF)
        ordered_ref[pl.ds(i * leaf_len, leaf_len), :] = ordered
        skeleton = dot(basis_ref[i], ordered).astype(BF)
        shared_ref[pl.ds(leaf + 1, 1)] = skeleton[None]
        root_ref[...] += dot(transfer_ref[i], skeleton)
        if i == 0:
            @pl.when(step == 0)
            def _():
                first_ref[...] = ordered
        if i == per - 1:
            @pl.when(step == pl.num_programs(0) - 1)
            def _():
                last_ref[...] = ordered

    @pl.when(step == pl.num_programs(0) - 1)
    def _():
        shared_ref[pl.ds(0, 1)] = root_ref[...].astype(BF)[None]


def skeletons(leaf_order, composition, leaf_basis, transfer, per=4):
    leaves, rank, leaf_len = leaf_basis.shape
    fields = composition.shape[1]
    return pl.pallas_call(
        functools.partial(skeleton_kernel, per),
        name="order_and_skeleton",
        grid=(leaves // per,),
        in_specs=[
            pl.BlockSpec((leaves, leaf_len), lambda s: (0, 0)),
            pl.BlockSpec((per * leaf_len, fields), lambda s: (s, 0)),
            pl.BlockSpec((per, rank, leaf_len), lambda s: (s, 0, 0)),
            pl.BlockSpec((per, rank, rank), lambda s: (s, 0, 0)),
        ],
        out_specs=[
            pl.BlockSpec((per * leaf_len, fields), lambda s: (s, 0)),
            pl.BlockSpec((leaves + 1, rank, fields), lambda s: (0, 0, 0)),
            pl.BlockSpec((leaf_len, fields), lambda s: (0, 0)),
            pl.BlockSpec((leaf_len, fields), lambda s: (0, 0)),
        ],
        out_shape=[
            jax.ShapeDtypeStruct((leaves * leaf_len, fields), BF),
            jax.ShapeDtypeStruct((leaves + 1, rank, fields), BF),
            jax.ShapeDtypeStruct((leaf_len, fields), BF),
            jax.ShapeDtypeStruct((leaf_len, fields), BF),
        ],
        scratch_shapes=[pltpu.VMEM((rank, fields), F32)],
        compiler_params=params(),
        cost_estimate=cost(leaves * leaf_len * leaf_len * fields * 2, 8 << 20),
    )(leaf_order, composition, leaf_basis, transfer)


def dense_kernel(slot_ref, owner_ref, far_ref, coupling_ref, top_ref, own_ref, other_ref):
    leaves, entries, rank, _ = coupling_ref.shape
    slots = own_ref.shape[2] // rank

    def block_of(plane, leaf, slot):
        entry = slot_ref[plane, leaf, slot]
        block = coupling_ref[leaf, jnp.minimum(entry, entries - 1)]
        return jnp.where(entry < entries, block, jnp.zeros_like(block))

    def top_of(plane, slot):
        block = top_ref[0, owner_ref[plane, slot]]
        return jnp.where(far_ref[plane, slot] > 0, block, jnp.zeros_like(block))

    for plane, out_ref in ((0, own_ref), (1, other_ref)):

        def body(leaf, carry, plane=plane, out_ref=out_ref):
            for slot in range(0, slots, 2):
                pair = [block_of(plane, leaf, slot), block_of(plane, leaf, slot + 1)]
                out_ref[leaf + 1, :, slot * rank:(slot + 2) * rank] = jnp.concatenate(pair, axis=1)
            return carry

        lax.fori_loop(0, leaves, body, 0)
        for slot in range(0, slots, 2):
            pair = [top_of(plane, slot), top_of(plane, slot + 1)]
            out_ref[0, :, slot * rank:(slot + 2) * rank] = jnp.concatenate(pair, axis=1)


def dense_couplings(slot_entry, owners, far, coupling, top_coupling):
    leaves, _, rank, _ = coupling.shape
    slots = owners.shape[1]
    shape = jax.ShapeDtypeStruct((leaves + 1, rank, slots * rank), BF)
    return pl.pallas_call(
        dense_kernel,
        name="couplings_by_owner",
        in_specs=[scalars(), scalars(), scalars(), whole(), whole()],
        out_specs=[whole(), whole()],
        out_shape=[shape, shape],
        compiler_params=params(),
        cost_estimate=cost(0, 8 << 20),
    )(slot_entry, owners, far, coupling, top_coupling)


def round_kernel(first, step, own_at, other_at, line_ref, x_ref, y_ref, low_ref, high_ref,
                 own_ref, other_ref, *refs):
    if first:
        own_out, other_out, diagonal = refs
    else:
        own_in, other_in, own_out, other_out, diagonal = refs
    cut = low_ref.shape[0]
    diagonal[:cut] = low_ref[...]
    diagonal[cut:] = high_ref[...]
    targets = own_ref.shape[0]
    sides = (line_ref, x_ref, y_ref, diagonal)
    for at_ref, blocks_ref, out in ((own_at, own_ref, own_out), (other_at, other_ref, other_out)):
        for target in range(targets):
            chosen = jnp.concatenate(
                [side[at_ref[target, step * 4 + q]] for q, side in enumerate(sides)], axis=0
            )
            value = dot(blocks_ref[target], chosen)
            if not first:
                value = value + (own_in if out is own_out else other_in)[target]
            out[target] = value


def far_round(step, own_at, other_at, parts, own_blocks, other_blocks, sums):
    targets, rank, _ = own_blocks.shape
    fields = parts[0].shape[2]
    first = sums is None
    sum_shape = jax.ShapeDtypeStruct((targets, rank, fields), F32)
    blocks = pl.BlockSpec((targets, rank, 4 * rank), lambda s: (0, 0, step))
    full = [pl.BlockSpec(p.shape, lambda s: (0, 0, 0)) for p in parts]
    total = pl.BlockSpec((targets, rank, fields), lambda s: (0, 0, 0))
    return pl.pallas_call(
        functools.partial(round_kernel, first, step),
        name=f"far_round_{step}",
        grid=(1,),
        in_specs=[scalars(), scalars()] + full + [blocks, blocks] + ([] if first else [total, total]),
        out_specs=[total, total],
        out_shape=[sum_shape, sum_shape],
        scratch_shapes=[pltpu.VMEM((targets, rank, fields), BF)],
        compiler_params=params(),
        cost_estimate=cost(2 * targets * rank * 4 * rank * fields * 2, 4 << 20),
    )(own_at, other_at, *parts, own_blocks, other_blocks, *([] if first else sums))


def near_kernel(edges, pair_of, last_pair, mask_ref, order_ref, table_ref, basis_ref,
                prev_ref, cur_ref, next_ref, *refs):
    if edges:
        before_ref, after_ref, _, _, near_ref, turned_ref = refs
    else:
        near_ref, turned_ref = refs
    pair = pair_of(pl.program_id(0))
    leaf_len = basis_ref.shape[2]
    low, high = cur_ref[:leaf_len, :], cur_ref[leaf_len:, :]
    prev, following = prev_ref[...], next_ref[...]
    if edges:
        prev = jnp.where(pair == 0, before_ref[...], prev)
        following = jnp.where(pair == last_pair, after_ref[...], following)

    def masked(leaf, side, value):
        return jnp.where(mask_ref[leaf, side] > 0, value, jnp.zeros_like(value))

    left = jnp.concatenate(
        [masked(2 * pair, 0, prev), low, masked(2 * pair, 1, high)], axis=0
    )
    right = jnp.concatenate(
        [masked(2 * pair + 1, 0, low), high, masked(2 * pair + 1, 1, following)], axis=0
    )
    near = dot(table_ref[...], jnp.concatenate([left, right], axis=1))
    fields = cur_ref.shape[1]
    rows = lax.broadcasted_iota(jnp.int32, (leaf_len, leaf_len), 0)
    for i in range(2):
        value = near[:, i * fields:(i + 1) * fields]
        coarse = value.astype(BF)
        fine = (value - coarse.astype(F32)).astype(BF)
        row = order_ref[pl.ds(2 * pair + i, 1), :]
        hot = jnp.where(rows == row, 1.0, 0.0).astype(BF)
        placed = dot(hot, jnp.concatenate([coarse, fine], axis=1))
        at = pl.ds(i * leaf_len, leaf_len)
        near_ref[at, :] = placed[:, :fields] + placed[:, fields:]
        turned_ref[at, :] = lax.dot_general(
            hot, basis_ref[i], (((1,), (1,)), ((), ())), preferred_element_type=F32
        ).astype(BF)


def near_field(pairs, near_list, leaf_order, tables, leaf_basis, ordered, edges=None):
    leaves, rank, leaf_len = leaf_basis.shape
    fields = ordered.shape[1]
    last = leaves // 2 - 1
    gap = pairs[1] - pairs[0] if len(pairs) > 1 else 1

    def pair_of(step):
        return pairs[0] + gap * step

    in_specs = [
        scalars(),
        pl.BlockSpec((leaves, leaf_len), lambda s: (0, 0)),
        pl.BlockSpec(tables.shape, lambda s: (0, 0)),
        pl.BlockSpec((2, rank, leaf_len), lambda s: (pair_of(s), 0, 0)),
        pl.BlockSpec((leaf_len, fields), lambda s: (jnp.maximum(2 * pair_of(s) - 1, 0), 0)),
        pl.BlockSpec((2 * leaf_len, fields), lambda s: (pair_of(s), 0)),
        pl.BlockSpec((leaf_len, fields), lambda s: (jnp.minimum(2 * pair_of(s) + 2, leaves - 1), 0)),
    ]
    args = [near_list, leaf_order, tables, leaf_basis, ordered, ordered, ordered]
    aliases = {}
    if edges is not None:
        before, after, near, turned = edges
        edge = pl.BlockSpec((leaf_len, fields), lambda s: (0, 0))
        in_specs += [edge, edge, pl.BlockSpec(memory_space=pl.ANY), pl.BlockSpec(memory_space=pl.ANY)]
        args += [before, after, near, turned]
        aliases = {9: 0, 10: 1}
    return pl.pallas_call(
        functools.partial(near_kernel, edges is not None, pair_of, last),
        name="near_and_turn",
        grid=(len(pairs),),
        in_specs=in_specs,
        out_specs=[
            pl.BlockSpec((2 * leaf_len, fields), lambda s: (pair_of(s), 0)),
            pl.BlockSpec((2 * leaf_len, rank), lambda s: (pair_of(s), 0)),
        ],
        out_shape=[
            jax.ShapeDtypeStruct((leaves * leaf_len, fields), F32),
            jax.ShapeDtypeStruct((leaves * leaf_len, rank), BF),
        ],
        input_output_aliases=aliases,
        compiler_params=params(),
        cost_estimate=cost(len(pairs) * 2 * leaf_len * leaf_len * fields * 12, len(pairs) << 20),
    )(*args)


def field_kernel(per, own_ref, other_ref, turned_transfer_ref, near_ref, turned_ref, out_ref):
    step = pl.program_id(0)
    leaf_len = near_ref.shape[0] // per
    local = own_ref[0] + other_ref[0]
    coarse = local.astype(BF)
    fine = (local - coarse.astype(F32)).astype(BF)
    both = jnp.concatenate([coarse, fine], axis=1)
    fields = local.shape[1]
    for i in range(per):
        leaf = step * per + i
        down = dot(turned_transfer_ref[i], both)
        value = own_ref[leaf + 1] + other_ref[leaf + 1] + (down[:, :fields] + down[:, fields:])
        at = pl.ds(i * leaf_len, leaf_len)
        far = dot(turned_ref[at, :], value.astype(BF))
        out_ref[at, :] = (near_ref[at, :] + far).astype(BF)


def field(own, other, turned_transfer, near, turned, per=2):
    leaves, rank, _ = turned_transfer.shape
    fields = near.shape[1]
    leaf_len = near.shape[0] // leaves
    total = pl.BlockSpec(own.shape, lambda s: (0, 0, 0))
    return pl.pallas_call(
        functools.partial(field_kernel, per),
        name="local_and_field",
        grid=(leaves // per,),
        in_specs=[
            total,
            total,
            pl.BlockSpec((per, rank, rank), lambda s: (s, 0, 0)),
            pl.BlockSpec((per * leaf_len, fields), lambda s: (s, 0)),
            pl.BlockSpec((per * leaf_len, rank), lambda s: (s, 0)),
        ],
        out_specs=pl.BlockSpec((per * leaf_len, fields), lambda s: (s, 0)),
        out_shape=jax.ShapeDtypeStruct(near.shape, BF),
        compiler_params=params(),
        cost_estimate=cost(leaves * leaf_len * rank * fields * 2, 6 << 20),
    )(own, other, turned_transfer, near, turned)


def on_device(
    composition,
    leaf_basis,
    transfer,
    coupling,
    top_coupling,
    admissible_owner,
    admissible_leaf,
    near_list,
    leaf_order,
):
    leaves, rank, leaf_len = leaf_basis.shape
    entries = coupling.shape[1]
    count = lax.axis_size("subtree")
    layers = count // 8
    my_index = lax.axis_index("subtree")

    ordered, shared, first, last = skeletons(leaf_order, composition, leaf_basis, transfer)

    owners = jnp.asarray(owner_table(count))[my_index]
    named = admissible_owner[None, :, None, :] == owners[:, None, :, None]
    entry = jnp.arange(entries, dtype=jnp.int32)
    slot_entry = jnp.min(jnp.where(named, entry, entries), axis=-1).astype(jnp.int32)
    slot_block = jnp.sum(
        jnp.where(named, admissible_leaf[None, :, None, :] + 1, 0), axis=-1
    ).astype(jnp.int32)
    slot_block = jnp.concatenate([jnp.zeros_like(slot_block[:, :1]), slot_block], axis=1)
    far = (jnp.abs(owners - my_index) >= 2).astype(jnp.int32)
    own_blocks, my_other = dense_couplings(slot_entry, owners, far, coupling, top_coupling)

    cut = (leaves + 2) // 2
    line = shared
    rounds = []
    for step in range(layers):
        from_x, from_y = over_x(line), over_y(line)
        following = along_z(line) if step < layers - 1 else None
        rounds.append([line, from_x, from_y, over_x(from_y[:cut]), over_y(from_x[cut:])])
        line = following

    before = lax.ppermute(last, "subtree", [(d, d + 1) for d in range(count - 1)])
    after = lax.ppermute(first, "subtree", [(d + 1, d) for d in range(count - 1)])
    other_blocks = over_core(my_other)
    other_at = over_core(slot_block[1])
    own_at = slot_block[0]

    tables = jnp.asarray(near_tables(leaf_len))
    near_args = (near_list, leaf_order, tables, leaf_basis, ordered)
    pairs = leaves // 2
    near, turned = near_field(list(range(1, pairs - 1)), *near_args)
    near, turned = near_field([0, pairs - 1], *near_args, edges=(before, after, near, turned))

    sums = None
    for step, parts in enumerate(rounds):
        sums = far_round(step, own_at, other_at, parts, own_blocks, other_blocks, sums)
    own_sum, other_sum = sums
    received = over_core(other_sum)
    return field(own_sum, received, transfer.transpose(0, 2, 1), near, turned)


def solution(mesh):
    placed = (
        P(("groups", "subtree"), None),
        P("subtree", None, None),
        P("subtree", None, None),
        P("subtree", None, None, None),
        P("subtree", None, None, None),
        P(("groups", "subtree"), None),
        P(("groups", "subtree"), None),
        P(("groups", "subtree"), None),
        P(("groups", "subtree"), None),
    )
    return jax.shard_map(
        on_device,
        mesh=mesh,
        in_specs=placed,
        out_specs=P(("groups", "subtree"), None),
        check_vma=False,
    )
```

```python
import functools

import jax
import jax.numpy as jnp
import ml_dtypes
import numpy as np
from jax import lax
from jax.experimental import pallas as pl
from jax.experimental.pallas import tpu as pltpu
from jax.sharding import PartitionSpec as P

COULOMB_SCALE = 0.15
SOFTENING = 0.25
BF = jnp.bfloat16
F32 = jnp.float32
MIB = 1 << 20


def near_tables(leaf_len):
    cells = np.arange(leaf_len)
    along = (cells // 64).astype(np.float32)
    across = (cells // 8 % 8).astype(np.float32)
    height = (cells % 8).astype(np.float32)
    extent = leaf_len // 64
    tables = []
    for offset in (-1, 0, 1):
        delta_x = along[:, None] - along[None, :] - np.float32(offset * extent)
        delta_y = across[:, None] - across[None, :]
        delta_z = height[:, None] - height[None, :]
        square = delta_x * delta_x + delta_y * delta_y + delta_z * delta_z
        value = np.float32(COULOMB_SCALE) / np.sqrt(square + np.float32(SOFTENING))
        tables.append(value.astype(ml_dtypes.bfloat16))
    return np.concatenate(tables, axis=1)


def ring_order(layers):
    return [0] + list(range(1, layers, 2)) + list(range(layers - 2, 0, -2))


def send(block, target):
    count = lax.axis_size("subtree")
    return lax.ppermute(block, "subtree", [(d, target(d)) for d in range(count)])


def over_core(block):
    return send(block, lambda d: d ^ 1)


def over_x(block):
    return send(block, lambda d: d ^ 2)


def over_y(block):
    return send(block, lambda d: d ^ 4)


def onward(block):
    return send(block, lambda d: d ^ (2 if d % 2 else 4))


def along_z(block):
    layers = lax.axis_size("subtree") // 8
    order = ring_order(layers)
    following = {order[i]: order[(i + 1) % layers] for i in range(layers)}
    return send(block, lambda d: following[d // 8] * 8 + d % 8)


def params(mib):
    return pltpu.CompilerParams(vmem_limit_bytes=mib * MIB)


def cost(flops, moved):
    return pl.CostEstimate(flops=flops, bytes_accessed=moved, transcendentals=0)


def whole():
    return pl.BlockSpec(memory_space=pltpu.VMEM)


def scalars():
    return pl.BlockSpec(memory_space=pltpu.SMEM)


def dot(a, b):
    return jnp.dot(a, b, preferred_element_type=F32)


def one_hot_grid(row, leaf_len):
    cells = lax.broadcasted_iota(jnp.int32, (leaf_len, leaf_len), 0)
    return jnp.where(cells == row, 1.0, 0.0).astype(BF)


def skeleton_kernel(per, order_ref, comp_ref, basis_ref, transfer_ref,
                    placed_ref, shared_ref, root_ref):
    step = pl.program_id(0)
    leaf_len = basis_ref.shape[2]

    @pl.when(step == 0)
    def _():
        root_ref[...] = jnp.zeros_like(root_ref)

    for i in range(per):
        leaf = step * per + i
        hot = one_hot_grid(order_ref[pl.ds(leaf, 1), :], leaf_len)
        placed = lax.dot_general(
            basis_ref[i], hot, (((1,), (1,)), ((), ())), preferred_element_type=F32
        ).astype(BF)
        placed_ref[i] = placed
        skeleton = dot(placed, comp_ref[pl.ds(i * leaf_len, leaf_len), :]).astype(BF)
        shared_ref[pl.ds(leaf + 1, 1)] = skeleton[None]
        root_ref[...] += dot(transfer_ref[i], skeleton)

    @pl.when(step == pl.num_programs(0) - 1)
    def _():
        shared_ref[pl.ds(0, 1)] = root_ref[...].astype(BF)[None]


def skeletons(leaf_order, composition, leaf_basis, transfer, per=4):
    leaves, rank, leaf_len = leaf_basis.shape
    fields = composition.shape[1]
    return pl.pallas_call(
        functools.partial(skeleton_kernel, per),
        name="basis_and_skeleton",
        grid=(leaves // per,),
        in_specs=[
            pl.BlockSpec((leaves, leaf_len), lambda s: (0, 0)),
            pl.BlockSpec((per * leaf_len, fields), lambda s: (s, 0)),
            pl.BlockSpec((per, rank, leaf_len), lambda s: (s, 0, 0)),
            pl.BlockSpec((per, rank, rank), lambda s: (s, 0, 0)),
        ],
        out_specs=[
            pl.BlockSpec((per, rank, leaf_len), lambda s: (s, 0, 0)),
            pl.BlockSpec((leaves + 1, rank, fields), lambda s: (0, 0, 0)),
        ],
        out_shape=[
            jax.ShapeDtypeStruct((leaves, rank, leaf_len), BF),
            jax.ShapeDtypeStruct((leaves + 1, rank, fields), BF),
        ],
        scratch_shapes=[pltpu.VMEM((rank, fields), F32)],
        compiler_params=params(16),
        cost_estimate=cost(leaves * leaf_len * leaf_len * rank * 2, 4 * MIB),
    )(leaf_order, composition, leaf_basis, transfer)


def owner_tables(me, layers, owners, blocks):
    leaves, entries = owners.shape
    slots = layers * 4
    rows = leaves + 1
    shape = (rows, 2 * slots)
    lane = lax.broadcasted_iota(jnp.int32, shape, 1)
    plane = (lane >= slots).astype(jnp.int32)
    slot = lane - plane * slots
    layer, chip, core = me // 8, (me // 2) & 3, me & 1
    half = layers // 2
    at = jnp.where(layer & 1 > 0, (layer + 1) // 2, jnp.where(layer > 0, layers - layer // 2, 0))
    back = at - (slot >> 2)
    back = jnp.where(back < 0, back + layers, back)
    source = jnp.where(back == 0, 0, jnp.where(back <= half, 2 * back - 1, 2 * (layers - back)))
    owner = source * 8 + (chip ^ (slot & 3)) * 2 + (core ^ plane)
    row = lax.broadcasted_iota(jnp.int32, shape, 0)
    distant = jnp.abs(owner - me) >= 2
    entry = jnp.where((row == 0) & distant, owner, -1)
    block = jnp.zeros(shape, jnp.int32)
    pad = jnp.full((1, entries), -1, jnp.int32)
    named = jnp.concatenate([pad, owners], axis=0)
    chosen = jnp.concatenate([pad, blocks], axis=0)
    for k in range(entries):
        match = named[:, k:k + 1] == owner
        entry = jnp.where(match, k, entry)
        block = jnp.where(match, chosen[:, k:k + 1] + 1, block)
    return entry, block


def order_kernel(per, layers, me_ref, order_ref, comp_ref, owner_ref, leaf_ref,
                 ordered_ref, first_ref, last_ref, table_ref):
    step = pl.program_id(0)
    leaf_len = order_ref.shape[1]
    for i in range(per):
        row = order_ref[pl.ds(step * per + i, 1), :]
        column = jnp.broadcast_to(row, (128, leaf_len)).T
        lanes = lax.broadcasted_iota(jnp.int32, (leaf_len, 128), 1)
        hot = jnp.concatenate(
            [
                jnp.where(column == lanes + 128 * t, 1.0, 0.0).astype(BF)
                for t in range(leaf_len // 128)
            ],
            axis=1,
        )
        at = pl.ds(i * leaf_len, leaf_len)
        ordered = dot(hot, comp_ref[at, :]).astype(BF)
        ordered_ref[at, :] = ordered
        if i == 0:
            @pl.when(step == 0)
            def _():
                first_ref[...] = ordered
        if i == per - 1:
            @pl.when(step == pl.num_programs(0) - 1)
            def _():
                last_ref[...] = ordered

    @pl.when(step == 0)
    def _():
        entry, block = owner_tables(me_ref[0], layers, owner_ref[...], leaf_ref[...])
        rows = entry.shape[0]
        table_ref[0, :rows, :entry.shape[1]] = entry
        table_ref[1, :rows, :entry.shape[1]] = block


def in_order(me, leaf_order, composition, owners, blocks, layers, per=4):
    leaves, leaf_len = leaf_order.shape
    fields = composition.shape[1]
    entries = owners.shape[1]
    edge = jax.ShapeDtypeStruct((leaf_len, fields), BF)
    return pl.pallas_call(
        functools.partial(order_kernel, per, layers),
        name="cluster_order",
        grid=(leaves // per,),
        in_specs=[
            scalars(),
            pl.BlockSpec((leaves, leaf_len), lambda s: (0, 0)),
            pl.BlockSpec((per * leaf_len, fields), lambda s: (s, 0)),
            pl.BlockSpec((leaves, entries), lambda s: (0, 0)),
            pl.BlockSpec((leaves, entries), lambda s: (0, 0)),
        ],
        out_specs=[
            pl.BlockSpec((per * leaf_len, fields), lambda s: (s, 0)),
            pl.BlockSpec((leaf_len, fields), lambda s: (0, 0)),
            pl.BlockSpec((leaf_len, fields), lambda s: (0, 0)),
            pl.BlockSpec((2, 16, 128), lambda s: (0, 0, 0)),
        ],
        out_shape=[
            jax.ShapeDtypeStruct((leaves * leaf_len, fields), BF),
            edge,
            edge,
            jax.ShapeDtypeStruct((2, 16, 128), jnp.int32),
        ],
        compiler_params=params(16),
        cost_estimate=cost(leaves * leaf_len * leaf_len * fields * 2, 4 * MIB),
    )(me, leaf_order, composition, owners, blocks)


def round_kernel(first, steps, slots, own_at, other_at, line_ref, x_ref, y_ref, far_ref,
                 own_coupling, own_top, other_coupling, other_top, *refs):
    if first:
        own_out, other_out = refs
    else:
        own_in, other_in, own_out, other_out = refs
    rows = own_out.shape[0]
    sides = (line_ref, x_ref, y_ref, far_ref)
    for plane, at_ref, coupling_ref, top_ref, out in (
        (0, own_at, own_coupling, own_top, own_out),
        (1, other_at, other_coupling, other_top, other_out),
    ):
        for row in range(rows):
            value = None
            for place, step in enumerate(steps):
                left, right = [], []
                for q, side in enumerate(sides):
                    lane = plane * slots + step * 4 + q
                    entry = at_ref[0, row, lane]
                    safe = jnp.maximum(entry, 0)
                    block = top_ref[0, safe] if row == 0 else coupling_ref[row - 1, safe]
                    left.append(jnp.where(entry >= 0, block, jnp.zeros_like(block)))
                    right.append(side[place * rows + at_ref[1, row, lane]])
                part = dot(jnp.concatenate(left, axis=1), jnp.concatenate(right, axis=0))
                value = part if value is None else value + part
            if not first:
                value = value + (own_in if plane == 0 else other_in)[row]
            out[row] = value


def far_round(steps, slots, own_at, other_at, parts, couplings, sums):
    rows = couplings[0].shape[0] + 1
    rank, fields = parts[0].shape[1:]
    first = sums is None
    sum_shape = jax.ShapeDtypeStruct((rows, rank, fields), F32)
    args = list(parts) + list(couplings) + ([] if first else list(sums))
    return pl.pallas_call(
        functools.partial(round_kernel, first, steps, slots),
        name="far_round_" + str(steps[0]),
        in_specs=[scalars(), scalars()] + [whole()] * len(args),
        out_specs=[whole(), whole()],
        out_shape=[sum_shape, sum_shape],
        compiler_params=params(16),
        cost_estimate=cost(2 * rows * rank * 4 * rank * fields * 2 * len(steps), 2 * MIB),
    )(own_at, other_at, *args)


def near_kernel(edges, pair_of, last_pair, mask_ref, order_ref, table_ref, placed_ref,
                prev_ref, cur_ref, next_ref, *refs):
    if edges:
        before_ref, after_ref = refs[:2]
    near_ref, turned_ref = refs[-2:]
    pair = pair_of(pl.program_id(0))
    leaf_len = placed_ref.shape[2]
    low, high = cur_ref[:leaf_len, :], cur_ref[leaf_len:, :]
    prev, following = prev_ref[...], next_ref[...]
    if edges:
        prev = jnp.where(pair == 0, before_ref[...], prev)
        following = jnp.where(pair == last_pair, after_ref[...], following)

    def masked(leaf, side, value):
        return jnp.where(mask_ref[leaf, side] > 0, value, jnp.zeros_like(value))

    left = jnp.concatenate(
        [masked(2 * pair, 0, prev), low, masked(2 * pair, 1, high)], axis=0
    )
    right = jnp.concatenate(
        [masked(2 * pair + 1, 0, low), high, masked(2 * pair + 1, 1, following)], axis=0
    )
    near = dot(table_ref[...], jnp.concatenate([left, right], axis=1)).astype(BF)
    fields = cur_ref.shape[1]
    for i in range(2):
        hot = one_hot_grid(order_ref[pl.ds(2 * pair + i, 1), :], leaf_len)
        at = pl.ds(i * leaf_len, leaf_len)
        near_ref[at, :] = dot(hot, near[:, i * fields:(i + 1) * fields]).astype(BF)
        turned_ref[at, :] = placed_ref[i].T


def near_field(pairs, near_list, leaf_order, tables, placed, ordered, halos=None, filled=None):
    leaves, rank, leaf_len = placed.shape
    fields = ordered.shape[1]
    last = leaves // 2 - 1
    gap = pairs[1] - pairs[0] if len(pairs) > 1 else 1

    def pair_of(step):
        return pairs[0] + gap * step

    in_specs = [
        scalars(),
        pl.BlockSpec((leaves, leaf_len), lambda s: (0, 0)),
        pl.BlockSpec(tables.shape, lambda s: (0, 0)),
        pl.BlockSpec((2, rank, leaf_len), lambda s: (pair_of(s), 0, 0)),
        pl.BlockSpec((leaf_len, fields), lambda s: (jnp.maximum(2 * pair_of(s) - 1, 0), 0)),
        pl.BlockSpec((2 * leaf_len, fields), lambda s: (pair_of(s), 0)),
        pl.BlockSpec((leaf_len, fields), lambda s: (jnp.minimum(2 * pair_of(s) + 2, leaves - 1), 0)),
    ]
    args = [near_list, leaf_order, tables, placed, ordered, ordered, ordered]
    aliases = {}
    if halos is not None:
        in_specs += [pl.BlockSpec((leaf_len, fields), lambda s: (0, 0))] * 2
        args += list(halos)
    if filled is not None:
        aliases = {len(args): 0, len(args) + 1: 1}
        in_specs += [pl.BlockSpec(memory_space=pl.ANY)] * 2
        args += list(filled)
    return pl.pallas_call(
        functools.partial(near_kernel, halos is not None, pair_of, last),
        name="near_" + str(pairs[0]),
        grid=(len(pairs),),
        in_specs=in_specs,
        out_specs=[
            pl.BlockSpec((2 * leaf_len, fields), lambda s: (pair_of(s), 0)),
            pl.BlockSpec((2 * leaf_len, rank), lambda s: (pair_of(s), 0)),
        ],
        out_shape=[
            jax.ShapeDtypeStruct((leaves * leaf_len, fields), BF),
            jax.ShapeDtypeStruct((leaves * leaf_len, rank), BF),
        ],
        input_output_aliases=aliases,
        compiler_params=params(16),
        cost_estimate=cost(len(pairs) * 2 * leaf_len * leaf_len * fields * 10, len(pairs) * MIB),
    )(*args)


def field_kernel(per, own_ref, other_ref, turned_transfer_ref, near_ref, turned_ref, out_ref):
    step = pl.program_id(0)
    leaf_len = near_ref.shape[0] // per
    local = own_ref[0] + other_ref[0]
    coarse = local.astype(BF)
    fine = (local - coarse.astype(F32)).astype(BF)
    both = jnp.concatenate([coarse, fine], axis=1)
    fields = local.shape[1]
    for i in range(per):
        leaf = step * per + i
        down = dot(turned_transfer_ref[i], both)
        value = own_ref[leaf + 1] + other_ref[leaf + 1] + (down[:, :fields] + down[:, fields:])
        at = pl.ds(i * leaf_len, leaf_len)
        far = dot(turned_ref[at, :], value.astype(BF))
        out_ref[at, :] = (near_ref[at, :].astype(F32) + far).astype(BF)


def field(own, other, turned_transfer, near, turned, per=4):
    leaves, rank, _ = turned_transfer.shape
    fields = near.shape[1]
    leaf_len = near.shape[0] // leaves
    total = pl.BlockSpec(own.shape, lambda s: (0, 0, 0))
    return pl.pallas_call(
        functools.partial(field_kernel, per),
        name="local_and_field",
        grid=(leaves // per,),
        in_specs=[
            total,
            total,
            pl.BlockSpec((per, rank, rank), lambda s: (s, 0, 0)),
            pl.BlockSpec((per * leaf_len, fields), lambda s: (s, 0)),
            pl.BlockSpec((per * leaf_len, rank), lambda s: (s, 0)),
        ],
        out_specs=pl.BlockSpec((per * leaf_len, fields), lambda s: (s, 0)),
        out_shape=jax.ShapeDtypeStruct(near.shape, BF),
        compiler_params=params(16),
        cost_estimate=cost(leaves * leaf_len * rank * fields * 2, 4 * MIB),
    )(own, other, turned_transfer, near, turned)


def after(block, *others):
    return lax.optimization_barrier((block,) + others)[0]


def on_device(
    composition,
    leaf_basis,
    transfer,
    coupling,
    top_coupling,
    admissible_owner,
    admissible_leaf,
    near_list,
    leaf_order,
):
    leaves, rank, leaf_len = leaf_basis.shape
    count = lax.axis_size("subtree")
    layers = count // 8
    slots = layers * 4
    my_index = lax.axis_index("subtree")
    even = my_index % 2 == 0

    placed, shared = skeletons(leaf_order, composition, leaf_basis, transfer)

    def plane(block):
        from_x, from_y = over_x(block), over_y(block)
        return block, from_x, from_y

    def diagonal(parts, *others):
        chosen = jnp.where(even, parts[1], parts[2])
        return parts + (onward(after(chosen, *others)),)

    near_plane = plane(shared)
    line = along_z(shared)
    ordered, first, last, table = in_order(
        my_index.reshape(1), leaf_order, composition, admissible_owner, admissible_leaf, layers
    )
    line = after(line, table)
    lines = [along_z(line)]
    next_plane = plane(after(line, near_plane[1], near_plane[2]))
    round_0 = diagonal(near_plane)
    for _ in range(layers - 3):
        lines.append(along_z(lines[-1]))
    before = lax.ppermute(last, "subtree", [(d, d + 1) for d in range(count - 1)])
    behind = lax.ppermute(first, "subtree", [(d + 1, d) for d in range(count - 1)])
    couplings = (coupling, top_coupling, over_core(coupling), over_core(top_coupling))
    other_table = over_core(table)

    tables = jnp.asarray(near_tables(leaf_len))
    near_args = (near_list, leaf_order, tables, placed, ordered)
    pairs = leaves // 2
    cut = pairs // 2
    filled = near_field(list(range(1, cut)), *near_args)
    round_1 = diagonal(next_plane, filled[0])
    last_plane = plane(after(jnp.concatenate(lines, axis=0), round_0[3], filled[0]))
    near_args = (near_list, leaf_order, tables, placed, after(ordered, round_1[3]))
    filled = near_field(list(range(cut, pairs - 1)), *near_args, filled=filled)
    sums = far_round([0], slots, table, other_table, round_0, couplings, None)
    sums = far_round([1], slots, table, other_table, round_1, couplings, sums)
    round_2 = diagonal(last_plane, sums[0], filled[0])
    filled = near_field([0, pairs - 1], *near_args, halos=(before, behind), filled=filled)
    round_2 = round_2[:3] + (after(round_2[3], filled[0]),)
    sums = far_round(list(range(2, layers)), slots, table, other_table, round_2, couplings, sums)
    received = over_core(sums[1])
    return field(sums[0], received, transfer.transpose(0, 2, 1), *filled)


def solution(mesh):
    placed = (
        P(("groups", "subtree"), None),
        P("subtree", None, None),
        P("subtree", None, None),
        P("subtree", None, None, None),
        P("subtree", None, None, None),
        P(("groups", "subtree"), None),
        P(("groups", "subtree"), None),
        P(("groups", "subtree"), None),
        P(("groups", "subtree"), None),
    )
    return jax.shard_map(
        on_device,
        mesh=mesh,
        in_specs=placed,
        out_specs=P(("groups", "subtree"), None),
        check_vma=False,
    )
```

```python
import functools

import jax
import jax.numpy as jnp
import ml_dtypes
import numpy as np
from jax import lax
from jax.experimental import pallas as pl
from jax.experimental.pallas import tpu as pltpu
from jax.sharding import PartitionSpec as P

COULOMB_SCALE = 0.15
SOFTENING = 0.25
BF = jnp.bfloat16
F32 = jnp.float32
MIB = 1 << 20


def near_tables(leaf_len):
    cells = np.arange(leaf_len)
    along = (cells // 64).astype(np.float32)
    across = (cells // 8 % 8).astype(np.float32)
    height = (cells % 8).astype(np.float32)
    extent = leaf_len // 64
    tables = []
    for offset in (-1, 0, 1):
        delta_x = along[:, None] - along[None, :] - np.float32(offset * extent)
        delta_y = across[:, None] - across[None, :]
        delta_z = height[:, None] - height[None, :]
        square = delta_x * delta_x + delta_y * delta_y + delta_z * delta_z
        value = np.float32(COULOMB_SCALE) / np.sqrt(square + np.float32(SOFTENING))
        tables.append(value.astype(ml_dtypes.bfloat16))
    return np.concatenate(tables, axis=1)


def send(block, target):
    count = lax.axis_size("subtree")
    return lax.ppermute(block, "subtree", [(d, target(d)) for d in range(count)])


def over_core(block):
    return send(block, lambda d: d ^ 1)


def over_x(block):
    return send(block, lambda d: d ^ 2)


def over_y(block):
    return send(block, lambda d: d ^ 4)


def onward(block):
    return send(block, lambda d: d ^ (2 if d % 2 else 4))


def along_z(block, step):
    layers = lax.axis_size("subtree") // 8
    return send(block, lambda d: (d // 8 + step) % layers * 8 + d % 8)


def params(mib):
    return pltpu.CompilerParams(vmem_limit_bytes=mib * MIB)


def cost(flops, moved):
    return pl.CostEstimate(flops=flops, bytes_accessed=moved, transcendentals=0)


def whole():
    return pl.BlockSpec(memory_space=pltpu.VMEM)


def scalars():
    return pl.BlockSpec(memory_space=pltpu.SMEM)


def dot(a, b):
    return jnp.dot(a, b, preferred_element_type=F32)


def in_hbm(*arrays):
    return [pltpu.with_memory_space_constraint(array, pltpu.HBM) for array in arrays]


def hbm(shape, dtype):
    return pltpu.HBM(shape, dtype)


def one_hot_leaf(row, leaf_len):
    column = jnp.broadcast_to(row, (128, leaf_len)).T
    lanes = lax.broadcasted_iota(jnp.int32, (leaf_len, 128), 1)
    return jnp.concatenate(
        [
            jnp.where(column == lanes + 128 * t, 1.0, 0.0).astype(BF)
            for t in range(leaf_len // 128)
        ],
        axis=1,
    )


def one_hot_grid(row, leaf_len):
    cells = lax.broadcasted_iota(jnp.int32, (leaf_len, leaf_len), 0)
    return jnp.where(cells == row, 1.0, 0.0).astype(BF)


def skeleton_kernel(per, order_ref, comp_ref, basis_ref, transfer_ref,
                    placed_ref, shared_ref, root_ref):
    step = pl.program_id(0)
    leaf_len = basis_ref.shape[2]

    @pl.when(step == 0)
    def _():
        root_ref[...] = jnp.zeros_like(root_ref)

    hots = [one_hot_leaf(order_ref[pl.ds(step * per + i, 1), :], leaf_len) for i in range(per)]
    placed = [dot(basis_ref[i], hots[i]).astype(BF) for i in range(per)]
    skeletons = [
        dot(placed[i], comp_ref[i * leaf_len:(i + 1) * leaf_len, :]).astype(BF)
        for i in range(per)
    ]
    across = jnp.concatenate([transfer_ref[i] for i in range(per)], axis=1)
    root_ref[...] += dot(across, jnp.concatenate(skeletons, axis=0))
    for i in range(per):
        placed_ref[i] = placed[i]
        shared_ref[pl.ds(step * per + i + 1, 1)] = skeletons[i][None]

    @pl.when(step == pl.num_programs(0) - 1)
    def _():
        shared_ref[pl.ds(0, 1)] = root_ref[...].astype(BF)[None]


def skeletons(leaf_order, composition, leaf_basis, transfer, per=4):
    leaves, rank, leaf_len = leaf_basis.shape
    fields = composition.shape[1]
    return pl.pallas_call(
        functools.partial(skeleton_kernel, per),
        name="basis_and_skeleton",
        grid=(leaves // per,),
        in_specs=[
            pl.BlockSpec((leaves, leaf_len), lambda s: (0, 0)),
            pl.BlockSpec((per * leaf_len, fields), lambda s: (s, 0)),
            pl.BlockSpec((per, rank, leaf_len), lambda s: (s, 0, 0)),
            pl.BlockSpec((per, rank, rank), lambda s: (s, 0, 0)),
        ],
        out_specs=[
            pl.BlockSpec((per, rank, leaf_len), lambda s: (s, 0, 0)),
            pl.BlockSpec((leaves + 1, rank, fields), lambda s: (0, 0, 0)),
        ],
        out_shape=[
            hbm((leaves, rank, leaf_len), BF),
            jax.ShapeDtypeStruct((leaves + 1, rank, fields), BF),
        ],
        scratch_shapes=[pltpu.VMEM((rank, fields), F32)],
        compiler_params=params(16),
        cost_estimate=cost(leaves * leaf_len * leaf_len * rank * 2, 4 * MIB),
    )(*in_hbm(leaf_order, composition, leaf_basis, transfer))


def owner_tables(me, layers, owners, blocks):
    leaves, entries = owners.shape
    slots = layers * 4
    rows = leaves + 1
    shape = (rows, 2 * slots)
    lane = lax.broadcasted_iota(jnp.int32, shape, 1)
    plane = (lane >= slots).astype(jnp.int32)
    slot = lane - plane * slots
    layer, chip, core = me // 8, (me // 2) & 3, me & 1
    source = layer - (slot >> 2)
    source = jnp.where(source < 0, source + layers, source)
    owner = source * 8 + (chip ^ (slot & 3)) * 2 + (core ^ plane)
    row = lax.broadcasted_iota(jnp.int32, shape, 0)
    distant = jnp.abs(owner - me) >= 2
    entry = jnp.where((row == 0) & distant, owner, -1)
    block = jnp.zeros(shape, jnp.int32)
    pad = jnp.full((1, entries), -1, jnp.int32)
    named = jnp.concatenate([pad, owners], axis=0)
    chosen = jnp.concatenate([pad, blocks], axis=0)
    for k in range(entries):
        match = named[:, k:k + 1] == owner
        entry = jnp.where(match, k, entry)
        block = jnp.where(match, chosen[:, k:k + 1] + 1, block)
    return entry, block


def order_kernel(per, layers, me_ref, order_ref, comp_ref, owner_ref, leaf_ref,
                 ordered_ref, first_ref, last_ref, table_ref):
    step = pl.program_id(0)
    leaf_len = order_ref.shape[1]
    for i in range(per):
        hot = one_hot_leaf(order_ref[pl.ds(step * per + i, 1), :], leaf_len)
        at = pl.ds(i * leaf_len, leaf_len)
        ordered = dot(hot, comp_ref[at, :]).astype(BF)
        ordered_ref[at, :] = ordered
        if i == 0:
            @pl.when(step == 0)
            def _():
                first_ref[...] = ordered
        if i == per - 1:
            @pl.when(step == pl.num_programs(0) - 1)
            def _():
                last_ref[...] = ordered

    @pl.when(step == 0)
    def _():
        entry, block = owner_tables(me_ref[0], layers, owner_ref[...], leaf_ref[...])
        rows = entry.shape[0]
        table_ref[0, :rows, :entry.shape[1]] = entry
        table_ref[1, :rows, :entry.shape[1]] = block


def in_order(me, leaf_order, composition, owners, blocks, layers, per=4):
    leaves, leaf_len = leaf_order.shape
    fields = composition.shape[1]
    entries = owners.shape[1]
    edge = jax.ShapeDtypeStruct((leaf_len, fields), BF)
    return pl.pallas_call(
        functools.partial(order_kernel, per, layers),
        name="cluster_order",
        grid=(leaves // per,),
        in_specs=[
            scalars(),
            pl.BlockSpec((leaves, leaf_len), lambda s: (0, 0)),
            pl.BlockSpec((per * leaf_len, fields), lambda s: (s, 0)),
            pl.BlockSpec((leaves, entries), lambda s: (0, 0)),
            pl.BlockSpec((leaves, entries), lambda s: (0, 0)),
        ],
        out_specs=[
            pl.BlockSpec((per * leaf_len, fields), lambda s: (s, 0)),
            pl.BlockSpec((leaf_len, fields), lambda s: (0, 0)),
            pl.BlockSpec((leaf_len, fields), lambda s: (0, 0)),
            pl.BlockSpec((2, 16, 128), lambda s: (0, 0, 0)),
        ],
        out_shape=[
            hbm((leaves * leaf_len, fields), BF),
            edge,
            edge,
            jax.ShapeDtypeStruct((2, 16, 128), jnp.int32),
        ],
        compiler_params=params(16),
        cost_estimate=cost(leaves * leaf_len * leaf_len * fields * 2, 4 * MIB),
    )(me, *in_hbm(leaf_order, composition, owners, blocks))


def dense_kernel(per, slots, table_ref, coupling_ref, top_ref, own_ref, other_ref):
    step = pl.program_id(0)
    rank = coupling_ref.shape[2]
    leaves = own_ref.shape[0] - 1

    def fill(out_ref, plane, row, entry_row, block_of):
        for slot in range(0, slots, 2):
            pair = []
            for one in (slot, slot + 1):
                entry = table_ref[0, entry_row, plane * slots + one]
                block = block_of(jnp.maximum(entry, 0))
                pair.append(jnp.where(entry >= 0, block, jnp.zeros_like(block)))
            out_ref[row, :, slot * rank:(slot + 2) * rank] = jnp.concatenate(pair, axis=1)

    for plane, out_ref in ((0, own_ref), (1, other_ref)):
        for i in range(per):
            leaf = step * per + i
            fill(out_ref, plane, leaf, leaf + 1, lambda entry, i=i: coupling_ref[i, entry])

        @pl.when(step == pl.num_programs(0) - 1)
        def _(plane=plane, out_ref=out_ref):
            fill(out_ref, plane, leaves, 0, lambda entry: top_ref[0, entry])


def dense_couplings(table, coupling, top_coupling, slots, per=4):
    leaves, entries, rank, _ = coupling.shape
    shape = jax.ShapeDtypeStruct((leaves + 1, rank, slots * rank), BF)
    full = pl.BlockSpec((leaves + 1, rank, slots * rank), lambda s: (0, 0, 0))
    return pl.pallas_call(
        functools.partial(dense_kernel, per, slots),
        name="couplings_by_owner",
        grid=(leaves // per,),
        in_specs=[
            scalars(),
            pl.BlockSpec((per, entries, rank, rank), lambda s: (s, 0, 0, 0)),
            pl.BlockSpec(top_coupling.shape, lambda s: (0, 0, 0, 0)),
        ],
        out_specs=[full, full],
        out_shape=[shape, shape],
        compiler_params=params(16 if slots <= 16 else 48),
        cost_estimate=cost(0, 8 * MIB),
    )(table, *in_hbm(coupling, top_coupling))


def round_kernel(first, steps, slots, own_at, other_at, line_ref, x_ref, y_ref, far_ref,
                 own_blocks, other_blocks, *refs):
    if first:
        own_out, other_out = refs
    else:
        own_in, other_in, own_out, other_out = refs
    rows, rank, _ = own_out.shape
    sides = (line_ref, x_ref, y_ref, far_ref)
    low, high = steps[0] * 4 * rank, (steps[-1] + 1) * 4 * rank
    for plane, at_ref, blocks_ref, out in (
        (0, own_at, own_blocks, own_out),
        (1, other_at, other_blocks, other_out),
    ):
        for row in range(rows):
            chosen = [
                side[place * rows + at_ref[1, (row + 1) % rows, plane * slots + step * 4 + q]]
                for place, step in enumerate(steps)
                for q, side in enumerate(sides)
            ]
            value = dot(blocks_ref[row, :, low:high], jnp.concatenate(chosen, axis=0))
            if not first:
                value = value + (own_in if plane == 0 else other_in)[row]
            out[row] = value


def far_round(steps, slots, own_at, other_at, parts, blocks, sums):
    rows, rank, _ = blocks[0].shape
    fields = parts[0].shape[2]
    first = sums is None
    sum_shape = jax.ShapeDtypeStruct((rows, rank, fields), F32)
    args = list(parts) + list(blocks) + ([] if first else list(sums))
    return pl.pallas_call(
        functools.partial(round_kernel, first, steps, slots),
        name="far_round_" + str(steps[0]),
        in_specs=[scalars(), scalars()] + [whole()] * len(args),
        out_specs=[whole(), whole()],
        out_shape=[sum_shape, sum_shape],
        compiler_params=params(16 if slots <= 16 else 48),
        cost_estimate=cost(2 * rows * rank * 4 * rank * fields * 2 * len(steps), 2 * MIB),
    )(own_at, other_at, *args)


def near_kernel(edges, pair_of, last_pair, mask_ref, order_ref, table_ref, placed_ref,
                prev_ref, cur_ref, next_ref, *refs):
    if edges:
        before_ref, after_ref = refs[:2]
    near_ref, turned_ref = refs[-2:]
    pair = pair_of(pl.program_id(0))
    leaf_len = placed_ref.shape[2]
    low, high = cur_ref[:leaf_len, :], cur_ref[leaf_len:, :]
    prev, following = prev_ref[...], next_ref[...]
    if edges:
        prev = jnp.where(pair == 0, before_ref[...], prev)
        following = jnp.where(pair == last_pair, after_ref[...], following)

    def masked(leaf, side, value):
        return jnp.where(mask_ref[side, leaf] > 0, value, jnp.zeros_like(value))

    left = jnp.concatenate(
        [masked(2 * pair, 0, prev), low, masked(2 * pair, 1, high)], axis=0
    )
    right = jnp.concatenate(
        [masked(2 * pair + 1, 0, low), high, masked(2 * pair + 1, 1, following)], axis=0
    )
    near = dot(table_ref[...], jnp.concatenate([left, right], axis=1)).astype(BF)
    fields = cur_ref.shape[1]
    for i in range(2):
        hot = one_hot_grid(order_ref[pl.ds(2 * pair + i, 1), :], leaf_len)
        at = pl.ds(i * leaf_len, leaf_len)
        near_ref[at, :] = dot(hot, near[:, i * fields:(i + 1) * fields]).astype(BF)
        turned_ref[at, :] = placed_ref[i].T


def near_field(pairs, near_list, leaf_order, tables, placed, ordered, halos=None, filled=None):
    leaves, rank, leaf_len = placed.shape
    fields = ordered.shape[1]
    last = leaves // 2 - 1
    gap = pairs[1] - pairs[0] if len(pairs) > 1 else 1

    def pair_of(step):
        return pairs[0] + gap * step

    in_specs = [
        scalars(),
        pl.BlockSpec((leaves, leaf_len), lambda s: (0, 0)),
        pl.BlockSpec(tables.shape, lambda s: (0, 0)),
        pl.BlockSpec((2, rank, leaf_len), lambda s: (pair_of(s), 0, 0)),
        pl.BlockSpec((leaf_len, fields), lambda s: (jnp.maximum(2 * pair_of(s) - 1, 0), 0)),
        pl.BlockSpec((2 * leaf_len, fields), lambda s: (pair_of(s), 0)),
        pl.BlockSpec((leaf_len, fields), lambda s: (jnp.minimum(2 * pair_of(s) + 2, leaves - 1), 0)),
    ]
    args = [near_list.T] + in_hbm(leaf_order, tables, placed, ordered, ordered, ordered)
    aliases = {}
    if halos is not None:
        in_specs += [pl.BlockSpec((leaf_len, fields), lambda s: (0, 0))] * 2
        args += list(halos)
    if filled is not None:
        aliases = {len(args): 0, len(args) + 1: 1}
        in_specs += [pl.BlockSpec(memory_space=pl.ANY)] * 2
        args += in_hbm(*filled)
    return pl.pallas_call(
        functools.partial(near_kernel, halos is not None, pair_of, last),
        name="near_" + str(pairs[0]),
        grid=(len(pairs),),
        in_specs=in_specs,
        out_specs=[
            pl.BlockSpec((2 * leaf_len, fields), lambda s: (pair_of(s), 0)),
            pl.BlockSpec((2 * leaf_len, rank), lambda s: (pair_of(s), 0)),
        ],
        out_shape=[
            hbm((leaves * leaf_len, fields), BF),
            hbm((leaves * leaf_len, rank), BF),
        ],
        input_output_aliases=aliases,
        compiler_params=params(16),
        cost_estimate=cost(len(pairs) * 2 * leaf_len * leaf_len * fields * 10, len(pairs) * MIB),
    )(*args)


def field_kernel(per, own_ref, other_ref, turned_transfer_ref, near_ref, turned_ref, out_ref):
    step = pl.program_id(0)
    leaf_len = near_ref.shape[0] // per
    root = own_ref.shape[0] - 1
    local = own_ref[root] + other_ref[root]
    coarse = local.astype(BF)
    fine = (local - coarse.astype(F32)).astype(BF)
    both = jnp.concatenate([coarse, fine], axis=1)
    fields = local.shape[1]
    for i in range(per):
        leaf = step * per + i
        down = dot(turned_transfer_ref[i], both)
        value = own_ref[leaf] + other_ref[leaf] + (down[:, :fields] + down[:, fields:])
        at = pl.ds(i * leaf_len, leaf_len)
        far = dot(turned_ref[at, :], value.astype(BF))
        out_ref[at, :] = (near_ref[at, :].astype(F32) + far).astype(BF)


def field(own, other, turned_transfer, near, turned, per=4):
    leaves, rank, _ = turned_transfer.shape
    fields = near.shape[1]
    leaf_len = near.shape[0] // leaves
    total = pl.BlockSpec(own.shape, lambda s: (0, 0, 0))
    return pl.pallas_call(
        functools.partial(field_kernel, per),
        name="local_and_field",
        grid=(leaves // per,),
        in_specs=[
            total,
            total,
            pl.BlockSpec((per, rank, rank), lambda s: (s, 0, 0)),
            pl.BlockSpec((per * leaf_len, fields), lambda s: (s, 0)),
            pl.BlockSpec((per * leaf_len, rank), lambda s: (s, 0)),
        ],
        out_specs=pl.BlockSpec((per * leaf_len, fields), lambda s: (s, 0)),
        out_shape=jax.ShapeDtypeStruct(near.shape, BF),
        compiler_params=params(16),
        cost_estimate=cost(leaves * leaf_len * rank * fields * 2, 4 * MIB),
    )(own, other, turned_transfer, *in_hbm(near, turned))


def after(block, *others):
    return lax.optimization_barrier((block,) + others)[0]


def on_device(
    composition,
    leaf_basis,
    transfer,
    coupling,
    top_coupling,
    admissible_owner,
    admissible_leaf,
    near_list,
    leaf_order,
):
    leaves, rank, leaf_len = leaf_basis.shape
    count = lax.axis_size("subtree")
    layers = count // 8
    slots = layers * 4
    my_index = lax.axis_index("subtree")
    even = my_index % 2 == 0

    placed, shared = skeletons(leaf_order, composition, leaf_basis, transfer)

    def plane(block):
        from_x, from_y = over_x(block), over_y(block)
        return block, from_x, from_y

    def diagonal(parts, *others):
        chosen = jnp.where(even, parts[1], parts[2])
        return parts + (onward(after(chosen, *others)),)

    half = layers // 2
    lines = [shared, along_z(shared, 1)]
    ordered, first, last, table = in_order(
        my_index.reshape(1), leaf_order, composition, admissible_owner, admissible_leaf, layers
    )
    for step in range(2, layers):
        lines.append(along_z(after(shared, table), step))
    planes = plane(after(jnp.concatenate(lines[:half], axis=0), table))
    tables = jnp.asarray(near_tables(leaf_len))
    near_args = (near_list, leaf_order, tables, placed)
    pairs = leaves // 2
    cut = pairs // 2
    filled = near_field(list(range(1, cut)), *near_args, ordered)
    own_blocks, my_other = dense_couplings(after(table, filled[0]), coupling, top_coupling, slots)
    other_blocks = over_core(my_other)
    round_0 = diagonal(planes)

    planes = plane(
        after(jnp.concatenate(lines[half:], axis=0), planes[1], planes[2], my_other, filled[0])
    )
    other_table = over_core(table)
    before = lax.ppermute(last, "subtree", [(d, d + 1) for d in range(count - 1)])
    behind = lax.ppermute(first, "subtree", [(d + 1, d) for d in range(count - 1)])
    blocks = (own_blocks, other_blocks)
    filled = near_field(
        list(range(cut, pairs - 1)), *near_args, after(ordered, other_table, before, behind), filled=filled
    )
    round_1 = diagonal(planes, filled[0])
    filled = near_field([0, pairs - 1], *near_args, ordered, halos=(before, behind), filled=filled)
    sums = far_round(list(range(half)), slots, table, other_table, round_0, blocks, None)
    round_1 = round_1[:3] + (after(round_1[3], filled[0], sums[0]),)
    sums = far_round(list(range(half, layers)), slots, table, other_table, round_1, blocks, sums)
    received = over_core(sums[1])
    return field(sums[0], received, transfer.transpose(0, 2, 1), *filled)


def solution(mesh):
    placed = (
        P(("groups", "subtree"), None),
        P("subtree", None, None),
        P("subtree", None, None),
        P("subtree", None, None, None),
        P("subtree", None, None, None),
        P(("groups", "subtree"), None),
        P(("groups", "subtree"), None),
        P(("groups", "subtree"), None),
        P(("groups", "subtree"), None),
    )
    return jax.shard_map(
        on_device,
        mesh=mesh,
        in_specs=placed,
        out_specs=P(("groups", "subtree"), None),
        check_vma=False,
    )
```

```python
import functools

import jax
import jax.numpy as jnp
import ml_dtypes
import numpy as np
from jax import lax
from jax.experimental import pallas as pl
from jax.experimental.pallas import tpu as pltpu
from jax.sharding import PartitionSpec as P

COULOMB_SCALE = 0.15
SOFTENING = 0.25
BF = jnp.bfloat16
F32 = jnp.float32
MIB = 1 << 20


def near_tables(leaf_len):
    cells = np.arange(leaf_len)
    along = (cells // 64).astype(np.float32)
    across = (cells // 8 % 8).astype(np.float32)
    height = (cells % 8).astype(np.float32)
    extent = leaf_len // 64
    tables = []
    for offset in (-1, 0, 1):
        delta_x = along[:, None] - along[None, :] - np.float32(offset * extent)
        delta_y = across[:, None] - across[None, :]
        delta_z = height[:, None] - height[None, :]
        square = delta_x * delta_x + delta_y * delta_y + delta_z * delta_z
        value = np.float32(COULOMB_SCALE) / np.sqrt(square + np.float32(SOFTENING))
        tables.append(value.astype(ml_dtypes.bfloat16))
    return np.concatenate(tables, axis=1)


def send(block, target):
    count = lax.axis_size("subtree")
    return lax.ppermute(block, "subtree", [(d, target(d)) for d in range(count)])


def over_core(block):
    return send(block, lambda d: d ^ 1)


def over_x(block):
    return send(block, lambda d: d ^ 2)


def over_y(block):
    return send(block, lambda d: d ^ 4)


def onward(block):
    return send(block, lambda d: d ^ (2 if d % 2 else 4))


def along_z(block, step):
    layers = lax.axis_size("subtree") // 8
    return send(block, lambda d: (d // 8 + step) % layers * 8 + d % 8)


def params(mib):
    return pltpu.CompilerParams(vmem_limit_bytes=mib * MIB)


def cost(flops, moved):
    return pl.CostEstimate(flops=flops // 64, bytes_accessed=moved // 64, transcendentals=0)


def whole():
    return pl.BlockSpec(memory_space=pltpu.VMEM)


def scalars():
    return pl.BlockSpec(memory_space=pltpu.SMEM)


def dot(a, b):
    return jnp.dot(a, b, preferred_element_type=F32)


def in_hbm(*arrays):
    return [pltpu.with_memory_space_constraint(array, pltpu.HBM) for array in arrays]


def one_hot_leaf(row, leaf_len):
    column = jnp.broadcast_to(row, (128, leaf_len)).T
    lanes = lax.broadcasted_iota(jnp.int32, (leaf_len, 128), 1)
    return jnp.concatenate(
        [
            jnp.where(column == lanes + 128 * t, 1.0, 0.0).astype(BF)
            for t in range(leaf_len // 128)
        ],
        axis=1,
    )


def one_hot_grid(row, leaf_len):
    cells = lax.broadcasted_iota(jnp.int32, (leaf_len, leaf_len), 0)
    return jnp.where(cells == row, 1.0, 0.0).astype(BF)


def owner_tables(me, layers, owners, blocks):
    leaves, entries = owners.shape
    slots = layers * 4
    rows = leaves + 1
    shape = (rows, 2 * slots)
    lane = lax.broadcasted_iota(jnp.int32, shape, 1)
    plane = (lane >= slots).astype(jnp.int32)
    slot = lane - plane * slots
    layer, chip, core = me // 8, (me // 2) & 3, me & 1
    turn = slot >> 2
    shift = jnp.where(turn < 2, turn, jnp.where(turn == 2, layers - 1, turn - 1))
    source = layer - shift
    source = jnp.where(source < 0, source + layers, source)
    owner = source * 8 + (chip ^ (slot & 3)) * 2 + (core ^ plane)
    row = lax.broadcasted_iota(jnp.int32, shape, 0)
    distant = jnp.abs(owner - me) >= 2
    entry = jnp.where((row == 0) & distant, owner, -1)
    block = jnp.zeros(shape, jnp.int32)
    pad = jnp.full((1, entries), -1, jnp.int32)
    named = jnp.concatenate([pad, owners], axis=0)
    chosen = jnp.concatenate([pad, blocks], axis=0)
    for k in range(entries):
        match = named[:, k:k + 1] == owner
        entry = jnp.where(match, k, entry)
        block = jnp.where(match, chosen[:, k:k + 1] + 1, block)
    return entry, block


def skeleton_kernel(per, layers, me_ref, order_ref, comp_ref, basis_ref, transfer_ref,
                    owner_ref, leaf_ref, ordered_ref, shared_ref, first_ref, last_ref,
                    table_ref, root_ref):
    step = pl.program_id(0)
    leaf_len = basis_ref.shape[2]

    @pl.when(step == 0)
    def _():
        root_ref[...] = jnp.zeros_like(root_ref)
        entry, block = owner_tables(me_ref[0], layers, owner_ref[...], leaf_ref[...])
        rows, lanes = entry.shape
        table_ref[0, :rows, :lanes] = entry
        table_ref[1, :rows, :lanes] = block

    hots = [one_hot_leaf(order_ref[pl.ds(step * per + i, 1), :], leaf_len) for i in range(per)]
    ordered = [
        dot(hots[i], comp_ref[i * leaf_len:(i + 1) * leaf_len, :]).astype(BF) for i in range(per)
    ]
    skeletons = [dot(basis_ref[i], ordered[i]).astype(BF) for i in range(per)]
    across = jnp.concatenate([transfer_ref[i] for i in range(per)], axis=1)
    root_ref[...] += dot(across, jnp.concatenate(skeletons, axis=0))
    for i in range(per):
        ordered_ref[i * leaf_len:(i + 1) * leaf_len, :] = ordered[i]
        shared_ref[pl.ds(step * per + i + 1, 1)] = skeletons[i][None]

    @pl.when(step == 0)
    def _():
        first_ref[...] = ordered[0]

    @pl.when(step == pl.num_programs(0) - 1)
    def _():
        last_ref[...] = ordered[-1]
        shared_ref[pl.ds(0, 1)] = root_ref[...].astype(BF)[None]


def skeletons_of(me, leaf_order, composition, leaf_basis, transfer, owners, blocks, layers, per=4):
    leaves, rank, leaf_len = leaf_basis.shape
    fields = composition.shape[1]
    entries = owners.shape[1]
    edge = jax.ShapeDtypeStruct((leaf_len, fields), BF)
    return pl.pallas_call(
        functools.partial(skeleton_kernel, per, layers),
        name="order_and_skeleton",
        grid=(leaves // per,),
        in_specs=[
            scalars(),
            pl.BlockSpec((leaves, leaf_len), lambda s: (0, 0)),
            pl.BlockSpec((per * leaf_len, fields), lambda s: (s, 0)),
            pl.BlockSpec((per, rank, leaf_len), lambda s: (s, 0, 0)),
            pl.BlockSpec((per, rank, rank), lambda s: (s, 0, 0)),
            pl.BlockSpec((leaves, entries), lambda s: (0, 0)),
            pl.BlockSpec((leaves, entries), lambda s: (0, 0)),
        ],
        out_specs=[
            pl.BlockSpec((per * leaf_len, fields), lambda s: (s, 0)),
            pl.BlockSpec((leaves + 1, rank, fields), lambda s: (0, 0, 0)),
            pl.BlockSpec((leaf_len, fields), lambda s: (0, 0)),
            pl.BlockSpec((leaf_len, fields), lambda s: (0, 0)),
            pl.BlockSpec((2, 16, 128), lambda s: (0, 0, 0)),
        ],
        out_shape=[
            jax.ShapeDtypeStruct((leaves * leaf_len, fields), BF),
            jax.ShapeDtypeStruct((leaves + 1, rank, fields), BF),
            edge,
            edge,
            jax.ShapeDtypeStruct((2, 16, 128), jnp.int32),
        ],
        scratch_shapes=[pltpu.VMEM((rank, fields), F32)],
        compiler_params=params(16),
        cost_estimate=cost(leaves * leaf_len * leaf_len * fields * 2, 4 * MIB),
    )(me, *in_hbm(leaf_order, composition, leaf_basis, transfer, owners, blocks))


def join_kernel(*refs):
    out = refs[-1]
    at = 0
    for ref in refs[:-1]:
        out[at:at + ref.shape[0]] = ref[...]
        at += ref.shape[0]


def join(parts):
    if len(parts) == 1:
        return parts[0]
    shape = (sum(part.shape[0] for part in parts),) + parts[0].shape[1:]
    return pl.pallas_call(
        join_kernel,
        name="join",
        in_specs=[whole()] * len(parts),
        out_specs=whole(),
        out_shape=jax.ShapeDtypeStruct(shape, BF),
        compiler_params=params(8 if shape[0] <= 32 else 32),
        cost_estimate=cost(0, MIB // 2),
    )(*parts)


def choose_kernel(me_ref, *refs):
    out = refs[-1]
    number = len(refs) // 2
    for core in range(2):
        @pl.when(me_ref[0] % 2 == core)
        def _(core=core):
            join_kernel(*refs[core * number:(core + 1) * number], out)


def choose(me, from_x, from_y):
    parts = list(from_x) + list(from_y)
    shape = (sum(part.shape[0] for part in from_x),) + from_x[0].shape[1:]
    return pl.pallas_call(
        choose_kernel,
        name="choose",
        in_specs=[scalars()] + [whole()] * len(parts),
        out_specs=whole(),
        out_shape=jax.ShapeDtypeStruct(shape, BF),
        compiler_params=params(8 if shape[0] <= 32 else 32),
        cost_estimate=cost(0, MIB // 2),
    )(me, *parts)


def dense_kernel(per, slots, table_ref, coupling_ref, top_ref, transfer_ref,
                 own_ref, other_ref, turned_ref):
    step = pl.program_id(0)
    rank = coupling_ref.shape[2]
    leaves = own_ref.shape[0] - 1

    for i in range(per):
        turned_ref[step * per + i] = transfer_ref[i].T

    def fill(out_ref, plane, row, entry_row, block_of):
        for slot in range(0, slots, 2):
            pair = []
            for one in (slot, slot + 1):
                entry = table_ref[0, entry_row, plane * slots + one]
                block = block_of(jnp.maximum(entry, 0))
                pair.append(jnp.where(entry >= 0, block, jnp.zeros_like(block)))
            out_ref[row, :, slot * rank:(slot + 2) * rank] = jnp.concatenate(pair, axis=1)

    for plane, out_ref in ((0, own_ref), (1, other_ref)):
        for i in range(per):
            leaf = step * per + i
            fill(out_ref, plane, leaf, leaf + 1, lambda entry, i=i: coupling_ref[i, entry])

        @pl.when(step == pl.num_programs(0) - 1)
        def _(plane=plane, out_ref=out_ref):
            fill(out_ref, plane, leaves, 0, lambda entry: top_ref[0, entry])


def dense_couplings(table, coupling, top_coupling, transfer, slots, per=4):
    leaves, entries, rank, _ = coupling.shape
    shape = jax.ShapeDtypeStruct((leaves + 1, rank, slots * rank), BF)
    full = pl.BlockSpec((leaves + 1, rank, slots * rank), lambda s: (0, 0, 0))
    return pl.pallas_call(
        functools.partial(dense_kernel, per, slots),
        name="couplings_by_owner",
        grid=(leaves // per,),
        in_specs=[
            scalars(),
            pl.BlockSpec((per, entries, rank, rank), lambda s: (s, 0, 0, 0)),
            pl.BlockSpec(top_coupling.shape, lambda s: (0, 0, 0, 0)),
            pl.BlockSpec((per, rank, rank), lambda s: (s, 0, 0)),
        ],
        out_specs=[full, full, pl.BlockSpec(transfer.shape, lambda s: (0, 0, 0))],
        out_shape=[shape, shape, jax.ShapeDtypeStruct(transfer.shape, BF)],
        compiler_params=params(16 if slots <= 16 else 48),
        cost_estimate=cost(0, 8 * MIB),
    )(table, *in_hbm(coupling, top_coupling, transfer))


def round_kernel(first, steps, slots, counts, own_at, other_at, *refs):
    sides = []
    for number in counts:
        sides.append(refs[:number])
        refs = refs[number:]
    own_blocks, other_blocks = refs[:2]
    refs = refs[2:]
    if first:
        own_out, other_out = refs
    else:
        own_in, other_in, own_out, other_out = refs
    rows, rank, _ = own_out.shape
    low, high = steps[0] * 4 * rank, (steps[-1] + 1) * 4 * rank

    def block_at(side, base, index):
        for ref in side:
            if base < ref.shape[0]:
                return ref[base + index]
            base -= ref.shape[0]

    for plane, at_ref, blocks_ref, out in (
        (0, own_at, own_blocks, own_out),
        (1, other_at, other_blocks, other_out),
    ):
        for row in range(rows):
            chosen = [
                block_at(side, place * rows, at_ref[1, (row + 1) % rows, plane * slots + step * 4 + q])
                for place, step in enumerate(steps)
                for q, side in enumerate(sides)
            ]
            value = dot(blocks_ref[row, :, low:high], jnp.concatenate(chosen, axis=0))
            if not first:
                value = value + (own_in if plane == 0 else other_in)[row]
            out[row] = value


def far_round(steps, slots, own_at, other_at, parts, blocks, sums):
    rows, rank, _ = blocks[0].shape
    fields = parts[0][0].shape[2]
    first = sums is None
    sum_shape = jax.ShapeDtypeStruct((rows, rank, fields), F32)
    args = [part for side in parts for part in side] + list(blocks) + ([] if first else list(sums))
    return pl.pallas_call(
        functools.partial(round_kernel, first, steps, slots, [len(side) for side in parts]),
        name="far_round_" + str(steps[0]),
        in_specs=[scalars(), scalars()] + [whole()] * len(args),
        out_specs=[whole(), whole()],
        out_shape=[sum_shape, sum_shape],
        compiler_params=params(16 if slots <= 16 else 48),
        cost_estimate=cost(2 * rows * rank * 4 * rank * fields * 2 * len(steps), 2 * MIB),
    )(own_at, other_at, *args)


def near_kernel(edges, pair_of, last_pair, mask_ref, order_ref, table_ref, basis_ref,
                prev_ref, cur_ref, next_ref, *refs):
    if edges:
        before_ref, after_ref = refs[:2]
    near_ref, turned_ref = refs[-2:]
    pair = pair_of(pl.program_id(0))
    leaf_len = basis_ref.shape[2]
    low, high = cur_ref[:leaf_len, :], cur_ref[leaf_len:, :]
    prev, following = prev_ref[...], next_ref[...]
    if edges:
        prev = jnp.where(pair == 0, before_ref[...], prev)
        following = jnp.where(pair == last_pair, after_ref[...], following)

    def masked(leaf, side, value):
        return jnp.where(mask_ref[side, leaf] > 0, value, jnp.zeros_like(value))

    left = jnp.concatenate(
        [masked(2 * pair, 0, prev), low, masked(2 * pair, 1, high)], axis=0
    )
    right = jnp.concatenate(
        [masked(2 * pair + 1, 0, low), high, masked(2 * pair + 1, 1, following)], axis=0
    )
    near = dot(table_ref[...], jnp.concatenate([left, right], axis=1)).astype(BF)
    fields = cur_ref.shape[1]
    for i in range(2):
        hot = one_hot_grid(order_ref[pl.ds(2 * pair + i, 1), :], leaf_len)
        at = pl.ds(i * leaf_len, leaf_len)
        both = jnp.concatenate([near[:, i * fields:(i + 1) * fields], basis_ref[i].T], axis=1)
        moved = dot(hot, both).astype(BF)
        near_ref[at, :] = moved[:, :fields]
        turned_ref[at, :] = moved[:, fields:]


def near_field(pairs, near_list, leaf_order, tables, basis, ordered, halos=None, filled=None):
    leaves, rank, leaf_len = basis.shape
    fields = ordered.shape[1]
    last = leaves // 2 - 1
    gap = pairs[1] - pairs[0] if len(pairs) > 1 else 1

    def pair_of(step):
        return pairs[0] + gap * step

    in_specs = [
        scalars(),
        pl.BlockSpec((leaves, leaf_len), lambda s: (0, 0)),
        pl.BlockSpec(tables.shape, lambda s: (0, 0)),
        pl.BlockSpec((2, rank, leaf_len), lambda s: (pair_of(s), 0, 0)),
        pl.BlockSpec((leaf_len, fields), lambda s: (jnp.maximum(2 * pair_of(s) - 1, 0), 0)),
        pl.BlockSpec((2 * leaf_len, fields), lambda s: (pair_of(s), 0)),
        pl.BlockSpec((leaf_len, fields), lambda s: (jnp.minimum(2 * pair_of(s) + 2, leaves - 1), 0)),
    ]
    args = [near_list.T, leaf_order, tables, basis, ordered, ordered, ordered]
    aliases = {}
    if halos is not None:
        in_specs += [pl.BlockSpec((leaf_len, fields), lambda s: (0, 0))] * 2
        args += list(halos)
    if filled is not None:
        aliases = {len(args): 0, len(args) + 1: 1}
        in_specs += [pl.BlockSpec(memory_space=pl.ANY)] * 2
        args += list(filled)
    return pl.pallas_call(
        functools.partial(near_kernel, halos is not None, pair_of, last),
        name="near_" + str(pairs[0]),
        grid=(len(pairs),),
        in_specs=in_specs,
        out_specs=[
            pl.BlockSpec((2 * leaf_len, fields), lambda s: (pair_of(s), 0)),
            pl.BlockSpec((2 * leaf_len, rank), lambda s: (pair_of(s), 0)),
        ],
        out_shape=[
            jax.ShapeDtypeStruct((leaves * leaf_len, fields), BF),
            jax.ShapeDtypeStruct((leaves * leaf_len, rank), BF),
        ],
        input_output_aliases=aliases,
        compiler_params=params(16),
        cost_estimate=cost(len(pairs) * 2 * leaf_len * leaf_len * fields * 10, len(pairs) * MIB),
    )(*args)


def field_kernel(per, own_ref, other_ref, turned_transfer_ref, near_ref, turned_ref, out_ref):
    step = pl.program_id(0)
    leaf_len = near_ref.shape[0] // per
    root = own_ref.shape[0] - 1
    local = own_ref[root] + other_ref[root]
    coarse = local.astype(BF)
    fine = (local - coarse.astype(F32)).astype(BF)
    both = jnp.concatenate([coarse, fine], axis=1)
    fields = local.shape[1]
    for i in range(per):
        leaf = step * per + i
        down = dot(turned_transfer_ref[i], both)
        value = own_ref[leaf] + other_ref[leaf] + (down[:, :fields] + down[:, fields:])
        at = pl.ds(i * leaf_len, leaf_len)
        far = dot(turned_ref[at, :], value.astype(BF))
        out_ref[at, :] = (near_ref[at, :].astype(F32) + far).astype(BF)


def field(own, other, turned_transfer, near, turned, per=4):
    leaves, rank, _ = turned_transfer.shape
    fields = near.shape[1]
    leaf_len = near.shape[0] // leaves
    total = pl.BlockSpec(own.shape, lambda s: (0, 0, 0))
    return pl.pallas_call(
        functools.partial(field_kernel, per),
        name="local_and_field",
        grid=(leaves // per,),
        in_specs=[
            total,
            total,
            pl.BlockSpec((per, rank, rank), lambda s: (s, 0, 0)),
            pl.BlockSpec((per * leaf_len, fields), lambda s: (s, 0)),
            pl.BlockSpec((per * leaf_len, rank), lambda s: (s, 0)),
        ],
        out_specs=pl.BlockSpec((per * leaf_len, fields), lambda s: (s, 0)),
        out_shape=jax.ShapeDtypeStruct(near.shape, BF),
        compiler_params=params(16),
        cost_estimate=cost(leaves * leaf_len * rank * fields * 2, 4 * MIB),
    )(own, other, turned_transfer, near, turned)


def after(block, *others):
    return lax.optimization_barrier((block,) + others)[0]


def on_device(
    composition,
    leaf_basis,
    transfer,
    coupling,
    top_coupling,
    admissible_owner,
    admissible_leaf,
    near_list,
    leaf_order,
):
    leaves, rank, leaf_len = leaf_basis.shape
    count = lax.axis_size("subtree")
    layers = count // 8
    slots = layers * 4
    pairs = leaves // 2
    cut = pairs // 2
    me = lax.axis_index("subtree").reshape(1)

    ordered, shared, first, last, table = skeletons_of(
        me, leaf_order, composition, leaf_basis, transfer, admissible_owner, admissible_leaf, layers
    )
    tables = jnp.asarray(near_tables(leaf_len))
    near_args = (near_list, leaf_order, tables, leaf_basis)

    line = along_z(shared, 1)
    from_x, from_y = over_x(shared), over_y(shared)
    own_blocks, my_other, turned_transfer = dense_couplings(
        table, coupling, top_coupling, transfer, slots
    )
    line = after(line, from_x, from_y, my_other)
    next_x, next_y = over_x(line), over_y(line)
    lines = [along_z(after(shared, my_other), layers - 1)]
    for _ in range(layers - 3):
        lines.append(along_z(line if len(lines) == 1 else lines[-1], 1))
    other_blocks = over_core(my_other)
    other_table = over_core(table)
    before = lax.ppermute(last, "subtree", [(d, d + 1) for d in range(count - 1)])
    behind = lax.ppermute(first, "subtree", [(d + 1, d) for d in range(count - 1)])
    round_0 = ((shared, line), (from_x, next_x), (from_y, next_y))
    far = onward(choose(me, (after(from_x, before, behind, other_table, *lines), next_x), round_0[2]))
    round_0 += ((far,),)
    held = after(ordered, next_x, next_y, before, behind, other_table, *lines)
    filled = near_field(list(range(1, cut)), *near_args, held)

    joined = join([after(lines[0], far, filled[0])] + lines[1:])
    last_x, last_y = over_x(joined), over_y(joined)
    held = after(ordered, joined)
    filled = near_field(list(range(cut, pairs - 1)), *near_args, held, filled=filled)
    filled = near_field([0, pairs - 1], *near_args, ordered, halos=(before, behind), filled=filled)
    blocks = (own_blocks, other_blocks)
    far = onward(choose(me, (after(last_x, filled[0]),), (last_y,)))
    sums = far_round([0, 1], slots, table, other_table, round_0, blocks, None)
    round_1 = ((joined,), (last_x,), (last_y,), (after(far, sums[0]),))
    sums = far_round(list(range(2, layers)), slots, table, other_table, round_1, blocks, sums)
    received = over_core(sums[1])
    return field(sums[0], received, turned_transfer, *filled)


def solution(mesh):
    placed = (
        P(("groups", "subtree"), None),
        P("subtree", None, None),
        P("subtree", None, None),
        P("subtree", None, None, None),
        P("subtree", None, None, None),
        P(("groups", "subtree"), None),
        P(("groups", "subtree"), None),
        P(("groups", "subtree"), None),
        P(("groups", "subtree"), None),
    )
    return jax.shard_map(
        on_device,
        mesh=mesh,
        in_specs=placed,
        out_specs=P(("groups", "subtree"), None),
        check_vma=False,
    )
```

```python
import functools

import jax
import jax.numpy as jnp
import ml_dtypes
import numpy as np
from jax import lax
from jax.experimental import pallas as pl
from jax.experimental.pallas import tpu as pltpu
from jax.sharding import PartitionSpec as P

COULOMB_SCALE = 0.15
SOFTENING = 0.25
BF = jnp.bfloat16
F32 = jnp.float32
MIB = 1 << 20


def near_tables(leaf_len):
    cells = np.arange(leaf_len)
    along = (cells // 64).astype(np.float32)
    across = (cells // 8 % 8).astype(np.float32)
    height = (cells % 8).astype(np.float32)
    extent = leaf_len // 64
    tables = []
    for offset in (-1, 0, 1):
        delta_x = along[:, None] - along[None, :] - np.float32(offset * extent)
        delta_y = across[:, None] - across[None, :]
        delta_z = height[:, None] - height[None, :]
        square = delta_x * delta_x + delta_y * delta_y + delta_z * delta_z
        value = np.float32(COULOMB_SCALE) / np.sqrt(square + np.float32(SOFTENING))
        tables.append(value.astype(ml_dtypes.bfloat16))
    return np.concatenate(tables, axis=1)


def send(block, target):
    count = lax.axis_size("subtree")
    return lax.ppermute(block, "subtree", [(d, target(d)) for d in range(count)])


def over_core(block):
    return send(block, lambda d: d ^ 1)


def over_x(block):
    return send(block, lambda d: d ^ 2)


def over_y(block):
    return send(block, lambda d: d ^ 4)


def onward(block):
    return send(block, lambda d: d ^ (2 if d % 2 else 4))


def along_z(block, step):
    layers = lax.axis_size("subtree") // 8
    return send(block, lambda d: (d // 8 + step) % layers * 8 + d % 8)


def params(mib):
    return pltpu.CompilerParams(vmem_limit_bytes=mib * MIB)


def cost(flops, moved):
    return pl.CostEstimate(flops=flops // 64, bytes_accessed=moved // 64, transcendentals=0)


def whole():
    return pl.BlockSpec(memory_space=pltpu.VMEM)


def scalars():
    return pl.BlockSpec(memory_space=pltpu.SMEM)


def dot(a, b):
    return jnp.dot(a, b, preferred_element_type=F32)


def in_hbm(*arrays):
    return [pltpu.with_memory_space_constraint(array, pltpu.HBM) for array in arrays]


def one_hot_leaf(row, leaf_len):
    column = jnp.broadcast_to(row, (128, leaf_len)).T
    lanes = lax.broadcasted_iota(jnp.int32, (leaf_len, 128), 1)
    return jnp.concatenate(
        [
            jnp.where(column == lanes + 128 * t, 1.0, 0.0).astype(BF)
            for t in range(leaf_len // 128)
        ],
        axis=1,
    )


def one_hot_grid(row, leaf_len):
    cells = lax.broadcasted_iota(jnp.int32, (leaf_len, leaf_len), 0)
    return jnp.where(cells == row, 1.0, 0.0).astype(BF)


def owner_tables(me, layers, owners, blocks):
    leaves, entries = owners.shape
    slots = layers * 4
    rows = leaves + 1
    shape = (rows, 2 * slots)
    lane = lax.broadcasted_iota(jnp.int32, shape, 1)
    plane = (lane >= slots).astype(jnp.int32)
    slot = lane - plane * slots
    layer, chip, core = me // 8, (me // 2) & 3, me & 1
    turn = slot >> 2
    shift = jnp.where(turn < 2, turn, jnp.where(turn == 2, layers - 1, turn - 1))
    source = layer - shift
    source = jnp.where(source < 0, source + layers, source)
    owner = source * 8 + (chip ^ (slot & 3)) * 2 + (core ^ plane)
    row = lax.broadcasted_iota(jnp.int32, shape, 0)
    distant = jnp.abs(owner - me) >= 2
    entry = jnp.where((row == 0) & distant, owner, -1)
    block = jnp.zeros(shape, jnp.int32)
    pad = jnp.full((1, entries), -1, jnp.int32)
    named = jnp.concatenate([pad, owners], axis=0)
    chosen = jnp.concatenate([pad, blocks], axis=0)
    for k in range(entries):
        match = named[:, k:k + 1] == owner
        entry = jnp.where(match, k, entry)
        block = jnp.where(match, chosen[:, k:k + 1] + 1, block)
    return entry, block


def skeleton_kernel(per, layers, me_ref, order_ref, comp_ref, basis_ref, transfer_ref,
                    owner_ref, leaf_ref, ordered_ref, shared_ref, first_ref, last_ref,
                    entry_ref, block_ref, root_ref):
    step = pl.program_id(0)
    leaf_len = basis_ref.shape[2]

    @pl.when(step == 0)
    def _():
        root_ref[...] = jnp.zeros_like(root_ref)
        entry, block = owner_tables(me_ref[0], layers, owner_ref[...], leaf_ref[...])
        rows, lanes = entry.shape
        entry_ref[:rows, :lanes] = entry
        block_ref[:rows, :lanes] = block

    hots = [one_hot_leaf(order_ref[pl.ds(step * per + i, 1), :], leaf_len) for i in range(per)]
    ordered = [
        dot(hots[i], comp_ref[i * leaf_len:(i + 1) * leaf_len, :]).astype(BF) for i in range(per)
    ]
    skeletons = [dot(basis_ref[i], ordered[i]).astype(BF) for i in range(per)]
    across = jnp.concatenate([transfer_ref[i] for i in range(per)], axis=1)
    root_ref[...] += dot(across, jnp.concatenate(skeletons, axis=0))
    for i in range(per):
        ordered_ref[i * leaf_len:(i + 1) * leaf_len, :] = ordered[i]
        shared_ref[pl.ds(step * per + i + 1, 1)] = skeletons[i][None]

    @pl.when(step == 0)
    def _():
        first_ref[...] = ordered[0]

    @pl.when(step == pl.num_programs(0) - 1)
    def _():
        last_ref[...] = ordered[-1]
        shared_ref[pl.ds(0, 1)] = root_ref[...].astype(BF)[None]


def skeletons_of(me, leaf_order, composition, leaf_basis, transfer, owners, blocks, layers, per=4):
    leaves, rank, leaf_len = leaf_basis.shape
    fields = composition.shape[1]
    entries = owners.shape[1]
    edge = jax.ShapeDtypeStruct((leaf_len, fields), BF)
    return pl.pallas_call(
        functools.partial(skeleton_kernel, per, layers),
        name="order_and_skeleton",
        grid=(leaves // per,),
        in_specs=[
            scalars(),
            pl.BlockSpec((leaves, leaf_len), lambda s: (0, 0)),
            pl.BlockSpec((per * leaf_len, fields), lambda s: (s, 0)),
            pl.BlockSpec((per, rank, leaf_len), lambda s: (s, 0, 0)),
            pl.BlockSpec((per, rank, rank), lambda s: (s, 0, 0)),
            pl.BlockSpec((leaves, entries), lambda s: (0, 0)),
            pl.BlockSpec((leaves, entries), lambda s: (0, 0)),
        ],
        out_specs=[
            pl.BlockSpec((per * leaf_len, fields), lambda s: (s, 0)),
            pl.BlockSpec((leaves + 1, rank, fields), lambda s: (0, 0, 0)),
            pl.BlockSpec((leaf_len, fields), lambda s: (0, 0)),
            pl.BlockSpec((leaf_len, fields), lambda s: (0, 0)),
            pl.BlockSpec((16, 128), lambda s: (0, 0)),
            pl.BlockSpec((16, 128), lambda s: (0, 0)),
        ],
        out_shape=[
            jax.ShapeDtypeStruct((leaves * leaf_len, fields), BF),
            jax.ShapeDtypeStruct((leaves + 1, rank, fields), BF),
            edge,
            edge,
            jax.ShapeDtypeStruct((16, 128), jnp.int32),
            jax.ShapeDtypeStruct((16, 128), jnp.int32),
        ],
        scratch_shapes=[pltpu.VMEM((rank, fields), F32)],
        compiler_params=params(16),
        cost_estimate=cost(leaves * leaf_len * leaf_len * fields * 2, 4 * MIB),
    )(me, *in_hbm(leaf_order, composition, leaf_basis, transfer, owners, blocks))


def join_kernel(*refs):
    out = refs[-1]
    at = 0
    for ref in refs[:-1]:
        out[at:at + ref.shape[0]] = ref[...]
        at += ref.shape[0]


def join(parts):
    if len(parts) == 1:
        return parts[0]
    shape = (sum(part.shape[0] for part in parts),) + parts[0].shape[1:]
    return pl.pallas_call(
        join_kernel,
        name="join",
        in_specs=[whole()] * len(parts),
        out_specs=whole(),
        out_shape=jax.ShapeDtypeStruct(shape, BF),
        compiler_params=params(8 if shape[0] <= 32 else 32),
        cost_estimate=cost(0, MIB // 2),
    )(*parts)


def choose_kernel(number, me_ref, *refs):
    ins, outs = refs[:2 * number], refs[2 * number:]
    for core in range(2):
        @pl.when(me_ref[0] % 2 == core)
        def _(core=core):
            at = 0
            for ref in ins[core * number:(core + 1) * number]:
                done = 0
                while done < ref.shape[0]:
                    out, base = outs[at // outs[0].shape[0]], at % outs[0].shape[0]
                    size = min(ref.shape[0] - done, out.shape[0] - base)
                    out[base:base + size] = ref[done:done + size]
                    done, at = done + size, at + size


def choose(me, from_x, from_y, streams):
    parts = list(from_x) + list(from_y)
    total = sum(part.shape[0] for part in from_x)
    shape = jax.ShapeDtypeStruct((total // streams,) + from_x[0].shape[1:], BF)
    return pl.pallas_call(
        functools.partial(choose_kernel, len(from_x)),
        name="choose",
        in_specs=[scalars()] + [whole()] * len(parts),
        out_specs=[whole()] * streams,
        out_shape=[shape] * streams,
        compiler_params=params(8 if total <= 32 else 32),
        cost_estimate=cost(0, MIB // 2),
    )(me, *parts)


def dense_kernel(per, slots, me_ref, entry_ref, block_ref, first_ref, last_ref, coupling_ref, top_ref,
                 transfer_ref, own_ref, other_ref, cross_ref, turned_ref):
    step = pl.program_id(0)
    rank = coupling_ref.shape[2]
    fields = first_ref.shape[1]
    leaves = own_ref.shape[0] - 1
    for i in range(per):
        turned_ref[step * per + i] = transfer_ref[i].T

    def fill(out_ref, plane, row, entry_row, block_of):
        for slot in range(0, slots, 2):
            pair = []
            for one in (slot, slot + 1):
                entry = entry_ref[entry_row, plane * slots + one]
                block = block_of(jnp.maximum(entry, 0))
                pair.append(jnp.where(entry >= 0, block, jnp.zeros_like(block)))
            out_ref[row, :, slot * rank:(slot + 2) * rank] = jnp.concatenate(pair, axis=1)

    for plane, out_ref in ((0, own_ref), (1, other_ref)):
        for i in range(per):
            leaf = step * per + i
            fill(out_ref, plane, leaf, leaf + 1, lambda entry, i=i: coupling_ref[i, entry])

        @pl.when(step == pl.num_programs(0) - 1)
        def _(plane=plane, out_ref=out_ref):
            fill(out_ref, plane, leaves, 0, lambda entry: top_ref[0, entry])

    @pl.when(step == 0)
    def _():
        even = me_ref[0] % 2 == 0
        first, last = first_ref[...], last_ref[...]
        cross_ref[...] = jnp.where(even, first, last)
        inner = jnp.where(even, last, first)
        for t in range(first.shape[0] // rank):
            other_ref[leaves + 1, :, t * fields:(t + 1) * fields] = inner[t * rank:(t + 1) * rank]
        other_ref[leaves + 2] = jnp.zeros(other_ref.shape[1:], BF)
        blocks = block_ref[...].astype(F32).astype(BF)
        other_ref[leaves + 2, :blocks.shape[0], :blocks.shape[1]] = blocks


def dense_couplings(me, entry, block, first, last, coupling, top_coupling, transfer, slots, per=4):
    leaves, entries, rank, _ = coupling.shape
    own = (leaves + 1, rank, slots * rank)
    other = (leaves + 3, rank, slots * rank)
    return pl.pallas_call(
        functools.partial(dense_kernel, per, slots),
        name="couplings_by_owner",
        grid=(leaves // per,),
        in_specs=[
            scalars(),
            scalars(),
            pl.BlockSpec(block.shape, lambda s: (0, 0)),
            pl.BlockSpec(first.shape, lambda s: (0, 0)),
            pl.BlockSpec(last.shape, lambda s: (0, 0)),
            pl.BlockSpec((per, entries, rank, rank), lambda s: (s, 0, 0, 0)),
            pl.BlockSpec(top_coupling.shape, lambda s: (0, 0, 0, 0)),
            pl.BlockSpec((per, rank, rank), lambda s: (s, 0, 0)),
        ],
        out_specs=[
            pl.BlockSpec(own, lambda s: (0, 0, 0)),
            pl.BlockSpec(other, lambda s: (0, 0, 0)),
            pl.BlockSpec(first.shape, lambda s: (0, 0)),
            pl.BlockSpec(transfer.shape, lambda s: (0, 0, 0)),
        ],
        out_shape=[
            jax.ShapeDtypeStruct(own, BF),
            jax.ShapeDtypeStruct(other, BF),
            jax.ShapeDtypeStruct(first.shape, BF),
            jax.ShapeDtypeStruct(transfer.shape, BF),
        ],
        compiler_params=params(16 if slots <= 16 else 48),
        cost_estimate=cost(0, 8 * MIB),
    )(me, entry, block, first, last, *in_hbm(coupling, top_coupling, transfer))


def round_kernel(plane, steps, slots, counts, at_ref, *refs):
    sides = []
    for number in counts:
        sides.append(refs[:number])
        refs = refs[number:]
    blocks_ref, out = refs[0], refs[-1]
    rows, rank, _ = out.shape
    low, high = steps[0] * 4 * rank, (steps[-1] + 1) * 4 * rank

    def block_at(side, base, index):
        for ref in side:
            if base < ref.shape[0]:
                return ref[base + index]
            base -= ref.shape[0]

    for row in range(rows):
        chosen = [
            block_at(side, place * rows, at_ref[(row + 1) % rows, plane * slots + step * 4 + q])
            for place, step in enumerate(steps)
            for q, side in enumerate(sides)
        ]
        value = dot(blocks_ref[row, :, low:high], jnp.concatenate(chosen, axis=0))
        if len(refs) > 2:
            value = value + refs[1][row]
        out[row] = value


def far_round(plane, steps, slots, at, parts, blocks, total=None):
    rank, fields = parts[0][0].shape[1:]
    rows = parts[0][0].shape[0] // (1 if len(parts[0]) > 1 else len(steps))
    args = [part for side in parts for part in side] + [blocks] + ([] if total is None else [total])
    return pl.pallas_call(
        functools.partial(round_kernel, plane, steps, slots, [len(side) for side in parts]),
        name="far_" + str(plane) + "_" + str(steps[0]),
        in_specs=[scalars()] + [whole()] * len(args),
        out_specs=whole(),
        out_shape=jax.ShapeDtypeStruct((rows, rank, fields), F32),
        compiler_params=params(16 if slots <= 16 else 48),
        cost_estimate=cost(rows * rank * 4 * rank * fields * 2 * len(steps), MIB),
    )(at, *args)


def near_kernel(edges, pair_of, last_pair, mask_ref, order_ref, table_ref, basis_ref,
                prev_ref, cur_ref, next_ref, *refs):
    if edges:
        me_ref, cross_ref, inner_ref, blocks_ref = refs[:4]
        near_ref, turned_ref, at_ref = refs[-3:]
    else:
        near_ref, turned_ref = refs[-2:]
    pair = pair_of(pl.program_id(0))
    leaf_len = basis_ref.shape[2]
    low, high = cur_ref[:leaf_len, :], cur_ref[leaf_len:, :]
    prev, following = prev_ref[...], next_ref[...]
    if edges:
        even = me_ref[0] % 2 == 0
        cross = cross_ref[...]
        wide = cross.shape[1]
        inner = jnp.concatenate(
            [inner_ref[0, :, t:t + wide] for t in range(0, inner_ref.shape[2], wide)], axis=0
        )[:leaf_len]
        prev = jnp.where(pair == 0, jnp.where(even, cross, inner), prev)
        following = jnp.where(pair == last_pair, jnp.where(even, inner, cross), following)

        @pl.when(pl.program_id(0) == 0)
        def _():
            rows, lanes = at_ref.shape
            at_ref[...] = blocks_ref[0, :rows, :lanes].astype(F32).astype(jnp.int32)


    def masked(leaf, side, value):
        return jnp.where(mask_ref[side, leaf] > 0, value, jnp.zeros_like(value))

    left = jnp.concatenate(
        [masked(2 * pair, 0, prev), low, masked(2 * pair, 1, high)], axis=0
    )
    right = jnp.concatenate(
        [masked(2 * pair + 1, 0, low), high, masked(2 * pair + 1, 1, following)], axis=0
    )
    near = dot(table_ref[...], jnp.concatenate([left, right], axis=1)).astype(BF)
    fields = cur_ref.shape[1]
    for i in range(2):
        hot = one_hot_grid(order_ref[pl.ds(2 * pair + i, 1), :], leaf_len)
        at = pl.ds(i * leaf_len, leaf_len)
        both = jnp.concatenate([near[:, i * fields:(i + 1) * fields], basis_ref[i].T], axis=1)
        moved = dot(hot, both).astype(BF)
        near_ref[at, :] = moved[:, :fields]
        turned_ref[at, :] = moved[:, fields:]


def near_field(pairs, near_list, leaf_order, tables, basis, ordered, halos=None, filled=None):
    leaves, rank, leaf_len = basis.shape
    fields = ordered.shape[1]
    last = leaves // 2 - 1
    gap = pairs[1] - pairs[0] if len(pairs) > 1 else 1

    def pair_of(step):
        return pairs[0] + gap * step

    in_specs = [
        scalars(),
        pl.BlockSpec((leaves, leaf_len), lambda s: (0, 0)),
        pl.BlockSpec(tables.shape, lambda s: (0, 0)),
        pl.BlockSpec((2, rank, leaf_len), lambda s: (pair_of(s), 0, 0)),
        pl.BlockSpec((leaf_len, fields), lambda s: (jnp.maximum(2 * pair_of(s) - 1, 0), 0)),
        pl.BlockSpec((2 * leaf_len, fields), lambda s: (pair_of(s), 0)),
        pl.BlockSpec((leaf_len, fields), lambda s: (jnp.minimum(2 * pair_of(s) + 2, leaves - 1), 0)),
    ]
    args = [near_list.T, leaf_order, tables, basis, ordered, ordered, ordered]
    aliases = {}
    extra = []
    if halos is not None:
        me, cross, other = halos
        row = (1,) + other.shape[1:]
        in_specs += [
            scalars(),
            pl.BlockSpec((leaf_len, fields), lambda s: (0, 0)),
            pl.BlockSpec(row, lambda s: (leaves + 1, 0, 0)),
            pl.BlockSpec(row, lambda s: (leaves + 2, 0, 0)),
        ]
        args += [me, cross, other, other]
        extra = [(16, 128)]
    if filled is not None:
        aliases = {len(args): 0, len(args) + 1: 1}
        in_specs += [pl.BlockSpec(memory_space=pl.ANY)] * 2
        args += list(filled)
    return pl.pallas_call(
        functools.partial(near_kernel, halos is not None, pair_of, last),
        name="near_" + str(pairs[0]),
        grid=(len(pairs),),
        in_specs=in_specs,
        out_specs=[
            pl.BlockSpec((2 * leaf_len, fields), lambda s: (pair_of(s), 0)),
            pl.BlockSpec((2 * leaf_len, rank), lambda s: (pair_of(s), 0)),
        ] + [pl.BlockSpec(shape, lambda s: (0, 0)) for shape in extra],
        out_shape=[
            jax.ShapeDtypeStruct((leaves * leaf_len, fields), BF),
            jax.ShapeDtypeStruct((leaves * leaf_len, rank), BF),
        ] + [jax.ShapeDtypeStruct(shape, jnp.int32) for shape in extra],
        input_output_aliases=aliases,
        compiler_params=params(16),
        cost_estimate=cost(len(pairs) * 2 * leaf_len * leaf_len * fields * 10, len(pairs) * MIB),
    )(*args)


def field_kernel(per, own_ref, other_ref, turned_transfer_ref, near_ref, turned_ref, out_ref):
    step = pl.program_id(0)
    leaf_len = near_ref.shape[0] // per
    root = own_ref.shape[0] - 1
    local = own_ref[root] + other_ref[root]
    coarse = local.astype(BF)
    fine = (local - coarse.astype(F32)).astype(BF)
    both = jnp.concatenate([coarse, fine], axis=1)
    fields = local.shape[1]
    for i in range(per):
        leaf = step * per + i
        down = dot(turned_transfer_ref[i], both)
        value = own_ref[leaf] + other_ref[leaf] + (down[:, :fields] + down[:, fields:])
        at = pl.ds(i * leaf_len, leaf_len)
        far = dot(turned_ref[at, :], value.astype(BF))
        out_ref[at, :] = (near_ref[at, :].astype(F32) + far).astype(BF)


def field(own, other, turned_transfer, near, turned, per=4):
    leaves, rank, _ = turned_transfer.shape
    fields = near.shape[1]
    leaf_len = near.shape[0] // leaves
    total = pl.BlockSpec(own.shape, lambda s: (0, 0, 0))
    return pl.pallas_call(
        functools.partial(field_kernel, per),
        name="local_and_field",
        grid=(leaves // per,),
        in_specs=[
            total,
            total,
            pl.BlockSpec((per, rank, rank), lambda s: (s, 0, 0)),
            pl.BlockSpec((per * leaf_len, fields), lambda s: (s, 0)),
            pl.BlockSpec((per * leaf_len, rank), lambda s: (s, 0)),
        ],
        out_specs=pl.BlockSpec((per * leaf_len, fields), lambda s: (s, 0)),
        out_shape=jax.ShapeDtypeStruct(near.shape, BF),
        compiler_params=params(16),
        cost_estimate=cost(leaves * leaf_len * rank * fields * 2, 4 * MIB),
    )(own, other, turned_transfer, near, turned)


def after(block, *others):
    return lax.optimization_barrier((block,) + others)[0]


def on_device(
    composition,
    leaf_basis,
    transfer,
    coupling,
    top_coupling,
    admissible_owner,
    admissible_leaf,
    near_list,
    leaf_order,
):
    leaves, rank, leaf_len = leaf_basis.shape
    count = lax.axis_size("subtree")
    layers = count // 8
    slots = layers * 4
    pairs = leaves // 2
    cut = pairs // 2
    me = lax.axis_index("subtree").reshape(1)

    ordered, shared, first, last, entry, own_at = skeletons_of(
        me, leaf_order, composition, leaf_basis, transfer, admissible_owner, admissible_leaf, layers
    )
    tables = jnp.asarray(near_tables(leaf_len))
    near_args = (near_list, leaf_order, tables, leaf_basis)

    line = along_z(shared, 1)
    from_x, from_y = over_x(shared), over_y(shared)
    lines = [along_z(shared, layers - 1)]
    own_blocks, my_other, cross, turned_transfer = dense_couplings(
        me, entry, own_at, first, last, coupling, top_coupling, transfer, slots
    )
    line = after(line, from_x, from_y, lines[0], my_other)
    next_x, next_y = over_x(line), over_y(line)
    for _ in range(layers - 3):
        lines.append(along_z(line if len(lines) == 1 else lines[-1], 1))
    filled = near_field(list(range(1, cut)), *near_args, after(ordered, line))

    joined = join([after(lines[0], next_x, next_y, filled[0])] + lines[1:])
    last_x, last_y = over_x(joined), over_y(joined)
    round_0 = ((shared, line), (from_x, next_x), (from_y, next_y))
    round_0 += (tuple(map(onward, choose(me, *round_0[1:], 1))),)
    other_blocks = over_core(after(my_other, joined))
    cross = lax.ppermute(
        cross,
        "subtree",
        [(d, d + 1) for d in range(1, count - 1, 2)] + [(d, d - 1) for d in range(2, count, 2)],
    )
    held = after(ordered, joined)
    filled = near_field(list(range(cut, pairs - 1)), *near_args, held, filled=filled)
    far = tuple(map(onward, choose(me, (after(last_x, filled[0], cross),), (last_y,), 2)))
    *filled, other_at = near_field(
        [0, pairs - 1], *near_args, after(ordered, filled[0]), halos=(me, cross, other_blocks), filled=filled
    )
    steps = [0, 1]
    own = far_round(0, steps, slots, own_at, round_0, own_blocks)
    other = far_round(1, steps, slots, other_at, round_0, other_blocks)
    steps = list(range(2, layers))
    round_1 = ((joined,), (last_x,), (last_y,), (after(far[0], own, other),) + far[1:])
    other = far_round(1, steps, slots, other_at, round_1, other_blocks, other)
    own = far_round(0, steps, slots, own_at, round_1, own_blocks, own)
    return field(own, over_core(other), turned_transfer, *filled)


def solution(mesh):
    placed = (
        P(("groups", "subtree"), None),
        P("subtree", None, None),
        P("subtree", None, None),
        P("subtree", None, None, None),
        P("subtree", None, None, None),
        P(("groups", "subtree"), None),
        P(("groups", "subtree"), None),
        P(("groups", "subtree"), None),
        P(("groups", "subtree"), None),
    )
    return jax.shard_map(
        on_device,
        mesh=mesh,
        in_specs=placed,
        out_specs=P(("groups", "subtree"), None),
        check_vma=False,
    )
```

```python
import functools

import jax
import jax.numpy as jnp
import ml_dtypes
import numpy as np
from jax import lax
from jax.experimental import pallas as pl
from jax.experimental.pallas import tpu as pltpu
from jax.sharding import PartitionSpec as P

COULOMB_SCALE = 0.15
SOFTENING = 0.25
BF = jnp.bfloat16
F32 = jnp.float32
MIB = 1 << 20


def near_tables(leaf_len):
    cells = np.arange(leaf_len)
    along = (cells // 64).astype(np.float32)
    across = (cells // 8 % 8).astype(np.float32)
    height = (cells % 8).astype(np.float32)
    extent = leaf_len // 64
    tables = []
    for offset in (-1, 0, 1):
        delta_x = along[:, None] - along[None, :] - np.float32(offset * extent)
        delta_y = across[:, None] - across[None, :]
        delta_z = height[:, None] - height[None, :]
        square = delta_x * delta_x + delta_y * delta_y + delta_z * delta_z
        value = np.float32(COULOMB_SCALE) / np.sqrt(square + np.float32(SOFTENING))
        tables.append(value.astype(ml_dtypes.bfloat16))
    return np.concatenate(tables, axis=1)


def send(block, target):
    count = lax.axis_size("subtree")
    return lax.ppermute(block, "subtree", [(d, target(d)) for d in range(count)])


def over_core(block):
    return send(block, lambda d: d ^ 1)


def over_x(block):
    return send(block, lambda d: d ^ 2)


def over_y(block):
    return send(block, lambda d: d ^ 4)


def onward(block):
    return send(block, lambda d: d ^ (2 if d % 2 else 4))


def along_z(block, step):
    layers = lax.axis_size("subtree") // 8
    return send(block, lambda d: (d // 8 + step) % layers * 8 + d % 8)


def params(mib):
    return pltpu.CompilerParams(vmem_limit_bytes=mib * MIB)


def cost(flops, moved):
    return pl.CostEstimate(flops=flops // 64, bytes_accessed=moved // 64, transcendentals=0)


def whole():
    return pl.BlockSpec(memory_space=pltpu.VMEM)


def scalars():
    return pl.BlockSpec(memory_space=pltpu.SMEM)


def dot(a, b):
    return jnp.dot(a, b, preferred_element_type=F32)


def in_hbm(*arrays):
    return [pltpu.with_memory_space_constraint(array, pltpu.HBM) for array in arrays]


def one_hot_leaf(row, leaf_len):
    column = jnp.broadcast_to(row, (128, leaf_len)).T
    lanes = lax.broadcasted_iota(jnp.int32, (leaf_len, 128), 1)
    return jnp.concatenate(
        [
            jnp.where(column == lanes + 128 * t, 1.0, 0.0).astype(BF)
            for t in range(leaf_len // 128)
        ],
        axis=1,
    )


def one_hot_grid(row, leaf_len):
    cells = lax.broadcasted_iota(jnp.int32, (leaf_len, leaf_len), 0)
    return jnp.where(cells == row, 1.0, 0.0).astype(BF)


def owner_tables(me, layers, owners, blocks):
    leaves, entries = owners.shape
    slots = layers * 4
    rows = leaves + 1
    shape = (rows, 2 * slots)
    lane = lax.broadcasted_iota(jnp.int32, shape, 1)
    plane = (lane >= slots).astype(jnp.int32)
    slot = lane - plane * slots
    layer, chip, core = me // 8, (me // 2) & 3, me & 1
    turn = slot >> 2
    shift = jnp.where(turn < 2, turn, jnp.where(turn == 2, layers - 1, turn - 1))
    source = layer - shift
    source = jnp.where(source < 0, source + layers, source)
    owner = source * 8 + (chip ^ (slot & 3)) * 2 + (core ^ plane)
    row = lax.broadcasted_iota(jnp.int32, shape, 0)
    distant = jnp.abs(owner - me) >= 2
    entry = jnp.where((row == 0) & distant, owner, -1)
    block = jnp.zeros(shape, jnp.int32)
    pad = jnp.full((1, entries), -1, jnp.int32)
    named = jnp.concatenate([pad, owners], axis=0)
    chosen = jnp.concatenate([pad, blocks], axis=0)
    for k in range(entries):
        match = named[:, k:k + 1] == owner
        entry = jnp.where(match, k, entry)
        block = jnp.where(match, chosen[:, k:k + 1] + 1, block)
    return entry, block


def skeleton_kernel(per, layers, me_ref, order_ref, comp_ref, basis_ref, transfer_ref,
                    owner_ref, leaf_ref, ordered_ref, shared_ref, cross_ref, inner_ref,
                    entry_ref, block_ref, root_ref):
    step = pl.program_id(0)
    leaf_len = basis_ref.shape[2]

    @pl.when(step == 0)
    def _():
        root_ref[...] = jnp.zeros_like(root_ref)
        entry, block = owner_tables(me_ref[0], layers, owner_ref[...], leaf_ref[...])
        rows, lanes = entry.shape
        entry_ref[:rows, :lanes] = entry
        block_ref[:rows, :lanes] = block

    hots = [one_hot_leaf(order_ref[pl.ds(step * per + i, 1), :], leaf_len) for i in range(per)]
    ordered = [
        dot(hots[i], comp_ref[i * leaf_len:(i + 1) * leaf_len, :]).astype(BF) for i in range(per)
    ]
    skeletons = [dot(basis_ref[i], ordered[i]).astype(BF) for i in range(per)]
    across = jnp.concatenate([transfer_ref[i] for i in range(per)], axis=1)
    root_ref[...] += dot(across, jnp.concatenate(skeletons, axis=0))
    for i in range(per):
        ordered_ref[i * leaf_len:(i + 1) * leaf_len, :] = ordered[i]
        shared_ref[pl.ds(step * per + i + 1, 1)] = skeletons[i][None]

    even = me_ref[0] % 2 == 0

    @pl.when((step == 0) & even)
    def _():
        cross_ref[...] = ordered[0]

    @pl.when((step == 0) & ~even)
    def _():
        inner_ref[...] = ordered[0]

    last = step == pl.num_programs(0) - 1

    @pl.when(last & even)
    def _():
        inner_ref[...] = ordered[-1]

    @pl.when(last & ~even)
    def _():
        cross_ref[...] = ordered[-1]

    @pl.when(last)
    def _():
        shared_ref[pl.ds(0, 1)] = root_ref[...].astype(BF)[None]


def skeletons_of(me, leaf_order, composition, leaf_basis, transfer, owners, blocks, layers, per=4):
    leaves, rank, leaf_len = leaf_basis.shape
    fields = composition.shape[1]
    entries = owners.shape[1]
    edge = jax.ShapeDtypeStruct((leaf_len, fields), BF)
    return pl.pallas_call(
        functools.partial(skeleton_kernel, per, layers),
        name="order_and_skeleton",
        grid=(leaves // per,),
        in_specs=[
            scalars(),
            pl.BlockSpec((leaves, leaf_len), lambda s: (0, 0)),
            pl.BlockSpec((per * leaf_len, fields), lambda s: (s, 0)),
            pl.BlockSpec((per, rank, leaf_len), lambda s: (s, 0, 0)),
            pl.BlockSpec((per, rank, rank), lambda s: (s, 0, 0)),
            pl.BlockSpec((leaves, entries), lambda s: (0, 0)),
            pl.BlockSpec((leaves, entries), lambda s: (0, 0)),
        ],
        out_specs=[
            pl.BlockSpec((per * leaf_len, fields), lambda s: (s, 0)),
            pl.BlockSpec((leaves + 1, rank, fields), lambda s: (0, 0, 0)),
            pl.BlockSpec((leaf_len, fields), lambda s: (0, 0)),
            pl.BlockSpec((leaf_len, fields), lambda s: (0, 0)),
            pl.BlockSpec((16, 128), lambda s: (0, 0)),
            pl.BlockSpec((16, 128), lambda s: (0, 0)),
        ],
        out_shape=[
            jax.ShapeDtypeStruct((leaves * leaf_len, fields), BF),
            jax.ShapeDtypeStruct((leaves + 1, rank, fields), BF),
            edge,
            edge,
            jax.ShapeDtypeStruct((16, 128), jnp.int32),
            jax.ShapeDtypeStruct((16, 128), jnp.int32),
        ],
        scratch_shapes=[pltpu.VMEM((rank, fields), F32)],
        compiler_params=params(16),
        cost_estimate=cost(leaves * leaf_len * leaf_len * fields * 2, 4 * MIB),
    )(me, *in_hbm(leaf_order, composition, leaf_basis, transfer, owners, blocks))


def join_kernel(*refs):
    out = refs[-1]
    at = 0
    for ref in refs[:-1]:
        out[at:at + ref.shape[0]] = ref[...]
        at += ref.shape[0]


def join(parts):
    if len(parts) == 1:
        return parts[0]
    shape = (sum(part.shape[0] for part in parts),) + parts[0].shape[1:]
    return pl.pallas_call(
        join_kernel,
        name="join",
        in_specs=[whole()] * len(parts),
        out_specs=whole(),
        out_shape=jax.ShapeDtypeStruct(shape, BF),
        compiler_params=params(8 if shape[0] <= 32 else 32),
        cost_estimate=cost(0, MIB // 2),
    )(*parts)


def choose_kernel(number, me_ref, *refs):
    ins, outs = refs[:2 * number], refs[2 * number:]
    for core in range(2):
        @pl.when(me_ref[0] % 2 == core)
        def _(core=core):
            at = 0
            for ref in ins[core * number:(core + 1) * number]:
                done = 0
                while done < ref.shape[0]:
                    out, base = outs[at // outs[0].shape[0]], at % outs[0].shape[0]
                    size = min(ref.shape[0] - done, out.shape[0] - base)
                    out[base:base + size] = ref[done:done + size]
                    done, at = done + size, at + size


def choose(me, from_x, from_y, streams):
    parts = list(from_x) + list(from_y)
    total = sum(part.shape[0] for part in from_x)
    shape = jax.ShapeDtypeStruct((total // streams,) + from_x[0].shape[1:], BF)
    return pl.pallas_call(
        functools.partial(choose_kernel, len(from_x)),
        name="choose",
        in_specs=[scalars()] + [whole()] * len(parts),
        out_specs=[whole()] * streams,
        out_shape=[shape] * streams,
        compiler_params=params(8 if total <= 32 else 32),
        cost_estimate=cost(0, MIB // 2),
    )(me, *parts)


def dense_kernel(per, slots, entry_ref, block_ref, inner_ref, coupling_ref, top_ref,
                 transfer_ref, own_ref, other_ref, turned_ref):
    step = pl.program_id(0)
    rank = coupling_ref.shape[2]
    fields = inner_ref.shape[1]
    leaves = own_ref.shape[0] - 1
    for i in range(per):
        turned_ref[step * per + i] = transfer_ref[i].T

    def fill(out_ref, plane, row, entry_row, block_of):
        for slot in range(0, slots, 2):
            pair = []
            for one in (slot, slot + 1):
                entry = entry_ref[entry_row, plane * slots + one]
                block = block_of(jnp.maximum(entry, 0))
                pair.append(jnp.where(entry >= 0, block, jnp.zeros_like(block)))
            out_ref[row, :, slot * rank:(slot + 2) * rank] = jnp.concatenate(pair, axis=1)

    for plane, out_ref in ((0, own_ref), (1, other_ref)):
        for i in range(per):
            leaf = step * per + i
            fill(out_ref, plane, leaf, leaf + 1, lambda entry, i=i: coupling_ref[i, entry])

        @pl.when(step == pl.num_programs(0) - 1)
        def _(plane=plane, out_ref=out_ref):
            fill(out_ref, plane, leaves, 0, lambda entry: top_ref[0, entry])

    @pl.when(step == 0)
    def _():
        for t in range(inner_ref.shape[0] // rank):
            part = inner_ref[t * rank:(t + 1) * rank, :]
            other_ref[leaves + 1, :, t * fields:(t + 1) * fields] = part
        other_ref[leaves + 2] = jnp.zeros(other_ref.shape[1:], BF)
        blocks = block_ref[...].astype(F32).astype(BF)
        other_ref[leaves + 2, :blocks.shape[0], :blocks.shape[1]] = blocks


def dense_couplings(entry, block, inner, coupling, top_coupling, transfer, slots, per=4):
    leaves, entries, rank, _ = coupling.shape
    own = (leaves + 1, rank, slots * rank)
    other = (leaves + 3, rank, slots * rank)
    return pl.pallas_call(
        functools.partial(dense_kernel, per, slots),
        name="couplings_by_owner",
        grid=(leaves // per,),
        in_specs=[
            scalars(),
            pl.BlockSpec(block.shape, lambda s: (0, 0)),
            pl.BlockSpec(inner.shape, lambda s: (0, 0)),
            pl.BlockSpec((per, entries, rank, rank), lambda s: (s, 0, 0, 0)),
            pl.BlockSpec(top_coupling.shape, lambda s: (0, 0, 0, 0)),
            pl.BlockSpec((per, rank, rank), lambda s: (s, 0, 0)),
        ],
        out_specs=[
            pl.BlockSpec(own, lambda s: (0, 0, 0)),
            pl.BlockSpec(other, lambda s: (0, 0, 0)),
            pl.BlockSpec(transfer.shape, lambda s: (0, 0, 0)),
        ],
        out_shape=[
            jax.ShapeDtypeStruct(own, BF),
            jax.ShapeDtypeStruct(other, BF),
            jax.ShapeDtypeStruct(transfer.shape, BF),
        ],
        compiler_params=params(16 if slots <= 16 else 48),
        cost_estimate=cost(0, 8 * MIB),
    )(entry, block, inner, *in_hbm(coupling, top_coupling, transfer))


def round_kernel(plane, steps, slots, counts, at_ref, *refs):
    sides = []
    for number in counts:
        sides.append(refs[:number])
        refs = refs[number:]
    blocks_ref, out = refs[0], refs[-1]
    rows, rank, _ = out.shape
    low, high = steps[0] * 4 * rank, (steps[-1] + 1) * 4 * rank

    def block_at(side, base, index):
        for ref in side:
            if base < ref.shape[0]:
                return ref[base + index]
            base -= ref.shape[0]

    for row in range(rows):
        chosen = [
            block_at(side, place * rows, at_ref[(row + 1) % rows, plane * slots + step * 4 + q])
            for place, step in enumerate(steps)
            for q, side in enumerate(sides)
        ]
        value = dot(blocks_ref[row, :, low:high], jnp.concatenate(chosen, axis=0))
        if len(refs) > 2:
            value = value + refs[1][row]
        out[row] = value


def far_round(plane, steps, slots, at, parts, blocks, total=None):
    rank, fields = parts[0][0].shape[1:]
    rows = parts[0][0].shape[0] // (1 if len(parts[0]) > 1 else len(steps))
    args = [part for side in parts for part in side] + [blocks] + ([] if total is None else [total])
    return pl.pallas_call(
        functools.partial(round_kernel, plane, steps, slots, [len(side) for side in parts]),
        name="far_" + str(plane) + "_" + str(steps[0]),
        in_specs=[scalars()] + [whole()] * len(args),
        out_specs=whole(),
        out_shape=jax.ShapeDtypeStruct((rows, rank, fields), F32),
        compiler_params=params(16 if slots <= 16 else 48),
        cost_estimate=cost(rows * rank * 4 * rank * fields * 2 * len(steps), MIB),
    )(at, *args)


def near_kernel(edges, pair_of, last_pair, mask_ref, order_ref, table_ref, basis_ref,
                prev_ref, cur_ref, next_ref, *refs):
    if edges:
        me_ref, cross_ref, inner_ref, blocks_ref = refs[:4]
        near_ref, turned_ref, at_ref = refs[-3:]
    else:
        near_ref, turned_ref = refs[-2:]
    pair = pair_of(pl.program_id(0))
    leaf_len = basis_ref.shape[2]
    low, high = cur_ref[:leaf_len, :], cur_ref[leaf_len:, :]
    prev, following = prev_ref[...], next_ref[...]
    if edges:
        even = me_ref[0] % 2 == 0
        cross = cross_ref[...]
        wide = cross.shape[1]
        inner = jnp.concatenate(
            [inner_ref[0, :, t:t + wide] for t in range(0, inner_ref.shape[2], wide)], axis=0
        )[:leaf_len]
        prev = jnp.where(pair == 0, jnp.where(even, cross, inner), prev)
        following = jnp.where(pair == last_pair, jnp.where(even, inner, cross), following)

        @pl.when(pl.program_id(0) == 0)
        def _():
            rows, lanes = at_ref.shape
            at_ref[...] = blocks_ref[0, :rows, :lanes].astype(F32).astype(jnp.int32)


    def masked(leaf, side, value):
        return jnp.where(mask_ref[side, leaf] > 0, value, jnp.zeros_like(value))

    left = jnp.concatenate(
        [masked(2 * pair, 0, prev), low, masked(2 * pair, 1, high)], axis=0
    )
    right = jnp.concatenate(
        [masked(2 * pair + 1, 0, low), high, masked(2 * pair + 1, 1, following)], axis=0
    )
    near = dot(table_ref[...], jnp.concatenate([left, right], axis=1)).astype(BF)
    fields = cur_ref.shape[1]
    for i in range(2):
        hot = one_hot_grid(order_ref[pl.ds(2 * pair + i, 1), :], leaf_len)
        at = pl.ds(i * leaf_len, leaf_len)
        both = jnp.concatenate([near[:, i * fields:(i + 1) * fields], basis_ref[i].T], axis=1)
        moved = dot(hot, both).astype(BF)
        near_ref[at, :] = moved[:, :fields]
        turned_ref[at, :] = moved[:, fields:]


def near_field(pairs, near_list, leaf_order, tables, basis, ordered, halos=None, filled=None):
    leaves, rank, leaf_len = basis.shape
    fields = ordered.shape[1]
    last = leaves // 2 - 1
    gap = pairs[1] - pairs[0] if len(pairs) > 1 else 1

    def pair_of(step):
        return pairs[0] + gap * step

    in_specs = [
        scalars(),
        pl.BlockSpec((leaves, leaf_len), lambda s: (0, 0)),
        pl.BlockSpec(tables.shape, lambda s: (0, 0)),
        pl.BlockSpec((2, rank, leaf_len), lambda s: (pair_of(s), 0, 0)),
        pl.BlockSpec((leaf_len, fields), lambda s: (jnp.maximum(2 * pair_of(s) - 1, 0), 0)),
        pl.BlockSpec((2 * leaf_len, fields), lambda s: (pair_of(s), 0)),
        pl.BlockSpec((leaf_len, fields), lambda s: (jnp.minimum(2 * pair_of(s) + 2, leaves - 1), 0)),
    ]
    args = [near_list.T, leaf_order, tables, basis, ordered, ordered, ordered]
    aliases = {}
    extra = []
    if halos is not None:
        me, cross, other = halos
        row = (1,) + other.shape[1:]
        in_specs += [
            scalars(),
            pl.BlockSpec((leaf_len, fields), lambda s: (0, 0)),
            pl.BlockSpec(row, lambda s: (leaves + 1, 0, 0)),
            pl.BlockSpec(row, lambda s: (leaves + 2, 0, 0)),
        ]
        args += [me, cross, other, other]
        extra = [(16, 128)]
    if filled is not None:
        aliases = {len(args): 0, len(args) + 1: 1}
        in_specs += [pl.BlockSpec(memory_space=pl.ANY)] * 2
        args += list(filled)
    return pl.pallas_call(
        functools.partial(near_kernel, halos is not None, pair_of, last),
        name="near_" + str(pairs[0]),
        grid=(len(pairs),),
        in_specs=in_specs,
        out_specs=[
            pl.BlockSpec((2 * leaf_len, fields), lambda s: (pair_of(s), 0)),
            pl.BlockSpec((2 * leaf_len, rank), lambda s: (pair_of(s), 0)),
        ] + [pl.BlockSpec(shape, lambda s: (0, 0)) for shape in extra],
        out_shape=[
            jax.ShapeDtypeStruct((leaves * leaf_len, fields), BF),
            jax.ShapeDtypeStruct((leaves * leaf_len, rank), BF),
        ] + [jax.ShapeDtypeStruct(shape, jnp.int32) for shape in extra],
        input_output_aliases=aliases,
        compiler_params=params(16),
        cost_estimate=cost(len(pairs) * 2 * leaf_len * leaf_len * fields * 10, len(pairs) * MIB),
    )(*args)


def field_kernel(per, own_ref, other_ref, turned_transfer_ref, near_ref, turned_ref, out_ref):
    step = pl.program_id(0)
    leaf_len = near_ref.shape[0] // per
    root = own_ref.shape[0] - 1
    local = own_ref[root] + other_ref[root]
    coarse = local.astype(BF)
    fine = (local - coarse.astype(F32)).astype(BF)
    both = jnp.concatenate([coarse, fine], axis=1)
    fields = local.shape[1]
    for i in range(per):
        leaf = step * per + i
        down = dot(turned_transfer_ref[i], both)
        value = own_ref[leaf] + other_ref[leaf] + (down[:, :fields] + down[:, fields:])
        at = pl.ds(i * leaf_len, leaf_len)
        far = dot(turned_ref[at, :], value.astype(BF))
        out_ref[at, :] = (near_ref[at, :].astype(F32) + far).astype(BF)


def field(own, other, turned_transfer, near, turned, per=4):
    leaves, rank, _ = turned_transfer.shape
    fields = near.shape[1]
    leaf_len = near.shape[0] // leaves
    total = pl.BlockSpec(own.shape, lambda s: (0, 0, 0))
    return pl.pallas_call(
        functools.partial(field_kernel, per),
        name="local_and_field",
        grid=(leaves // per,),
        in_specs=[
            total,
            total,
            pl.BlockSpec((per, rank, rank), lambda s: (s, 0, 0)),
            pl.BlockSpec((per * leaf_len, fields), lambda s: (s, 0)),
            pl.BlockSpec((per * leaf_len, rank), lambda s: (s, 0)),
        ],
        out_specs=pl.BlockSpec((per * leaf_len, fields), lambda s: (s, 0)),
        out_shape=jax.ShapeDtypeStruct(near.shape, BF),
        compiler_params=params(16),
        cost_estimate=cost(leaves * leaf_len * rank * fields * 2, 4 * MIB),
    )(own, other, turned_transfer, near, turned)


def after(block, *others):
    return lax.optimization_barrier((block,) + others)[0]


def on_device(
    composition,
    leaf_basis,
    transfer,
    coupling,
    top_coupling,
    admissible_owner,
    admissible_leaf,
    near_list,
    leaf_order,
):
    leaves, rank, leaf_len = leaf_basis.shape
    count = lax.axis_size("subtree")
    layers = count // 8
    slots = layers * 4
    pairs = leaves // 2
    cut = pairs // 2
    me = lax.axis_index("subtree").reshape(1)

    ordered, shared, cross, inner, entry, own_at = skeletons_of(
        me, leaf_order, composition, leaf_basis, transfer, admissible_owner, admissible_leaf, layers
    )
    tables = jnp.asarray(near_tables(leaf_len))
    near_args = (near_list, leaf_order, tables, leaf_basis)

    line = along_z(shared, 1)
    from_x, from_y = over_x(shared), over_y(shared)
    filled = near_field(list(range(1, cut)), *near_args, ordered)
    line = after(line, from_x, from_y, filled[0])
    next_x, next_y = over_x(line), over_y(line)
    lines = [along_z(after(shared, line), layers - 1)]
    for _ in range(layers - 3):
        lines.append(along_z(line if len(lines) == 1 else lines[-1], 1))
    cross = lax.ppermute(
        cross,
        "subtree",
        [(d, d + 1) for d in range(1, count - 1, 2)] + [(d, d - 1) for d in range(2, count, 2)],
    )
    own_blocks, my_other, turned_transfer = dense_couplings(
        after(entry, line), own_at, inner, coupling, top_coupling, transfer, slots
    )

    joined = join([after(lines[0], next_x, next_y, cross, my_other)] + lines[1:])
    last_x, last_y = over_x(joined), over_y(joined)
    round_0 = ((shared, line), (from_x, next_x), (from_y, next_y))
    chosen = choose(me, (after(from_x, joined), next_x), round_0[2], 1)
    round_0 += (tuple(map(onward, chosen)),)
    other_blocks = over_core(after(my_other, *chosen))
    held = after(ordered, joined)
    filled = near_field(list(range(cut, pairs - 1)), *near_args, held, filled=filled)
    far = tuple(map(onward, choose(me, (after(last_x, filled[0]),), (last_y,), 2)))
    *filled, other_at = near_field(
        [0, pairs - 1], *near_args, after(ordered, filled[0]), halos=(me, cross, other_blocks), filled=filled
    )
    steps = [0, 1]
    own = far_round(0, steps, slots, own_at, round_0, own_blocks)
    other = far_round(1, steps, slots, other_at, round_0, other_blocks)
    steps = list(range(2, layers))
    round_1 = ((joined,), (last_x,), (last_y,), (after(far[0], own, other),) + far[1:])
    other = far_round(1, steps, slots, other_at, round_1, other_blocks, other)
    own = far_round(0, steps, slots, own_at, round_1, own_blocks, own)
    return field(own, over_core(other), turned_transfer, *filled)


def solution(mesh):
    placed = (
        P(("groups", "subtree"), None),
        P("subtree", None, None),
        P("subtree", None, None),
        P("subtree", None, None, None),
        P("subtree", None, None, None),
        P(("groups", "subtree"), None),
        P(("groups", "subtree"), None),
        P(("groups", "subtree"), None),
        P(("groups", "subtree"), None),
    )
    return jax.shard_map(
        on_device,
        mesh=mesh,
        in_specs=placed,
        out_specs=P(("groups", "subtree"), None),
        check_vma=False,
    )
```

```python
import functools

import jax
import jax.numpy as jnp
import ml_dtypes
import numpy as np
from jax import lax
from jax.experimental import pallas as pl
from jax.experimental.pallas import tpu as pltpu
from jax.sharding import PartitionSpec as P

COULOMB_SCALE = 0.15
SOFTENING = 0.25
BF = jnp.bfloat16
F32 = jnp.float32
MIB = 1 << 20


def near_tables(leaf_len):
    cells = np.arange(leaf_len)
    along = (cells // 64).astype(np.float32)
    across = (cells // 8 % 8).astype(np.float32)
    height = (cells % 8).astype(np.float32)
    extent = leaf_len // 64
    tables = []
    for offset in (-1, 0, 1):
        delta_x = along[:, None] - along[None, :] - np.float32(offset * extent)
        delta_y = across[:, None] - across[None, :]
        delta_z = height[:, None] - height[None, :]
        square = delta_x * delta_x + delta_y * delta_y + delta_z * delta_z
        value = np.float32(COULOMB_SCALE) / np.sqrt(square + np.float32(SOFTENING))
        tables.append(value.astype(ml_dtypes.bfloat16))
    return np.concatenate(tables, axis=1)


def send(block, target):
    count = lax.axis_size("subtree")
    return lax.ppermute(block, "subtree", [(d, target(d)) for d in range(count)])


def over_core(block):
    return send(block, lambda d: d ^ 1)


def over_x(block):
    return send(block, lambda d: d ^ 2)


def over_y(block):
    return send(block, lambda d: d ^ 4)


def onward(block):
    return send(block, lambda d: d ^ (2 if d % 2 else 4))


def along_z(block, step):
    layers = lax.axis_size("subtree") // 8
    return send(block, lambda d: (d // 8 + step) % layers * 8 + d % 8)


def params(mib):
    return pltpu.CompilerParams(vmem_limit_bytes=mib * MIB)


def cost(flops, moved):
    return pl.CostEstimate(flops=flops // 64, bytes_accessed=moved // 64, transcendentals=0)


def whole():
    return pl.BlockSpec(memory_space=pltpu.VMEM)


def scalars():
    return pl.BlockSpec(memory_space=pltpu.SMEM)


def dot(a, b):
    return jnp.dot(a, b, preferred_element_type=F32)


def in_hbm(*arrays):
    return [pltpu.with_memory_space_constraint(array, pltpu.HBM) for array in arrays]


def one_hot_leaf(row, leaf_len):
    column = jnp.broadcast_to(row, (128, leaf_len)).T
    lanes = lax.broadcasted_iota(jnp.int32, (leaf_len, 128), 1)
    return jnp.concatenate(
        [
            jnp.where(column == lanes + 128 * t, 1.0, 0.0).astype(BF)
            for t in range(leaf_len // 128)
        ],
        axis=1,
    )


def one_hot_grid(row, leaf_len):
    cells = lax.broadcasted_iota(jnp.int32, (leaf_len, leaf_len), 0)
    return jnp.where(cells == row, 1.0, 0.0).astype(BF)


def owner_tables(me, layers, owners, blocks):
    leaves, entries = owners.shape
    slots = layers * 4
    rows = leaves + 1
    shape = (rows, 2 * slots)
    lane = lax.broadcasted_iota(jnp.int32, shape, 1)
    plane = (lane >= slots).astype(jnp.int32)
    slot = lane - plane * slots
    layer, chip, core = me // 8, (me // 2) & 3, me & 1
    turn = slot >> 2
    shift = jnp.where(turn < 2, turn, jnp.where(turn == 2, layers - 1, turn - 1))
    source = layer - shift
    source = jnp.where(source < 0, source + layers, source)
    owner = source * 8 + (chip ^ (slot & 3)) * 2 + (core ^ plane)
    row = lax.broadcasted_iota(jnp.int32, shape, 0)
    distant = jnp.abs(owner - me) >= 2
    entry = jnp.where((row == 0) & distant, owner, -1)
    block = jnp.zeros(shape, jnp.int32)
    pad = jnp.full((1, entries), -1, jnp.int32)
    named = jnp.concatenate([pad, owners], axis=0)
    chosen = jnp.concatenate([pad, blocks], axis=0)
    for k in range(entries):
        match = named[:, k:k + 1] == owner
        entry = jnp.where(match, k, entry)
        block = jnp.where(match, chosen[:, k:k + 1] + 1, block)
    return entry, block


def skeleton_kernel(per, layers, me_ref, order_ref, comp_ref, basis_ref, transfer_ref,
                    owner_ref, leaf_ref, ordered_ref, shared_ref, cross_ref, inner_ref,
                    entry_ref, block_ref, root_ref):
    step = pl.program_id(0)
    leaf_len = basis_ref.shape[2]

    @pl.when(step == 0)
    def _():
        root_ref[...] = jnp.zeros_like(root_ref)
        entry, block = owner_tables(me_ref[0], layers, owner_ref[...], leaf_ref[...])
        rows, lanes = entry.shape
        entry_ref[:rows, :lanes] = entry
        block_ref[:rows, :lanes] = block

    hots = [one_hot_leaf(order_ref[pl.ds(step * per + i, 1), :], leaf_len) for i in range(per)]
    ordered = [
        dot(hots[i], comp_ref[i * leaf_len:(i + 1) * leaf_len, :]).astype(BF) for i in range(per)
    ]
    skeletons = [dot(basis_ref[i], ordered[i]).astype(BF) for i in range(per)]
    across = jnp.concatenate([transfer_ref[i] for i in range(per)], axis=1)
    root_ref[...] += dot(across, jnp.concatenate(skeletons, axis=0))
    for i in range(per):
        ordered_ref[i * leaf_len:(i + 1) * leaf_len, :] = ordered[i]
        shared_ref[pl.ds(step * per + i + 1, 1)] = skeletons[i][None]

    even = me_ref[0] % 2 == 0

    @pl.when((step == 0) & even)
    def _():
        cross_ref[...] = ordered[0]

    @pl.when((step == 0) & ~even)
    def _():
        inner_ref[...] = ordered[0]

    last = step == pl.num_programs(0) - 1

    @pl.when(last & even)
    def _():
        inner_ref[...] = ordered[-1]

    @pl.when(last & ~even)
    def _():
        cross_ref[...] = ordered[-1]

    @pl.when(last)
    def _():
        shared_ref[pl.ds(0, 1)] = root_ref[...].astype(BF)[None]


def skeletons_of(me, leaf_order, composition, leaf_basis, transfer, owners, blocks, layers, per=4):
    leaves, rank, leaf_len = leaf_basis.shape
    fields = composition.shape[1]
    entries = owners.shape[1]
    edge = jax.ShapeDtypeStruct((leaf_len, fields), BF)
    return pl.pallas_call(
        functools.partial(skeleton_kernel, per, layers),
        name="order_and_skeleton",
        grid=(leaves // per,),
        in_specs=[
            scalars(),
            pl.BlockSpec((leaves, leaf_len), lambda s: (0, 0)),
            pl.BlockSpec((per * leaf_len, fields), lambda s: (s, 0)),
            pl.BlockSpec((per, rank, leaf_len), lambda s: (s, 0, 0)),
            pl.BlockSpec((per, rank, rank), lambda s: (s, 0, 0)),
            pl.BlockSpec((leaves, entries), lambda s: (0, 0)),
            pl.BlockSpec((leaves, entries), lambda s: (0, 0)),
        ],
        out_specs=[
            pl.BlockSpec((per * leaf_len, fields), lambda s: (s, 0)),
            pl.BlockSpec((leaves + 1, rank, fields), lambda s: (0, 0, 0)),
            pl.BlockSpec((leaf_len, fields), lambda s: (0, 0)),
            pl.BlockSpec((leaf_len, fields), lambda s: (0, 0)),
            pl.BlockSpec((16, 128), lambda s: (0, 0)),
            pl.BlockSpec((16, 128), lambda s: (0, 0)),
        ],
        out_shape=[
            jax.ShapeDtypeStruct((leaves * leaf_len, fields), BF),
            jax.ShapeDtypeStruct((leaves + 1, rank, fields), BF),
            edge,
            edge,
            jax.ShapeDtypeStruct((16, 128), jnp.int32),
            jax.ShapeDtypeStruct((16, 128), jnp.int32),
        ],
        scratch_shapes=[pltpu.VMEM((rank, fields), F32)],
        compiler_params=params(16),
        cost_estimate=cost(leaves * leaf_len * leaf_len * fields * 2, 4 * MIB),
    )(me, *in_hbm(leaf_order, composition, leaf_basis, transfer, owners, blocks))


def join_kernel(*refs):
    out = refs[-1]
    at = 0
    for ref in refs[:-1]:
        out[at:at + ref.shape[0]] = ref[...]
        at += ref.shape[0]


def join(parts):
    if len(parts) == 1:
        return parts[0]
    shape = (sum(part.shape[0] for part in parts),) + parts[0].shape[1:]
    return pl.pallas_call(
        join_kernel,
        name="join",
        in_specs=[whole()] * len(parts),
        out_specs=whole(),
        out_shape=jax.ShapeDtypeStruct(shape, BF),
        compiler_params=params(8 if shape[0] <= 32 else 32),
        cost_estimate=cost(0, MIB // 2),
    )(*parts)


def choose_kernel(number, me_ref, *refs):
    ins, outs = refs[:2 * number], refs[2 * number:]
    for core in range(2):
        @pl.when(me_ref[0] % 2 == core)
        def _(core=core):
            at = 0
            for ref in ins[core * number:(core + 1) * number]:
                done = 0
                while done < ref.shape[0]:
                    out, base = outs[at // outs[0].shape[0]], at % outs[0].shape[0]
                    size = min(ref.shape[0] - done, out.shape[0] - base)
                    out[base:base + size] = ref[done:done + size]
                    done, at = done + size, at + size


def choose(me, from_x, from_y, streams):
    parts = list(from_x) + list(from_y)
    total = sum(part.shape[0] for part in from_x)
    shape = jax.ShapeDtypeStruct((total // streams,) + from_x[0].shape[1:], BF)
    return pl.pallas_call(
        functools.partial(choose_kernel, len(from_x)),
        name="choose",
        in_specs=[scalars()] + [whole()] * len(parts),
        out_specs=[whole()] * streams,
        out_shape=[shape] * streams,
        compiler_params=params(8 if total <= 32 else 32),
        cost_estimate=cost(0, MIB // 2),
    )(me, *parts)


def dense_kernel(per, slots, entry_ref, block_ref, inner_ref, coupling_ref, top_ref,
                 transfer_ref, own_ref, other_ref, turned_ref):
    step = pl.program_id(0)
    rank = coupling_ref.shape[2]
    fields = inner_ref.shape[1]
    leaves = own_ref.shape[0] - 1
    for i in range(per):
        turned_ref[step * per + i] = transfer_ref[i].T

    def fill(out_ref, plane, row, entry_row, block_of):
        for slot in range(0, slots, 2):
            pair = []
            for one in (slot, slot + 1):
                entry = entry_ref[entry_row, plane * slots + one]
                block = block_of(jnp.maximum(entry, 0))
                pair.append(jnp.where(entry >= 0, block, jnp.zeros_like(block)))
            out_ref[row, :, slot * rank:(slot + 2) * rank] = jnp.concatenate(pair, axis=1)

    for plane, out_ref in ((0, own_ref), (1, other_ref)):
        for i in range(per):
            leaf = step * per + i
            fill(out_ref, plane, leaf, leaf + 1, lambda entry, i=i: coupling_ref[i, entry])

        @pl.when(step == pl.num_programs(0) - 1)
        def _(plane=plane, out_ref=out_ref):
            fill(out_ref, plane, leaves, 0, lambda entry: top_ref[0, entry])

    @pl.when(step == 0)
    def _():
        for t in range(inner_ref.shape[0] // rank):
            part = inner_ref[t * rank:(t + 1) * rank, :]
            other_ref[leaves + 1, :, t * fields:(t + 1) * fields] = part
        other_ref[leaves + 2] = jnp.zeros(other_ref.shape[1:], BF)
        blocks = block_ref[...].astype(F32).astype(BF)
        other_ref[leaves + 2, :blocks.shape[0], :blocks.shape[1]] = blocks


def dense_couplings(entry, block, inner, coupling, top_coupling, transfer, slots, per=4):
    leaves, entries, rank, _ = coupling.shape
    own = (leaves + 1, rank, slots * rank)
    other = (leaves + 3, rank, slots * rank)
    return pl.pallas_call(
        functools.partial(dense_kernel, per, slots),
        name="couplings_by_owner",
        grid=(leaves // per,),
        in_specs=[
            scalars(),
            pl.BlockSpec(block.shape, lambda s: (0, 0)),
            pl.BlockSpec(inner.shape, lambda s: (0, 0)),
            pl.BlockSpec((per, entries, rank, rank), lambda s: (s, 0, 0, 0)),
            pl.BlockSpec(top_coupling.shape, lambda s: (0, 0, 0, 0)),
            pl.BlockSpec((per, rank, rank), lambda s: (s, 0, 0)),
        ],
        out_specs=[
            pl.BlockSpec(own, lambda s: (0, 0, 0)),
            pl.BlockSpec(other, lambda s: (0, 0, 0)),
            pl.BlockSpec(transfer.shape, lambda s: (0, 0, 0)),
        ],
        out_shape=[
            jax.ShapeDtypeStruct(own, BF),
            jax.ShapeDtypeStruct(other, BF),
            jax.ShapeDtypeStruct(transfer.shape, BF),
        ],
        compiler_params=params(16 if slots <= 16 else 48),
        cost_estimate=cost(0, 8 * MIB),
    )(entry, block, inner, *in_hbm(coupling, top_coupling, transfer))


def round_kernel(plane, steps, slots, counts, at_ref, *refs):
    sides = []
    for number in counts:
        sides.append(refs[:number])
        refs = refs[number:]
    blocks_ref, out = refs[0], refs[-1]
    rows, rank, _ = out.shape
    low, high = steps[0] * 4 * rank, (steps[-1] + 1) * 4 * rank

    def block_at(side, base, index):
        for ref in side:
            if base < ref.shape[0]:
                return ref[base + index]
            base -= ref.shape[0]

    for row in range(rows):
        chosen = [
            block_at(side, place * rows, at_ref[(row + 1) % rows, plane * slots + step * 4 + q])
            for place, step in enumerate(steps)
            for q, side in enumerate(sides)
        ]
        value = dot(blocks_ref[row, :, low:high], jnp.concatenate(chosen, axis=0))
        if len(refs) > 2:
            value = value + refs[1][row]
        out[row] = value


def far_round(plane, steps, slots, at, parts, blocks, total=None):
    rank, fields = parts[0][0].shape[1:]
    rows = parts[0][0].shape[0] // (1 if len(parts[0]) > 1 else len(steps))
    args = [part for side in parts for part in side] + [blocks] + ([] if total is None else [total])
    return pl.pallas_call(
        functools.partial(round_kernel, plane, steps, slots, [len(side) for side in parts]),
        name="far_" + str(plane) + "_" + str(steps[0]),
        in_specs=[scalars()] + [whole()] * len(args),
        out_specs=whole(),
        out_shape=jax.ShapeDtypeStruct((rows, rank, fields), F32),
        compiler_params=params(16 if slots <= 16 else 48),
        cost_estimate=cost(rows * rank * 4 * rank * fields * 2 * len(steps), MIB),
    )(at, *args)


def near_kernel(edges, pair_of, last_pair, mask_ref, order_ref, table_ref, basis_ref,
                ordered_ref, *refs):
    if edges:
        me_ref, cross_ref, inner_ref, blocks_ref = refs[:4]
        near_ref, turned_ref, at_ref = refs[-3:]
    else:
        near_ref, turned_ref = refs[-2:]
    pair = pair_of(pl.program_id(0))
    leaf_len = basis_ref.shape[2]
    leaves = basis_ref.shape[0]

    def leaf_at(leaf):
        return ordered_ref[pl.ds(pl.multiple_of(leaf * leaf_len, leaf_len), leaf_len), :]

    low, high = leaf_at(2 * pair), leaf_at(2 * pair + 1)
    prev, following = leaf_at(jnp.maximum(2 * pair - 1, 0)), leaf_at(jnp.minimum(2 * pair + 2, leaves - 1))
    if edges:
        even = me_ref[0] % 2 == 0
        cross = cross_ref[...]
        wide = cross.shape[1]
        inner = jnp.concatenate(
            [inner_ref[0, :, t:t + wide] for t in range(0, inner_ref.shape[2], wide)], axis=0
        )[:leaf_len]
        prev = jnp.where(pair == 0, jnp.where(even, cross, inner), prev)
        following = jnp.where(pair == last_pair, jnp.where(even, inner, cross), following)

        @pl.when(pl.program_id(0) == 0)
        def _():
            rows, lanes = at_ref.shape
            at_ref[...] = blocks_ref[0, :rows, :lanes].astype(F32).astype(jnp.int32)


    def masked(leaf, side, value):
        return jnp.where(mask_ref[side, leaf] > 0, value, jnp.zeros_like(value))

    left = jnp.concatenate(
        [masked(2 * pair, 0, prev), low, masked(2 * pair, 1, high)], axis=0
    )
    right = jnp.concatenate(
        [masked(2 * pair + 1, 0, low), high, masked(2 * pair + 1, 1, following)], axis=0
    )
    near = dot(table_ref[...], jnp.concatenate([left, right], axis=1)).astype(BF)
    fields = ordered_ref.shape[1]
    for i in range(2):
        hot = one_hot_grid(order_ref[pl.ds(2 * pair + i, 1), :], leaf_len)
        at = pl.ds(i * leaf_len, leaf_len)
        both = jnp.concatenate([near[:, i * fields:(i + 1) * fields], basis_ref[2 * pair + i].T], axis=1)
        moved = dot(hot, both).astype(BF)
        near_ref[at, :] = moved[:, :fields]
        turned_ref[at, :] = moved[:, fields:]


def near_field(pairs, near_list, leaf_order, tables, basis, ordered, halos=None, filled=None):
    leaves, rank, leaf_len = basis.shape
    fields = ordered.shape[1]
    last = leaves // 2 - 1
    gap = pairs[1] - pairs[0] if len(pairs) > 1 else 1

    def pair_of(step):
        return pairs[0] + gap * step

    in_specs = [
        scalars(),
        whole(),
        whole(),
        whole(),
        whole(),
    ]
    args = [near_list.T, leaf_order, tables, basis, ordered]
    aliases = {}
    extra = []
    if halos is not None:
        me, cross, other = halos
        row = (1,) + other.shape[1:]
        in_specs += [
            scalars(),
            pl.BlockSpec((leaf_len, fields), lambda s: (0, 0)),
            pl.BlockSpec(row, lambda s: (leaves + 1, 0, 0)),
            pl.BlockSpec(row, lambda s: (leaves + 2, 0, 0)),
        ]
        args += [me, cross, other, other]
        extra = [(16, 128)]
    if filled is not None:
        aliases = {len(args): 0, len(args) + 1: 1}
        in_specs += [pl.BlockSpec(memory_space=pl.ANY)] * 2
        args += list(filled)
    return pl.pallas_call(
        functools.partial(near_kernel, halos is not None, pair_of, last),
        name="near_" + str(pairs[0]),
        grid=(len(pairs),),
        in_specs=in_specs,
        out_specs=[
            pl.BlockSpec((2 * leaf_len, fields), lambda s: (pair_of(s), 0)),
            pl.BlockSpec((2 * leaf_len, rank), lambda s: (pair_of(s), 0)),
        ] + [pl.BlockSpec(shape, lambda s: (0, 0)) for shape in extra],
        out_shape=[
            jax.ShapeDtypeStruct((leaves * leaf_len, fields), BF),
            jax.ShapeDtypeStruct((leaves * leaf_len, rank), BF),
        ] + [jax.ShapeDtypeStruct(shape, jnp.int32) for shape in extra],
        input_output_aliases=aliases,
        compiler_params=params(16),
        cost_estimate=cost(len(pairs) * 2 * leaf_len * leaf_len * fields * 10, len(pairs) * MIB),
    )(*args)


def field_kernel(per, own_ref, other_ref, turned_transfer_ref, near_ref, turned_ref, out_ref):
    step = pl.program_id(0)
    leaf_len = out_ref.shape[0] // per
    root = own_ref.shape[0] - 1
    local = own_ref[root] + other_ref[root]
    coarse = local.astype(BF)
    fine = (local - coarse.astype(F32)).astype(BF)
    both = jnp.concatenate([coarse, fine], axis=1)
    fields = local.shape[1]
    for i in range(per):
        leaf = step * per + i
        down = dot(turned_transfer_ref[leaf], both)
        value = own_ref[leaf] + other_ref[leaf] + (down[:, :fields] + down[:, fields:])
        at = pl.ds(pl.multiple_of(leaf * leaf_len, leaf_len), leaf_len)
        far = dot(turned_ref[at, :], value.astype(BF))
        out_ref[i * leaf_len:(i + 1) * leaf_len, :] = (near_ref[at, :].astype(F32) + far).astype(BF)


def field(own, other, turned_transfer, near, turned, per=4):
    leaves, rank, _ = turned_transfer.shape
    fields = near.shape[1]
    leaf_len = near.shape[0] // leaves
    return pl.pallas_call(
        functools.partial(field_kernel, per),
        name="local_and_field",
        grid=(leaves // per,),
        in_specs=[whole()] * 5,
        out_specs=pl.BlockSpec((per * leaf_len, fields), lambda s: (s, 0)),
        out_shape=jax.ShapeDtypeStruct(near.shape, BF),
        compiler_params=params(16),
        cost_estimate=cost(leaves * leaf_len * rank * fields * 2, 4 * MIB),
    )(own, other, turned_transfer, near, turned)


def after(block, *others):
    return lax.optimization_barrier((block,) + others)[0]


def on_device(
    composition,
    leaf_basis,
    transfer,
    coupling,
    top_coupling,
    admissible_owner,
    admissible_leaf,
    near_list,
    leaf_order,
):
    leaves, rank, leaf_len = leaf_basis.shape
    count = lax.axis_size("subtree")
    layers = count // 8
    slots = layers * 4
    pairs = leaves // 2
    cut = pairs // 2
    me = lax.axis_index("subtree").reshape(1)

    ordered, shared, cross, inner, entry, own_at = skeletons_of(
        me, leaf_order, composition, leaf_basis, transfer, admissible_owner, admissible_leaf, layers
    )
    tables = jnp.asarray(near_tables(leaf_len))
    near_args = (near_list, leaf_order, tables, leaf_basis)

    line = along_z(shared, 1)
    from_x, from_y = over_x(shared), over_y(shared)
    filled = near_field(list(range(1, cut)), *near_args, ordered)
    line = after(line, filled[0])
    lines = [along_z(after(shared, filled[0]), layers - 1)]
    for _ in range(layers - 3):
        lines.append(along_z(line if len(lines) == 1 else lines[-1], 1))
    ready = after(line, from_x, from_y)
    next_x, next_y = over_x(ready), over_y(ready)
    cross = lax.ppermute(
        cross,
        "subtree",
        [(d, d + 1) for d in range(1, count - 1, 2)] + [(d, d - 1) for d in range(2, count, 2)],
    )
    own_blocks, my_other, turned_transfer = dense_couplings(
        after(entry, ready), own_at, inner, coupling, top_coupling, transfer, slots
    )
    round_0 = ((shared, line), (from_x, next_x), (from_y, next_y))
    chosen = choose(me, (after(from_x, cross, my_other), next_x), round_0[2], 1)
    round_0 += (tuple(map(onward, chosen)),)

    joined = join([after(lines[0], *chosen)] + lines[1:])
    last_x, last_y = over_x(joined), over_y(joined)
    other_blocks = over_core(after(my_other, *chosen))
    held = after(ordered, joined, *round_0[3])
    filled = near_field(list(range(cut, pairs - 1)), *near_args, held, filled=filled)
    *filled, other_at = near_field(
        [0, pairs - 1], *near_args, after(ordered, filled[0]), halos=(me, cross, other_blocks), filled=filled
    )
    far = tuple(map(onward, choose(me, (after(last_x, filled[0]),), (last_y,), 2)))
    steps = [0, 1]
    own = far_round(0, steps, slots, own_at, round_0, own_blocks)
    other = far_round(1, steps, slots, other_at, round_0, other_blocks)
    steps = list(range(2, layers))
    round_1 = ((joined,), (last_x,), (last_y,), (after(far[0], own, other),) + far[1:])
    other = far_round(1, steps, slots, other_at, round_1, other_blocks, other)
    own = far_round(0, steps, slots, own_at, round_1, own_blocks, own)
    return field(own, over_core(other), turned_transfer, *filled)


def solution(mesh):
    placed = (
        P(("groups", "subtree"), None),
        P("subtree", None, None),
        P("subtree", None, None),
        P("subtree", None, None, None),
        P("subtree", None, None, None),
        P(("groups", "subtree"), None),
        P(("groups", "subtree"), None),
        P(("groups", "subtree"), None),
        P(("groups", "subtree"), None),
    )
    return jax.shard_map(
        on_device,
        mesh=mesh,
        in_specs=placed,
        out_specs=P(("groups", "subtree"), None),
        check_vma=False,
    )
```

```python
import functools

import jax
import jax.numpy as jnp
import ml_dtypes
import numpy as np
from jax import lax
from jax.experimental import pallas as pl
from jax.experimental.pallas import tpu as pltpu
from jax.sharding import PartitionSpec as P

COULOMB_SCALE = 0.15
SOFTENING = 0.25
BF = jnp.bfloat16
F32 = jnp.float32
MIB = 1 << 20


def near_tables(leaf_len):
    cells = np.arange(leaf_len)
    along = (cells // 64).astype(np.float32)
    across = (cells // 8 % 8).astype(np.float32)
    height = (cells % 8).astype(np.float32)
    extent = leaf_len // 64
    tables = []
    for offset in (-1, 0, 1):
        delta_x = along[:, None] - along[None, :] - np.float32(offset * extent)
        delta_y = across[:, None] - across[None, :]
        delta_z = height[:, None] - height[None, :]
        square = delta_x * delta_x + delta_y * delta_y + delta_z * delta_z
        value = np.float32(COULOMB_SCALE) / np.sqrt(square + np.float32(SOFTENING))
        tables.append(value.astype(ml_dtypes.bfloat16))
    return np.concatenate(tables, axis=1)


def send(block, target):
    count = lax.axis_size("subtree")
    return lax.ppermute(block, "subtree", [(d, target(d)) for d in range(count)])


def over_core(block):
    return send(block, lambda d: d ^ 1)


def over_x(block):
    return send(block, lambda d: d ^ 2)


def over_y(block):
    return send(block, lambda d: d ^ 4)


def onward(block):
    return send(block, lambda d: d ^ (2 if d % 2 else 4))


def along_z(block, step):
    layers = lax.axis_size("subtree") // 8
    return send(block, lambda d: (d // 8 + step) % layers * 8 + d % 8)


def params(mib):
    return pltpu.CompilerParams(vmem_limit_bytes=mib * MIB)


def cost(flops, moved):
    return pl.CostEstimate(flops=flops // 64, bytes_accessed=moved // 64, transcendentals=0)


def whole():
    return pl.BlockSpec(memory_space=pltpu.VMEM)


def scalars():
    return pl.BlockSpec(memory_space=pltpu.SMEM)


def dot(a, b):
    return jnp.dot(a, b, preferred_element_type=F32)


def in_hbm(*arrays):
    return [pltpu.with_memory_space_constraint(array, pltpu.HBM) for array in arrays]


def one_hot_leaf(row, leaf_len):
    column = jnp.broadcast_to(row, (128, leaf_len)).T
    lanes = lax.broadcasted_iota(jnp.int32, (leaf_len, 128), 1)
    return jnp.concatenate(
        [
            jnp.where(column == lanes + 128 * t, 1.0, 0.0).astype(BF)
            for t in range(leaf_len // 128)
        ],
        axis=1,
    )


def one_hot_grid(row, leaf_len):
    cells = lax.broadcasted_iota(jnp.int32, (leaf_len, leaf_len), 0)
    return jnp.where(cells == row, 1.0, 0.0).astype(BF)


def owner_tables(me, layers, owners, blocks):
    leaves, entries = owners.shape
    slots = layers * 4
    rows = leaves + 1
    shape = (rows, 2 * slots)
    lane = lax.broadcasted_iota(jnp.int32, shape, 1)
    plane = (lane >= slots).astype(jnp.int32)
    slot = lane - plane * slots
    layer, chip, core = me // 8, (me // 2) & 3, me & 1
    turn = slot >> 2
    shift = jnp.where(turn < 2, turn, jnp.where(turn == 2, layers - 1, turn - 1))
    source = layer - shift
    source = jnp.where(source < 0, source + layers, source)
    owner = source * 8 + (chip ^ (slot & 3)) * 2 + (core ^ plane)
    row = lax.broadcasted_iota(jnp.int32, shape, 0)
    distant = jnp.abs(owner - me) >= 2
    entry = jnp.where((row == 0) & distant, owner, -1)
    block = jnp.zeros(shape, jnp.int32)
    pad = jnp.full((1, entries), -1, jnp.int32)
    named = jnp.concatenate([pad, owners], axis=0)
    chosen = jnp.concatenate([pad, blocks], axis=0)
    for k in range(entries):
        match = named[:, k:k + 1] == owner
        entry = jnp.where(match, k, entry)
        block = jnp.where(match, chosen[:, k:k + 1] + 1, block)
    return entry, block


def skeleton_kernel(per, layers, me_ref, order_ref, comp_ref, basis_ref, transfer_ref,
                    owner_ref, leaf_ref, ordered_ref, shared_ref, cross_ref, inner_ref,
                    entry_ref, block_ref, root_ref):
    step = pl.program_id(0)
    leaf_len = basis_ref.shape[2]

    @pl.when(step == 0)
    def _():
        root_ref[...] = jnp.zeros_like(root_ref)
        entry, block = owner_tables(me_ref[0], layers, owner_ref[...], leaf_ref[...])
        rows, lanes = entry.shape
        entry_ref[:rows, :lanes] = entry
        block_ref[:rows, :lanes] = block

    hots = [one_hot_leaf(order_ref[pl.ds(step * per + i, 1), :], leaf_len) for i in range(per)]
    ordered = [
        dot(hots[i], comp_ref[i * leaf_len:(i + 1) * leaf_len, :]).astype(BF) for i in range(per)
    ]
    skeletons = [dot(basis_ref[i], ordered[i]).astype(BF) for i in range(per)]
    across = jnp.concatenate([transfer_ref[i] for i in range(per)], axis=1)
    root_ref[...] += dot(across, jnp.concatenate(skeletons, axis=0))
    for i in range(per):
        ordered_ref[i * leaf_len:(i + 1) * leaf_len, :] = ordered[i]
        shared_ref[pl.ds(step * per + i + 1, 1)] = skeletons[i][None]

    even = me_ref[0] % 2 == 0

    @pl.when((step == 0) & even)
    def _():
        cross_ref[...] = ordered[0]

    @pl.when((step == 0) & ~even)
    def _():
        inner_ref[...] = ordered[0]

    last = step == pl.num_programs(0) - 1

    @pl.when(last & even)
    def _():
        inner_ref[...] = ordered[-1]

    @pl.when(last & ~even)
    def _():
        cross_ref[...] = ordered[-1]

    @pl.when(last)
    def _():
        shared_ref[pl.ds(0, 1)] = root_ref[...].astype(BF)[None]


def skeletons_of(me, leaf_order, composition, leaf_basis, transfer, owners, blocks, layers, per=4):
    leaves, rank, leaf_len = leaf_basis.shape
    fields = composition.shape[1]
    entries = owners.shape[1]
    edge = jax.ShapeDtypeStruct((leaf_len, fields), BF)
    return pl.pallas_call(
        functools.partial(skeleton_kernel, per, layers),
        name="order_and_skeleton",
        grid=(leaves // per,),
        in_specs=[
            scalars(),
            pl.BlockSpec((leaves, leaf_len), lambda s: (0, 0)),
            pl.BlockSpec((per * leaf_len, fields), lambda s: (s, 0)),
            pl.BlockSpec((per, rank, leaf_len), lambda s: (s, 0, 0)),
            pl.BlockSpec((per, rank, rank), lambda s: (s, 0, 0)),
            pl.BlockSpec((leaves, entries), lambda s: (0, 0)),
            pl.BlockSpec((leaves, entries), lambda s: (0, 0)),
        ],
        out_specs=[
            pl.BlockSpec((per * leaf_len, fields), lambda s: (s, 0)),
            pl.BlockSpec((leaves + 1, rank, fields), lambda s: (0, 0, 0)),
            pl.BlockSpec((leaf_len, fields), lambda s: (0, 0)),
            pl.BlockSpec((leaf_len, fields), lambda s: (0, 0)),
            pl.BlockSpec((16, 128), lambda s: (0, 0)),
            pl.BlockSpec((16, 128), lambda s: (0, 0)),
        ],
        out_shape=[
            jax.ShapeDtypeStruct((leaves * leaf_len, fields), BF),
            jax.ShapeDtypeStruct((leaves + 1, rank, fields), BF),
            edge,
            edge,
            jax.ShapeDtypeStruct((16, 128), jnp.int32),
            jax.ShapeDtypeStruct((16, 128), jnp.int32),
        ],
        scratch_shapes=[pltpu.VMEM((rank, fields), F32)],
        compiler_params=params(16),
        cost_estimate=cost(leaves * leaf_len * leaf_len * fields * 2, 4 * MIB),
    )(me, *in_hbm(leaf_order, composition, leaf_basis, transfer, owners, blocks))


def join_kernel(*refs):
    out = refs[-1]
    at = 0
    for ref in refs[:-1]:
        out[at:at + ref.shape[0]] = ref[...]
        at += ref.shape[0]


def join(parts):
    if len(parts) == 1:
        return parts[0]
    shape = (sum(part.shape[0] for part in parts),) + parts[0].shape[1:]
    return pl.pallas_call(
        join_kernel,
        name="join",
        in_specs=[whole()] * len(parts),
        out_specs=whole(),
        out_shape=jax.ShapeDtypeStruct(shape, BF),
        compiler_params=params(8 if shape[0] <= 32 else 32),
        cost_estimate=cost(0, MIB // 2),
    )(*parts)


def choose_kernel(me_ref, x_ref, y_ref, out_ref):
    @pl.when(me_ref[0] % 2 == 0)
    def _():
        out_ref[...] = x_ref[...]

    @pl.when(me_ref[0] % 2 == 1)
    def _():
        out_ref[...] = y_ref[...]


def choose(me, from_x, from_y):
    return pl.pallas_call(
        choose_kernel,
        name="choose",
        in_specs=[scalars(), whole(), whole()],
        out_specs=whole(),
        out_shape=jax.ShapeDtypeStruct(from_x.shape, BF),
        compiler_params=params(8),
        cost_estimate=cost(0, MIB // 4),
    )(me, from_x, from_y)


def dense_kernel(per, slots, entry_ref, block_ref, inner_ref, coupling_ref, top_ref,
                 transfer_ref, own_ref, other_ref, turned_ref):
    step = pl.program_id(0)
    rank = coupling_ref.shape[2]
    fields = inner_ref.shape[1]
    leaves = own_ref.shape[0] - 1
    for i in range(per):
        turned_ref[step * per + i] = transfer_ref[i].T

    def fill(out_ref, plane, row, entry_row, block_of):
        for slot in range(0, slots, 2):
            pair = []
            for one in (slot, slot + 1):
                entry = entry_ref[entry_row, plane * slots + one]
                block = block_of(jnp.maximum(entry, 0))
                pair.append(jnp.where(entry >= 0, block, jnp.zeros_like(block)))
            out_ref[row, :, slot * rank:(slot + 2) * rank] = jnp.concatenate(pair, axis=1)

    for plane, out_ref in ((0, own_ref), (1, other_ref)):
        for i in range(per):
            leaf = step * per + i
            fill(out_ref, plane, leaf, leaf + 1, lambda entry, i=i: coupling_ref[i, entry])

        @pl.when(step == pl.num_programs(0) - 1)
        def _(plane=plane, out_ref=out_ref):
            fill(out_ref, plane, leaves, 0, lambda entry: top_ref[0, entry])

    @pl.when(step == 0)
    def _():
        for t in range(inner_ref.shape[0] // rank):
            part = inner_ref[t * rank:(t + 1) * rank, :]
            other_ref[leaves + 1, :, t * fields:(t + 1) * fields] = part
        other_ref[leaves + 2] = jnp.zeros(other_ref.shape[1:], BF)
        blocks = block_ref[...].astype(F32).astype(BF)
        other_ref[leaves + 2, :blocks.shape[0], :blocks.shape[1]] = blocks


def dense_couplings(entry, block, inner, coupling, top_coupling, transfer, slots, per=4):
    leaves, entries, rank, _ = coupling.shape
    own = (leaves + 1, rank, slots * rank)
    other = (leaves + 3, rank, slots * rank)
    return pl.pallas_call(
        functools.partial(dense_kernel, per, slots),
        name="couplings_by_owner",
        grid=(leaves // per,),
        in_specs=[
            scalars(),
            pl.BlockSpec(block.shape, lambda s: (0, 0)),
            pl.BlockSpec(inner.shape, lambda s: (0, 0)),
            pl.BlockSpec((per, entries, rank, rank), lambda s: (s, 0, 0, 0)),
            pl.BlockSpec(top_coupling.shape, lambda s: (0, 0, 0, 0)),
            pl.BlockSpec((per, rank, rank), lambda s: (s, 0, 0)),
        ],
        out_specs=[
            pl.BlockSpec(own, lambda s: (0, 0, 0)),
            pl.BlockSpec(other, lambda s: (0, 0, 0)),
            pl.BlockSpec(transfer.shape, lambda s: (0, 0, 0)),
        ],
        out_shape=[
            jax.ShapeDtypeStruct(own, BF),
            jax.ShapeDtypeStruct(other, BF),
            jax.ShapeDtypeStruct(transfer.shape, BF),
        ],
        compiler_params=params(16 if slots <= 16 else 48),
        cost_estimate=cost(0, 8 * MIB),
    )(entry, block, inner, *in_hbm(coupling, top_coupling, transfer))


def round_kernel(plane, steps, slots, counts, at_ref, *refs):
    sides = []
    for number in counts:
        sides.append(refs[:number])
        refs = refs[number:]
    blocks_ref, out = refs[0], refs[-1]
    rows, rank, _ = out.shape
    low, high = steps[0] * 4 * rank, (steps[-1] + 1) * 4 * rank

    def block_at(side, base, index):
        for ref in side:
            if base < ref.shape[0]:
                return ref[base + index]
            base -= ref.shape[0]

    for row in range(rows):
        chosen = [
            block_at(side, place * rows, at_ref[(row + 1) % rows, plane * slots + step * 4 + q])
            for place, step in enumerate(steps)
            for q, side in enumerate(sides)
        ]
        value = dot(blocks_ref[row, :, low:high], jnp.concatenate(chosen, axis=0))
        if len(refs) > 2:
            value = value + refs[1][row]
        out[row] = value


def far_round(plane, steps, slots, at, parts, blocks, total=None):
    rank, fields = parts[0][0].shape[1:]
    rows = parts[0][0].shape[0] // (1 if len(parts[0]) > 1 else len(steps))
    args = [part for side in parts for part in side] + [blocks] + ([] if total is None else [total])
    return pl.pallas_call(
        functools.partial(round_kernel, plane, steps, slots, [len(side) for side in parts]),
        name="far_" + str(plane) + "_" + str(steps[0]),
        in_specs=[scalars()] + [whole()] * len(args),
        out_specs=whole(),
        out_shape=jax.ShapeDtypeStruct((rows, rank, fields), F32),
        compiler_params=params(16 if slots <= 16 else 48),
        cost_estimate=cost(rows * rank * 4 * rank * fields * 2 * len(steps), MIB),
    )(at, *args)


def near_kernel(edges, pair_of, last_pair, mask_ref, order_ref, table_ref, basis_ref,
                ordered_ref, *refs):
    if edges:
        me_ref, cross_ref, inner_ref, blocks_ref = refs[:4]
        near_ref, turned_ref, at_ref = refs[-3:]
    else:
        near_ref, turned_ref = refs[-2:]
    pair = pair_of(pl.program_id(0))
    leaf_len = basis_ref.shape[2]
    leaves = basis_ref.shape[0]

    def leaf_at(leaf):
        return ordered_ref[pl.ds(pl.multiple_of(leaf * leaf_len, leaf_len), leaf_len), :]

    low, high = leaf_at(2 * pair), leaf_at(2 * pair + 1)
    prev, following = leaf_at(jnp.maximum(2 * pair - 1, 0)), leaf_at(jnp.minimum(2 * pair + 2, leaves - 1))
    if edges:
        even = me_ref[0] % 2 == 0
        cross = cross_ref[...]
        wide = cross.shape[1]
        inner = jnp.concatenate(
            [inner_ref[0, :, t:t + wide] for t in range(0, inner_ref.shape[2], wide)], axis=0
        )[:leaf_len]
        prev = jnp.where(pair == 0, jnp.where(even, cross, inner), prev)
        following = jnp.where(pair == last_pair, jnp.where(even, inner, cross), following)

        @pl.when(pl.program_id(0) == 0)
        def _():
            rows, lanes = at_ref.shape
            at_ref[...] = blocks_ref[0, :rows, :lanes].astype(F32).astype(jnp.int32)


    def masked(leaf, side, value):
        return jnp.where(mask_ref[side, leaf] > 0, value, jnp.zeros_like(value))

    left = jnp.concatenate(
        [masked(2 * pair, 0, prev), low, masked(2 * pair, 1, high)], axis=0
    )
    right = jnp.concatenate(
        [masked(2 * pair + 1, 0, low), high, masked(2 * pair + 1, 1, following)], axis=0
    )
    near = dot(table_ref[...], jnp.concatenate([left, right], axis=1)).astype(BF)
    fields = ordered_ref.shape[1]
    for i in range(2):
        hot = one_hot_grid(order_ref[pl.ds(2 * pair + i, 1), :], leaf_len)
        at = pl.ds(i * leaf_len, leaf_len)
        both = jnp.concatenate([near[:, i * fields:(i + 1) * fields], basis_ref[2 * pair + i].T], axis=1)
        moved = dot(hot, both).astype(BF)
        near_ref[at, :] = moved[:, :fields]
        turned_ref[at, :] = moved[:, fields:]


def near_field(pairs, near_list, leaf_order, tables, basis, ordered, halos=None, filled=None):
    leaves, rank, leaf_len = basis.shape
    fields = ordered.shape[1]
    last = leaves // 2 - 1
    gap = pairs[1] - pairs[0] if len(pairs) > 1 else 1

    def pair_of(step):
        return pairs[0] + gap * step

    in_specs = [
        scalars(),
        whole(),
        whole(),
        whole(),
        whole(),
    ]
    args = [near_list.T, leaf_order, tables, basis, ordered]
    aliases = {}
    extra = []
    if halos is not None:
        me, cross, other = halos
        row = (1,) + other.shape[1:]
        in_specs += [
            scalars(),
            pl.BlockSpec((leaf_len, fields), lambda s: (0, 0)),
            pl.BlockSpec(row, lambda s: (leaves + 1, 0, 0)),
            pl.BlockSpec(row, lambda s: (leaves + 2, 0, 0)),
        ]
        args += [me, cross, other, other]
        extra = [(16, 128)]
    if filled is not None:
        aliases = {len(args): 0, len(args) + 1: 1}
        in_specs += [pl.BlockSpec(memory_space=pl.ANY)] * 2
        args += list(filled)
    return pl.pallas_call(
        functools.partial(near_kernel, halos is not None, pair_of, last),
        name="near_" + str(pairs[0]),
        grid=(len(pairs),),
        in_specs=in_specs,
        out_specs=[
            pl.BlockSpec((2 * leaf_len, fields), lambda s: (pair_of(s), 0)),
            pl.BlockSpec((2 * leaf_len, rank), lambda s: (pair_of(s), 0)),
        ] + [pl.BlockSpec(shape, lambda s: (0, 0)) for shape in extra],
        out_shape=[
            jax.ShapeDtypeStruct((leaves * leaf_len, fields), BF),
            jax.ShapeDtypeStruct((leaves * leaf_len, rank), BF),
        ] + [jax.ShapeDtypeStruct(shape, jnp.int32) for shape in extra],
        input_output_aliases=aliases,
        compiler_params=params(16),
        cost_estimate=cost(len(pairs) * 2 * leaf_len * leaf_len * fields * 10, len(pairs) * MIB),
    )(*args)


def field_kernel(per, own_ref, other_ref, turned_transfer_ref, near_ref, turned_ref, out_ref):
    step = pl.program_id(0)
    leaf_len = out_ref.shape[0] // per
    root = own_ref.shape[0] - 1
    local = own_ref[root] + other_ref[root]
    coarse = local.astype(BF)
    fine = (local - coarse.astype(F32)).astype(BF)
    both = jnp.concatenate([coarse, fine], axis=1)
    fields = local.shape[1]
    for i in range(per):
        leaf = step * per + i
        down = dot(turned_transfer_ref[leaf], both)
        value = own_ref[leaf] + other_ref[leaf] + (down[:, :fields] + down[:, fields:])
        at = pl.ds(pl.multiple_of(leaf * leaf_len, leaf_len), leaf_len)
        far = dot(turned_ref[at, :], value.astype(BF))
        out_ref[i * leaf_len:(i + 1) * leaf_len, :] = (near_ref[at, :].astype(F32) + far).astype(BF)


def field(own, other, turned_transfer, near, turned, per=4):
    leaves, rank, _ = turned_transfer.shape
    fields = near.shape[1]
    leaf_len = near.shape[0] // leaves
    return pl.pallas_call(
        functools.partial(field_kernel, per),
        name="local_and_field",
        grid=(leaves // per,),
        in_specs=[whole()] * 5,
        out_specs=pl.BlockSpec((per * leaf_len, fields), lambda s: (s, 0)),
        out_shape=jax.ShapeDtypeStruct(near.shape, BF),
        compiler_params=params(16),
        cost_estimate=cost(leaves * leaf_len * rank * fields * 2, 4 * MIB),
    )(own, other, turned_transfer, near, turned)


def after(block, *others):
    return lax.optimization_barrier((block,) + others)[0]


def on_device(
    composition,
    leaf_basis,
    transfer,
    coupling,
    top_coupling,
    admissible_owner,
    admissible_leaf,
    near_list,
    leaf_order,
):
    leaves, rank, leaf_len = leaf_basis.shape
    count = lax.axis_size("subtree")
    layers = count // 8
    slots = layers * 4
    pairs = leaves // 2
    cut = pairs // 2
    me = lax.axis_index("subtree").reshape(1)

    ordered, shared, cross, inner, entry, own_at = skeletons_of(
        me, leaf_order, composition, leaf_basis, transfer, admissible_owner, admissible_leaf, layers
    )
    tables = jnp.asarray(near_tables(leaf_len))
    near_args = (near_list, leaf_order, tables, leaf_basis)

    line = along_z(shared, 1)
    from_x, from_y = over_x(shared), over_y(shared)
    filled = near_field(list(range(1, cut)), *near_args, ordered)
    line = after(line, filled[0])
    lines = [along_z(after(shared, filled[0]), layers - 1)]
    for _ in range(layers - 3):
        lines.append(along_z(line if len(lines) == 1 else lines[-1], 1))
    ready = after(line, from_x, from_y)
    next_x, next_y = over_x(ready), over_y(ready)
    far = onward(choose(me, after(from_x, ready), from_y))
    cross = lax.ppermute(
        cross,
        "subtree",
        [(d, d + 1) for d in range(1, count - 1, 2)] + [(d, d - 1) for d in range(2, count, 2)],
    )
    own_blocks, my_other, turned_transfer = dense_couplings(
        after(entry, ready), own_at, inner, coupling, top_coupling, transfer, slots
    )
    chosen = choose(me, after(next_x, cross, my_other), next_y)
    next_far = onward(chosen)

    joined = join([after(lines[0], chosen, far)] + lines[1:])
    last_x, last_y = over_x(joined), over_y(joined)
    other_blocks = over_core(after(my_other, joined))
    held = after(ordered, joined)
    filled = near_field(list(range(cut, pairs - 1)), *near_args, held, filled=filled)
    next_far = after(next_far, filled[0])
    last_far = [along_z(far, layers - 1)]
    for _ in range(layers - 3):
        last_far.append(along_z(next_far if len(last_far) == 1 else last_far[-1], 1))
    held = after(ordered, filled[0])
    *filled, other_at = near_field(
        [0, pairs - 1], *near_args, held, halos=(me, cross, other_blocks), filled=filled
    )
    round_0 = ((shared, line), (from_x, next_x), (from_y, next_y), (far, next_far))
    steps = [0, 1]
    own = far_round(0, steps, slots, own_at, round_0, own_blocks)
    other = far_round(1, steps, slots, other_at, round_0, other_blocks)
    steps = list(range(2, layers))
    round_1 = ((joined,), (last_x,), (last_y,), (after(last_far[0], own, other), *last_far[1:]))
    other = far_round(1, steps, slots, other_at, round_1, other_blocks, other)
    own = far_round(0, steps, slots, own_at, round_1, own_blocks, own)
    return field(own, over_core(other), turned_transfer, *filled)


def solution(mesh):
    placed = (
        P(("groups", "subtree"), None),
        P("subtree", None, None),
        P("subtree", None, None),
        P("subtree", None, None, None),
        P("subtree", None, None, None),
        P(("groups", "subtree"), None),
        P(("groups", "subtree"), None),
        P(("groups", "subtree"), None),
        P(("groups", "subtree"), None),
    )
    return jax.shard_map(
        on_device,
        mesh=mesh,
        in_specs=placed,
        out_specs=P(("groups", "subtree"), None),
        check_vma=False,
    )
```

```python
import functools

import jax
import jax.numpy as jnp
import ml_dtypes
import numpy as np
from jax import lax
from jax.experimental import pallas as pl
from jax.experimental.pallas import tpu as pltpu
from jax.sharding import PartitionSpec as P

COULOMB_SCALE = 0.15
SOFTENING = 0.25
BF = jnp.bfloat16
F32 = jnp.float32
MIB = 1 << 20


def near_tables(leaf_len):
    cells = np.arange(leaf_len)
    along = (cells // 64).astype(np.float32)
    across = (cells // 8 % 8).astype(np.float32)
    height = (cells % 8).astype(np.float32)
    extent = leaf_len // 64
    tables = []
    for offset in (-1, 0, 1):
        delta_x = along[:, None] - along[None, :] - np.float32(offset * extent)
        delta_y = across[:, None] - across[None, :]
        delta_z = height[:, None] - height[None, :]
        square = delta_x * delta_x + delta_y * delta_y + delta_z * delta_z
        value = np.float32(COULOMB_SCALE) / np.sqrt(square + np.float32(SOFTENING))
        tables.append(value.astype(ml_dtypes.bfloat16))
    return np.concatenate(tables, axis=1)


def send(block, target):
    count = lax.axis_size("subtree")
    return lax.ppermute(block, "subtree", [(d, target(d)) for d in range(count)])


def over_core(block):
    return send(block, lambda d: d ^ 1)


def over_x(block):
    return send(block, lambda d: d ^ 2)


def over_y(block):
    return send(block, lambda d: d ^ 4)


def onward(block):
    return send(block, lambda d: d ^ (2 if d % 2 else 4))


def along_z(block, step):
    layers = lax.axis_size("subtree") // 8
    return send(block, lambda d: (d // 8 + step) % layers * 8 + d % 8)


def params(mib):
    return pltpu.CompilerParams(vmem_limit_bytes=mib * MIB)


def cost(flops, moved):
    return pl.CostEstimate(flops=flops // 64, bytes_accessed=moved // 64, transcendentals=0)


def whole():
    return pl.BlockSpec(memory_space=pltpu.VMEM)


def scalars():
    return pl.BlockSpec(memory_space=pltpu.SMEM)


def dot(a, b):
    return jnp.dot(a, b, preferred_element_type=F32)


def in_hbm(*arrays):
    return [pltpu.with_memory_space_constraint(array, pltpu.HBM) for array in arrays]


def one_hot_leaf(row, leaf_len):
    column = jnp.broadcast_to(row, (128, leaf_len)).T
    lanes = lax.broadcasted_iota(jnp.int32, (leaf_len, 128), 1)
    return jnp.concatenate(
        [
            jnp.where(column == lanes + 128 * t, 1.0, 0.0).astype(BF)
            for t in range(leaf_len // 128)
        ],
        axis=1,
    )


def one_hot_grid(row, leaf_len):
    cells = lax.broadcasted_iota(jnp.int32, (leaf_len, leaf_len), 0)
    return jnp.where(cells == row, 1.0, 0.0).astype(BF)


def owner_tables(me, layers, owners, blocks):
    leaves, entries = owners.shape
    slots = layers * 4
    layer, chip, core = me // 8, (me // 2) & 3, me & 1

    back = layer - owners // 8
    back = jnp.where(back < 0, back + layers, back)
    turn = jnp.where(back < 2, back, jnp.where(back == layers - 1, 2, back + 1))
    slot_of = ((owners & 1) ^ core) * slots + turn * 4 + (((owners // 2) & 3) ^ chip)

    shape = (leaves + 1, 2 * slots)
    lane = lax.broadcasted_iota(jnp.int32, shape, 1)
    pad = jnp.full((1, entries), -1, jnp.int32)
    named = jnp.concatenate([pad, slot_of], axis=0)
    chosen = jnp.concatenate([pad, blocks], axis=0)
    block = jnp.zeros(shape, jnp.int32)
    for k in range(entries):
        block = jnp.where(named[:, k:k + 1] == lane, chosen[:, k:k + 1] + 1, block)
    return slot_of, block


def owner_at(me, layers, plane, slot):
    turn, side = slot // 4, slot % 4
    shift = (0, 1, layers - 1)[turn] if turn < 3 else turn - 1
    source = me // 8 - shift
    source = jnp.where(source < 0, source + layers, source)
    return source * 8 + (((me // 2) & 3) ^ side) * 2 + ((me & 1) ^ plane)


def skeleton_kernel(per, layers, me_ref, order_ref, comp_ref, basis_ref, transfer_ref,
                    owner_ref, leaf_ref, ordered_ref, shared_ref, cross_ref, inner_ref,
                    entry_ref, block_ref, root_ref):
    step = pl.program_id(0)
    leaf_len = basis_ref.shape[2]

    @pl.when(step == 0)
    def _():
        root_ref[...] = jnp.zeros_like(root_ref)
        slot_of, block = owner_tables(me_ref[0], layers, owner_ref[...], leaf_ref[...])
        rows, lanes = block.shape
        entry_ref[...] = slot_of
        block_ref[:rows, :lanes] = block

    hots = [one_hot_leaf(order_ref[pl.ds(step * per + i, 1), :], leaf_len) for i in range(per)]
    ordered = [
        dot(hots[i], comp_ref[i * leaf_len:(i + 1) * leaf_len, :]).astype(BF) for i in range(per)
    ]
    skeletons = [dot(basis_ref[i], ordered[i]).astype(BF) for i in range(per)]
    across = jnp.concatenate([transfer_ref[i] for i in range(per)], axis=1)
    root_ref[...] += dot(across, jnp.concatenate(skeletons, axis=0))
    for i in range(per):
        ordered_ref[i * leaf_len:(i + 1) * leaf_len, :] = ordered[i]
        shared_ref[pl.ds(step * per + i + 1, 1)] = skeletons[i][None]

    even = me_ref[0] % 2 == 0

    @pl.when((step == 0) & even)
    def _():
        cross_ref[...] = ordered[0]

    @pl.when((step == 0) & ~even)
    def _():
        inner_ref[...] = ordered[0]

    last = step == pl.num_programs(0) - 1

    @pl.when(last & even)
    def _():
        inner_ref[...] = ordered[-1]

    @pl.when(last & ~even)
    def _():
        cross_ref[...] = ordered[-1]

    @pl.when(last)
    def _():
        shared_ref[pl.ds(0, 1)] = root_ref[...].astype(BF)[None]


def skeletons_of(me, leaf_order, composition, leaf_basis, transfer, owners, blocks, layers, per=4):
    leaves, rank, leaf_len = leaf_basis.shape
    fields = composition.shape[1]
    entries = owners.shape[1]
    edge = jax.ShapeDtypeStruct((leaf_len, fields), BF)
    return pl.pallas_call(
        functools.partial(skeleton_kernel, per, layers),
        name="order_and_skeleton",
        grid=(leaves // per,),
        in_specs=[
            scalars(),
            pl.BlockSpec((leaves, leaf_len), lambda s: (0, 0)),
            pl.BlockSpec((per * leaf_len, fields), lambda s: (s, 0)),
            pl.BlockSpec((per, rank, leaf_len), lambda s: (s, 0, 0)),
            pl.BlockSpec((per, rank, rank), lambda s: (s, 0, 0)),
            pl.BlockSpec((leaves, entries), lambda s: (0, 0)),
            pl.BlockSpec((leaves, entries), lambda s: (0, 0)),
        ],
        out_specs=[
            pl.BlockSpec((per * leaf_len, fields), lambda s: (s, 0)),
            pl.BlockSpec((leaves + 1, rank, fields), lambda s: (0, 0, 0)),
            pl.BlockSpec((leaf_len, fields), lambda s: (0, 0)),
            pl.BlockSpec((leaf_len, fields), lambda s: (0, 0)),
            pl.BlockSpec((leaves, entries), lambda s: (0, 0)),
            pl.BlockSpec((16, 128), lambda s: (0, 0)),
        ],
        out_shape=[
            jax.ShapeDtypeStruct((leaves * leaf_len, fields), BF),
            jax.ShapeDtypeStruct((leaves + 1, rank, fields), BF),
            edge,
            edge,
            jax.ShapeDtypeStruct((leaves, entries), jnp.int32),
            jax.ShapeDtypeStruct((16, 128), jnp.int32),
        ],
        scratch_shapes=[pltpu.VMEM((rank, fields), F32)],
        compiler_params=params(16),
        cost_estimate=cost(leaves * leaf_len * leaf_len * fields * 2, 4 * MIB),
    )(me, *in_hbm(leaf_order, composition, leaf_basis, transfer, owners, blocks))


def join_kernel(*refs):
    out = refs[-1]
    at = 0
    for ref in refs[:-1]:
        out[at:at + ref.shape[0]] = ref[...]
        at += ref.shape[0]


def join(parts):
    if len(parts) == 1:
        return parts[0]
    shape = (sum(part.shape[0] for part in parts),) + parts[0].shape[1:]
    return pl.pallas_call(
        join_kernel,
        name="join",
        in_specs=[whole()] * len(parts),
        out_specs=whole(),
        out_shape=jax.ShapeDtypeStruct(shape, BF),
        compiler_params=params(8 if shape[0] <= 32 else 32),
        cost_estimate=cost(0, MIB // 2),
    )(*parts)


def choose_kernel(me_ref, x_ref, y_ref, out_ref):
    @pl.when(me_ref[0] % 2 == 0)
    def _():
        out_ref[...] = x_ref[...]

    @pl.when(me_ref[0] % 2 == 1)
    def _():
        out_ref[...] = y_ref[...]


def choose(me, from_x, from_y):
    return pl.pallas_call(
        choose_kernel,
        name="choose",
        in_specs=[scalars(), whole(), whole()],
        out_specs=whole(),
        out_shape=jax.ShapeDtypeStruct(from_x.shape, BF),
        compiler_params=params(8),
        cost_estimate=cost(0, MIB // 4),
    )(me, from_x, from_y)


def dense_kernel(per, layers, me_ref, slot_ref, block_ref, inner_ref, coupling_ref, top_ref,
                 transfer_ref, own_ref, other_ref, turned_ref):
    step = pl.program_id(0)
    entries, rank = coupling_ref.shape[1:3]
    fields = inner_ref.shape[1]
    leaves = own_ref.shape[0] - 1
    slots = layers * 4
    upper = lax.broadcasted_iota(jnp.int32, (rank, 2 * rank), 1) // rank
    for i in range(per):
        leaf = step * per + i
        turned_ref[leaf] = transfer_ref[i].T
        own_ref[leaf] = jnp.zeros(own_ref.shape[1:], BF)
        other_ref[leaf] = jnp.zeros(other_ref.shape[1:], BF)
        for k in range(entries):
            slot = slot_ref[leaf, k]
            block = coupling_ref[i, k]
            both = jnp.concatenate([block, block], axis=1)
            for plane, out_ref in ((0, own_ref), (1, other_ref)):
                here = slot - plane * slots

                @pl.when((here >= 0) & (here < slots))
                def _(here=here, out_ref=out_ref, both=both, leaf=leaf):
                    at = pl.ds(pl.multiple_of(here // 2 * 2 * rank, 2 * rank), 2 * rank)
                    out_ref[leaf, :, at] = jnp.where(upper == here % 2, both, out_ref[leaf, :, at])

    @pl.when(step == pl.num_programs(0) - 1)
    def _():
        me = me_ref[0]
        for plane, out_ref in ((0, own_ref), (1, other_ref)):
            for slot in range(0, slots, 2):
                pair = []
                for one in (slot, slot + 1):
                    owner = owner_at(me, layers, plane, one)
                    block = top_ref[0, owner]
                    pair.append(jnp.where(jnp.abs(owner - me) >= 2, block, jnp.zeros_like(block)))
                out_ref[leaves, :, slot * rank:(slot + 2) * rank] = jnp.concatenate(pair, axis=1)

    @pl.when(step == 0)
    def _():
        for t in range(inner_ref.shape[0] // rank):
            part = inner_ref[t * rank:(t + 1) * rank, :]
            other_ref[leaves + 1, :, t * fields:(t + 1) * fields] = part
        other_ref[leaves + 2] = jnp.zeros(other_ref.shape[1:], BF)
        blocks = block_ref[...].astype(F32).astype(BF)
        other_ref[leaves + 2, :blocks.shape[0], :blocks.shape[1]] = blocks


def dense_couplings(me, slot_of, block, inner, coupling, top_coupling, transfer, layers, per=4):
    leaves, entries, rank, _ = coupling.shape
    slots = layers * 4
    own = (leaves + 1, rank, slots * rank)
    other = (leaves + 3, rank, slots * rank)
    return pl.pallas_call(
        functools.partial(dense_kernel, per, layers),
        name="couplings_by_owner",
        grid=(leaves // per,),
        in_specs=[
            scalars(),
            scalars(),
            pl.BlockSpec(block.shape, lambda s: (0, 0)),
            pl.BlockSpec(inner.shape, lambda s: (0, 0)),
            pl.BlockSpec((per, entries, rank, rank), lambda s: (s, 0, 0, 0)),
            pl.BlockSpec(top_coupling.shape, lambda s: (0, 0, 0, 0)),
            pl.BlockSpec((per, rank, rank), lambda s: (s, 0, 0)),
        ],
        out_specs=[
            pl.BlockSpec(own, lambda s: (0, 0, 0)),
            pl.BlockSpec(other, lambda s: (0, 0, 0)),
            pl.BlockSpec(transfer.shape, lambda s: (0, 0, 0)),
        ],
        out_shape=[
            jax.ShapeDtypeStruct(own, BF),
            jax.ShapeDtypeStruct(other, BF),
            jax.ShapeDtypeStruct(transfer.shape, BF),
        ],
        compiler_params=params(16 if slots <= 16 else 48),
        cost_estimate=cost(0, 8 * MIB),
    )(me, slot_of, block, inner, *in_hbm(coupling, top_coupling, transfer))


def round_kernel(plane, steps, slots, counts, at_ref, *refs):
    sides = []
    for number in counts:
        sides.append(refs[:number])
        refs = refs[number:]
    blocks_ref, out = refs[0], refs[-1]
    rows, rank, _ = out.shape
    low, high = steps[0] * 4 * rank, (steps[-1] + 1) * 4 * rank

    def block_at(side, base, index):
        for ref in side:
            if base < ref.shape[0]:
                return ref[base + index]
            base -= ref.shape[0]

    for row in range(rows):
        chosen = [
            block_at(side, place * rows, at_ref[(row + 1) % rows, plane * slots + step * 4 + q])
            for place, step in enumerate(steps)
            for q, side in enumerate(sides)
        ]
        value = dot(blocks_ref[row, :, low:high], jnp.concatenate(chosen, axis=0))
        if len(refs) > 2:
            value = value + refs[1][row]
        out[row] = value


def far_round(plane, steps, slots, at, parts, blocks, total=None):
    rank, fields = parts[0][0].shape[1:]
    rows = parts[0][0].shape[0] // (1 if len(parts[0]) > 1 else len(steps))
    args = [part for side in parts for part in side] + [blocks] + ([] if total is None else [total])
    return pl.pallas_call(
        functools.partial(round_kernel, plane, steps, slots, [len(side) for side in parts]),
        name="far_" + str(plane) + "_" + str(steps[0]),
        in_specs=[scalars()] + [whole()] * len(args),
        out_specs=whole(),
        out_shape=jax.ShapeDtypeStruct((rows, rank, fields), F32),
        compiler_params=params(16 if slots <= 16 else 48),
        cost_estimate=cost(rows * rank * 4 * rank * fields * 2 * len(steps), MIB),
    )(at, *args)


def near_kernel(edges, pair_of, last_pair, mask_ref, order_ref, table_ref, basis_ref,
                ordered_ref, *refs):
    if edges:
        me_ref, cross_ref, inner_ref, blocks_ref = refs[:4]
        near_ref, turned_ref, at_ref = refs[-3:]
    else:
        near_ref, turned_ref = refs[-2:]
    pair = pair_of(pl.program_id(0))
    leaf_len = basis_ref.shape[2]
    leaves = basis_ref.shape[0]

    def leaf_at(leaf):
        return ordered_ref[pl.ds(pl.multiple_of(leaf * leaf_len, leaf_len), leaf_len), :]

    low, high = leaf_at(2 * pair), leaf_at(2 * pair + 1)
    prev, following = leaf_at(jnp.maximum(2 * pair - 1, 0)), leaf_at(jnp.minimum(2 * pair + 2, leaves - 1))
    if edges:
        even = me_ref[0] % 2 == 0
        cross = cross_ref[...]
        wide = cross.shape[1]
        inner = jnp.concatenate(
            [inner_ref[0, :, t:t + wide] for t in range(0, inner_ref.shape[2], wide)], axis=0
        )[:leaf_len]
        prev = jnp.where(pair == 0, jnp.where(even, cross, inner), prev)
        following = jnp.where(pair == last_pair, jnp.where(even, inner, cross), following)

        @pl.when(pl.program_id(0) == 0)
        def _():
            rows, lanes = at_ref.shape
            at_ref[...] = blocks_ref[0, :rows, :lanes].astype(F32).astype(jnp.int32)


    def masked(leaf, side, value):
        return jnp.where(mask_ref[side, leaf] > 0, value, jnp.zeros_like(value))

    left = jnp.concatenate(
        [masked(2 * pair, 0, prev), low, masked(2 * pair, 1, high)], axis=0
    )
    right = jnp.concatenate(
        [masked(2 * pair + 1, 0, low), high, masked(2 * pair + 1, 1, following)], axis=0
    )
    near = dot(table_ref[...], jnp.concatenate([left, right], axis=1)).astype(BF)
    fields = ordered_ref.shape[1]
    turned = []
    for i in range(2):
        hot = one_hot_grid(order_ref[pl.ds(2 * pair + i, 1), :], leaf_len)
        at = pl.ds(i * leaf_len, leaf_len)
        both = jnp.concatenate([near[:, i * fields:(i + 1) * fields], basis_ref[2 * pair + i].T], axis=1)
        moved = dot(hot, both).astype(BF)
        near_ref[at, :] = moved[:, :fields]
        turned.append(moved[:, fields:])
    turned_ref[...] = jnp.concatenate(turned, axis=1)


def near_field(pairs, near_list, leaf_order, tables, basis, ordered, halos=None, filled=None):
    leaves, rank, leaf_len = basis.shape
    fields = ordered.shape[1]
    last = leaves // 2 - 1
    gap = pairs[1] - pairs[0] if len(pairs) > 1 else 1

    def pair_of(step):
        return pairs[0] + gap * step

    in_specs = [
        scalars(),
        whole(),
        whole(),
        whole(),
        whole(),
    ]
    args = [near_list.T, leaf_order, tables, basis, ordered]
    aliases = {}
    extra = []
    if halos is not None:
        me, cross, other = halos
        row = (1,) + other.shape[1:]
        in_specs += [
            scalars(),
            pl.BlockSpec((leaf_len, fields), lambda s: (0, 0)),
            pl.BlockSpec(row, lambda s: (leaves + 1, 0, 0)),
            pl.BlockSpec(row, lambda s: (leaves + 2, 0, 0)),
        ]
        args += [me, cross, other, other]
        extra = [(16, 128)]
    if filled is not None:
        aliases = {len(args): 0, len(args) + 1: 1}
        in_specs += [pl.BlockSpec(memory_space=pl.ANY)] * 2
        args += list(filled)
    return pl.pallas_call(
        functools.partial(near_kernel, halos is not None, pair_of, last),
        name="near_" + str(pairs[0]),
        grid=(len(pairs),),
        in_specs=in_specs,
        out_specs=[
            pl.BlockSpec((2 * leaf_len, fields), lambda s: (pair_of(s), 0)),
            pl.BlockSpec((leaf_len, 2 * rank), lambda s: (pair_of(s), 0)),
        ] + [pl.BlockSpec(shape, lambda s: (0, 0)) for shape in extra],
        out_shape=[
            jax.ShapeDtypeStruct((leaves * leaf_len, fields), BF),
            jax.ShapeDtypeStruct((leaves // 2 * leaf_len, 2 * rank), BF),
        ] + [jax.ShapeDtypeStruct(shape, jnp.int32) for shape in extra],
        input_output_aliases=aliases,
        compiler_params=params(16),
        cost_estimate=cost(len(pairs) * 2 * leaf_len * leaf_len * fields * 10, len(pairs) * MIB),
    )(*args)


def field_kernel(per, own_ref, other_ref, turned_transfer_ref, near_ref, turned_ref, out_ref):
    step = pl.program_id(0)
    leaf_len = out_ref.shape[0] // per
    root = own_ref.shape[0] - 1
    local = own_ref[root] + other_ref[root]
    coarse = local.astype(BF)
    fine = (local - coarse.astype(F32)).astype(BF)
    both = jnp.concatenate([coarse, fine], axis=1)
    fields = local.shape[1]
    for pair in range(per // 2):
        values = []
        for i in range(2):
            leaf = step * per + 2 * pair + i
            down = dot(turned_transfer_ref[leaf], both)
            value = own_ref[leaf] + other_ref[leaf] + (down[:, :fields] + down[:, fields:])
            values.append(value.astype(BF))
        zero = jnp.zeros_like(values[0])
        corner = jnp.concatenate(
            [
                jnp.concatenate([values[0], zero], axis=1),
                jnp.concatenate([zero, values[1]], axis=1),
            ],
            axis=0,
        )
        at = pl.multiple_of((step * (per // 2) + pair) * leaf_len, leaf_len)
        far = dot(turned_ref[pl.ds(at, leaf_len), :], corner)
        for i in range(2):
            near = near_ref[pl.ds(2 * at + i * leaf_len, leaf_len), :].astype(F32)
            rows = slice((2 * pair + i) * leaf_len, (2 * pair + i + 1) * leaf_len)
            out_ref[rows, :] = (near + far[:, i * fields:(i + 1) * fields]).astype(BF)


def field(own, other, turned_transfer, near, turned, per=4):
    leaves, rank, _ = turned_transfer.shape
    fields = near.shape[1]
    leaf_len = near.shape[0] // leaves
    return pl.pallas_call(
        functools.partial(field_kernel, per),
        name="local_and_field",
        grid=(leaves // per,),
        in_specs=[whole()] * 5,
        out_specs=pl.BlockSpec((per * leaf_len, fields), lambda s: (s, 0)),
        out_shape=jax.ShapeDtypeStruct(near.shape, BF),
        compiler_params=params(16),
        cost_estimate=cost(leaves * leaf_len * rank * fields * 2, 4 * MIB),
    )(own, other, turned_transfer, near, turned)


def after(block, *others):
    return lax.optimization_barrier((block,) + others)[0]


def on_device(
    composition,
    leaf_basis,
    transfer,
    coupling,
    top_coupling,
    admissible_owner,
    admissible_leaf,
    near_list,
    leaf_order,
):
    leaves, rank, leaf_len = leaf_basis.shape
    count = lax.axis_size("subtree")
    layers = count // 8
    slots = layers * 4
    pairs = leaves // 2
    cut = pairs // 2
    me = lax.axis_index("subtree").reshape(1)

    ordered, shared, cross, inner, slot_of, own_at = skeletons_of(
        me, leaf_order, composition, leaf_basis, transfer, admissible_owner, admissible_leaf, layers
    )
    tables = jnp.asarray(near_tables(leaf_len))
    near_args = (near_list, leaf_order, tables, leaf_basis)

    line = along_z(shared, 1)
    from_x, from_y = over_x(shared), over_y(shared)
    filled = near_field(list(range(1, cut)), *near_args, ordered)
    line = after(line, filled[0])
    lines = [along_z(shared, layers - 1)]
    for _ in range(layers - 3):
        lines.append(along_z(line if len(lines) == 1 else lines[-1], 1))
    ready = after(line, from_x, from_y, lines[0])
    next_x, next_y = over_x(ready), over_y(ready)
    far = onward(choose(me, after(from_x, ready), from_y))
    cross = lax.ppermute(
        cross,
        "subtree",
        [(d, d + 1) for d in range(1, count - 1, 2)] + [(d, d - 1) for d in range(2, count, 2)],
    )
    own_blocks, my_other, turned_transfer = dense_couplings(
        me, after(slot_of, ready), own_at, inner, coupling, top_coupling, transfer, layers
    )

    joined = after(join([after(lines[0], my_other)] + lines[1:]), next_x, next_y, far, cross)
    last_x, last_y = over_x(joined), over_y(joined)
    chosen = choose(me, after(next_x, joined), next_y)
    next_far = onward(chosen)
    other_blocks = over_core(after(my_other, chosen))
    held = after(ordered, joined)
    filled = near_field(list(range(cut, pairs - 1)), *near_args, held, filled=filled)
    next_far = after(next_far, filled[0])
    last_far = [along_z(far, layers - 1)]
    for _ in range(layers - 3):
        last_far.append(along_z(next_far if len(last_far) == 1 else last_far[-1], 1))
    held = after(ordered, filled[0])
    *filled, other_at = near_field(
        [0, pairs - 1], *near_args, held, halos=(me, cross, other_blocks), filled=filled
    )
    round_0 = ((shared, line), (from_x, next_x), (from_y, next_y), (far, next_far))
    steps = [0, 1]
    own = far_round(0, steps, slots, own_at, round_0, own_blocks)
    other = far_round(1, steps, slots, other_at, round_0, other_blocks)
    steps = list(range(2, layers))
    round_1 = ((joined,), (last_x,), (last_y,), (after(last_far[0], own, other), *last_far[1:]))
    other = far_round(1, steps, slots, other_at, round_1, other_blocks, other)
    own = far_round(0, steps, slots, own_at, round_1, own_blocks, own)
    return field(own, over_core(other), turned_transfer, *filled)


def solution(mesh):
    placed = (
        P(("groups", "subtree"), None),
        P("subtree", None, None),
        P("subtree", None, None),
        P("subtree", None, None, None),
        P("subtree", None, None, None),
        P(("groups", "subtree"), None),
        P(("groups", "subtree"), None),
        P(("groups", "subtree"), None),
        P(("groups", "subtree"), None),
    )
    return jax.shard_map(
        on_device,
        mesh=mesh,
        in_specs=placed,
        out_specs=P(("groups", "subtree"), None),
        check_vma=False,
    )
```

```python
import functools

import jax
import jax.numpy as jnp
import ml_dtypes
import numpy as np
from jax import lax
from jax.experimental import pallas as pl
from jax.experimental.pallas import tpu as pltpu
from jax.sharding import PartitionSpec as P

COULOMB_SCALE = 0.15
SOFTENING = 0.25
BF = jnp.bfloat16
F32 = jnp.float32
MIB = 1 << 20


def near_tables(leaf_len):
    cells = np.arange(leaf_len)
    along = (cells // 64).astype(np.float32)
    across = (cells // 8 % 8).astype(np.float32)
    height = (cells % 8).astype(np.float32)
    extent = leaf_len // 64
    tables = []
    for offset in (-1, 0, 1):
        delta_x = along[:, None] - along[None, :] - np.float32(offset * extent)
        delta_y = across[:, None] - across[None, :]
        delta_z = height[:, None] - height[None, :]
        square = delta_x * delta_x + delta_y * delta_y + delta_z * delta_z
        value = np.float32(COULOMB_SCALE) / np.sqrt(square + np.float32(SOFTENING))
        tables.append(value.astype(ml_dtypes.bfloat16))
    return np.concatenate(tables, axis=1)


def send(block, target):
    count = lax.axis_size("subtree")
    return lax.ppermute(block, "subtree", [(d, target(d)) for d in range(count)])


def over_core(block):
    return send(block, lambda d: d ^ 1)


def over_x(block):
    return send(block, lambda d: d ^ 2)


def over_y(block):
    return send(block, lambda d: d ^ 4)


def onward(block):
    return send(block, lambda d: d ^ (2 if d % 2 else 4))


def along_z(block, step):
    layers = lax.axis_size("subtree") // 8
    return send(block, lambda d: (d // 8 + step) % layers * 8 + d % 8)


def params(mib):
    return pltpu.CompilerParams(vmem_limit_bytes=mib * MIB)


def cost(flops, moved):
    return pl.CostEstimate(flops=flops // 64, bytes_accessed=moved // 64, transcendentals=0)


def whole():
    return pl.BlockSpec(memory_space=pltpu.VMEM)


def scalars():
    return pl.BlockSpec(memory_space=pltpu.SMEM)


def dot(a, b):
    return jnp.dot(a, b, preferred_element_type=F32)


def in_hbm(*arrays):
    return [pltpu.with_memory_space_constraint(array, pltpu.HBM) for array in arrays]


def one_hot_leaf(row, leaf_len):
    column = jnp.broadcast_to(row, (128, leaf_len)).T
    lanes = lax.broadcasted_iota(jnp.int32, (leaf_len, 128), 1)
    return jnp.concatenate(
        [
            jnp.where(column == lanes + 128 * t, 1.0, 0.0).astype(BF)
            for t in range(leaf_len // 128)
        ],
        axis=1,
    )


def one_hot_grid(row, leaf_len):
    cells = lax.broadcasted_iota(jnp.int32, (leaf_len, leaf_len), 0)
    return jnp.where(cells == row, 1.0, 0.0).astype(BF)


def owner_tables(me, layers, owners, blocks):
    leaves, entries = owners.shape
    slots = layers * 4
    rows = leaves + 1
    shape = (rows, 2 * slots)
    lane = lax.broadcasted_iota(jnp.int32, shape, 1)
    plane = (lane >= slots).astype(jnp.int32)
    slot = lane - plane * slots
    layer, chip, core = me // 8, (me // 2) & 3, me & 1
    turn = slot >> 2
    shift = jnp.where(turn < 2, turn, jnp.where(turn == 2, layers - 1, turn - 1))
    source = layer - shift
    source = jnp.where(source < 0, source + layers, source)
    owner = source * 8 + (chip ^ (slot & 3)) * 2 + (core ^ plane)
    row = lax.broadcasted_iota(jnp.int32, shape, 0)
    distant = jnp.abs(owner - me) >= 2
    entry = jnp.where((row == 0) & distant, owner, -1)
    block = jnp.zeros(shape, jnp.int32)
    pad = jnp.full((1, entries), -1, jnp.int32)
    named = jnp.concatenate([pad, owners], axis=0)
    chosen = jnp.concatenate([pad, blocks], axis=0)
    for k in range(entries):
        match = named[:, k:k + 1] == owner
        entry = jnp.where(match, k, entry)
        block = jnp.where(match, chosen[:, k:k + 1] + 1, block)
    return entry, block


def skeleton_kernel(per, layers, me_ref, order_ref, comp_ref, basis_ref, transfer_ref,
                    owner_ref, leaf_ref, ordered_ref, shared_ref, cross_ref, inner_ref,
                    entry_ref, block_ref, root_ref):
    step = pl.program_id(0)
    leaf_len = basis_ref.shape[2]

    @pl.when(step == 0)
    def _():
        root_ref[...] = jnp.zeros_like(root_ref)
        entry, block = owner_tables(me_ref[0], layers, owner_ref[...], leaf_ref[...])
        rows, lanes = entry.shape
        entry_ref[:rows, :lanes] = entry
        block_ref[:rows, :lanes] = block

    hots = [one_hot_leaf(order_ref[pl.ds(step * per + i, 1), :], leaf_len) for i in range(per)]
    ordered = [
        dot(hots[i], comp_ref[i * leaf_len:(i + 1) * leaf_len, :]).astype(BF) for i in range(per)
    ]
    skeletons = [dot(basis_ref[i], ordered[i]).astype(BF) for i in range(per)]
    across = jnp.concatenate([transfer_ref[i] for i in range(per)], axis=1)
    root_ref[...] += dot(across, jnp.concatenate(skeletons, axis=0))
    for i in range(per):
        ordered_ref[i * leaf_len:(i + 1) * leaf_len, :] = ordered[i]
        shared_ref[pl.ds(step * per + i + 1, 1)] = skeletons[i][None]

    even = me_ref[0] % 2 == 0

    @pl.when((step == 0) & even)
    def _():
        cross_ref[...] = ordered[0]

    @pl.when((step == 0) & ~even)
    def _():
        inner_ref[...] = ordered[0]

    last = step == pl.num_programs(0) - 1

    @pl.when(last & even)
    def _():
        inner_ref[...] = ordered[-1]

    @pl.when(last & ~even)
    def _():
        cross_ref[...] = ordered[-1]

    @pl.when(last)
    def _():
        shared_ref[pl.ds(0, 1)] = root_ref[...].astype(BF)[None]


def skeletons_of(me, leaf_order, composition, leaf_basis, transfer, owners, blocks, layers, per=4):
    leaves, rank, leaf_len = leaf_basis.shape
    fields = composition.shape[1]
    entries = owners.shape[1]
    edge = jax.ShapeDtypeStruct((leaf_len, fields), BF)
    return pl.pallas_call(
        functools.partial(skeleton_kernel, per, layers),
        name="order_and_skeleton",
        grid=(leaves // per,),
        in_specs=[
            scalars(),
            pl.BlockSpec((leaves, leaf_len), lambda s: (0, 0)),
            pl.BlockSpec((per * leaf_len, fields), lambda s: (s, 0)),
            pl.BlockSpec((per, rank, leaf_len), lambda s: (s, 0, 0)),
            pl.BlockSpec((per, rank, rank), lambda s: (s, 0, 0)),
            pl.BlockSpec((leaves, entries), lambda s: (0, 0)),
            pl.BlockSpec((leaves, entries), lambda s: (0, 0)),
        ],
        out_specs=[
            pl.BlockSpec((per * leaf_len, fields), lambda s: (s, 0)),
            pl.BlockSpec((leaves + 1, rank, fields), lambda s: (0, 0, 0)),
            pl.BlockSpec((leaf_len, fields), lambda s: (0, 0)),
            pl.BlockSpec((leaf_len, fields), lambda s: (0, 0)),
            pl.BlockSpec((16, 128), lambda s: (0, 0)),
            pl.BlockSpec((16, 128), lambda s: (0, 0)),
        ],
        out_shape=[
            jax.ShapeDtypeStruct((leaves * leaf_len, fields), BF),
            jax.ShapeDtypeStruct((leaves + 1, rank, fields), BF),
            edge,
            edge,
            jax.ShapeDtypeStruct((16, 128), jnp.int32),
            jax.ShapeDtypeStruct((16, 128), jnp.int32),
        ],
        scratch_shapes=[pltpu.VMEM((rank, fields), F32)],
        compiler_params=params(16),
        cost_estimate=cost(leaves * leaf_len * leaf_len * fields * 2, 4 * MIB),
    )(me, *in_hbm(leaf_order, composition, leaf_basis, transfer, owners, blocks))


def join_kernel(*refs):
    out = refs[-1]
    at = 0
    for ref in refs[:-1]:
        out[at:at + ref.shape[0]] = ref[...]
        at += ref.shape[0]


def join(parts):
    if len(parts) == 1:
        return parts[0]
    shape = (sum(part.shape[0] for part in parts),) + parts[0].shape[1:]
    return pl.pallas_call(
        join_kernel,
        name="join",
        in_specs=[whole()] * len(parts),
        out_specs=whole(),
        out_shape=jax.ShapeDtypeStruct(shape, BF),
        compiler_params=params(8 if shape[0] <= 32 else 32),
        cost_estimate=cost(0, MIB // 2),
    )(*parts)


def choose_kernel(me_ref, x_ref, y_ref, out_ref):
    @pl.when(me_ref[0] % 2 == 0)
    def _():
        out_ref[...] = x_ref[...]

    @pl.when(me_ref[0] % 2 == 1)
    def _():
        out_ref[...] = y_ref[...]


def choose(me, from_x, from_y):
    return pl.pallas_call(
        choose_kernel,
        name="choose",
        in_specs=[scalars(), whole(), whole()],
        out_specs=whole(),
        out_shape=jax.ShapeDtypeStruct(from_x.shape, BF),
        compiler_params=params(8),
        cost_estimate=cost(0, MIB // 4),
    )(me, from_x, from_y)


def dense_kernel(per, slots, entry_ref, block_ref, inner_ref, coupling_ref, top_ref,
                 transfer_ref, own_ref, other_ref, turned_ref):
    step = pl.program_id(0)
    rank = coupling_ref.shape[2]
    fields = inner_ref.shape[1]
    leaves = own_ref.shape[0] - 1
    for i in range(per):
        turned_ref[step * per + i] = transfer_ref[i].T

    def fill(out_ref, plane, row, entry_row, block_of):
        for slot in range(0, slots, 2):
            pair = []
            for one in (slot, slot + 1):
                entry = entry_ref[entry_row, plane * slots + one]
                block = block_of(jnp.maximum(entry, 0))
                pair.append(jnp.where(entry >= 0, block, jnp.zeros_like(block)))
            out_ref[row, :, slot * rank:(slot + 2) * rank] = jnp.concatenate(pair, axis=1)

    for plane, out_ref in ((0, own_ref), (1, other_ref)):
        for i in range(per):
            leaf = step * per + i
            fill(out_ref, plane, leaf, leaf + 1, lambda entry, i=i: coupling_ref[i, entry])

        @pl.when(step == pl.num_programs(0) - 1)
        def _(plane=plane, out_ref=out_ref):
            fill(out_ref, plane, leaves, 0, lambda entry: top_ref[0, entry])

    @pl.when(step == 0)
    def _():
        for t in range(inner_ref.shape[0] // rank):
            part = inner_ref[t * rank:(t + 1) * rank, :]
            other_ref[leaves + 1, :, t * fields:(t + 1) * fields] = part
        other_ref[leaves + 2] = jnp.zeros(other_ref.shape[1:], BF)
        blocks = block_ref[...].astype(F32).astype(BF)
        other_ref[leaves + 2, :blocks.shape[0], :blocks.shape[1]] = blocks


def dense_couplings(entry, block, inner, coupling, top_coupling, transfer, slots, per=4):
    leaves, entries, rank, _ = coupling.shape
    own = (leaves + 1, rank, slots * rank)
    other = (leaves + 3, rank, slots * rank)
    return pl.pallas_call(
        functools.partial(dense_kernel, per, slots),
        name="couplings_by_owner",
        grid=(leaves // per,),
        in_specs=[
            scalars(),
            pl.BlockSpec(block.shape, lambda s: (0, 0)),
            pl.BlockSpec(inner.shape, lambda s: (0, 0)),
            pl.BlockSpec((per, entries, rank, rank), lambda s: (s, 0, 0, 0)),
            pl.BlockSpec(top_coupling.shape, lambda s: (0, 0, 0, 0)),
            pl.BlockSpec((per, rank, rank), lambda s: (s, 0, 0)),
        ],
        out_specs=[
            pl.BlockSpec(own, lambda s: (0, 0, 0)),
            pl.BlockSpec(other, lambda s: (0, 0, 0)),
            pl.BlockSpec(transfer.shape, lambda s: (0, 0, 0)),
        ],
        out_shape=[
            jax.ShapeDtypeStruct(own, BF),
            jax.ShapeDtypeStruct(other, BF),
            jax.ShapeDtypeStruct(transfer.shape, BF),
        ],
        compiler_params=params(16 if slots <= 16 else 48),
        cost_estimate=cost(0, 8 * MIB),
    )(entry, block, inner, *in_hbm(coupling, top_coupling, transfer))


def round_kernel(plane, steps, slots, counts, at_ref, *refs):
    sides = []
    for number in counts:
        sides.append(refs[:number])
        refs = refs[number:]
    blocks_ref, out = refs[0], refs[-1]
    rows, rank, _ = out.shape
    low, high = steps[0] * 4 * rank, (steps[-1] + 1) * 4 * rank

    def block_at(side, base, index):
        for ref in side:
            if base < ref.shape[0]:
                return ref[base + index]
            base -= ref.shape[0]

    for row in range(rows):
        chosen = [
            block_at(side, place * rows, at_ref[(row + 1) % rows, plane * slots + step * 4 + q])
            for place, step in enumerate(steps)
            for q, side in enumerate(sides)
        ]
        value = dot(blocks_ref[row, :, low:high], jnp.concatenate(chosen, axis=0))
        if len(refs) > 2:
            value = value + refs[1][row]
        out[row] = value


def far_round(plane, steps, slots, at, parts, blocks, total=None):
    rank, fields = parts[0][0].shape[1:]
    rows = parts[0][0].shape[0] // (1 if len(parts[0]) > 1 else len(steps))
    args = [part for side in parts for part in side] + [blocks] + ([] if total is None else [total])
    return pl.pallas_call(
        functools.partial(round_kernel, plane, steps, slots, [len(side) for side in parts]),
        name="far_" + str(plane) + "_" + str(steps[0]),
        in_specs=[scalars()] + [whole()] * len(args),
        out_specs=whole(),
        out_shape=jax.ShapeDtypeStruct((rows, rank, fields), F32),
        compiler_params=params(16 if slots <= 16 else 48),
        cost_estimate=cost(rows * rank * 4 * rank * fields * 2 * len(steps), MIB),
    )(at, *args)


def near_kernel(edges, pair_of, last_pair, mask_ref, order_ref, table_ref, basis_ref,
                ordered_ref, *refs):
    if edges:
        me_ref, cross_ref, inner_ref, blocks_ref = refs[:4]
        near_ref, turned_ref, at_ref = refs[-3:]
    else:
        near_ref, turned_ref = refs[-2:]
    pair = pair_of(pl.program_id(0))
    leaf_len = basis_ref.shape[2]
    leaves = basis_ref.shape[0]

    def leaf_at(leaf):
        return ordered_ref[pl.ds(pl.multiple_of(leaf * leaf_len, leaf_len), leaf_len), :]

    low, high = leaf_at(2 * pair), leaf_at(2 * pair + 1)
    prev, following = leaf_at(jnp.maximum(2 * pair - 1, 0)), leaf_at(jnp.minimum(2 * pair + 2, leaves - 1))
    if edges:
        even = me_ref[0] % 2 == 0
        cross = cross_ref[...]
        wide = cross.shape[1]
        inner = jnp.concatenate(
            [inner_ref[0, :, t:t + wide] for t in range(0, inner_ref.shape[2], wide)], axis=0
        )[:leaf_len]
        prev = jnp.where(pair == 0, jnp.where(even, cross, inner), prev)
        following = jnp.where(pair == last_pair, jnp.where(even, inner, cross), following)

        @pl.when(pl.program_id(0) == 0)
        def _():
            rows, lanes = at_ref.shape
            at_ref[...] = blocks_ref[0, :rows, :lanes].astype(F32).astype(jnp.int32)


    def masked(leaf, side, value):
        return jnp.where(mask_ref[side, leaf] > 0, value, jnp.zeros_like(value))

    left = jnp.concatenate(
        [masked(2 * pair, 0, prev), low, masked(2 * pair, 1, high)], axis=0
    )
    right = jnp.concatenate(
        [masked(2 * pair + 1, 0, low), high, masked(2 * pair + 1, 1, following)], axis=0
    )
    near = dot(table_ref[...], jnp.concatenate([left, right], axis=1)).astype(BF)
    fields = ordered_ref.shape[1]
    turned = []
    for i in range(2):
        hot = one_hot_grid(order_ref[pl.ds(2 * pair + i, 1), :], leaf_len)
        at = pl.ds(i * leaf_len, leaf_len)
        both = jnp.concatenate([near[:, i * fields:(i + 1) * fields], basis_ref[2 * pair + i].T], axis=1)
        moved = dot(hot, both).astype(BF)
        near_ref[at, :] = moved[:, :fields]
        turned.append(moved[:, fields:])
    turned_ref[...] = jnp.concatenate(turned, axis=1)


def near_field(pairs, near_list, leaf_order, tables, basis, ordered, halos=None, filled=None):
    leaves, rank, leaf_len = basis.shape
    fields = ordered.shape[1]
    last = leaves // 2 - 1
    gap = pairs[1] - pairs[0] if len(pairs) > 1 else 1

    def pair_of(step):
        return pairs[0] + gap * step

    in_specs = [
        scalars(),
        whole(),
        whole(),
        whole(),
        whole(),
    ]
    args = [near_list.T, leaf_order, tables, basis, ordered]
    aliases = {}
    extra = []
    if halos is not None:
        me, cross, other = halos
        row = (1,) + other.shape[1:]
        in_specs += [
            scalars(),
            pl.BlockSpec((leaf_len, fields), lambda s: (0, 0)),
            pl.BlockSpec(row, lambda s: (leaves + 1, 0, 0)),
            pl.BlockSpec(row, lambda s: (leaves + 2, 0, 0)),
        ]
        args += [me, cross, other, other]
        extra = [(16, 128)]
    if filled is not None:
        aliases = {len(args): 0, len(args) + 1: 1}
        in_specs += [pl.BlockSpec(memory_space=pl.ANY)] * 2
        args += list(filled)
    return pl.pallas_call(
        functools.partial(near_kernel, halos is not None, pair_of, last),
        name="near_" + str(pairs[0]),
        grid=(len(pairs),),
        in_specs=in_specs,
        out_specs=[
            pl.BlockSpec((2 * leaf_len, fields), lambda s: (pair_of(s), 0)),
            pl.BlockSpec((leaf_len, 2 * rank), lambda s: (pair_of(s), 0)),
        ] + [pl.BlockSpec(shape, lambda s: (0, 0)) for shape in extra],
        out_shape=[
            jax.ShapeDtypeStruct((leaves * leaf_len, fields), BF),
            jax.ShapeDtypeStruct((leaves // 2 * leaf_len, 2 * rank), BF),
        ] + [jax.ShapeDtypeStruct(shape, jnp.int32) for shape in extra],
        input_output_aliases=aliases,
        compiler_params=params(16),
        cost_estimate=cost(len(pairs) * 2 * leaf_len * leaf_len * fields * 10, len(pairs) * MIB),
    )(*args)


def field_kernel(per, own_ref, other_ref, turned_transfer_ref, near_ref, turned_ref, out_ref):
    step = pl.program_id(0)
    leaf_len = out_ref.shape[0] // per
    root = own_ref.shape[0] - 1
    local = own_ref[root] + other_ref[root]
    coarse = local.astype(BF)
    fine = (local - coarse.astype(F32)).astype(BF)
    both = jnp.concatenate([coarse, fine], axis=1)
    fields = local.shape[1]
    for pair in range(per // 2):
        values = []
        for i in range(2):
            leaf = step * per + 2 * pair + i
            down = dot(turned_transfer_ref[leaf], both)
            value = own_ref[leaf] + other_ref[leaf] + (down[:, :fields] + down[:, fields:])
            values.append(value.astype(BF))
        zero = jnp.zeros_like(values[0])
        corner = jnp.concatenate(
            [
                jnp.concatenate([values[0], zero], axis=1),
                jnp.concatenate([zero, values[1]], axis=1),
            ],
            axis=0,
        )
        at = pl.multiple_of((step * (per // 2) + pair) * leaf_len, leaf_len)
        far = dot(turned_ref[pl.ds(at, leaf_len), :], corner)
        for i in range(2):
            near = near_ref[pl.ds(2 * at + i * leaf_len, leaf_len), :].astype(F32)
            rows = slice((2 * pair + i) * leaf_len, (2 * pair + i + 1) * leaf_len)
            out_ref[rows, :] = (near + far[:, i * fields:(i + 1) * fields]).astype(BF)


def field(own, other, turned_transfer, near, turned, per=4):
    leaves, rank, _ = turned_transfer.shape
    fields = near.shape[1]
    leaf_len = near.shape[0] // leaves
    return pl.pallas_call(
        functools.partial(field_kernel, per),
        name="local_and_field",
        grid=(leaves // per,),
        in_specs=[whole()] * 5,
        out_specs=pl.BlockSpec((per * leaf_len, fields), lambda s: (s, 0)),
        out_shape=jax.ShapeDtypeStruct(near.shape, BF),
        compiler_params=params(16),
        cost_estimate=cost(leaves * leaf_len * rank * fields * 2, 4 * MIB),
    )(own, other, turned_transfer, near, turned)


def after(block, *others):
    return lax.optimization_barrier((block,) + others)[0]


def on_device(
    composition,
    leaf_basis,
    transfer,
    coupling,
    top_coupling,
    admissible_owner,
    admissible_leaf,
    near_list,
    leaf_order,
):
    leaves, rank, leaf_len = leaf_basis.shape
    count = lax.axis_size("subtree")
    layers = count // 8
    slots = layers * 4
    pairs = leaves // 2
    cut = pairs // 2
    me = lax.axis_index("subtree").reshape(1)

    ordered, shared, cross, inner, entry, own_at = skeletons_of(
        me, leaf_order, composition, leaf_basis, transfer, admissible_owner, admissible_leaf, layers
    )
    tables = jnp.asarray(near_tables(leaf_len))
    near_args = (near_list, leaf_order, tables, leaf_basis)

    line = along_z(shared, 1)
    from_x, from_y = over_x(shared), over_y(shared)
    filled = near_field(list(range(1, cut)), *near_args, ordered)
    line = after(line, filled[0])
    lines = [along_z(shared, layers - 1)]
    for _ in range(layers - 3):
        lines.append(along_z(line if len(lines) == 1 else lines[-1], 1))
    ready = after(line, from_x, from_y)
    next_x, next_y = over_x(ready), over_y(ready)
    far = onward(choose(me, after(from_x, ready, lines[0]), from_y))
    cross = lax.ppermute(
        cross,
        "subtree",
        [(d, d + 1) for d in range(1, count - 1, 2)] + [(d, d - 1) for d in range(2, count, 2)],
    )
    own_blocks, my_other, turned_transfer = dense_couplings(
        after(entry, ready), own_at, inner, coupling, top_coupling, transfer, slots
    )

    joined = after(join([after(lines[0], my_other)] + lines[1:]), next_x, next_y, cross)
    last_x, last_y = over_x(joined), over_y(joined)
    chosen = choose(me, after(next_x, joined, far), next_y)
    next_far = onward(chosen)
    other_blocks = over_core(after(my_other, chosen))
    held = after(ordered, joined)
    filled = near_field(list(range(cut, pairs - 1)), *near_args, held, filled=filled)
    next_far = after(next_far, filled[0])
    last_far = [along_z(far, layers - 1)]
    for _ in range(layers - 3):
        last_far.append(along_z(next_far if len(last_far) == 1 else last_far[-1], 1))
    held = after(ordered, filled[0])
    *filled, other_at = near_field(
        [0, pairs - 1], *near_args, held, halos=(me, cross, other_blocks), filled=filled
    )
    round_0 = ((shared, line), (from_x, next_x), (from_y, next_y), (far, next_far))
    steps = [0, 1]
    own = far_round(0, steps, slots, own_at, round_0, own_blocks)
    other = far_round(1, steps, slots, other_at, round_0, other_blocks)
    steps = list(range(2, layers))
    round_1 = ((joined,), (last_x,), (last_y,), (after(last_far[0], own, other), *last_far[1:]))
    other = far_round(1, steps, slots, other_at, round_1, other_blocks, other)
    own = far_round(0, steps, slots, own_at, round_1, own_blocks, own)
    return field(own, over_core(other), turned_transfer, *filled)


def solution(mesh):
    placed = (
        P(("groups", "subtree"), None),
        P("subtree", None, None),
        P("subtree", None, None),
        P("subtree", None, None, None),
        P("subtree", None, None, None),
        P(("groups", "subtree"), None),
        P(("groups", "subtree"), None),
        P(("groups", "subtree"), None),
        P(("groups", "subtree"), None),
    )
    return jax.shard_map(
        on_device,
        mesh=mesh,
        in_specs=placed,
        out_specs=P(("groups", "subtree"), None),
        check_vma=False,
    )
```

```python
import functools

import jax
import jax.numpy as jnp
import ml_dtypes
import numpy as np
from jax import lax
from jax.experimental import pallas as pl
from jax.experimental.pallas import tpu as pltpu
from jax.sharding import PartitionSpec as P

COULOMB_SCALE = 0.15
SOFTENING = 0.25
BF = jnp.bfloat16
F32 = jnp.float32
MIB = 1 << 20


def near_tables(leaf_len):
    cells = np.arange(leaf_len)
    along = (cells // 64).astype(np.float32)
    across = (cells // 8 % 8).astype(np.float32)
    height = (cells % 8).astype(np.float32)
    extent = leaf_len // 64
    tables = []
    for offset in (-1, 0, 1):
        delta_x = along[:, None] - along[None, :] - np.float32(offset * extent)
        delta_y = across[:, None] - across[None, :]
        delta_z = height[:, None] - height[None, :]
        square = delta_x * delta_x + delta_y * delta_y + delta_z * delta_z
        value = np.float32(COULOMB_SCALE) / np.sqrt(square + np.float32(SOFTENING))
        tables.append(value.astype(ml_dtypes.bfloat16))
    return np.concatenate(tables, axis=1)


def send(block, target):
    count = lax.axis_size("subtree")
    return lax.ppermute(block, "subtree", [(d, target(d)) for d in range(count)])


def over_core(block):
    return send(block, lambda d: d ^ 1)


def over_x(block):
    return send(block, lambda d: d ^ 2)


def over_y(block):
    return send(block, lambda d: d ^ 4)


def onward(block):
    return send(block, lambda d: d ^ (2 if d % 2 else 4))


def along_z(block, step):
    layers = lax.axis_size("subtree") // 8
    return send(block, lambda d: (d // 8 + step) % layers * 8 + d % 8)


def params(mib):
    return pltpu.CompilerParams(vmem_limit_bytes=mib * MIB)


def cost(flops, moved):
    return pl.CostEstimate(flops=flops // 64, bytes_accessed=moved // 64, transcendentals=0)


def whole():
    return pl.BlockSpec(memory_space=pltpu.VMEM)


def scalars():
    return pl.BlockSpec(memory_space=pltpu.SMEM)


def dot(a, b):
    return jnp.dot(a, b, preferred_element_type=F32)


def in_hbm(*arrays):
    return [pltpu.with_memory_space_constraint(array, pltpu.HBM) for array in arrays]


def one_hot_leaf(row, leaf_len):
    column = jnp.broadcast_to(row, (128, leaf_len)).T
    lanes = lax.broadcasted_iota(jnp.int32, (leaf_len, 128), 1)
    return jnp.concatenate(
        [
            jnp.where(column == lanes + 128 * t, 1.0, 0.0).astype(BF)
            for t in range(leaf_len // 128)
        ],
        axis=1,
    )


def one_hot_grid(row, leaf_len):
    cells = lax.broadcasted_iota(jnp.int32, (leaf_len, leaf_len), 0)
    return jnp.where(cells == row, 1.0, 0.0).astype(BF)


def owner_tables(me, layers, owners, blocks):
    leaves, entries = owners.shape
    slots = layers * 4
    rows = leaves + 1
    shape = (rows, 2 * slots)
    lane = lax.broadcasted_iota(jnp.int32, shape, 1)
    plane = (lane >= slots).astype(jnp.int32)
    slot = lane - plane * slots
    layer, chip, core = me // 8, (me // 2) & 3, me & 1
    turn = slot >> 2
    shift = jnp.where(turn < 2, turn, jnp.where(turn == 2, layers - 1, turn - 1))
    source = layer - shift
    source = jnp.where(source < 0, source + layers, source)
    owner = source * 8 + (chip ^ (slot & 3)) * 2 + (core ^ plane)
    row = lax.broadcasted_iota(jnp.int32, shape, 0)
    distant = jnp.abs(owner - me) >= 2
    entry = jnp.where((row == 0) & distant, owner, -1)
    block = jnp.zeros(shape, jnp.int32)
    pad = jnp.full((1, entries), -1, jnp.int32)
    named = jnp.concatenate([pad, owners], axis=0)
    chosen = jnp.concatenate([pad, blocks], axis=0)
    for k in range(entries):
        match = named[:, k:k + 1] == owner
        entry = jnp.where(match, k, entry)
        block = jnp.where(match, chosen[:, k:k + 1] + 1, block)
    return entry, block


def skeleton_kernel(per, layers, me_ref, order_ref, comp_ref, basis_ref, transfer_ref,
                    owner_ref, leaf_ref, ordered_ref, shared_ref, cross_ref, inner_ref,
                    entry_ref, block_ref, root_ref):
    step = pl.program_id(0)
    leaf_len = basis_ref.shape[2]

    @pl.when(step == 0)
    def _():
        root_ref[...] = jnp.zeros_like(root_ref)
        entry, block = owner_tables(me_ref[0], layers, owner_ref[...], leaf_ref[...])
        rows, lanes = entry.shape
        entry_ref[:rows, :lanes] = entry
        block_ref[:rows, :lanes] = block

    hots = [one_hot_leaf(order_ref[pl.ds(step * per + i, 1), :], leaf_len) for i in range(per)]
    ordered = [
        dot(hots[i], comp_ref[i * leaf_len:(i + 1) * leaf_len, :]).astype(BF) for i in range(per)
    ]
    skeletons = [dot(basis_ref[i], ordered[i]).astype(BF) for i in range(per)]
    across = jnp.concatenate([transfer_ref[i] for i in range(per)], axis=1)
    root_ref[...] += dot(across, jnp.concatenate(skeletons, axis=0))
    for i in range(per):
        ordered_ref[i * leaf_len:(i + 1) * leaf_len, :] = ordered[i]
        shared_ref[pl.ds(step * per + i + 1, 1)] = skeletons[i][None]

    even = me_ref[0] % 2 == 0

    @pl.when((step == 0) & even)
    def _():
        cross_ref[...] = ordered[0]

    @pl.when((step == 0) & ~even)
    def _():
        inner_ref[...] = ordered[0]

    last = step == pl.num_programs(0) - 1

    @pl.when(last & even)
    def _():
        inner_ref[...] = ordered[-1]

    @pl.when(last & ~even)
    def _():
        cross_ref[...] = ordered[-1]

    @pl.when(last)
    def _():
        shared_ref[pl.ds(0, 1)] = root_ref[...].astype(BF)[None]


def skeletons_of(me, leaf_order, composition, leaf_basis, transfer, owners, blocks, layers, per=4):
    leaves, rank, leaf_len = leaf_basis.shape
    fields = composition.shape[1]
    entries = owners.shape[1]
    edge = jax.ShapeDtypeStruct((leaf_len, fields), BF)
    return pl.pallas_call(
        functools.partial(skeleton_kernel, per, layers),
        name="order_and_skeleton",
        grid=(leaves // per,),
        in_specs=[
            scalars(),
            pl.BlockSpec((leaves, leaf_len), lambda s: (0, 0)),
            pl.BlockSpec((per * leaf_len, fields), lambda s: (s, 0)),
            pl.BlockSpec((per, rank, leaf_len), lambda s: (s, 0, 0)),
            pl.BlockSpec((per, rank, rank), lambda s: (s, 0, 0)),
            pl.BlockSpec((leaves, entries), lambda s: (0, 0)),
            pl.BlockSpec((leaves, entries), lambda s: (0, 0)),
        ],
        out_specs=[
            pl.BlockSpec((per * leaf_len, fields), lambda s: (s, 0)),
            pl.BlockSpec((leaves + 1, rank, fields), lambda s: (0, 0, 0)),
            pl.BlockSpec((leaf_len, fields), lambda s: (0, 0)),
            pl.BlockSpec((leaf_len, fields), lambda s: (0, 0)),
            pl.BlockSpec((16, 128), lambda s: (0, 0)),
            pl.BlockSpec((16, 128), lambda s: (0, 0)),
        ],
        out_shape=[
            jax.ShapeDtypeStruct((leaves * leaf_len, fields), BF),
            jax.ShapeDtypeStruct((leaves + 1, rank, fields), BF),
            edge,
            edge,
            jax.ShapeDtypeStruct((16, 128), jnp.int32),
            jax.ShapeDtypeStruct((16, 128), jnp.int32),
        ],
        scratch_shapes=[pltpu.VMEM((rank, fields), F32)],
        compiler_params=params(16),
        cost_estimate=cost(leaves * leaf_len * leaf_len * fields * 2, 4 * MIB),
    )(me, *in_hbm(leaf_order, composition, leaf_basis, transfer, owners, blocks))


def join_kernel(*refs):
    out = refs[-1]
    at = 0
    for ref in refs[:-1]:
        out[at:at + ref.shape[0]] = ref[...]
        at += ref.shape[0]


def join(parts):
    if len(parts) == 1:
        return parts[0]
    shape = (sum(part.shape[0] for part in parts),) + parts[0].shape[1:]
    return pl.pallas_call(
        join_kernel,
        name="join",
        in_specs=[whole()] * len(parts),
        out_specs=whole(),
        out_shape=jax.ShapeDtypeStruct(shape, BF),
        compiler_params=params(8 if shape[0] <= 32 else 32),
        cost_estimate=cost(0, MIB // 2),
    )(*parts)


def choose_kernel(me_ref, x_ref, y_ref, out_ref):
    @pl.when(me_ref[0] % 2 == 0)
    def _():
        out_ref[...] = x_ref[...]

    @pl.when(me_ref[0] % 2 == 1)
    def _():
        out_ref[...] = y_ref[...]


def choose(me, from_x, from_y):
    return pl.pallas_call(
        choose_kernel,
        name="choose",
        in_specs=[scalars(), whole(), whole()],
        out_specs=whole(),
        out_shape=jax.ShapeDtypeStruct(from_x.shape, BF),
        compiler_params=params(8),
        cost_estimate=cost(0, MIB // 4),
    )(me, from_x, from_y)


def dense_kernel(per, slots, entry_ref, block_ref, inner_ref, coupling_ref, top_ref,
                 transfer_ref, own_ref, other_ref, turned_ref):
    step = pl.program_id(0)
    rank = coupling_ref.shape[2]
    fields = inner_ref.shape[1]
    leaves = own_ref.shape[0] - 1
    for i in range(per):
        turned_ref[step * per + i] = transfer_ref[i].T

    def fill(out_ref, plane, row, entry_row, block_of):
        blocks = []
        for slot in range(slots):
            entry = entry_ref[entry_row, plane * slots + slot]
            block = block_of(jnp.maximum(entry, 0))
            blocks.append(jnp.where(entry >= 0, block, jnp.zeros_like(block)))
        out_ref[row, :, :slots * rank] = jnp.concatenate(blocks, axis=1)

    for plane, out_ref in ((0, own_ref), (1, other_ref)):
        for i in range(per):
            leaf = step * per + i
            fill(out_ref, plane, leaf, leaf + 1, lambda entry, i=i: coupling_ref[i, entry])

        @pl.when(step == pl.num_programs(0) - 1)
        def _(plane=plane, out_ref=out_ref):
            fill(out_ref, plane, leaves, 0, lambda entry: top_ref[0, entry])

    @pl.when(step == 0)
    def _():
        for t in range(inner_ref.shape[0] // rank):
            part = inner_ref[t * rank:(t + 1) * rank, :]
            other_ref[leaves + 1, :, t * fields:(t + 1) * fields] = part
        other_ref[leaves + 2] = jnp.zeros(other_ref.shape[1:], BF)
        blocks = block_ref[...].astype(F32).astype(BF)
        other_ref[leaves + 2, :blocks.shape[0], :blocks.shape[1]] = blocks


def dense_couplings(entry, block, inner, coupling, top_coupling, transfer, slots, per=4):
    leaves, entries, rank, _ = coupling.shape
    own = (leaves + 1, rank, slots * rank)
    other = (leaves + 3, rank, slots * rank)
    return pl.pallas_call(
        functools.partial(dense_kernel, per, slots),
        name="couplings_by_owner",
        grid=(leaves // per,),
        in_specs=[
            scalars(),
            pl.BlockSpec(block.shape, lambda s: (0, 0)),
            pl.BlockSpec(inner.shape, lambda s: (0, 0)),
            pl.BlockSpec((per, entries, rank, rank), lambda s: (s, 0, 0, 0)),
            pl.BlockSpec(top_coupling.shape, lambda s: (0, 0, 0, 0)),
            pl.BlockSpec((per, rank, rank), lambda s: (s, 0, 0)),
        ],
        out_specs=[
            pl.BlockSpec(own, lambda s: (0, 0, 0)),
            pl.BlockSpec(other, lambda s: (0, 0, 0)),
            pl.BlockSpec(transfer.shape, lambda s: (0, 0, 0)),
        ],
        out_shape=[
            jax.ShapeDtypeStruct(own, BF),
            jax.ShapeDtypeStruct(other, BF),
            jax.ShapeDtypeStruct(transfer.shape, BF),
        ],
        compiler_params=params(16 if slots <= 16 else 48),
        cost_estimate=cost(0, 8 * MIB),
    )(entry, block, inner, *in_hbm(coupling, top_coupling, transfer))


def round_kernel(plane, steps, slots, counts, at_ref, *refs):
    sides = []
    for number in counts:
        sides.append(refs[:number])
        refs = refs[number:]
    blocks_ref, out = refs[0], refs[-1]
    rows, rank, _ = out.shape
    low, high = steps[0] * 4 * rank, (steps[-1] + 1) * 4 * rank

    def block_at(side, base, index):
        for ref in side:
            if base < ref.shape[0]:
                return ref[base + index]
            base -= ref.shape[0]

    values = []
    for row in range(rows):
        chosen = [
            block_at(side, place * rows, at_ref[(row + 1) % rows, plane * slots + step * 4 + q])
            for place, step in enumerate(steps)
            for q, side in enumerate(sides)
        ]
        value = dot(blocks_ref[row, :, low:high], jnp.concatenate(chosen, axis=0))
        if len(refs) > 2:
            value = value + refs[1][row]
        values.append(value)
    for row in range(rows):
        out[row] = values[row]


def far_round(plane, steps, slots, at, parts, blocks, total=None):
    rank, fields = parts[0][0].shape[1:]
    rows = parts[0][0].shape[0] // (1 if len(parts[0]) > 1 else len(steps))
    args = [part for side in parts for part in side] + [blocks] + ([] if total is None else [total])
    return pl.pallas_call(
        functools.partial(round_kernel, plane, steps, slots, [len(side) for side in parts]),
        name="far_" + str(plane) + "_" + str(steps[0]),
        in_specs=[scalars()] + [whole()] * len(args),
        out_specs=whole(),
        out_shape=jax.ShapeDtypeStruct((rows, rank, fields), F32),
        compiler_params=params(16 if slots <= 16 else 48),
        cost_estimate=cost(rows * rank * 4 * rank * fields * 2 * len(steps), MIB),
    )(at, *args)


def near_kernel(edges, pair_of, last_pair, mask_ref, order_ref, table_ref, basis_ref,
                ordered_ref, *refs):
    if edges:
        me_ref, cross_ref, inner_ref, blocks_ref = refs[:4]
        near_ref, turned_ref, at_ref = refs[-3:]
    else:
        near_ref, turned_ref = refs[-2:]
    pair = pair_of(pl.program_id(0))
    leaf_len = basis_ref.shape[2]
    leaves = basis_ref.shape[0]

    def leaf_at(leaf):
        return ordered_ref[pl.ds(pl.multiple_of(leaf * leaf_len, leaf_len), leaf_len), :]

    low, high = leaf_at(2 * pair), leaf_at(2 * pair + 1)
    prev, following = leaf_at(jnp.maximum(2 * pair - 1, 0)), leaf_at(jnp.minimum(2 * pair + 2, leaves - 1))
    if edges:
        even = me_ref[0] % 2 == 0
        cross = cross_ref[...]
        wide = cross.shape[1]
        inner = jnp.concatenate(
            [inner_ref[0, :, t:t + wide] for t in range(0, inner_ref.shape[2], wide)], axis=0
        )[:leaf_len]
        prev = jnp.where(pair == 0, jnp.where(even, cross, inner), prev)
        following = jnp.where(pair == last_pair, jnp.where(even, inner, cross), following)

        @pl.when(pl.program_id(0) == 0)
        def _():
            rows, lanes = at_ref.shape
            at_ref[...] = blocks_ref[0, :rows, :lanes].astype(F32).astype(jnp.int32)


    def masked(leaf, side, value):
        return jnp.where(mask_ref[side, leaf] > 0, value, jnp.zeros_like(value))

    left = jnp.concatenate(
        [masked(2 * pair, 0, prev), low, masked(2 * pair, 1, high)], axis=0
    )
    right = jnp.concatenate(
        [masked(2 * pair + 1, 0, low), high, masked(2 * pair + 1, 1, following)], axis=0
    )
    near = dot(table_ref[...], jnp.concatenate([left, right], axis=1)).astype(BF)
    fields = ordered_ref.shape[1]
    moved = []
    for i in range(2):
        hot = one_hot_grid(order_ref[pl.ds(2 * pair + i, 1), :], leaf_len)
        both = jnp.concatenate([near[:, i * fields:(i + 1) * fields], basis_ref[2 * pair + i].T], axis=1)
        moved.append(dot(hot, both).astype(BF))
    near_ref[...] = jnp.concatenate([part[:, :fields] for part in moved], axis=0)
    turned_ref[...] = jnp.concatenate([part[:, fields:] for part in moved], axis=1)


def near_field(pairs, near_list, leaf_order, tables, basis, ordered, halos=None, filled=None):
    leaves, rank, leaf_len = basis.shape
    fields = ordered.shape[1]
    last = leaves // 2 - 1
    gap = pairs[1] - pairs[0] if len(pairs) > 1 else 1

    def pair_of(step):
        return pairs[0] + gap * step

    in_specs = [
        scalars(),
        whole(),
        whole(),
        whole(),
        whole(),
    ]
    args = [near_list.T, leaf_order, tables, basis, ordered]
    aliases = {}
    extra = []
    if halos is not None:
        me, cross, other = halos
        row = (1,) + other.shape[1:]
        in_specs += [
            scalars(),
            pl.BlockSpec((leaf_len, fields), lambda s: (0, 0)),
            pl.BlockSpec(row, lambda s: (leaves + 1, 0, 0)),
            pl.BlockSpec(row, lambda s: (leaves + 2, 0, 0)),
        ]
        args += [me, cross, other, other]
        extra = [(16, 128)]
    if filled is not None:
        aliases = {len(args): 0, len(args) + 1: 1}
        in_specs += [pl.BlockSpec(memory_space=pl.ANY)] * 2
        args += list(filled)
    return pl.pallas_call(
        functools.partial(near_kernel, halos is not None, pair_of, last),
        name="near_" + str(pairs[0]),
        grid=(len(pairs),),
        in_specs=in_specs,
        out_specs=[
            pl.BlockSpec((2 * leaf_len, fields), lambda s: (pair_of(s), 0)),
            pl.BlockSpec((leaf_len, 2 * rank), lambda s: (pair_of(s), 0)),
        ] + [pl.BlockSpec(shape, lambda s: (0, 0)) for shape in extra],
        out_shape=[
            jax.ShapeDtypeStruct((leaves * leaf_len, fields), BF),
            jax.ShapeDtypeStruct((leaves // 2 * leaf_len, 2 * rank), BF),
        ] + [jax.ShapeDtypeStruct(shape, jnp.int32) for shape in extra],
        input_output_aliases=aliases,
        compiler_params=params(16),
        cost_estimate=cost(len(pairs) * 2 * leaf_len * leaf_len * fields * 10, len(pairs) * MIB),
    )(*args)


def field_kernel(per, own_ref, other_ref, turned_transfer_ref, near_ref, turned_ref, out_ref):
    step = pl.program_id(0)
    leaf_len = out_ref.shape[0] // per
    root = own_ref.shape[0] - 1
    local = own_ref[root] + other_ref[root]
    coarse = local.astype(BF)
    fine = (local - coarse.astype(F32)).astype(BF)
    both = jnp.concatenate([coarse, fine], axis=1)
    fields = local.shape[1]
    for pair in range(per // 2):
        values = []
        for i in range(2):
            leaf = step * per + 2 * pair + i
            down = dot(turned_transfer_ref[leaf], both)
            value = own_ref[leaf] + other_ref[leaf] + (down[:, :fields] + down[:, fields:])
            values.append(value.astype(BF))
        zero = jnp.zeros_like(values[0])
        corner = jnp.concatenate(
            [
                jnp.concatenate([values[0], zero], axis=1),
                jnp.concatenate([zero, values[1]], axis=1),
            ],
            axis=0,
        )
        at = pl.multiple_of((step * (per // 2) + pair) * leaf_len, leaf_len)
        far = dot(turned_ref[pl.ds(at, leaf_len), :], corner)
        for i in range(2):
            near = near_ref[pl.ds(2 * at + i * leaf_len, leaf_len), :].astype(F32)
            rows = slice((2 * pair + i) * leaf_len, (2 * pair + i + 1) * leaf_len)
            out_ref[rows, :] = (near + far[:, i * fields:(i + 1) * fields]).astype(BF)


def field(own, other, turned_transfer, near, turned, per=4):
    leaves, rank, _ = turned_transfer.shape
    fields = near.shape[1]
    leaf_len = near.shape[0] // leaves
    return pl.pallas_call(
        functools.partial(field_kernel, per),
        name="local_and_field",
        grid=(leaves // per,),
        in_specs=[whole()] * 5,
        out_specs=pl.BlockSpec((per * leaf_len, fields), lambda s: (s, 0)),
        out_shape=jax.ShapeDtypeStruct(near.shape, BF),
        compiler_params=params(16),
        cost_estimate=cost(leaves * leaf_len * rank * fields * 2, 4 * MIB),
    )(own, other, turned_transfer, near, turned)


def after(block, *others):
    return lax.optimization_barrier((block,) + others)[0]


def on_device(
    composition,
    leaf_basis,
    transfer,
    coupling,
    top_coupling,
    admissible_owner,
    admissible_leaf,
    near_list,
    leaf_order,
):
    leaves, rank, leaf_len = leaf_basis.shape
    count = lax.axis_size("subtree")
    layers = count // 8
    slots = layers * 4
    pairs = leaves // 2
    cut = pairs // 2
    me = lax.axis_index("subtree").reshape(1)

    ordered, shared, cross, inner, entry, own_at = skeletons_of(
        me, leaf_order, composition, leaf_basis, transfer, admissible_owner, admissible_leaf, layers
    )
    tables = jnp.asarray(near_tables(leaf_len))
    near_args = (near_list, leaf_order, tables, leaf_basis)

    line = along_z(shared, 1)
    from_x, from_y = over_x(shared), over_y(shared)
    own_blocks, my_other, turned_transfer = dense_couplings(
        entry, own_at, inner, coupling, top_coupling, transfer, slots
    )
    line = after(line, my_other)
    lines = [along_z(shared, layers - 1)]
    for _ in range(layers - 3):
        lines.append(along_z(line if len(lines) == 1 else lines[-1], 1))
    ready = after(line, from_x, from_y)
    next_x, next_y = over_x(ready), over_y(ready)
    far = onward(choose(me, after(from_x, ready, lines[0]), from_y))
    cross = lax.ppermute(
        cross,
        "subtree",
        [(d, d + 1) for d in range(1, count - 1, 2)] + [(d, d - 1) for d in range(2, count, 2)],
    )

    joined = after(join(lines), next_x, next_y, cross)
    last_x, last_y = over_x(joined), over_y(joined)
    chosen = choose(me, after(next_x, joined, far), next_y)
    next_far = onward(chosen)
    other_blocks = over_core(after(my_other, chosen))
    filled = near_field(list(range(1, cut)), *near_args, after(ordered, joined))
    next_far = after(next_far, filled[0])
    filled = near_field(list(range(cut, pairs - 1)), *near_args, ordered, filled=filled)
    last_far = [along_z(far, layers - 1)]
    for _ in range(layers - 3):
        last_far.append(along_z(next_far if len(last_far) == 1 else last_far[-1], 1))
    held = after(ordered, filled[0])
    *filled, other_at = near_field(
        [0, pairs - 1], *near_args, held, halos=(me, cross, other_blocks), filled=filled
    )
    round_0 = ((shared, line), (from_x, next_x), (from_y, next_y), (far, next_far))
    steps = [0, 1]
    own = far_round(0, steps, slots, own_at, round_0, own_blocks)
    other = far_round(1, steps, slots, other_at, round_0, other_blocks)
    steps = list(range(2, layers))
    round_1 = ((joined,), (last_x,), (last_y,), (after(last_far[0], own, other), *last_far[1:]))
    other = far_round(1, steps, slots, other_at, round_1, other_blocks, other)
    own = far_round(0, steps, slots, own_at, round_1, own_blocks, own)
    return field(own, over_core(other), turned_transfer, *filled)


def solution(mesh):
    placed = (
        P(("groups", "subtree"), None),
        P("subtree", None, None),
        P("subtree", None, None),
        P("subtree", None, None, None),
        P("subtree", None, None, None),
        P(("groups", "subtree"), None),
        P(("groups", "subtree"), None),
        P(("groups", "subtree"), None),
        P(("groups", "subtree"), None),
    )
    return jax.shard_map(
        on_device,
        mesh=mesh,
        in_specs=placed,
        out_specs=P(("groups", "subtree"), None),
        check_vma=False,
    )
```

```python
import functools

import jax
import jax.numpy as jnp
import ml_dtypes
import numpy as np
from jax import lax
from jax.experimental import pallas as pl
from jax.experimental.pallas import tpu as pltpu
from jax.sharding import PartitionSpec as P

COULOMB_SCALE = 0.15
SOFTENING = 0.25
BF = jnp.bfloat16
F32 = jnp.float32
MIB = 1 << 20


def near_tables(leaf_len):
    cells = np.arange(leaf_len)
    along = (cells // 64).astype(np.float32)
    across = (cells // 8 % 8).astype(np.float32)
    height = (cells % 8).astype(np.float32)
    extent = leaf_len // 64
    tables = []
    for offset in (-1, 0, 1):
        delta_x = along[:, None] - along[None, :] - np.float32(offset * extent)
        delta_y = across[:, None] - across[None, :]
        delta_z = height[:, None] - height[None, :]
        square = delta_x * delta_x + delta_y * delta_y + delta_z * delta_z
        value = np.float32(COULOMB_SCALE) / np.sqrt(square + np.float32(SOFTENING))
        tables.append(value.astype(ml_dtypes.bfloat16))
    return np.concatenate(tables, axis=1)


def send(block, target):
    count = lax.axis_size("subtree")
    return lax.ppermute(block, "subtree", [(d, target(d)) for d in range(count)])


def over_core(block):
    return send(block, lambda d: d ^ 1)


def over_x(block):
    return send(block, lambda d: d ^ 2)


def over_y(block):
    return send(block, lambda d: d ^ 4)


def onward(block):
    return send(block, lambda d: d ^ (2 if d % 2 else 4))


def along_z(block, step):
    layers = lax.axis_size("subtree") // 8
    return send(block, lambda d: (d // 8 + step) % layers * 8 + d % 8)


def params(mib):
    return pltpu.CompilerParams(vmem_limit_bytes=mib * MIB)


def cost(flops, moved):
    return pl.CostEstimate(flops=flops // 64, bytes_accessed=moved // 64, transcendentals=0)


def whole():
    return pl.BlockSpec(memory_space=pltpu.VMEM)


def scalars():
    return pl.BlockSpec(memory_space=pltpu.SMEM)


def dot(a, b):
    return jnp.dot(a, b, preferred_element_type=F32)


def in_hbm(*arrays):
    return [pltpu.with_memory_space_constraint(array, pltpu.HBM) for array in arrays]


def one_hot_leaf(row, leaf_len):
    column = jnp.broadcast_to(row, (128, leaf_len)).T.astype(jnp.int16)
    lanes = lax.broadcasted_iota(jnp.int32, (leaf_len, 128), 1)
    one, zero = jnp.ones((), BF), jnp.zeros((), BF)
    return jnp.concatenate(
        [
            jnp.where(column == (lanes + 128 * t).astype(jnp.int16), one, zero)
            for t in range(leaf_len // 128)
        ],
        axis=1,
    )


def one_hot_grid(row, leaf_len):
    cells = lax.broadcasted_iota(jnp.int32, (16, leaf_len), 0).astype(jnp.int16)
    wide = jnp.broadcast_to(row, (16, leaf_len)).astype(jnp.int16)
    one, zero = jnp.ones((), BF), jnp.zeros((), BF)
    return jnp.concatenate(
        [jnp.where(cells + jnp.int16(t) == wide, one, zero) for t in range(0, leaf_len, 16)], axis=0
    )


def owner_tables(me, layers, owners, blocks):
    leaves, entries = owners.shape
    slots = layers * 4
    rows = leaves + 1
    shape = (rows, 2 * slots)
    lane = lax.broadcasted_iota(jnp.int32, shape, 1)
    plane = (lane >= slots).astype(jnp.int32)
    slot = lane - plane * slots
    layer, chip, core = me // 8, (me // 2) & 3, me & 1
    turn = slot >> 2
    shift = jnp.where(turn < 2, turn, jnp.where(turn == 2, layers - 1, turn - 1))
    source = layer - shift
    source = jnp.where(source < 0, source + layers, source)
    owner = source * 8 + (chip ^ (slot & 3)) * 2 + (core ^ plane)
    row = lax.broadcasted_iota(jnp.int32, shape, 0)
    distant = jnp.abs(owner - me) >= 2
    entry = jnp.where((row == 0) & distant, owner, -1)
    block = jnp.zeros(shape, jnp.int32)
    pad = jnp.full((1, entries), -1, jnp.int32)
    named = jnp.concatenate([pad, owners], axis=0)
    chosen = jnp.concatenate([pad, blocks], axis=0)
    for k in range(entries):
        match = named[:, k:k + 1] == owner
        entry = jnp.where(match, k, entry)
        block = jnp.where(match, chosen[:, k:k + 1] + 1, block)
    return entry, block


def skeleton_kernel(per, layers, me_ref, order_ref, comp_ref, basis_ref, transfer_ref,
                    owner_ref, leaf_ref, ordered_ref, shared_ref, cross_ref, inner_ref,
                    entry_ref, block_ref, root_ref):
    step = pl.program_id(0)
    leaf_len = basis_ref.shape[2]

    @pl.when(step == 0)
    def _():
        root_ref[...] = jnp.zeros_like(root_ref)
        entry, block = owner_tables(me_ref[0], layers, owner_ref[...], leaf_ref[...])
        rows, lanes = entry.shape
        entry_ref[:rows, :lanes] = entry
        block_ref[:rows, :lanes] = block

    hots = [one_hot_leaf(order_ref[pl.ds(step * per + i, 1), :], leaf_len) for i in range(per)]
    ordered = [
        dot(hots[i], comp_ref[i * leaf_len:(i + 1) * leaf_len, :]).astype(BF) for i in range(per)
    ]
    skeletons = [dot(basis_ref[i], ordered[i]).astype(BF) for i in range(per)]
    across = jnp.concatenate([transfer_ref[i] for i in range(per)], axis=1)
    root_ref[...] += dot(across, jnp.concatenate(skeletons, axis=0))
    for i in range(per):
        ordered_ref[i * leaf_len:(i + 1) * leaf_len, :] = ordered[i]
        shared_ref[pl.ds(step * per + i + 1, 1)] = skeletons[i][None]

    even = me_ref[0] % 2 == 0

    @pl.when((step == 0) & even)
    def _():
        cross_ref[...] = ordered[0]

    @pl.when((step == 0) & ~even)
    def _():
        inner_ref[...] = ordered[0]

    last = step == pl.num_programs(0) - 1

    @pl.when(last & even)
    def _():
        inner_ref[...] = ordered[-1]

    @pl.when(last & ~even)
    def _():
        cross_ref[...] = ordered[-1]

    @pl.when(last)
    def _():
        shared_ref[pl.ds(0, 1)] = root_ref[...].astype(BF)[None]


def skeletons_of(me, leaf_order, composition, leaf_basis, transfer, owners, blocks, layers, per=4):
    leaves, rank, leaf_len = leaf_basis.shape
    fields = composition.shape[1]
    entries = owners.shape[1]
    edge = jax.ShapeDtypeStruct((leaf_len, fields), BF)
    return pl.pallas_call(
        functools.partial(skeleton_kernel, per, layers),
        name="order_and_skeleton",
        grid=(leaves // per,),
        in_specs=[
            scalars(),
            pl.BlockSpec((leaves, leaf_len), lambda s: (0, 0)),
            pl.BlockSpec((per * leaf_len, fields), lambda s: (s, 0)),
            pl.BlockSpec((per, rank, leaf_len), lambda s: (s, 0, 0)),
            pl.BlockSpec((per, rank, rank), lambda s: (s, 0, 0)),
            pl.BlockSpec((leaves, entries), lambda s: (0, 0)),
            pl.BlockSpec((leaves, entries), lambda s: (0, 0)),
        ],
        out_specs=[
            pl.BlockSpec((per * leaf_len, fields), lambda s: (s, 0)),
            pl.BlockSpec((leaves + 1, rank, fields), lambda s: (0, 0, 0)),
            pl.BlockSpec((leaf_len, fields), lambda s: (0, 0)),
            pl.BlockSpec((leaf_len, fields), lambda s: (0, 0)),
            pl.BlockSpec((16, 128), lambda s: (0, 0)),
            pl.BlockSpec((16, 128), lambda s: (0, 0)),
        ],
        out_shape=[
            jax.ShapeDtypeStruct((leaves * leaf_len, fields), BF),
            jax.ShapeDtypeStruct((leaves + 1, rank, fields), BF),
            edge,
            edge,
            jax.ShapeDtypeStruct((16, 128), jnp.int32),
            jax.ShapeDtypeStruct((16, 128), jnp.int32),
        ],
        scratch_shapes=[pltpu.VMEM((rank, fields), F32)],
        compiler_params=params(16),
        cost_estimate=cost(leaves * leaf_len * leaf_len * fields * 2, 4 * MIB),
    )(me, *in_hbm(leaf_order, composition, leaf_basis, transfer, owners, blocks))


def join_kernel(*refs):
    out = refs[-1]
    at = 0
    for ref in refs[:-1]:
        out[at:at + ref.shape[0]] = ref[...]
        at += ref.shape[0]


def join(parts):
    if len(parts) == 1:
        return parts[0]
    shape = (sum(part.shape[0] for part in parts),) + parts[0].shape[1:]
    return pl.pallas_call(
        join_kernel,
        name="join",
        in_specs=[whole()] * len(parts),
        out_specs=whole(),
        out_shape=jax.ShapeDtypeStruct(shape, BF),
        compiler_params=params(8 if shape[0] <= 32 else 32),
        cost_estimate=cost(0, MIB // 2),
    )(*parts)


def choose_kernel(me_ref, x_ref, y_ref, out_ref):
    @pl.when(me_ref[0] % 2 == 0)
    def _():
        out_ref[...] = x_ref[...]

    @pl.when(me_ref[0] % 2 == 1)
    def _():
        out_ref[...] = y_ref[...]


def choose(me, from_x, from_y):
    return pl.pallas_call(
        choose_kernel,
        name="choose",
        in_specs=[scalars(), whole(), whole()],
        out_specs=whole(),
        out_shape=jax.ShapeDtypeStruct(from_x.shape, BF),
        compiler_params=params(8),
        cost_estimate=cost(0, MIB // 4),
    )(me, from_x, from_y)


def dense_kernel(per, slots, entry_ref, block_ref, inner_ref, coupling_ref, top_ref,
                 transfer_ref, own_ref, other_ref, turned_ref):
    step = pl.program_id(0)
    rank = coupling_ref.shape[2]
    fields = inner_ref.shape[1]
    leaves = own_ref.shape[0] - 1
    for i in range(per):
        turned_ref[step * per + i] = transfer_ref[i].T

    def fill(out_ref, plane, row, entry_row, block_of):
        for slot in range(0, slots, 2):
            pair = []
            for one in (slot, slot + 1):
                entry = entry_ref[entry_row, plane * slots + one]
                block = block_of(jnp.maximum(entry, 0))
                pair.append(jnp.where(entry >= 0, block, jnp.zeros_like(block)))
            out_ref[row, :, slot * rank:(slot + 2) * rank] = jnp.concatenate(pair, axis=1)

    for plane, out_ref in ((0, own_ref), (1, other_ref)):
        for i in range(per):
            leaf = step * per + i
            fill(out_ref, plane, leaf, leaf + 1, lambda entry, i=i: coupling_ref[i, entry])

        @pl.when(step == pl.num_programs(0) - 1)
        def _(plane=plane, out_ref=out_ref):
            fill(out_ref, plane, leaves, 0, lambda entry: top_ref[0, entry])

    @pl.when(step == 0)
    def _():
        for t in range(inner_ref.shape[0] // rank):
            part = inner_ref[t * rank:(t + 1) * rank, :]
            other_ref[leaves + 1, :, t * fields:(t + 1) * fields] = part
        other_ref[leaves + 2] = jnp.zeros(other_ref.shape[1:], BF)
        blocks = block_ref[...].astype(F32).astype(BF)
        other_ref[leaves + 2, :blocks.shape[0], :blocks.shape[1]] = blocks


def dense_couplings(entry, block, inner, coupling, top_coupling, transfer, slots, per=4):
    leaves, entries, rank, _ = coupling.shape
    own = (leaves + 1, rank, slots * rank)
    other = (leaves + 3, rank, slots * rank)
    return pl.pallas_call(
        functools.partial(dense_kernel, per, slots),
        name="couplings_by_owner",
        grid=(leaves // per,),
        in_specs=[
            scalars(),
            pl.BlockSpec(block.shape, lambda s: (0, 0)),
            pl.BlockSpec(inner.shape, lambda s: (0, 0)),
            pl.BlockSpec((per, entries, rank, rank), lambda s: (s, 0, 0, 0)),
            pl.BlockSpec(top_coupling.shape, lambda s: (0, 0, 0, 0)),
            pl.BlockSpec((per, rank, rank), lambda s: (s, 0, 0)),
        ],
        out_specs=[
            pl.BlockSpec(own, lambda s: (0, 0, 0)),
            pl.BlockSpec(other, lambda s: (0, 0, 0)),
            pl.BlockSpec(transfer.shape, lambda s: (0, 0, 0)),
        ],
        out_shape=[
            jax.ShapeDtypeStruct(own, BF),
            jax.ShapeDtypeStruct(other, BF),
            jax.ShapeDtypeStruct(transfer.shape, BF),
        ],
        compiler_params=params(16 if slots <= 16 else 48),
        cost_estimate=cost(0, 8 * MIB),
    )(entry, block, inner, *in_hbm(coupling, top_coupling, transfer))


def round_kernel(plane, steps, slots, counts, at_ref, *refs):
    sides = []
    for number in counts:
        sides.append(refs[:number])
        refs = refs[number:]
    blocks_ref, out = refs[0], refs[-1]
    rows, rank, _ = out.shape
    low, high = steps[0] * 4 * rank, (steps[-1] + 1) * 4 * rank

    def block_at(side, base, index):
        for ref in side:
            if base < ref.shape[0]:
                return ref[base + index]
            base -= ref.shape[0]

    for row in range(rows):
        chosen = [
            block_at(side, place * rows, at_ref[(row + 1) % rows, plane * slots + step * 4 + q])
            for place, step in enumerate(steps)
            for q, side in enumerate(sides)
        ]
        value = dot(blocks_ref[row, :, low:high], jnp.concatenate(chosen, axis=0))
        if len(refs) > 2:
            value = value + refs[1][row]
        out[row] = value


def far_round(plane, steps, slots, at, parts, blocks, total=None):
    rank, fields = parts[0][0].shape[1:]
    rows = parts[0][0].shape[0] // (1 if len(parts[0]) > 1 else len(steps))
    args = [part for side in parts for part in side] + [blocks] + ([] if total is None else [total])
    return pl.pallas_call(
        functools.partial(round_kernel, plane, steps, slots, [len(side) for side in parts]),
        name="far_" + str(plane) + "_" + str(steps[0]),
        in_specs=[scalars()] + [whole()] * len(args),
        out_specs=whole(),
        out_shape=jax.ShapeDtypeStruct((rows, rank, fields), F32),
        compiler_params=params(16 if slots <= 16 else 48),
        cost_estimate=cost(rows * rank * 4 * rank * fields * 2 * len(steps), MIB),
    )(at, *args)


def near_kernel(edges, pair_of, last_pair, mask_ref, order_ref, table_ref, basis_ref,
                ordered_ref, *refs):
    if edges:
        me_ref, cross_ref, inner_ref, blocks_ref = refs[:4]
        near_ref, turned_ref, at_ref = refs[-3:]
    else:
        near_ref, turned_ref = refs[-2:]
    pair = pair_of(pl.program_id(0))
    leaf_len = basis_ref.shape[2]
    leaves = basis_ref.shape[0]

    def leaf_at(leaf):
        return ordered_ref[pl.ds(pl.multiple_of(leaf * leaf_len, leaf_len), leaf_len), :]

    low, high = leaf_at(2 * pair), leaf_at(2 * pair + 1)
    prev, following = leaf_at(jnp.maximum(2 * pair - 1, 0)), leaf_at(jnp.minimum(2 * pair + 2, leaves - 1))
    if edges:
        even = me_ref[0] % 2 == 0
        cross = cross_ref[...]
        wide = cross.shape[1]
        inner = jnp.concatenate(
            [inner_ref[0, :, t:t + wide] for t in range(0, inner_ref.shape[2], wide)], axis=0
        )[:leaf_len]
        prev = jnp.where(pair == 0, jnp.where(even, cross, inner), prev)
        following = jnp.where(pair == last_pair, jnp.where(even, inner, cross), following)

        @pl.when(pl.program_id(0) == 0)
        def _():
            rows, lanes = at_ref.shape
            at_ref[...] = blocks_ref[0, :rows, :lanes].astype(F32).astype(jnp.int32)


    def masked(leaf, side, value):
        return jnp.where(mask_ref[side, leaf] > 0, value, jnp.zeros_like(value))

    left = jnp.concatenate(
        [masked(2 * pair, 0, prev), low, masked(2 * pair, 1, high)], axis=0
    )
    right = jnp.concatenate(
        [masked(2 * pair + 1, 0, low), high, masked(2 * pair + 1, 1, following)], axis=0
    )
    near = dot(table_ref[...], jnp.concatenate([left, right], axis=1)).astype(BF)
    fields = ordered_ref.shape[1]
    turned = []
    for i in range(2):
        hot = one_hot_grid(order_ref[pl.ds(2 * pair + i, 1), :], leaf_len)
        at = pl.ds(i * leaf_len, leaf_len)
        both = jnp.concatenate([near[:, i * fields:(i + 1) * fields], basis_ref[2 * pair + i].T], axis=1)
        moved = dot(hot, both).astype(BF)
        near_ref[at, :] = moved[:, :fields]
        turned.append(moved[:, fields:])
    turned_ref[...] = jnp.concatenate(turned, axis=1)


def near_field(pairs, near_list, leaf_order, tables, basis, ordered, halos=None, filled=None):
    leaves, rank, leaf_len = basis.shape
    fields = ordered.shape[1]
    last = leaves // 2 - 1
    gap = pairs[1] - pairs[0] if len(pairs) > 1 else 1

    def pair_of(step):
        return pairs[0] + gap * step

    in_specs = [
        scalars(),
        whole(),
        whole(),
        whole(),
        whole(),
    ]
    args = [near_list.T, leaf_order, tables, basis, ordered]
    aliases = {}
    extra = []
    if halos is not None:
        me, cross, other = halos
        row = (1,) + other.shape[1:]
        in_specs += [
            scalars(),
            pl.BlockSpec((leaf_len, fields), lambda s: (0, 0)),
            pl.BlockSpec(row, lambda s: (leaves + 1, 0, 0)),
            pl.BlockSpec(row, lambda s: (leaves + 2, 0, 0)),
        ]
        args += [me, cross, other, other]
        extra = [(16, 128)]
    if filled is not None:
        aliases = {len(args): 0, len(args) + 1: 1}
        in_specs += [pl.BlockSpec(memory_space=pl.ANY)] * 2
        args += list(filled)
    return pl.pallas_call(
        functools.partial(near_kernel, halos is not None, pair_of, last),
        name="near_" + str(pairs[0]),
        grid=(len(pairs),),
        in_specs=in_specs,
        out_specs=[
            pl.BlockSpec((2 * leaf_len, fields), lambda s: (pair_of(s), 0)),
            pl.BlockSpec((leaf_len, 2 * rank), lambda s: (pair_of(s), 0)),
        ] + [pl.BlockSpec(shape, lambda s: (0, 0)) for shape in extra],
        out_shape=[
            jax.ShapeDtypeStruct((leaves * leaf_len, fields), BF),
            jax.ShapeDtypeStruct((leaves // 2 * leaf_len, 2 * rank), BF),
        ] + [jax.ShapeDtypeStruct(shape, jnp.int32) for shape in extra],
        input_output_aliases=aliases,
        compiler_params=params(16),
        cost_estimate=cost(len(pairs) * 2 * leaf_len * leaf_len * fields * 10, len(pairs) * MIB),
    )(*args)


def field_kernel(per, own_ref, other_ref, turned_transfer_ref, near_ref, turned_ref, out_ref):
    step = pl.program_id(0)
    leaf_len = out_ref.shape[0] // per
    root = own_ref.shape[0] - 1
    local = own_ref[root] + other_ref[root]
    coarse = local.astype(BF)
    fine = (local - coarse.astype(F32)).astype(BF)
    both = jnp.concatenate([coarse, fine], axis=1)
    fields = local.shape[1]
    for pair in range(per // 2):
        values = []
        for i in range(2):
            leaf = step * per + 2 * pair + i
            down = dot(turned_transfer_ref[leaf], both)
            value = own_ref[leaf] + other_ref[leaf] + (down[:, :fields] + down[:, fields:])
            values.append(value.astype(BF))
        zero = jnp.zeros_like(values[0])
        corner = jnp.concatenate(
            [
                jnp.concatenate([values[0], zero], axis=1),
                jnp.concatenate([zero, values[1]], axis=1),
            ],
            axis=0,
        )
        at = pl.multiple_of((step * (per // 2) + pair) * leaf_len, leaf_len)
        far = dot(turned_ref[pl.ds(at, leaf_len), :], corner)
        for i in range(2):
            near = near_ref[pl.ds(2 * at + i * leaf_len, leaf_len), :].astype(F32)
            rows = slice((2 * pair + i) * leaf_len, (2 * pair + i + 1) * leaf_len)
            out_ref[rows, :] = (near + far[:, i * fields:(i + 1) * fields]).astype(BF)


def field(own, other, turned_transfer, near, turned, per=4):
    leaves, rank, _ = turned_transfer.shape
    fields = near.shape[1]
    leaf_len = near.shape[0] // leaves
    return pl.pallas_call(
        functools.partial(field_kernel, per),
        name="local_and_field",
        grid=(leaves // per,),
        in_specs=[whole()] * 5,
        out_specs=pl.BlockSpec((per * leaf_len, fields), lambda s: (s, 0)),
        out_shape=jax.ShapeDtypeStruct(near.shape, BF),
        compiler_params=params(16),
        cost_estimate=cost(leaves * leaf_len * rank * fields * 2, 4 * MIB),
    )(own, other, turned_transfer, near, turned)


def after(block, *others):
    return lax.optimization_barrier((block,) + others)[0]


def on_device(
    composition,
    leaf_basis,
    transfer,
    coupling,
    top_coupling,
    admissible_owner,
    admissible_leaf,
    near_list,
    leaf_order,
):
    leaves, rank, leaf_len = leaf_basis.shape
    count = lax.axis_size("subtree")
    layers = count // 8
    slots = layers * 4
    pairs = leaves // 2
    cut = pairs // 2
    me = lax.axis_index("subtree").reshape(1)

    ordered, shared, cross, inner, entry, own_at = skeletons_of(
        me, leaf_order, composition, leaf_basis, transfer, admissible_owner, admissible_leaf, layers
    )
    tables = jnp.asarray(near_tables(leaf_len))
    near_args = (near_list, leaf_order, tables, leaf_basis)

    line = along_z(shared, 1)
    from_x, from_y = over_x(shared), over_y(shared)
    filled = near_field(list(range(1, cut)), *near_args, ordered)
    line = after(line, filled[0])
    lines = [along_z(shared, layers - 1)]
    for _ in range(layers - 3):
        lines.append(along_z(line if len(lines) == 1 else lines[-1], 1))
    ready = after(line, from_x, from_y)
    next_x, next_y = over_x(ready), over_y(ready)
    far = onward(choose(me, after(from_x, ready, lines[0]), from_y))
    cross = lax.ppermute(
        cross,
        "subtree",
        [(d, d + 1) for d in range(1, count - 1, 2)] + [(d, d - 1) for d in range(2, count, 2)],
    )
    own_blocks, my_other, turned_transfer = dense_couplings(
        after(entry, ready), own_at, inner, coupling, top_coupling, transfer, slots
    )

    joined = after(join([after(lines[0], my_other)] + lines[1:]), next_x, next_y, cross)
    last_x, last_y = over_x(joined), over_y(joined)
    chosen = choose(me, after(next_x, joined, far), next_y)
    next_far = onward(chosen)
    other_blocks = over_core(after(my_other, chosen))
    held = after(ordered, joined)
    filled = near_field(list(range(cut, pairs - 1)), *near_args, held, filled=filled)
    next_far = after(next_far, filled[0])
    last_far = [along_z(far, layers - 1)]
    for _ in range(layers - 3):
        last_far.append(along_z(next_far if len(last_far) == 1 else last_far[-1], 1))
    held = after(ordered, filled[0])
    *filled, other_at = near_field(
        [0, pairs - 1], *near_args, held, halos=(me, cross, other_blocks), filled=filled
    )
    round_0 = ((shared, line), (from_x, next_x), (from_y, next_y), (far, next_far))
    steps = [0, 1]
    own = far_round(0, steps, slots, own_at, round_0, own_blocks)
    other = far_round(1, steps, slots, other_at, round_0, other_blocks)
    steps = list(range(2, layers))
    round_1 = ((joined,), (last_x,), (last_y,), (after(last_far[0], own, other), *last_far[1:]))
    other = far_round(1, steps, slots, other_at, round_1, other_blocks, other)
    own = far_round(0, steps, slots, own_at, round_1, own_blocks, own)
    return field(own, over_core(other), turned_transfer, *filled)


def solution(mesh):
    placed = (
        P(("groups", "subtree"), None),
        P("subtree", None, None),
        P("subtree", None, None),
        P("subtree", None, None, None),
        P("subtree", None, None, None),
        P(("groups", "subtree"), None),
        P(("groups", "subtree"), None),
        P(("groups", "subtree"), None),
        P(("groups", "subtree"), None),
    )
    return jax.shard_map(
        on_device,
        mesh=mesh,
        in_specs=placed,
        out_specs=P(("groups", "subtree"), None),
        check_vma=False,
    )
```

```python
import functools

import jax
import jax.numpy as jnp
import ml_dtypes
import numpy as np
from jax import lax
from jax.experimental import pallas as pl
from jax.experimental.pallas import tpu as pltpu
from jax.sharding import PartitionSpec as P

COULOMB_SCALE = 0.15
SOFTENING = 0.25
BF = jnp.bfloat16
F32 = jnp.float32
MIB = 1 << 20


def near_tables(leaf_len):
    cells = np.arange(leaf_len)
    along = (cells // 64).astype(np.float32)
    across = (cells // 8 % 8).astype(np.float32)
    height = (cells % 8).astype(np.float32)
    extent = leaf_len // 64
    tables = []
    for offset in (-1, 0, 1):
        delta_x = along[:, None] - along[None, :] - np.float32(offset * extent)
        delta_y = across[:, None] - across[None, :]
        delta_z = height[:, None] - height[None, :]
        square = delta_x * delta_x + delta_y * delta_y + delta_z * delta_z
        value = np.float32(COULOMB_SCALE) / np.sqrt(square + np.float32(SOFTENING))
        tables.append(value.astype(ml_dtypes.bfloat16))
    return np.concatenate(tables, axis=1)


def send(block, target):
    count = lax.axis_size("subtree")
    return lax.ppermute(block, "subtree", [(d, target(d)) for d in range(count)])


def over_core(block):
    return send(block, lambda d: d ^ 1)


def over_x(block):
    return send(block, lambda d: d ^ 2)


def over_y(block):
    return send(block, lambda d: d ^ 4)


def onward(block):
    return send(block, lambda d: d ^ (2 if d % 2 else 4))


def along_z(block, step):
    layers = lax.axis_size("subtree") // 8
    return send(block, lambda d: (d // 8 + step) % layers * 8 + d % 8)


def params(mib):
    return pltpu.CompilerParams(vmem_limit_bytes=mib * MIB)


def cost(flops, moved):
    return pl.CostEstimate(flops=flops // 64, bytes_accessed=moved // 64, transcendentals=0)


def whole():
    return pl.BlockSpec(memory_space=pltpu.VMEM)


def scalars():
    return pl.BlockSpec(memory_space=pltpu.SMEM)


def dot(a, b):
    return jnp.dot(a, b, preferred_element_type=F32)


def in_hbm(*arrays):
    return [pltpu.with_memory_space_constraint(array, pltpu.HBM) for array in arrays]


def one_hot_leaf(row, leaf_len):
    column = jnp.broadcast_to(row, (128, leaf_len)).astype(jnp.int16).T
    lanes = lax.broadcasted_iota(jnp.int32, (leaf_len, 128), 1)
    one, zero = jnp.ones((), BF), jnp.zeros((), BF)
    return jnp.concatenate(
        [
            jnp.where(column == (lanes + 128 * t).astype(jnp.int16), one, zero)
            for t in range(leaf_len // 128)
        ],
        axis=1,
    )


def one_hot_grid(row, leaf_len):
    cells = lax.broadcasted_iota(jnp.int32, (16, leaf_len), 0).astype(jnp.int16)
    wide = jnp.broadcast_to(row, (16, leaf_len)).astype(jnp.int16)
    one, zero = jnp.ones((), BF), jnp.zeros((), BF)
    return jnp.concatenate(
        [jnp.where(cells + jnp.int16(t) == wide, one, zero) for t in range(0, leaf_len, 16)], axis=0
    )


def owner_tables(me, layers, owners, blocks):
    leaves, entries = owners.shape
    slots = layers * 4
    rows = leaves + 1
    shape = (rows, 2 * slots)
    lane = lax.broadcasted_iota(jnp.int32, shape, 1)
    plane = (lane >= slots).astype(jnp.int32)
    slot = lane - plane * slots
    layer, chip, core = me // 8, (me // 2) & 3, me & 1
    turn = slot >> 2
    shift = jnp.where(turn < 2, turn, jnp.where(turn == 2, layers - 1, turn - 1))
    source = layer - shift
    source = jnp.where(source < 0, source + layers, source)
    owner = source * 8 + (chip ^ (slot & 3)) * 2 + (core ^ plane)
    row = lax.broadcasted_iota(jnp.int32, shape, 0)
    distant = jnp.abs(owner - me) >= 2
    entry = jnp.where((row == 0) & distant, owner, -1)
    block = jnp.zeros(shape, jnp.int32)
    pad = jnp.full((1, entries), -1, jnp.int32)
    named = jnp.concatenate([pad, owners], axis=0)
    chosen = jnp.concatenate([pad, blocks], axis=0)
    for k in range(entries):
        match = named[:, k:k + 1] == owner
        entry = jnp.where(match, k, entry)
        block = jnp.where(match, chosen[:, k:k + 1] + 1, block)
    return entry, block


def skeleton_kernel(per, layers, me_ref, order_ref, comp_ref, basis_ref, transfer_ref,
                    owner_ref, leaf_ref, ordered_ref, shared_ref, cross_ref, inner_ref,
                    entry_ref, block_ref, root_ref):
    step = pl.program_id(0)
    leaf_len = basis_ref.shape[2]

    @pl.when(step == 0)
    def _():
        root_ref[...] = jnp.zeros_like(root_ref)
        entry, block = owner_tables(me_ref[0], layers, owner_ref[...], leaf_ref[...])
        rows, lanes = entry.shape
        entry_ref[:rows, :lanes] = entry
        block_ref[:rows, :lanes] = block

    hots = [one_hot_leaf(order_ref[pl.ds(step * per + i, 1), :], leaf_len) for i in range(per)]
    ordered = [
        dot(hots[i], comp_ref[i * leaf_len:(i + 1) * leaf_len, :]).astype(BF) for i in range(per)
    ]
    skeletons = [dot(basis_ref[i], ordered[i]).astype(BF) for i in range(per)]
    across = jnp.concatenate([transfer_ref[i] for i in range(per)], axis=1)
    root_ref[...] += dot(across, jnp.concatenate(skeletons, axis=0))
    for i in range(per):
        at = pl.multiple_of((step * per + i) * leaf_len, leaf_len)
        ordered_ref[pl.ds(at, leaf_len), :] = ordered[i]
        shared_ref[pl.ds(step * per + i + 1, 1)] = skeletons[i][None]

    even = me_ref[0] % 2 == 0

    @pl.when((step == 0) & even)
    def _():
        cross_ref[...] = ordered[0]

    @pl.when((step == 0) & ~even)
    def _():
        inner_ref[...] = ordered[0]

    last = step == pl.num_programs(0) - 1

    @pl.when(last & even)
    def _():
        inner_ref[...] = ordered[-1]

    @pl.when(last & ~even)
    def _():
        cross_ref[...] = ordered[-1]

    @pl.when(last)
    def _():
        shared_ref[pl.ds(0, 1)] = root_ref[...].astype(BF)[None]


def skeletons_of(me, leaf_order, composition, leaf_basis, transfer, owners, blocks, layers, per=4):
    leaves, rank, leaf_len = leaf_basis.shape
    fields = composition.shape[1]
    entries = owners.shape[1]
    edge = jax.ShapeDtypeStruct((leaf_len, fields), BF)
    return pl.pallas_call(
        functools.partial(skeleton_kernel, per, layers),
        name="order_and_skeleton",
        grid=(leaves // per,),
        in_specs=[
            scalars(),
            pl.BlockSpec((leaves, leaf_len), lambda s: (0, 0)),
            pl.BlockSpec((per * leaf_len, fields), lambda s: (s, 0)),
            pl.BlockSpec((per, rank, leaf_len), lambda s: (s, 0, 0)),
            pl.BlockSpec((per, rank, rank), lambda s: (s, 0, 0)),
            pl.BlockSpec((leaves, entries), lambda s: (0, 0)),
            pl.BlockSpec((leaves, entries), lambda s: (0, 0)),
        ],
        out_specs=[whole()] * 6,
        out_shape=[
            jax.ShapeDtypeStruct((leaves * leaf_len, fields), BF),
            jax.ShapeDtypeStruct((leaves + 1, rank, fields), BF),
            edge,
            edge,
            jax.ShapeDtypeStruct((16, 128), jnp.int32),
            jax.ShapeDtypeStruct((16, 128), jnp.int32),
        ],
        scratch_shapes=[pltpu.VMEM((rank, fields), F32)],
        compiler_params=params(16),
        cost_estimate=cost(leaves * leaf_len * leaf_len * fields * 2, 4 * MIB),
    )(me, *in_hbm(leaf_order, composition, leaf_basis, transfer, owners, blocks))


def join_kernel(*refs):
    out = refs[-1]
    at = 0
    for ref in refs[:-1]:
        out[at:at + ref.shape[0]] = ref[...]
        at += ref.shape[0]


def join(parts):
    if len(parts) == 1:
        return parts[0]
    shape = (sum(part.shape[0] for part in parts),) + parts[0].shape[1:]
    return pl.pallas_call(
        join_kernel,
        name="join",
        in_specs=[whole()] * len(parts),
        out_specs=whole(),
        out_shape=jax.ShapeDtypeStruct(shape, BF),
        compiler_params=params(8 if shape[0] <= 32 else 32),
        cost_estimate=cost(0, MIB // 2),
    )(*parts)


def choose_kernel(me_ref, x_ref, y_ref, out_ref):
    @pl.when(me_ref[0] % 2 == 0)
    def _():
        out_ref[...] = x_ref[...]

    @pl.when(me_ref[0] % 2 == 1)
    def _():
        out_ref[...] = y_ref[...]


def choose(me, from_x, from_y):
    return pl.pallas_call(
        choose_kernel,
        name="choose",
        in_specs=[scalars(), whole(), whole()],
        out_specs=whole(),
        out_shape=jax.ShapeDtypeStruct(from_x.shape, BF),
        compiler_params=params(8),
        cost_estimate=cost(0, MIB // 4),
    )(me, from_x, from_y)


def dense_kernel(per, slots, entry_ref, block_ref, inner_ref, coupling_ref, top_ref,
                 transfer_ref, own_ref, other_ref, turned_ref):
    step = pl.program_id(0)
    rank = coupling_ref.shape[2]
    fields = inner_ref.shape[1]
    leaves = own_ref.shape[0] - 1
    for i in range(per):
        turned_ref[step * per + i] = transfer_ref[i].T

    def fill(out_ref, plane, row, entry_row, block_of):
        for slot in range(0, slots, 2):
            pair = []
            for one in (slot, slot + 1):
                entry = entry_ref[entry_row, plane * slots + one]
                block = block_of(jnp.maximum(entry, 0))
                pair.append(jnp.where(entry >= 0, block, jnp.zeros_like(block)))
            out_ref[row, :, slot * rank:(slot + 2) * rank] = jnp.concatenate(pair, axis=1)

    for plane, out_ref in ((0, own_ref), (1, other_ref)):
        for i in range(per):
            leaf = step * per + i
            fill(out_ref, plane, leaf, leaf + 1, lambda entry, i=i: coupling_ref[i, entry])

        @pl.when(step == pl.num_programs(0) - 1)
        def _(plane=plane, out_ref=out_ref):
            fill(out_ref, plane, leaves, 0, lambda entry: top_ref[0, entry])

    @pl.when(step == 0)
    def _():
        for t in range(inner_ref.shape[0] // rank):
            part = inner_ref[t * rank:(t + 1) * rank, :]
            other_ref[leaves + 1, :, t * fields:(t + 1) * fields] = part
        other_ref[leaves + 2] = jnp.zeros(other_ref.shape[1:], BF)
        blocks = block_ref[...].astype(F32).astype(BF)
        other_ref[leaves + 2, :blocks.shape[0], :blocks.shape[1]] = blocks


def dense_couplings(entry, block, inner, coupling, top_coupling, transfer, slots, per=4):
    leaves, entries, rank, _ = coupling.shape
    own = (leaves + 1, rank, slots * rank)
    other = (leaves + 3, rank, slots * rank)
    return pl.pallas_call(
        functools.partial(dense_kernel, per, slots),
        name="couplings_by_owner",
        grid=(leaves // per,),
        in_specs=[
            scalars(),
            pl.BlockSpec(block.shape, lambda s: (0, 0)),
            pl.BlockSpec(inner.shape, lambda s: (0, 0)),
            pl.BlockSpec((per, entries, rank, rank), lambda s: (s, 0, 0, 0)),
            pl.BlockSpec(top_coupling.shape, lambda s: (0, 0, 0, 0)),
            pl.BlockSpec((per, rank, rank), lambda s: (s, 0, 0)),
        ],
        out_specs=[whole()] * 3,
        out_shape=[
            jax.ShapeDtypeStruct(own, BF),
            jax.ShapeDtypeStruct(other, BF),
            jax.ShapeDtypeStruct(transfer.shape, BF),
        ],
        compiler_params=params(16 if slots <= 16 else 48),
        cost_estimate=cost(0, 8 * MIB),
    )(entry, block, inner, *in_hbm(coupling, top_coupling, transfer))


def round_kernel(plane, steps, slots, counts, at_ref, *refs):
    sides = []
    for number in counts:
        sides.append(refs[:number])
        refs = refs[number:]
    blocks_ref, out = refs[0], refs[-1]
    rows, rank, _ = out.shape
    low, high = steps[0] * 4 * rank, (steps[-1] + 1) * 4 * rank

    def block_at(side, base, index):
        for ref in side:
            if base < ref.shape[0]:
                return ref[base + index]
            base -= ref.shape[0]

    for row in range(rows):
        chosen = [
            block_at(side, place * rows, at_ref[(row + 1) % rows, plane * slots + step * 4 + q])
            for place, step in enumerate(steps)
            for q, side in enumerate(sides)
        ]
        value = dot(blocks_ref[row, :, low:high], jnp.concatenate(chosen, axis=0))
        if len(refs) > 2:
            value = value + refs[1][row]
        out[row] = value


def far_round(plane, steps, slots, at, parts, blocks, total=None):
    rank, fields = parts[0][0].shape[1:]
    rows = parts[0][0].shape[0] // (1 if len(parts[0]) > 1 else len(steps))
    args = [part for side in parts for part in side] + [blocks] + ([] if total is None else [total])
    return pl.pallas_call(
        functools.partial(round_kernel, plane, steps, slots, [len(side) for side in parts]),
        name="far_" + str(plane) + "_" + str(steps[0]),
        in_specs=[scalars()] + [whole()] * len(args),
        out_specs=whole(),
        out_shape=jax.ShapeDtypeStruct((rows, rank, fields), F32),
        compiler_params=params(16 if slots <= 16 else 48),
        cost_estimate=cost(rows * rank * 4 * rank * fields * 2 * len(steps), MIB),
    )(at, *args)


def near_kernel(edges, pair_of, last_pair, mask_ref, order_ref, table_ref, basis_ref,
                ordered_ref, *refs):
    if edges:
        me_ref, cross_ref, inner_ref, blocks_ref = refs[:4]
        near_ref, turned_ref, at_ref = refs[-3:]
    else:
        near_ref, turned_ref = refs[-2:]
    pair = pair_of(pl.program_id(0))
    leaf_len = basis_ref.shape[2]
    leaves = basis_ref.shape[0]

    def leaf_at(leaf):
        return ordered_ref[pl.ds(pl.multiple_of(leaf * leaf_len, leaf_len), leaf_len), :]

    low, high = leaf_at(2 * pair), leaf_at(2 * pair + 1)
    prev, following = leaf_at(jnp.maximum(2 * pair - 1, 0)), leaf_at(jnp.minimum(2 * pair + 2, leaves - 1))
    if edges:
        even = me_ref[0] % 2 == 0
        cross = cross_ref[...]
        wide = cross.shape[1]
        inner = jnp.concatenate(
            [inner_ref[0, :, t:t + wide] for t in range(0, inner_ref.shape[2], wide)], axis=0
        )[:leaf_len]
        prev = jnp.where(pair == 0, jnp.where(even, cross, inner), prev)
        following = jnp.where(pair == last_pair, jnp.where(even, inner, cross), following)

        @pl.when(pl.program_id(0) == 0)
        def _():
            rows, lanes = at_ref.shape
            at_ref[...] = blocks_ref[0, :rows, :lanes].astype(F32).astype(jnp.int32)


    def masked(leaf, side, value):
        return jnp.where(mask_ref[side, leaf] > 0, value, jnp.zeros_like(value))

    left = jnp.concatenate(
        [masked(2 * pair, 0, prev), low, masked(2 * pair, 1, high)], axis=0
    )
    right = jnp.concatenate(
        [masked(2 * pair + 1, 0, low), high, masked(2 * pair + 1, 1, following)], axis=0
    )
    near = dot(table_ref[...], jnp.concatenate([left, right], axis=1)).astype(BF)
    fields = ordered_ref.shape[1]
    turned = []
    for i in range(2):
        hot = one_hot_grid(order_ref[pl.ds(2 * pair + i, 1), :], leaf_len)
        at = pl.ds(pl.multiple_of((2 * pair + i) * leaf_len, leaf_len), leaf_len)
        both = jnp.concatenate([near[:, i * fields:(i + 1) * fields], basis_ref[2 * pair + i].T], axis=1)
        moved = dot(hot, both).astype(BF)
        near_ref[at, :] = moved[:, :fields]
        turned.append(moved[:, fields:])
    at = pl.multiple_of(pair * leaf_len, leaf_len)
    turned_ref[pl.ds(at, leaf_len), :] = jnp.concatenate(turned, axis=1)


def near_field(pairs, near_list, leaf_order, tables, basis, ordered, halos=None, filled=None):
    leaves, rank, leaf_len = basis.shape
    fields = ordered.shape[1]
    last = leaves // 2 - 1
    gap = pairs[1] - pairs[0] if len(pairs) > 1 else 1

    def pair_of(step):
        return pairs[0] + gap * step

    in_specs = [
        scalars(),
        whole(),
        whole(),
        whole(),
        whole(),
    ]
    args = [near_list.T, leaf_order, tables, basis, ordered]
    aliases = {}
    extra = []
    if halos is not None:
        me, cross, other = halos
        row = (1,) + other.shape[1:]
        in_specs += [
            scalars(),
            pl.BlockSpec((leaf_len, fields), lambda s: (0, 0)),
            pl.BlockSpec(row, lambda s: (leaves + 1, 0, 0)),
            pl.BlockSpec(row, lambda s: (leaves + 2, 0, 0)),
        ]
        args += [me, cross, other, other]
        extra = [(16, 128)]
    if filled is not None:
        aliases = {len(args): 0, len(args) + 1: 1}
        in_specs += [whole()] * 2
        args += list(filled)
    return pl.pallas_call(
        functools.partial(near_kernel, halos is not None, pair_of, last),
        name="near_" + str(pairs[0]),
        grid=(len(pairs),),
        in_specs=in_specs,
        out_specs=[whole()] * (2 + len(extra)),
        out_shape=[
            jax.ShapeDtypeStruct((leaves * leaf_len, fields), BF),
            jax.ShapeDtypeStruct((leaves // 2 * leaf_len, 2 * rank), BF),
        ] + [jax.ShapeDtypeStruct(shape, jnp.int32) for shape in extra],
        input_output_aliases=aliases,
        compiler_params=params(16),
        cost_estimate=cost(len(pairs) * 2 * leaf_len * leaf_len * fields * 10, len(pairs) * MIB),
    )(*args)


def field_kernel(per, own_ref, other_ref, turned_transfer_ref, near_ref, turned_ref, out_ref):
    step = pl.program_id(0)
    leaf_len = out_ref.shape[0] // per
    root = own_ref.shape[0] - 1
    local = own_ref[root] + other_ref[root]
    coarse = local.astype(BF)
    fine = (local - coarse.astype(F32)).astype(BF)
    both = jnp.concatenate([coarse, fine], axis=1)
    fields = local.shape[1]
    for pair in range(per // 2):
        values = []
        for i in range(2):
            leaf = step * per + 2 * pair + i
            down = dot(turned_transfer_ref[leaf], both)
            value = own_ref[leaf] + other_ref[leaf] + (down[:, :fields] + down[:, fields:])
            values.append(value.astype(BF))
        zero = jnp.zeros_like(values[0])
        corner = jnp.concatenate(
            [
                jnp.concatenate([values[0], zero], axis=1),
                jnp.concatenate([zero, values[1]], axis=1),
            ],
            axis=0,
        )
        at = pl.multiple_of((step * (per // 2) + pair) * leaf_len, leaf_len)
        far = dot(turned_ref[pl.ds(at, leaf_len), :], corner)
        for i in range(2):
            near = near_ref[pl.ds(2 * at + i * leaf_len, leaf_len), :].astype(F32)
            rows = slice((2 * pair + i) * leaf_len, (2 * pair + i + 1) * leaf_len)
            out_ref[rows, :] = (near + far[:, i * fields:(i + 1) * fields]).astype(BF)


def field(own, other, turned_transfer, near, turned, per=2):
    leaves, rank, _ = turned_transfer.shape
    fields = near.shape[1]
    leaf_len = near.shape[0] // leaves
    return pl.pallas_call(
        functools.partial(field_kernel, per),
        name="local_and_field",
        grid=(leaves // per,),
        in_specs=[whole()] * 5,
        out_specs=pl.BlockSpec((per * leaf_len, fields), lambda s: (s, 0)),
        out_shape=jax.ShapeDtypeStruct(near.shape, BF),
        compiler_params=params(16),
        cost_estimate=cost(leaves * leaf_len * rank * fields * 2, 4 * MIB),
    )(own, other, turned_transfer, near, turned)


def after(block, *others):
    return lax.optimization_barrier((block,) + others)[0]


def on_device(
    composition,
    leaf_basis,
    transfer,
    coupling,
    top_coupling,
    admissible_owner,
    admissible_leaf,
    near_list,
    leaf_order,
):
    leaves, rank, leaf_len = leaf_basis.shape
    count = lax.axis_size("subtree")
    layers = count // 8
    slots = layers * 4
    pairs = leaves // 2
    cut = pairs // 2
    me = lax.axis_index("subtree").reshape(1)

    ordered, shared, cross, inner, entry, own_at = skeletons_of(
        me, leaf_order, composition, leaf_basis, transfer, admissible_owner, admissible_leaf, layers
    )
    tables = jnp.asarray(near_tables(leaf_len))
    near_args = (near_list, leaf_order, tables, leaf_basis)

    line = along_z(shared, 1)
    from_x, from_y = over_x(shared), over_y(shared)
    filled = near_field(list(range(1, cut)), *near_args, ordered)
    line = after(line, filled[0])
    lines = [along_z(shared, layers - 1)]
    for _ in range(layers - 3):
        lines.append(along_z(line if len(lines) == 1 else lines[-1], 1))
    ready = after(line, from_x, from_y)
    next_x, next_y = over_x(ready), over_y(ready)
    far = onward(choose(me, after(from_x, ready, lines[0]), from_y))
    cross = lax.ppermute(
        cross,
        "subtree",
        [(d, d + 1) for d in range(1, count - 1, 2)] + [(d, d - 1) for d in range(2, count, 2)],
    )
    own_blocks, my_other, turned_transfer = dense_couplings(
        after(entry, ready), own_at, inner, coupling, top_coupling, transfer, slots
    )

    joined = after(join([after(lines[0], my_other)] + lines[1:]), next_x, next_y, cross)
    last_x, last_y = over_x(joined), over_y(joined)
    chosen = choose(me, after(next_x, joined, far), next_y)
    next_far = onward(chosen)
    other_blocks = over_core(after(my_other, chosen))
    held = after(ordered, joined)
    filled = near_field(list(range(cut, pairs - 1)), *near_args, held, filled=filled)
    next_far = after(next_far, filled[0])
    last_far = [along_z(far, layers - 1)]
    for _ in range(layers - 3):
        last_far.append(along_z(next_far if len(last_far) == 1 else last_far[-1], 1))
    held = after(ordered, filled[0])
    *filled, other_at = near_field(
        [0, pairs - 1], *near_args, held, halos=(me, cross, other_blocks), filled=filled
    )
    round_0 = ((shared, line), (from_x, next_x), (from_y, next_y), (far, next_far))
    steps = [0, 1]
    own = far_round(0, steps, slots, own_at, round_0, own_blocks)
    other = far_round(1, steps, slots, other_at, round_0, other_blocks)
    steps = list(range(2, layers))
    round_1 = ((joined,), (last_x,), (last_y,), (after(last_far[0], own, other), *last_far[1:]))
    other = far_round(1, steps, slots, other_at, round_1, other_blocks, other)
    own = far_round(0, steps, slots, own_at, round_1, own_blocks, own)
    return field(own, over_core(other), turned_transfer, *filled)


def solution(mesh):
    placed = (
        P(("groups", "subtree"), None),
        P("subtree", None, None),
        P("subtree", None, None),
        P("subtree", None, None, None),
        P("subtree", None, None, None),
        P(("groups", "subtree"), None),
        P(("groups", "subtree"), None),
        P(("groups", "subtree"), None),
        P(("groups", "subtree"), None),
    )
    return jax.shard_map(
        on_device,
        mesh=mesh,
        in_specs=placed,
        out_specs=P(("groups", "subtree"), None),
        check_vma=False,
    )
```

```python
import functools

import jax
import jax.numpy as jnp
import ml_dtypes
import numpy as np
from jax import lax
from jax.experimental import pallas as pl
from jax.experimental.pallas import tpu as pltpu
from jax.sharding import PartitionSpec as P

COULOMB_SCALE = 0.15
SOFTENING = 0.25
BF = jnp.bfloat16
F32 = jnp.float32
MIB = 1 << 20


def near_tables(leaf_len):
    cells = np.arange(leaf_len)
    along = (cells // 64).astype(np.float32)
    across = (cells // 8 % 8).astype(np.float32)
    height = (cells % 8).astype(np.float32)
    extent = leaf_len // 64
    tables = []
    for offset in (-1, 0, 1):
        delta_x = along[:, None] - along[None, :] - np.float32(offset * extent)
        delta_y = across[:, None] - across[None, :]
        delta_z = height[:, None] - height[None, :]
        square = delta_x * delta_x + delta_y * delta_y + delta_z * delta_z
        value = np.float32(COULOMB_SCALE) / np.sqrt(square + np.float32(SOFTENING))
        tables.append(value.astype(ml_dtypes.bfloat16))
    return np.concatenate(tables, axis=1)


def send(block, target):
    count = lax.axis_size("subtree")
    return lax.ppermute(block, "subtree", [(d, target(d)) for d in range(count)])


def over_core(block):
    return send(block, lambda d: d ^ 1)


def over_x(block):
    return send(block, lambda d: d ^ 2)


def over_y(block):
    return send(block, lambda d: d ^ 4)


def onward(block):
    return send(block, lambda d: d ^ (2 if d % 2 else 4))


def along_z(block, step):
    layers = lax.axis_size("subtree") // 8
    return send(block, lambda d: (d // 8 + step) % layers * 8 + d % 8)


def params(mib):
    return pltpu.CompilerParams(vmem_limit_bytes=mib * MIB)


def cost(flops, moved):
    return pl.CostEstimate(flops=flops // 64, bytes_accessed=moved // 64, transcendentals=0)


def whole():
    return pl.BlockSpec(memory_space=pltpu.VMEM)


def scalars():
    return pl.BlockSpec(memory_space=pltpu.SMEM)


def dot(a, b):
    return jnp.dot(a, b, preferred_element_type=F32)


def in_hbm(*arrays):
    return [pltpu.with_memory_space_constraint(array, pltpu.HBM) for array in arrays]


def one_hot_leaf(row, leaf_len):
    column = jnp.broadcast_to(row, (128, leaf_len)).astype(jnp.int16).T
    lanes = lax.broadcasted_iota(jnp.int32, (leaf_len, 128), 1)
    one, zero = jnp.ones((), BF), jnp.zeros((), BF)
    return jnp.concatenate(
        [
            jnp.where(column == (lanes + 128 * t).astype(jnp.int16), one, zero)
            for t in range(leaf_len // 128)
        ],
        axis=1,
    )


def one_hot_grid(row, leaf_len):
    cells = lax.broadcasted_iota(jnp.int32, (16, leaf_len), 0).astype(jnp.int16)
    wide = jnp.broadcast_to(row, (16, leaf_len)).astype(jnp.int16)
    one, zero = jnp.ones((), BF), jnp.zeros((), BF)
    return jnp.concatenate(
        [jnp.where(cells + jnp.int16(t) == wide, one, zero) for t in range(0, leaf_len, 16)], axis=0
    )


def owner_tables(me, layers, owners, blocks):
    leaves, entries = owners.shape
    slots = layers * 4
    rows = leaves + 1
    shape = (rows, 2 * slots)
    lane = lax.broadcasted_iota(jnp.int32, shape, 1)
    plane = (lane >= slots).astype(jnp.int32)
    slot = lane - plane * slots
    layer, chip, core = me // 8, (me // 2) & 3, me & 1
    turn = slot >> 2
    shift = jnp.where(turn < 2, turn, jnp.where(turn == 2, layers - 1, turn - 1))
    source = layer - shift
    source = jnp.where(source < 0, source + layers, source)
    owner = source * 8 + (chip ^ (slot & 3)) * 2 + (core ^ plane)
    row = lax.broadcasted_iota(jnp.int32, shape, 0)
    distant = jnp.abs(owner - me) >= 2
    entry = jnp.where((row == 0) & distant, owner, -1)
    block = jnp.zeros(shape, jnp.int32)
    pad = jnp.full((1, entries), -1, jnp.int32)
    named = jnp.concatenate([pad, owners], axis=0)
    chosen = jnp.concatenate([pad, blocks], axis=0)
    for k in range(entries):
        match = named[:, k:k + 1] == owner
        entry = jnp.where(match, k, entry)
        block = jnp.where(match, chosen[:, k:k + 1] + 1, block)
    return entry, block


def skeleton_kernel(per, layers, me_ref, order_ref, comp_ref, basis_ref, transfer_ref,
                    owner_ref, leaf_ref, ordered_ref, shared_ref, cross_ref, inner_ref,
                    entry_ref, block_ref, root_ref):
    step = pl.program_id(0)
    leaf_len = basis_ref.shape[2]

    @pl.when(step == 0)
    def _():
        root_ref[...] = jnp.zeros_like(root_ref)
        entry, block = owner_tables(me_ref[0], layers, owner_ref[...], leaf_ref[...])
        rows, lanes = entry.shape
        entry_ref[:rows, :lanes] = entry
        block_ref[:rows, :lanes] = block

    hots = [one_hot_leaf(order_ref[pl.ds(step * per + i, 1), :], leaf_len) for i in range(per)]
    ordered = [
        dot(hots[i], comp_ref[i * leaf_len:(i + 1) * leaf_len, :]).astype(BF) for i in range(per)
    ]
    skeletons = [dot(basis_ref[i], ordered[i]).astype(BF) for i in range(per)]
    across = jnp.concatenate([transfer_ref[i] for i in range(per)], axis=1)
    root_ref[...] += dot(across, jnp.concatenate(skeletons, axis=0))
    for i in range(per):
        at = pl.multiple_of((step * per + i) * leaf_len, leaf_len)
        ordered_ref[pl.ds(at, leaf_len), :] = ordered[i]
        shared_ref[pl.ds(step * per + i + 1, 1)] = skeletons[i][None]

    even = me_ref[0] % 2 == 0

    @pl.when((step == 0) & even)
    def _():
        cross_ref[...] = ordered[0]

    @pl.when((step == 0) & ~even)
    def _():
        inner_ref[...] = ordered[0]

    last = step == pl.num_programs(0) - 1

    @pl.when(last & even)
    def _():
        inner_ref[...] = ordered[-1]

    @pl.when(last & ~even)
    def _():
        cross_ref[...] = ordered[-1]

    @pl.when(last)
    def _():
        shared_ref[pl.ds(0, 1)] = root_ref[...].astype(BF)[None]


def skeletons_of(me, leaf_order, composition, leaf_basis, transfer, owners, blocks, layers, per=6):
    leaves, rank, leaf_len = leaf_basis.shape
    fields = composition.shape[1]
    entries = owners.shape[1]
    edge = jax.ShapeDtypeStruct((leaf_len, fields), BF)
    return pl.pallas_call(
        functools.partial(skeleton_kernel, per, layers),
        name="order_and_skeleton",
        grid=(leaves // per,),
        in_specs=[
            scalars(),
            pl.BlockSpec((leaves, leaf_len), lambda s: (0, 0)),
            pl.BlockSpec((per * leaf_len, fields), lambda s: (s, 0)),
            pl.BlockSpec((per, rank, leaf_len), lambda s: (s, 0, 0)),
            pl.BlockSpec((per, rank, rank), lambda s: (s, 0, 0)),
            pl.BlockSpec((leaves, entries), lambda s: (0, 0)),
            pl.BlockSpec((leaves, entries), lambda s: (0, 0)),
        ],
        out_specs=[whole()] * 6,
        out_shape=[
            jax.ShapeDtypeStruct((leaves * leaf_len, fields), BF),
            jax.ShapeDtypeStruct((leaves + 1, rank, fields), BF),
            edge,
            edge,
            jax.ShapeDtypeStruct((16, 128), jnp.int32),
            jax.ShapeDtypeStruct((16, 128), jnp.int32),
        ],
        scratch_shapes=[pltpu.VMEM((rank, fields), F32)],
        compiler_params=params(16),
        cost_estimate=cost(leaves * leaf_len * leaf_len * fields * 2, 4 * MIB),
    )(me, *in_hbm(leaf_order, composition, leaf_basis, transfer, owners, blocks))


def join_kernel(*refs):
    out = refs[-1]
    at = 0
    for ref in refs[:-1]:
        out[at:at + ref.shape[0]] = ref[...]
        at += ref.shape[0]


def join(parts):
    if len(parts) == 1:
        return parts[0]
    shape = (sum(part.shape[0] for part in parts),) + parts[0].shape[1:]
    return pl.pallas_call(
        join_kernel,
        name="join",
        in_specs=[whole()] * len(parts),
        out_specs=whole(),
        out_shape=jax.ShapeDtypeStruct(shape, BF),
        compiler_params=params(8 if shape[0] <= 32 else 32),
        cost_estimate=cost(0, MIB // 2),
    )(*parts)


def choose_kernel(me_ref, x_ref, y_ref, out_ref):
    @pl.when(me_ref[0] % 2 == 0)
    def _():
        out_ref[...] = x_ref[...]

    @pl.when(me_ref[0] % 2 == 1)
    def _():
        out_ref[...] = y_ref[...]


def choose(me, from_x, from_y):
    return pl.pallas_call(
        choose_kernel,
        name="choose",
        in_specs=[scalars(), whole(), whole()],
        out_specs=whole(),
        out_shape=jax.ShapeDtypeStruct(from_x.shape, BF),
        compiler_params=params(8),
        cost_estimate=cost(0, MIB // 4),
    )(me, from_x, from_y)


def dense_kernel(per, slots, entry_ref, block_ref, inner_ref, coupling_ref, top_ref,
                 transfer_ref, own_ref, other_ref, turned_ref):
    step = pl.program_id(0)
    rank = coupling_ref.shape[2]
    fields = inner_ref.shape[1]
    leaves = own_ref.shape[0] - 1
    for i in range(per):
        turned_ref[step * per + i] = transfer_ref[i].T

    def fill(out_ref, plane, row, entry_row, block_of):
        for slot in range(0, slots, 2):
            pair = []
            for one in (slot, slot + 1):
                entry = entry_ref[entry_row, plane * slots + one]
                block = block_of(jnp.maximum(entry, 0))
                pair.append(jnp.where(entry >= 0, block, jnp.zeros_like(block)))
            out_ref[row, :, slot * rank:(slot + 2) * rank] = jnp.concatenate(pair, axis=1)

    for plane, out_ref in ((0, own_ref), (1, other_ref)):
        for i in range(per):
            leaf = step * per + i
            fill(out_ref, plane, leaf, leaf + 1, lambda entry, i=i: coupling_ref[i, entry])

        @pl.when(step == pl.num_programs(0) - 1)
        def _(plane=plane, out_ref=out_ref):
            fill(out_ref, plane, leaves, 0, lambda entry: top_ref[0, entry])

    @pl.when(step == 0)
    def _():
        for t in range(inner_ref.shape[0] // rank):
            part = inner_ref[t * rank:(t + 1) * rank, :]
            other_ref[leaves + 1, :, t * fields:(t + 1) * fields] = part
        other_ref[leaves + 2] = jnp.zeros(other_ref.shape[1:], BF)
        blocks = block_ref[...].astype(F32).astype(BF)
        other_ref[leaves + 2, :blocks.shape[0], :blocks.shape[1]] = blocks


def dense_couplings(entry, block, inner, coupling, top_coupling, transfer, slots, per=6):
    leaves, entries, rank, _ = coupling.shape
    own = (leaves + 1, rank, slots * rank)
    other = (leaves + 3, rank, slots * rank)
    return pl.pallas_call(
        functools.partial(dense_kernel, per, slots),
        name="couplings_by_owner",
        grid=(leaves // per,),
        in_specs=[
            scalars(),
            pl.BlockSpec(block.shape, lambda s: (0, 0)),
            pl.BlockSpec(inner.shape, lambda s: (0, 0)),
            pl.BlockSpec((per, entries, rank, rank), lambda s: (s, 0, 0, 0)),
            pl.BlockSpec(top_coupling.shape, lambda s: (0, 0, 0, 0)),
            pl.BlockSpec((per, rank, rank), lambda s: (s, 0, 0)),
        ],
        out_specs=[whole()] * 3,
        out_shape=[
            jax.ShapeDtypeStruct(own, BF),
            jax.ShapeDtypeStruct(other, BF),
            jax.ShapeDtypeStruct(transfer.shape, BF),
        ],
        compiler_params=params(16 if slots <= 16 else 48),
        cost_estimate=cost(0, 8 * MIB),
    )(entry, block, inner, *in_hbm(coupling, top_coupling, transfer))


def round_kernel(plane, steps, slots, counts, at_ref, *refs):
    sides = []
    for number in counts:
        sides.append(refs[:number])
        refs = refs[number:]
    blocks_ref, out = refs[0], refs[-1]
    rows, rank, _ = out.shape
    low, high = steps[0] * 4 * rank, (steps[-1] + 1) * 4 * rank

    def block_at(side, base, index):
        for ref in side:
            if base < ref.shape[0]:
                return ref[base + index]
            base -= ref.shape[0]

    for row in range(rows):
        chosen = [
            block_at(side, place * rows, at_ref[(row + 1) % rows, plane * slots + step * 4 + q])
            for place, step in enumerate(steps)
            for q, side in enumerate(sides)
        ]
        value = dot(blocks_ref[row, :, low:high], jnp.concatenate(chosen, axis=0))
        if len(refs) > 2:
            value = value + refs[1][row]
        out[row] = value


def far_round(plane, steps, slots, at, parts, blocks, total=None):
    rank, fields = parts[0][0].shape[1:]
    rows = parts[0][0].shape[0] // (1 if len(parts[0]) > 1 else len(steps))
    args = [part for side in parts for part in side] + [blocks] + ([] if total is None else [total])
    return pl.pallas_call(
        functools.partial(round_kernel, plane, steps, slots, [len(side) for side in parts]),
        name="far_" + str(plane) + "_" + str(steps[0]),
        in_specs=[scalars()] + [whole()] * len(args),
        out_specs=whole(),
        out_shape=jax.ShapeDtypeStruct((rows, rank, fields), F32),
        compiler_params=params(16 if slots <= 16 else 48),
        cost_estimate=cost(rows * rank * 4 * rank * fields * 2 * len(steps), MIB),
    )(at, *args)


def near_kernel(edges, pairs, mask_ref, order_ref, table_ref, basis_ref, ordered_ref, *refs):
    if edges:
        me_ref, cross_ref, inner_ref = refs[:3]
        near_ref, turned_ref, at_ref = refs[-3:]
        even = me_ref[0] % 2 == 0
    else:
        near_ref, turned_ref = refs[-2:]
    leaves, _, leaf_len = basis_ref.shape
    fields = ordered_ref.shape[1]
    if edges:
        rows, rank = at_ref.shape[0], basis_ref.shape[1]
        blocks = inner_ref[leaves + 2, :rows, :at_ref.shape[1]]
        at_ref[...] = blocks.astype(F32).astype(jnp.int32)
        inner = jnp.concatenate(
            [
                inner_ref[leaves + 1, :, t * fields:(t + 1) * fields]
                for t in range(leaf_len // rank)
            ],
            axis=0,
        )

    def leaf_at(leaf):
        if leaf < 0:
            return jnp.where(even, cross_ref[...], inner)
        if leaf >= leaves:
            return jnp.where(even, inner, cross_ref[...])
        return ordered_ref[leaf * leaf_len:(leaf + 1) * leaf_len, :]

    def masked(leaf, side):
        value = leaf_at(leaf - 1 + 2 * side)
        return jnp.where(mask_ref[side, leaf] > 0, value, jnp.zeros_like(value))

    for pair in pairs:
        columns = [
            jnp.concatenate([masked(leaf, 0), leaf_at(leaf), masked(leaf, 1)], axis=0)
            for leaf in (2 * pair, 2 * pair + 1)
        ]
        near = dot(table_ref[...], jnp.concatenate(columns, axis=1)).astype(BF)
        turned = []
        for i in range(2):
            leaf = 2 * pair + i
            hot = one_hot_grid(order_ref[leaf:leaf + 1, :], leaf_len)
            both = jnp.concatenate([near[:, i * fields:(i + 1) * fields], basis_ref[leaf].T], axis=1)
            moved = dot(hot, both).astype(BF)
            near_ref[leaf * leaf_len:(leaf + 1) * leaf_len, :] = moved[:, :fields]
            turned.append(moved[:, fields:])
        turned_ref[pair * leaf_len:(pair + 1) * leaf_len, :] = jnp.concatenate(turned, axis=1)


def near_field(pairs, near_list, leaf_order, tables, basis, ordered, halos=None, filled=None):
    leaves, rank, leaf_len = basis.shape
    fields = ordered.shape[1]
    args = [near_list.T, leaf_order, tables, basis, ordered]
    in_specs = [scalars()] + [whole()] * 4
    out_shape = [
        jax.ShapeDtypeStruct((leaves * leaf_len, fields), BF),
        jax.ShapeDtypeStruct((leaves // 2 * leaf_len, 2 * rank), BF),
    ]
    aliases = {}
    if halos is not None:
        in_specs += [scalars(), whole(), whole()]
        args += list(halos)
        out_shape.append(jax.ShapeDtypeStruct((16, 128), jnp.int32))
    if filled is not None:
        aliases = {len(args): 0, len(args) + 1: 1}
        in_specs += [whole()] * 2
        args += list(filled)
    return pl.pallas_call(
        functools.partial(near_kernel, halos is not None, tuple(pairs)),
        name="near_" + str(pairs[0]),
        in_specs=in_specs,
        out_specs=[whole()] * len(out_shape),
        out_shape=out_shape,
        input_output_aliases=aliases,
        compiler_params=params(16),
        cost_estimate=cost(len(pairs) * 2 * leaf_len * leaf_len * fields * 10, len(pairs) * MIB),
    )(*args)


def field_kernel(per, own_ref, other_ref, turned_transfer_ref, near_ref, turned_ref, out_ref):
    step = pl.program_id(0)
    leaf_len = out_ref.shape[0] // per
    root = own_ref.shape[0] - 1
    local = own_ref[root] + other_ref[root]
    coarse = local.astype(BF)
    fine = (local - coarse.astype(F32)).astype(BF)
    both = jnp.concatenate([coarse, fine], axis=1)
    fields = local.shape[1]
    for pair in range(per // 2):
        values = []
        for i in range(2):
            leaf = step * per + 2 * pair + i
            down = dot(turned_transfer_ref[leaf], both)
            value = own_ref[leaf] + other_ref[leaf] + (down[:, :fields] + down[:, fields:])
            values.append(value.astype(BF))
        zero = jnp.zeros_like(values[0])
        corner = jnp.concatenate(
            [
                jnp.concatenate([values[0], zero], axis=1),
                jnp.concatenate([zero, values[1]], axis=1),
            ],
            axis=0,
        )
        at = pl.multiple_of((step * (per // 2) + pair) * leaf_len, leaf_len)
        far = dot(turned_ref[pl.ds(at, leaf_len), :], corner)
        for i in range(2):
            near = near_ref[pl.ds(2 * at + i * leaf_len, leaf_len), :].astype(F32)
            rows = slice((2 * pair + i) * leaf_len, (2 * pair + i + 1) * leaf_len)
            out_ref[rows, :] = (near + far[:, i * fields:(i + 1) * fields]).astype(BF)


def field(own, other, turned_transfer, near, turned, per=6):
    leaves, rank, _ = turned_transfer.shape
    fields = near.shape[1]
    leaf_len = near.shape[0] // leaves
    return pl.pallas_call(
        functools.partial(field_kernel, per),
        name="local_and_field",
        grid=(leaves // per,),
        in_specs=[whole()] * 5,
        out_specs=pl.BlockSpec((per * leaf_len, fields), lambda s: (s, 0)),
        out_shape=jax.ShapeDtypeStruct(near.shape, BF),
        compiler_params=params(16),
        cost_estimate=cost(leaves * leaf_len * rank * fields * 2, 4 * MIB),
    )(own, other, turned_transfer, near, turned)


def after(block, *others):
    return lax.optimization_barrier((block,) + others)[0]


def on_device(
    composition,
    leaf_basis,
    transfer,
    coupling,
    top_coupling,
    admissible_owner,
    admissible_leaf,
    near_list,
    leaf_order,
):
    leaves, rank, leaf_len = leaf_basis.shape
    count = lax.axis_size("subtree")
    layers = count // 8
    slots = layers * 4
    pairs = leaves // 2
    cut = pairs // 2
    me = lax.axis_index("subtree").reshape(1)

    ordered, shared, cross, inner, entry, own_at = skeletons_of(
        me, leaf_order, composition, leaf_basis, transfer, admissible_owner, admissible_leaf, layers
    )
    tables = jnp.asarray(near_tables(leaf_len))
    near_args = (near_list, leaf_order, tables, leaf_basis)

    line = along_z(shared, 1)
    from_x, from_y = over_x(shared), over_y(shared)
    filled = near_field(list(range(1, cut)), *near_args, ordered)
    line = after(line, filled[0])
    lines = [along_z(shared, layers - 1)]
    for _ in range(layers - 3):
        lines.append(along_z(line if len(lines) == 1 else lines[-1], 1))
    ready = after(line, from_x, from_y)
    next_x, next_y = over_x(ready), over_y(ready)
    far = onward(choose(me, after(from_x, ready, lines[0]), from_y))
    cross = lax.ppermute(
        cross,
        "subtree",
        [(d, d + 1) for d in range(1, count - 1, 2)] + [(d, d - 1) for d in range(2, count, 2)],
    )
    own_blocks, my_other, turned_transfer = dense_couplings(
        after(entry, ready), own_at, inner, coupling, top_coupling, transfer, slots
    )

    joined = after(join([after(lines[0], my_other)] + lines[1:]), next_x, next_y, cross)
    last_x, last_y = over_x(joined), over_y(joined)
    chosen = choose(me, after(next_x, joined, far), next_y)
    next_far = onward(chosen)
    other_blocks = over_core(after(my_other, chosen))
    held = after(ordered, joined)
    filled = near_field(list(range(cut, pairs - 1)), *near_args, held, filled=filled)
    next_far = after(next_far, filled[0])
    last_far = [along_z(far, layers - 1)]
    for _ in range(layers - 3):
        last_far.append(along_z(next_far if len(last_far) == 1 else last_far[-1], 1))
    held = after(ordered, filled[0])
    *filled, other_at = near_field(
        [0, pairs - 1], *near_args, held, halos=(me, cross, other_blocks), filled=filled
    )
    round_0 = ((shared, line), (from_x, next_x), (from_y, next_y), (far, next_far))
    steps = [0, 1]
    own = far_round(0, steps, slots, own_at, round_0, own_blocks)
    other = far_round(1, steps, slots, other_at, round_0, other_blocks)
    steps = list(range(2, layers))
    round_1 = ((joined,), (last_x,), (last_y,), (after(last_far[0], own, other), *last_far[1:]))
    other = far_round(1, steps, slots, other_at, round_1, other_blocks, other)
    own = far_round(0, steps, slots, own_at, round_1, own_blocks, own)
    return field(own, over_core(other), turned_transfer, *filled)


def solution(mesh):
    placed = (
        P(("groups", "subtree"), None),
        P("subtree", None, None),
        P("subtree", None, None),
        P("subtree", None, None, None),
        P("subtree", None, None, None),
        P(("groups", "subtree"), None),
        P(("groups", "subtree"), None),
        P(("groups", "subtree"), None),
        P(("groups", "subtree"), None),
    )
    return jax.shard_map(
        on_device,
        mesh=mesh,
        in_specs=placed,
        out_specs=P(("groups", "subtree"), None),
        check_vma=False,
    )
```

```python
import functools

import jax
import jax.numpy as jnp
import ml_dtypes
import numpy as np
from jax import lax
from jax.experimental import pallas as pl
from jax.experimental.pallas import tpu as pltpu
from jax.sharding import PartitionSpec as P

COULOMB_SCALE = 0.15
SOFTENING = 0.25
BF = jnp.bfloat16
F32 = jnp.float32
MIB = 1 << 20


def near_tables(leaf_len):
    cells = np.arange(leaf_len)
    along = (cells // 64).astype(np.float32)
    across = (cells // 8 % 8).astype(np.float32)
    height = (cells % 8).astype(np.float32)
    extent = leaf_len // 64
    tables = []
    for offset in (-1, 0, 1):
        delta_x = along[:, None] - along[None, :] - np.float32(offset * extent)
        delta_y = across[:, None] - across[None, :]
        delta_z = height[:, None] - height[None, :]
        square = delta_x * delta_x + delta_y * delta_y + delta_z * delta_z
        value = np.float32(COULOMB_SCALE) / np.sqrt(square + np.float32(SOFTENING))
        tables.append(value.astype(ml_dtypes.bfloat16))
    return np.concatenate(tables, axis=1)


def send(block, target):
    count = lax.axis_size("subtree")
    return lax.ppermute(block, "subtree", [(d, target(d)) for d in range(count)])


def over_core(block):
    return send(block, lambda d: d ^ 1)


def over_x(block):
    return send(block, lambda d: d ^ 2)


def over_y(block):
    return send(block, lambda d: d ^ 4)


def onward(block):
    return send(block, lambda d: d ^ (2 if d % 2 else 4))


def along_z(block, step):
    layers = lax.axis_size("subtree") // 8
    return send(block, lambda d: (d // 8 + step) % layers * 8 + d % 8)


def params(mib):
    return pltpu.CompilerParams(vmem_limit_bytes=mib * MIB)


def cost(flops, moved):
    return pl.CostEstimate(flops=flops // 64, bytes_accessed=moved // 64, transcendentals=0)


def whole():
    return pl.BlockSpec(memory_space=pltpu.VMEM)


def scalars():
    return pl.BlockSpec(memory_space=pltpu.SMEM)


def dot(a, b):
    return jnp.dot(a, b, preferred_element_type=F32)


def in_hbm(*arrays):
    return [pltpu.with_memory_space_constraint(array, pltpu.HBM) for array in arrays]


def one_hot_leaf(row, leaf_len):
    column = jnp.broadcast_to(row, (128, leaf_len)).astype(jnp.int16).T
    lanes = lax.broadcasted_iota(jnp.int32, (leaf_len, 128), 1)
    one, zero = jnp.ones((), BF), jnp.zeros((), BF)
    return jnp.concatenate(
        [
            jnp.where(column == (lanes + 128 * t).astype(jnp.int16), one, zero)
            for t in range(leaf_len // 128)
        ],
        axis=1,
    )


def one_hot_grid(row, leaf_len):
    cells = lax.broadcasted_iota(jnp.int32, (16, leaf_len), 0).astype(jnp.int16)
    wide = jnp.broadcast_to(row, (16, leaf_len)).astype(jnp.int16)
    one, zero = jnp.ones((), BF), jnp.zeros((), BF)
    return jnp.concatenate(
        [jnp.where(cells + jnp.int16(t) == wide, one, zero) for t in range(0, leaf_len, 16)], axis=0
    )


def owner_tables(me, layers, owners, blocks):
    leaves, entries = owners.shape
    slots = layers * 4
    rows = leaves + 1
    shape = (rows, 2 * slots)
    lane = lax.broadcasted_iota(jnp.int32, shape, 1)
    plane = (lane >= slots).astype(jnp.int32)
    slot = lane - plane * slots
    layer, chip, core = me // 8, (me // 2) & 3, me & 1
    turn = slot >> 2
    shift = jnp.where(turn < 2, turn, jnp.where(turn == 2, layers - 1, turn - 1))
    source = layer - shift
    source = jnp.where(source < 0, source + layers, source)
    owner = source * 8 + (chip ^ (slot & 3)) * 2 + (core ^ plane)
    row = lax.broadcasted_iota(jnp.int32, shape, 0)
    distant = jnp.abs(owner - me) >= 2
    entry = jnp.where((row == 0) & distant, owner, -1)
    block = jnp.zeros(shape, jnp.int32)
    pad = jnp.full((1, entries), -1, jnp.int32)
    named = jnp.concatenate([pad, owners], axis=0)
    chosen = jnp.concatenate([pad, blocks], axis=0)
    for k in range(entries):
        match = named[:, k:k + 1] == owner
        entry = jnp.where(match, k, entry)
        block = jnp.where(match, chosen[:, k:k + 1] + 1, block)
    return entry, block


def skeleton_kernel(per, layers, me_ref, order_ref, comp_ref, basis_ref, transfer_ref,
                    owner_ref, leaf_ref, ordered_ref, shared_ref, cross_ref, inner_ref,
                    entry_ref, block_ref, root_ref):
    step = pl.program_id(0)
    leaf_len = basis_ref.shape[2]

    @pl.when(step == 0)
    def _():
        root_ref[...] = jnp.zeros_like(root_ref)
        entry, block = owner_tables(me_ref[0], layers, owner_ref[...], leaf_ref[...])
        rows, lanes = entry.shape
        entry_ref[:rows, :lanes] = entry
        block_ref[:rows, :lanes] = block

    hots = [one_hot_leaf(order_ref[pl.ds(step * per + i, 1), :], leaf_len) for i in range(per)]
    ordered = [
        dot(hots[i], comp_ref[i * leaf_len:(i + 1) * leaf_len, :]).astype(BF) for i in range(per)
    ]
    skeletons = [dot(basis_ref[i], ordered[i]).astype(BF) for i in range(per)]
    across = jnp.concatenate([transfer_ref[i] for i in range(per)], axis=1)
    root_ref[...] += dot(across, jnp.concatenate(skeletons, axis=0))
    for i in range(per):
        at = pl.multiple_of((step * per + i) * leaf_len, leaf_len)
        ordered_ref[pl.ds(at, leaf_len), :] = ordered[i]
        shared_ref[pl.ds(step * per + i + 1, 1)] = skeletons[i][None]

    even = me_ref[0] % 2 == 0

    @pl.when((step == 0) & even)
    def _():
        cross_ref[...] = ordered[0]

    @pl.when((step == 0) & ~even)
    def _():
        inner_ref[...] = ordered[0]

    last = step == pl.num_programs(0) - 1

    @pl.when(last & even)
    def _():
        inner_ref[...] = ordered[-1]

    @pl.when(last & ~even)
    def _():
        cross_ref[...] = ordered[-1]

    @pl.when(last)
    def _():
        shared_ref[pl.ds(0, 1)] = root_ref[...].astype(BF)[None]


def skeletons_of(me, leaf_order, composition, leaf_basis, transfer, owners, blocks, layers, per=6):
    leaves, rank, leaf_len = leaf_basis.shape
    fields = composition.shape[1]
    entries = owners.shape[1]
    edge = jax.ShapeDtypeStruct((leaf_len, fields), BF)
    return pl.pallas_call(
        functools.partial(skeleton_kernel, per, layers),
        name="order_and_skeleton",
        grid=(leaves // per,),
        in_specs=[
            scalars(),
            pl.BlockSpec((leaves, leaf_len), lambda s: (0, 0)),
            pl.BlockSpec((per * leaf_len, fields), lambda s: (s, 0)),
            pl.BlockSpec((per, rank, leaf_len), lambda s: (s, 0, 0)),
            pl.BlockSpec((per, rank, rank), lambda s: (s, 0, 0)),
            pl.BlockSpec((leaves, entries), lambda s: (0, 0)),
            pl.BlockSpec((leaves, entries), lambda s: (0, 0)),
        ],
        out_specs=[whole()] * 6,
        out_shape=[
            jax.ShapeDtypeStruct((leaves * leaf_len, fields), BF),
            jax.ShapeDtypeStruct((leaves + 1, rank, fields), BF),
            edge,
            edge,
            jax.ShapeDtypeStruct((16, 128), jnp.int32),
            jax.ShapeDtypeStruct((16, 128), jnp.int32),
        ],
        scratch_shapes=[pltpu.VMEM((rank, fields), F32)],
        compiler_params=params(16),
        cost_estimate=cost(leaves * leaf_len * leaf_len * fields * 2, 4 * MIB),
    )(me, *in_hbm(leaf_order, composition, leaf_basis, transfer, owners, blocks))


def join_kernel(*refs):
    out = refs[-1]
    at = 0
    for ref in refs[:-1]:
        out[at:at + ref.shape[0]] = ref[...]
        at += ref.shape[0]


def join(parts):
    if len(parts) == 1:
        return parts[0]
    shape = (sum(part.shape[0] for part in parts),) + parts[0].shape[1:]
    return pl.pallas_call(
        join_kernel,
        name="join",
        in_specs=[whole()] * len(parts),
        out_specs=whole(),
        out_shape=jax.ShapeDtypeStruct(shape, BF),
        compiler_params=params(8 if shape[0] <= 32 else 32),
        cost_estimate=cost(0, MIB // 2),
    )(*parts)


def choose_kernel(me_ref, x_ref, y_ref, out_ref):
    @pl.when(me_ref[0] % 2 == 0)
    def _():
        out_ref[...] = x_ref[...]

    @pl.when(me_ref[0] % 2 == 1)
    def _():
        out_ref[...] = y_ref[...]


def choose(me, from_x, from_y):
    return pl.pallas_call(
        choose_kernel,
        name="choose",
        in_specs=[scalars(), whole(), whole()],
        out_specs=whole(),
        out_shape=jax.ShapeDtypeStruct(from_x.shape, BF),
        compiler_params=params(8),
        cost_estimate=cost(0, MIB // 4),
    )(me, from_x, from_y)


def dense_kernel(per, slots, entry_ref, block_ref, inner_ref, coupling_ref, top_ref,
                 transfer_ref, own_ref, other_ref, turned_ref):
    step = pl.program_id(0)
    rank = coupling_ref.shape[2]
    fields = inner_ref.shape[1]
    leaves = own_ref.shape[0] - 1
    for i in range(per):
        turned_ref[step * per + i] = transfer_ref[i].T

    def fill(out_ref, plane, row, entry_row, block_of):
        for slot in range(0, slots, 2):
            pair = []
            for one in (slot, slot + 1):
                entry = entry_ref[entry_row, plane * slots + one]
                block = block_of(jnp.maximum(entry, 0))
                pair.append(jnp.where(entry >= 0, block, jnp.zeros_like(block)))
            out_ref[row, :, slot * rank:(slot + 2) * rank] = jnp.concatenate(pair, axis=1)

    for plane, out_ref in ((0, own_ref), (1, other_ref)):
        for i in range(per):
            leaf = step * per + i
            fill(out_ref, plane, leaf, leaf + 1, lambda entry, i=i: coupling_ref[i, entry])

        @pl.when(step == pl.num_programs(0) - 1)
        def _(plane=plane, out_ref=out_ref):
            fill(out_ref, plane, leaves, 0, lambda entry: top_ref[0, entry])

    @pl.when(step == 0)
    def _():
        for t in range(inner_ref.shape[0] // rank):
            part = inner_ref[t * rank:(t + 1) * rank, :]
            other_ref[leaves + 1, :, t * fields:(t + 1) * fields] = part
        other_ref[leaves + 2] = jnp.zeros(other_ref.shape[1:], BF)
        blocks = block_ref[...].astype(F32).astype(BF)
        other_ref[leaves + 2, :blocks.shape[0], :blocks.shape[1]] = blocks


def dense_couplings(entry, block, inner, coupling, top_coupling, transfer, slots, per=6):
    leaves, entries, rank, _ = coupling.shape
    own = (leaves + 1, rank, slots * rank)
    other = (leaves + 3, rank, slots * rank)
    return pl.pallas_call(
        functools.partial(dense_kernel, per, slots),
        name="couplings_by_owner",
        grid=(leaves // per,),
        in_specs=[
            scalars(),
            pl.BlockSpec(block.shape, lambda s: (0, 0)),
            pl.BlockSpec(inner.shape, lambda s: (0, 0)),
            pl.BlockSpec((per, entries, rank, rank), lambda s: (s, 0, 0, 0)),
            pl.BlockSpec(top_coupling.shape, lambda s: (0, 0, 0, 0)),
            pl.BlockSpec((per, rank, rank), lambda s: (s, 0, 0)),
        ],
        out_specs=[whole()] * 3,
        out_shape=[
            jax.ShapeDtypeStruct(own, BF),
            jax.ShapeDtypeStruct(other, BF),
            jax.ShapeDtypeStruct(transfer.shape, BF),
        ],
        compiler_params=params(16 if slots <= 16 else 48),
        cost_estimate=cost(0, 8 * MIB),
    )(entry, block, inner, *in_hbm(coupling, top_coupling, transfer))


def round_kernel(plane, steps, slots, counts, at_ref, *refs):
    sides = []
    for number in counts:
        sides.append(refs[:number])
        refs = refs[number:]
    blocks_ref, out = refs[0], refs[-1]
    rows, rank, _ = out.shape
    low, high = steps[0] * 4 * rank, (steps[-1] + 1) * 4 * rank

    def block_at(side, base, index):
        for ref in side:
            if base < ref.shape[0]:
                return ref[base + index]
            base -= ref.shape[0]

    for row in range(rows):
        chosen = [
            block_at(side, place * rows, at_ref[(row + 1) % rows, plane * slots + step * 4 + q])
            for place, step in enumerate(steps)
            for q, side in enumerate(sides)
        ]
        value = dot(blocks_ref[row, :, low:high], jnp.concatenate(chosen, axis=0))
        if len(refs) > 2:
            value = value + refs[1][row]
        out[row] = value


def far_round(plane, steps, slots, at, parts, blocks, total=None):
    rank, fields = parts[0][0].shape[1:]
    rows = parts[0][0].shape[0] // (1 if len(parts[0]) > 1 else len(steps))
    args = [part for side in parts for part in side] + [blocks] + ([] if total is None else [total])
    return pl.pallas_call(
        functools.partial(round_kernel, plane, steps, slots, [len(side) for side in parts]),
        name="far_" + str(plane) + "_" + str(steps[0]),
        in_specs=[scalars()] + [whole()] * len(args),
        out_specs=whole(),
        out_shape=jax.ShapeDtypeStruct((rows, rank, fields), F32),
        compiler_params=params(16 if slots <= 16 else 48),
        cost_estimate=cost(rows * rank * 4 * rank * fields * 2 * len(steps), MIB),
    )(at, *args)


def table_kernel(row, blocks_ref, at_ref):
    rows, lanes = at_ref.shape
    at_ref[...] = blocks_ref[row, :rows, :lanes].astype(F32).astype(jnp.int32)


def table_of(other_blocks):
    return pl.pallas_call(
        functools.partial(table_kernel, other_blocks.shape[0] - 1),
        name="table",
        in_specs=[whole()],
        out_specs=whole(),
        out_shape=jax.ShapeDtypeStruct((16, 128), jnp.int32),
        compiler_params=params(16),
        cost_estimate=cost(0, MIB // 16),
    )(other_blocks)


def near_kernel(edges, pairs, mask_ref, order_ref, table_ref, basis_ref, ordered_ref, *refs):
    if edges:
        me_ref, cross_ref, inner_ref = refs[:3]
        even = me_ref[0] % 2 == 0
    near_ref, turned_ref = refs[-2:]
    leaves, _, leaf_len = basis_ref.shape
    fields = ordered_ref.shape[1]
    if edges:
        rank = basis_ref.shape[1]
        inner = jnp.concatenate(
            [
                inner_ref[leaves + 1, :, t * fields:(t + 1) * fields]
                for t in range(leaf_len // rank)
            ],
            axis=0,
        )

    def leaf_at(leaf):
        if leaf < 0:
            return jnp.where(even, cross_ref[...], inner)
        if leaf >= leaves:
            return jnp.where(even, inner, cross_ref[...])
        return ordered_ref[leaf * leaf_len:(leaf + 1) * leaf_len, :]

    def masked(leaf, side):
        value = leaf_at(leaf - 1 + 2 * side)
        return jnp.where(mask_ref[side, leaf] > 0, value, jnp.zeros_like(value))

    for pair in pairs:
        columns = [
            jnp.concatenate([masked(leaf, 0), leaf_at(leaf), masked(leaf, 1)], axis=0)
            for leaf in (2 * pair, 2 * pair + 1)
        ]
        near = dot(table_ref[...], jnp.concatenate(columns, axis=1)).astype(BF)
        turned = []
        for i in range(2):
            leaf = 2 * pair + i
            hot = one_hot_grid(order_ref[leaf:leaf + 1, :], leaf_len)
            both = jnp.concatenate([near[:, i * fields:(i + 1) * fields], basis_ref[leaf].T], axis=1)
            moved = dot(hot, both).astype(BF)
            near_ref[leaf * leaf_len:(leaf + 1) * leaf_len, :] = moved[:, :fields]
            turned.append(moved[:, fields:])
        turned_ref[pair * leaf_len:(pair + 1) * leaf_len, :] = jnp.concatenate(turned, axis=1)


def near_field(pairs, near_list, leaf_order, tables, basis, ordered, halos=None, filled=None):
    leaves, rank, leaf_len = basis.shape
    fields = ordered.shape[1]
    args = [near_list.T, leaf_order, tables, basis, ordered]
    in_specs = [scalars()] + [whole()] * 4
    out_shape = [
        jax.ShapeDtypeStruct((leaves * leaf_len, fields), BF),
        jax.ShapeDtypeStruct((leaves // 2 * leaf_len, 2 * rank), BF),
    ]
    aliases = {}
    if halos is not None:
        in_specs += [scalars(), whole(), whole()]
        args += list(halos)
    if filled is not None:
        aliases = {len(args): 0, len(args) + 1: 1}
        in_specs += [whole()] * 2
        args += list(filled)
    return pl.pallas_call(
        functools.partial(near_kernel, halos is not None, tuple(pairs)),
        name="near_" + str(pairs[0]),
        in_specs=in_specs,
        out_specs=[whole()] * len(out_shape),
        out_shape=out_shape,
        input_output_aliases=aliases,
        compiler_params=params(16),
        cost_estimate=cost(len(pairs) * 2 * leaf_len * leaf_len * fields * 10, len(pairs) * MIB),
    )(*args)


def field_kernel(per, own_ref, other_ref, turned_transfer_ref, near_ref, turned_ref, out_ref):
    step = pl.program_id(0)
    leaf_len = out_ref.shape[0] // per
    root = own_ref.shape[0] - 1
    local = own_ref[root] + other_ref[root]
    coarse = local.astype(BF)
    fine = (local - coarse.astype(F32)).astype(BF)
    both = jnp.concatenate([coarse, fine], axis=1)
    fields = local.shape[1]
    for pair in range(per // 2):
        values = []
        for i in range(2):
            leaf = step * per + 2 * pair + i
            down = dot(turned_transfer_ref[leaf], both)
            value = own_ref[leaf] + other_ref[leaf] + (down[:, :fields] + down[:, fields:])
            values.append(value.astype(BF))
        zero = jnp.zeros_like(values[0])
        corner = jnp.concatenate(
            [
                jnp.concatenate([values[0], zero], axis=1),
                jnp.concatenate([zero, values[1]], axis=1),
            ],
            axis=0,
        )
        at = pl.multiple_of((step * (per // 2) + pair) * leaf_len, leaf_len)
        far = dot(turned_ref[pl.ds(at, leaf_len), :], corner)
        for i in range(2):
            near = near_ref[pl.ds(2 * at + i * leaf_len, leaf_len), :].astype(F32)
            rows = slice((2 * pair + i) * leaf_len, (2 * pair + i + 1) * leaf_len)
            out_ref[rows, :] = (near + far[:, i * fields:(i + 1) * fields]).astype(BF)


def field(own, other, turned_transfer, near, turned, per=6):
    leaves, rank, _ = turned_transfer.shape
    fields = near.shape[1]
    leaf_len = near.shape[0] // leaves
    return pl.pallas_call(
        functools.partial(field_kernel, per),
        name="local_and_field",
        grid=(leaves // per,),
        in_specs=[whole()] * 5,
        out_specs=pl.BlockSpec((per * leaf_len, fields), lambda s: (s, 0)),
        out_shape=jax.ShapeDtypeStruct(near.shape, BF),
        compiler_params=params(16),
        cost_estimate=cost(leaves * leaf_len * rank * fields * 2, 4 * MIB),
    )(own, other, turned_transfer, near, turned)


def after(block, *others):
    return lax.optimization_barrier((block,) + others)[0]


def on_device(
    composition,
    leaf_basis,
    transfer,
    coupling,
    top_coupling,
    admissible_owner,
    admissible_leaf,
    near_list,
    leaf_order,
):
    leaves, rank, leaf_len = leaf_basis.shape
    count = lax.axis_size("subtree")
    layers = count // 8
    slots = layers * 4
    pairs = leaves // 2
    cut = pairs // 2
    me = lax.axis_index("subtree").reshape(1)

    ordered, shared, cross, inner, entry, own_at = skeletons_of(
        me, leaf_order, composition, leaf_basis, transfer, admissible_owner, admissible_leaf, layers
    )
    tables = jnp.asarray(near_tables(leaf_len))
    near_args = (near_list, leaf_order, tables, leaf_basis)

    line = along_z(shared, 1)
    from_x, from_y = over_x(shared), over_y(shared)
    filled = near_field(list(range(1, cut)), *near_args, ordered)
    line = after(line, filled[0])
    lines = [along_z(shared, layers - 1)]
    for _ in range(layers - 3):
        lines.append(along_z(line if len(lines) == 1 else lines[-1], 1))
    ready = after(line, from_x, from_y)
    next_x, next_y = over_x(ready), over_y(ready)
    far = onward(choose(me, after(from_x, ready, lines[0]), from_y))
    own_blocks, my_other, turned_transfer = dense_couplings(
        after(entry, ready), own_at, inner, coupling, top_coupling, transfer, slots
    )

    joined = after(join([after(lines[0], my_other)] + lines[1:]), next_x, next_y)
    cross = lax.ppermute(
        after(cross, joined),
        "subtree",
        [(d, d + 1) for d in range(1, count - 1, 2)] + [(d, d - 1) for d in range(2, count, 2)],
    )
    last_x, last_y = over_x(joined), over_y(joined)
    chosen = choose(me, after(next_x, joined, far), next_y)
    next_far = onward(chosen)
    other_blocks = over_core(after(my_other, chosen))
    held = after(ordered, joined)
    filled = near_field(list(range(cut, pairs - 1)), *near_args, held, filled=filled)
    next_far = after(next_far, filled[0])
    last_far = [along_z(far, layers - 1)]
    for _ in range(layers - 3):
        last_far.append(along_z(next_far if len(last_far) == 1 else last_far[-1], 1))
    round_0 = ((shared, line), (from_x, next_x), (from_y, next_y), (far, next_far))
    steps = [0, 1]
    other_at = table_of(other_blocks)
    own = far_round(0, steps, slots, own_at, round_0, own_blocks)
    other = far_round(1, steps, slots, other_at, round_0, other_blocks)
    held = after(ordered, filled[0], last_far[0], own, other)
    filled = near_field(
        [0, pairs - 1], *near_args, held, halos=(me, cross, other_blocks), filled=filled
    )
    steps = list(range(2, layers))
    round_1 = ((joined,), (last_x,), (last_y,), (after(last_far[0], filled[0]), *last_far[1:]))
    other = far_round(1, steps, slots, other_at, round_1, other_blocks, other)
    own = far_round(0, steps, slots, own_at, round_1, own_blocks, own)
    return field(own, over_core(other), turned_transfer, *filled)


def solution(mesh):
    placed = (
        P(("groups", "subtree"), None),
        P("subtree", None, None),
        P("subtree", None, None),
        P("subtree", None, None, None),
        P("subtree", None, None, None),
        P(("groups", "subtree"), None),
        P(("groups", "subtree"), None),
        P(("groups", "subtree"), None),
        P(("groups", "subtree"), None),
    )
    return jax.shard_map(
        on_device,
        mesh=mesh,
        in_specs=placed,
        out_specs=P(("groups", "subtree"), None),
        check_vma=False,
    )
```

```python
import functools

import jax
import jax.numpy as jnp
import ml_dtypes
import numpy as np
from jax import lax
from jax.experimental import pallas as pl
from jax.experimental.pallas import tpu as pltpu
from jax.sharding import PartitionSpec as P

COULOMB_SCALE = 0.15
SOFTENING = 0.25
BF = jnp.bfloat16
F32 = jnp.float32
MIB = 1 << 20


def near_tables(leaf_len):
    cells = np.arange(leaf_len)
    along = (cells // 64).astype(np.float32)
    across = (cells // 8 % 8).astype(np.float32)
    height = (cells % 8).astype(np.float32)
    extent = leaf_len // 64
    tables = []
    for offset in (-1, 0, 1):
        delta_x = along[:, None] - along[None, :] - np.float32(offset * extent)
        delta_y = across[:, None] - across[None, :]
        delta_z = height[:, None] - height[None, :]
        square = delta_x * delta_x + delta_y * delta_y + delta_z * delta_z
        value = np.float32(COULOMB_SCALE) / np.sqrt(square + np.float32(SOFTENING))
        tables.append(value.astype(ml_dtypes.bfloat16))
    return np.concatenate(tables, axis=1)


def send(block, target):
    count = lax.axis_size("subtree")
    return lax.ppermute(block, "subtree", [(d, target(d)) for d in range(count)])


def over_core(block):
    return send(block, lambda d: d ^ 1)


def over_x(block):
    return send(block, lambda d: d ^ 2)


def over_y(block):
    return send(block, lambda d: d ^ 4)


def onward(block):
    return send(block, lambda d: d ^ (2 if d % 2 else 4))


def along_z(block, step):
    layers = lax.axis_size("subtree") // 8
    return send(block, lambda d: (d // 8 + step) % layers * 8 + d % 8)


def params(mib):
    return pltpu.CompilerParams(vmem_limit_bytes=mib * MIB)


def cost(flops, moved):
    return pl.CostEstimate(flops=flops // 64, bytes_accessed=moved // 64, transcendentals=0)


def whole():
    return pl.BlockSpec(memory_space=pltpu.VMEM)


def scalars():
    return pl.BlockSpec(memory_space=pltpu.SMEM)


def dot(a, b):
    return jnp.dot(a, b, preferred_element_type=F32)


def in_hbm(*arrays):
    return [pltpu.with_memory_space_constraint(array, pltpu.HBM) for array in arrays]


def one_hot_leaf(row, leaf_len):
    column = jnp.broadcast_to(row, (128, leaf_len)).astype(jnp.int16).T
    lanes = lax.broadcasted_iota(jnp.int32, (leaf_len, 128), 1)
    one, zero = jnp.ones((), BF), jnp.zeros((), BF)
    return jnp.concatenate(
        [
            jnp.where(column == (lanes + 128 * t).astype(jnp.int16), one, zero)
            for t in range(leaf_len // 128)
        ],
        axis=1,
    )


def one_hot_grid(row, leaf_len):
    cells = lax.broadcasted_iota(jnp.int32, (16, leaf_len), 0).astype(jnp.int16)
    wide = jnp.broadcast_to(row, (16, leaf_len)).astype(jnp.int16)
    one, zero = jnp.ones((), BF), jnp.zeros((), BF)
    return jnp.concatenate(
        [jnp.where(cells + jnp.int16(t) == wide, one, zero) for t in range(0, leaf_len, 16)], axis=0
    )


def owner_tables(me, layers, owners, blocks):
    leaves, entries = owners.shape
    slots = layers * 4
    rows = leaves + 1
    shape = (rows, 2 * slots)
    lane = lax.broadcasted_iota(jnp.int32, shape, 1)
    plane = (lane >= slots).astype(jnp.int32)
    slot = lane - plane * slots
    layer, chip, core = me // 8, (me // 2) & 3, me & 1
    turn = slot >> 2
    shift = jnp.where(turn < 2, turn, jnp.where(turn == 2, layers - 1, turn - 1))
    source = layer - shift
    source = jnp.where(source < 0, source + layers, source)
    owner = source * 8 + (chip ^ (slot & 3)) * 2 + (core ^ plane)
    row = lax.broadcasted_iota(jnp.int32, shape, 0)
    distant = jnp.abs(owner - me) >= 2
    entry = jnp.where((row == 0) & distant, owner, -1)
    block = jnp.zeros(shape, jnp.int32)
    pad = jnp.full((1, entries), -1, jnp.int32)
    named = jnp.concatenate([pad, owners], axis=0)
    chosen = jnp.concatenate([pad, blocks], axis=0)
    for k in range(entries):
        match = named[:, k:k + 1] == owner
        entry = jnp.where(match, k, entry)
        block = jnp.where(match, chosen[:, k:k + 1] + 1, block)
    return entry, block


def skeleton_kernel(per, layers, me_ref, order_ref, comp_ref, basis_ref, transfer_ref,
                    owner_ref, leaf_ref, ordered_ref, shared_ref, cross_ref, inner_ref,
                    entry_ref, block_ref, root_ref):
    step = pl.program_id(0)
    leaf_len = basis_ref.shape[2]

    @pl.when(step == 0)
    def _():
        root_ref[...] = jnp.zeros_like(root_ref)
        entry, block = owner_tables(me_ref[0], layers, owner_ref[...], leaf_ref[...])
        rows, lanes = entry.shape
        entry_ref[:rows, :lanes] = entry
        block_ref[:rows, :lanes] = block

    hots = [one_hot_leaf(order_ref[pl.ds(step * per + i, 1), :], leaf_len) for i in range(per)]
    ordered = [
        dot(hots[i], comp_ref[i * leaf_len:(i + 1) * leaf_len, :]).astype(BF) for i in range(per)
    ]
    skeletons = [dot(basis_ref[i], ordered[i]).astype(BF) for i in range(per)]
    across = jnp.concatenate([transfer_ref[i] for i in range(per)], axis=1)
    root_ref[...] += dot(across, jnp.concatenate(skeletons, axis=0))
    for i in range(per):
        at = pl.multiple_of((step * per + i) * leaf_len, leaf_len)
        ordered_ref[pl.ds(at, leaf_len), :] = ordered[i]
        shared_ref[pl.ds(step * per + i + 1, 1)] = skeletons[i][None]

    even = me_ref[0] % 2 == 0

    @pl.when((step == 0) & even)
    def _():
        cross_ref[...] = ordered[0]

    @pl.when((step == 0) & ~even)
    def _():
        inner_ref[...] = ordered[0]

    last = step == pl.num_programs(0) - 1

    @pl.when(last & even)
    def _():
        inner_ref[...] = ordered[-1]

    @pl.when(last & ~even)
    def _():
        cross_ref[...] = ordered[-1]

    @pl.when(last)
    def _():
        shared_ref[pl.ds(0, 1)] = root_ref[...].astype(BF)[None]


def skeletons_of(me, leaf_order, composition, leaf_basis, transfer, owners, blocks, layers, per=6):
    leaves, rank, leaf_len = leaf_basis.shape
    fields = composition.shape[1]
    entries = owners.shape[1]
    edge = jax.ShapeDtypeStruct((leaf_len, fields), BF)
    return pl.pallas_call(
        functools.partial(skeleton_kernel, per, layers),
        name="order_and_skeleton",
        grid=(leaves // per,),
        in_specs=[
            scalars(),
            pl.BlockSpec((leaves, leaf_len), lambda s: (0, 0)),
            pl.BlockSpec((per * leaf_len, fields), lambda s: (s, 0)),
            pl.BlockSpec((per, rank, leaf_len), lambda s: (s, 0, 0)),
            pl.BlockSpec((per, rank, rank), lambda s: (s, 0, 0)),
            pl.BlockSpec((leaves, entries), lambda s: (0, 0)),
            pl.BlockSpec((leaves, entries), lambda s: (0, 0)),
        ],
        out_specs=[whole()] * 6,
        out_shape=[
            jax.ShapeDtypeStruct((leaves * leaf_len, fields), BF),
            jax.ShapeDtypeStruct((leaves + 1, rank, fields), BF),
            edge,
            edge,
            jax.ShapeDtypeStruct((16, 128), jnp.int32),
            jax.ShapeDtypeStruct((16, 128), jnp.int32),
        ],
        scratch_shapes=[pltpu.VMEM((rank, fields), F32)],
        compiler_params=params(16),
        cost_estimate=cost(leaves * leaf_len * leaf_len * fields * 2, 4 * MIB),
    )(me, *in_hbm(leaf_order, composition, leaf_basis, transfer, owners, blocks))


def join_kernel(*refs):
    out = refs[-1]
    at = 0
    for ref in refs[:-1]:
        out[at:at + ref.shape[0]] = ref[...]
        at += ref.shape[0]


def join(parts):
    if len(parts) == 1:
        return parts[0]
    shape = (sum(part.shape[0] for part in parts),) + parts[0].shape[1:]
    return pl.pallas_call(
        join_kernel,
        name="join",
        in_specs=[whole()] * len(parts),
        out_specs=whole(),
        out_shape=jax.ShapeDtypeStruct(shape, BF),
        compiler_params=params(8 if shape[0] <= 32 else 32),
        cost_estimate=cost(0, MIB // 2),
    )(*parts)


def choose_kernel(me_ref, x_ref, y_ref, out_ref):
    @pl.when(me_ref[0] % 2 == 0)
    def _():
        out_ref[...] = x_ref[...]

    @pl.when(me_ref[0] % 2 == 1)
    def _():
        out_ref[...] = y_ref[...]


def choose(me, from_x, from_y):
    return pl.pallas_call(
        choose_kernel,
        name="choose",
        in_specs=[scalars(), whole(), whole()],
        out_specs=whole(),
        out_shape=jax.ShapeDtypeStruct(from_x.shape, BF),
        compiler_params=params(8),
        cost_estimate=cost(0, MIB // 4),
    )(me, from_x, from_y)


def dense_kernel(per, slots, entry_ref, block_ref, inner_ref, coupling_ref, top_ref,
                 transfer_ref, own_ref, other_ref, turned_ref):
    step = pl.program_id(0)
    rank = coupling_ref.shape[2]
    fields = inner_ref.shape[1]
    leaves = own_ref.shape[0] - 1
    for i in range(per):
        turned_ref[step * per + i] = transfer_ref[i].T

    def fill(out_ref, plane, row, entry_row, block_of):
        for slot in range(0, slots, 2):
            pair = []
            for one in (slot, slot + 1):
                entry = entry_ref[entry_row, plane * slots + one]
                block = block_of(jnp.maximum(entry, 0))
                pair.append(jnp.where(entry >= 0, block, jnp.zeros_like(block)))
            out_ref[row, :, slot * rank:(slot + 2) * rank] = jnp.concatenate(pair, axis=1)

    for plane, out_ref in ((0, own_ref), (1, other_ref)):
        for i in range(per):
            leaf = step * per + i
            fill(out_ref, plane, leaf, leaf + 1, lambda entry, i=i: coupling_ref[i, entry])

        @pl.when(step == pl.num_programs(0) - 1)
        def _(plane=plane, out_ref=out_ref):
            fill(out_ref, plane, leaves, 0, lambda entry: top_ref[0, entry])

    @pl.when(step == 0)
    def _():
        for t in range(inner_ref.shape[0] // rank):
            part = inner_ref[t * rank:(t + 1) * rank, :]
            other_ref[leaves + 1, :, t * fields:(t + 1) * fields] = part
        other_ref[leaves + 2] = jnp.zeros(other_ref.shape[1:], BF)
        blocks = block_ref[...].astype(F32).astype(BF)
        other_ref[leaves + 2, :blocks.shape[0], :blocks.shape[1]] = blocks


def dense_couplings(entry, block, inner, coupling, top_coupling, transfer, slots, per=6):
    leaves, entries, rank, _ = coupling.shape
    own = (leaves + 1, rank, slots * rank)
    other = (leaves + 3, rank, slots * rank)
    return pl.pallas_call(
        functools.partial(dense_kernel, per, slots),
        name="couplings_by_owner",
        grid=(leaves // per,),
        in_specs=[
            scalars(),
            pl.BlockSpec(block.shape, lambda s: (0, 0)),
            pl.BlockSpec(inner.shape, lambda s: (0, 0)),
            pl.BlockSpec((per, entries, rank, rank), lambda s: (s, 0, 0, 0)),
            pl.BlockSpec(top_coupling.shape, lambda s: (0, 0, 0, 0)),
            pl.BlockSpec((per, rank, rank), lambda s: (s, 0, 0)),
        ],
        out_specs=[whole()] * 3,
        out_shape=[
            jax.ShapeDtypeStruct(own, BF),
            jax.ShapeDtypeStruct(other, BF),
            jax.ShapeDtypeStruct(transfer.shape, BF),
        ],
        compiler_params=params(16 if slots <= 16 else 48),
        cost_estimate=cost(0, 8 * MIB),
    )(entry, block, inner, *in_hbm(coupling, top_coupling, transfer))


def round_kernel(planes, steps, slots, counts, *refs):
    number = len(planes)
    tables, refs = refs[:number], refs[number:]
    sides = []
    for length in counts:
        sides.append(refs[:length])
        refs = refs[length:]
    blocks, totals, outs = refs[:number], refs[number:-number], refs[-number:]
    rows, rank, _ = outs[0].shape
    low, high = steps[0] * 4 * rank, (steps[-1] + 1) * 4 * rank

    def block_at(side, base, index):
        for ref in side:
            if base < ref.shape[0]:
                return ref[base + index]
            base -= ref.shape[0]

    for place, plane in enumerate(planes):
        for row in range(rows):
            chosen = [
                block_at(
                    side, at * rows, tables[place][(row + 1) % rows, plane * slots + step * 4 + q]
                )
                for at, step in enumerate(steps)
                for q, side in enumerate(sides)
            ]
            value = dot(blocks[place][row, :, low:high], jnp.concatenate(chosen, axis=0))
            if totals:
                value = value + totals[place][row]
            outs[place][row] = value


def far_rounds(planes, steps, slots, tables, parts, blocks, totals=()):
    rank, fields = parts[0][0].shape[1:]
    rows = parts[0][0].shape[0] // (1 if len(parts[0]) > 1 else len(steps))
    args = [part for side in parts for part in side] + list(blocks) + list(totals)
    shape = jax.ShapeDtypeStruct((rows, rank, fields), F32)
    return pl.pallas_call(
        functools.partial(round_kernel, planes, steps, slots, [len(side) for side in parts]),
        name="far_" + str(planes[-1]) + "_" + str(steps[0]),
        in_specs=[scalars()] * len(planes) + [whole()] * len(args),
        out_specs=[whole()] * len(planes),
        out_shape=[shape] * len(planes),
        compiler_params=params(16 if slots <= 16 else 48),
        cost_estimate=cost(rows * rank * 4 * rank * fields * 2 * len(steps), MIB),
    )(*tables, *args)


def near_kernel(edges, pairs, mask_ref, order_ref, table_ref, basis_ref, ordered_ref, *refs):
    if edges:
        me_ref, cross_ref, inner_ref = refs[:3]
        near_ref, turned_ref, at_ref = refs[-3:]
        even = me_ref[0] % 2 == 0
    else:
        near_ref, turned_ref = refs[-2:]
    leaves, _, leaf_len = basis_ref.shape
    fields = ordered_ref.shape[1]
    if edges:
        rows, rank = at_ref.shape[0], basis_ref.shape[1]
        blocks = inner_ref[leaves + 2, :rows, :at_ref.shape[1]]
        at_ref[...] = blocks.astype(F32).astype(jnp.int32)
        inner = jnp.concatenate(
            [
                inner_ref[leaves + 1, :, t * fields:(t + 1) * fields]
                for t in range(leaf_len // rank)
            ],
            axis=0,
        )

    def leaf_at(leaf):
        if leaf < 0:
            return jnp.where(even, cross_ref[...], inner)
        if leaf >= leaves:
            return jnp.where(even, inner, cross_ref[...])
        return ordered_ref[leaf * leaf_len:(leaf + 1) * leaf_len, :]

    def masked(leaf, side):
        value = leaf_at(leaf - 1 + 2 * side)
        return jnp.where(mask_ref[side, leaf] > 0, value, jnp.zeros_like(value))

    for pair in pairs:
        columns = [
            jnp.concatenate([masked(leaf, 0), leaf_at(leaf), masked(leaf, 1)], axis=0)
            for leaf in (2 * pair, 2 * pair + 1)
        ]
        near = dot(table_ref[...], jnp.concatenate(columns, axis=1)).astype(BF)
        turned = []
        for i in range(2):
            leaf = 2 * pair + i
            hot = one_hot_grid(order_ref[leaf:leaf + 1, :], leaf_len)
            both = jnp.concatenate([near[:, i * fields:(i + 1) * fields], basis_ref[leaf].T], axis=1)
            moved = dot(hot, both).astype(BF)
            near_ref[leaf * leaf_len:(leaf + 1) * leaf_len, :] = moved[:, :fields]
            turned.append(moved[:, fields:])
        turned_ref[pair * leaf_len:(pair + 1) * leaf_len, :] = jnp.concatenate(turned, axis=1)


def near_field(pairs, near_list, leaf_order, tables, basis, ordered, halos=None, filled=None):
    leaves, rank, leaf_len = basis.shape
    fields = ordered.shape[1]
    args = [near_list.T, leaf_order, tables, basis, ordered]
    in_specs = [scalars()] + [whole()] * 4
    out_shape = [
        jax.ShapeDtypeStruct((leaves * leaf_len, fields), BF),
        jax.ShapeDtypeStruct((leaves // 2 * leaf_len, 2 * rank), BF),
    ]
    aliases = {}
    if halos is not None:
        in_specs += [scalars(), whole(), whole()]
        args += list(halos)
        out_shape.append(jax.ShapeDtypeStruct((16, 128), jnp.int32))
    if filled is not None:
        aliases = {len(args): 0, len(args) + 1: 1}
        in_specs += [whole()] * 2
        args += list(filled)
    return pl.pallas_call(
        functools.partial(near_kernel, halos is not None, tuple(pairs)),
        name="near_" + str(pairs[0]),
        in_specs=in_specs,
        out_specs=[whole()] * len(out_shape),
        out_shape=out_shape,
        input_output_aliases=aliases,
        compiler_params=params(16),
        cost_estimate=cost(len(pairs) * 2 * leaf_len * leaf_len * fields * 10, len(pairs) * MIB),
    )(*args)


def field_kernel(per, own_ref, other_ref, turned_transfer_ref, near_ref, turned_ref, out_ref):
    step = pl.program_id(0)
    leaf_len = out_ref.shape[0] // per
    root = own_ref.shape[0] - 1
    local = own_ref[root] + other_ref[root]
    coarse = local.astype(BF)
    fine = (local - coarse.astype(F32)).astype(BF)
    both = jnp.concatenate([coarse, fine], axis=1)
    fields = local.shape[1]
    for pair in range(per // 2):
        values = []
        for i in range(2):
            leaf = step * per + 2 * pair + i
            down = dot(turned_transfer_ref[leaf], both)
            value = own_ref[leaf] + other_ref[leaf] + (down[:, :fields] + down[:, fields:])
            values.append(value.astype(BF))
        zero = jnp.zeros_like(values[0])
        corner = jnp.concatenate(
            [
                jnp.concatenate([values[0], zero], axis=1),
                jnp.concatenate([zero, values[1]], axis=1),
            ],
            axis=0,
        )
        at = pl.multiple_of((step * (per // 2) + pair) * leaf_len, leaf_len)
        far = dot(turned_ref[pl.ds(at, leaf_len), :], corner)
        for i in range(2):
            near = near_ref[pl.ds(2 * at + i * leaf_len, leaf_len), :].astype(F32)
            rows = slice((2 * pair + i) * leaf_len, (2 * pair + i + 1) * leaf_len)
            out_ref[rows, :] = (near + far[:, i * fields:(i + 1) * fields]).astype(BF)


def field(own, other, turned_transfer, near, turned, per=6):
    leaves, rank, _ = turned_transfer.shape
    fields = near.shape[1]
    leaf_len = near.shape[0] // leaves
    return pl.pallas_call(
        functools.partial(field_kernel, per),
        name="local_and_field",
        grid=(leaves // per,),
        in_specs=[whole()] * 5,
        out_specs=pl.BlockSpec((per * leaf_len, fields), lambda s: (s, 0)),
        out_shape=jax.ShapeDtypeStruct(near.shape, BF),
        compiler_params=params(16),
        cost_estimate=cost(leaves * leaf_len * rank * fields * 2, 4 * MIB),
    )(own, other, turned_transfer, near, turned)


def after(block, *others):
    return lax.optimization_barrier((block,) + others)[0]


def on_device(
    composition,
    leaf_basis,
    transfer,
    coupling,
    top_coupling,
    admissible_owner,
    admissible_leaf,
    near_list,
    leaf_order,
):
    leaves, rank, leaf_len = leaf_basis.shape
    count = lax.axis_size("subtree")
    layers = count // 8
    slots = layers * 4
    pairs = leaves // 2
    cut = pairs // 2
    me = lax.axis_index("subtree").reshape(1)

    ordered, shared, cross, inner, entry, own_at = skeletons_of(
        me, leaf_order, composition, leaf_basis, transfer, admissible_owner, admissible_leaf, layers
    )
    tables = jnp.asarray(near_tables(leaf_len))
    near_args = (near_list, leaf_order, tables, leaf_basis)

    line = along_z(shared, 1)
    from_x, from_y = over_x(shared), over_y(shared)
    filled = near_field(list(range(1, cut)), *near_args, ordered)
    line = after(line, filled[0])
    lines = [along_z(shared, layers - 1)]
    for _ in range(layers - 3):
        lines.append(along_z(line if len(lines) == 1 else lines[-1], 1))
    ready = after(line, from_x, from_y)
    next_x, next_y = over_x(ready), over_y(ready)
    far = onward(choose(me, after(from_x, ready, lines[0]), from_y))
    cross = lax.ppermute(
        cross,
        "subtree",
        [(d, d + 1) for d in range(1, count - 1, 2)] + [(d, d - 1) for d in range(2, count, 2)],
    )
    own_blocks, my_other, turned_transfer = dense_couplings(
        after(entry, ready), own_at, inner, coupling, top_coupling, transfer, slots
    )

    joined = after(join([after(lines[0], my_other)] + lines[1:]), next_x, next_y, cross)
    last_x, last_y = over_x(joined), over_y(joined)
    chosen = choose(me, after(next_x, joined, far), next_y)
    next_far = onward(chosen)
    other_blocks = over_core(after(my_other, chosen))
    held = after(ordered, joined)
    filled = near_field(list(range(cut, pairs - 2)), *near_args, held, filled=filled)
    next_far = after(next_far, filled[0])
    last_far = [along_z(far, layers - 1)]
    for _ in range(layers - 3):
        last_far.append(along_z(next_far if len(last_far) == 1 else last_far[-1], 1))
    filled = near_field([pairs - 2], *near_args, ordered, filled=filled)
    held = after(ordered, filled[0])
    *filled, other_at = near_field(
        [0, pairs - 1], *near_args, held, halos=(me, cross, other_blocks), filled=filled
    )
    round_0 = ((shared, line), (from_x, next_x), (from_y, next_y), (far, next_far))
    own, other = far_rounds(
        (0, 1), [0, 1], slots, (own_at, other_at), round_0, (own_blocks, other_blocks)
    )
    steps = list(range(2, layers))
    round_1 = ((joined,), (last_x,), (last_y,), (after(last_far[0], own), *last_far[1:]))
    (other,) = far_rounds((1,), steps, slots, (other_at,), round_1, (other_blocks,), (other,))
    (own,) = far_rounds((0,), steps, slots, (own_at,), round_1, (own_blocks,), (own,))
    return field(own, over_core(other), turned_transfer, *filled)


def solution(mesh):
    placed = (
        P(("groups", "subtree"), None),
        P("subtree", None, None),
        P("subtree", None, None),
        P("subtree", None, None, None),
        P("subtree", None, None, None),
        P(("groups", "subtree"), None),
        P(("groups", "subtree"), None),
        P(("groups", "subtree"), None),
        P(("groups", "subtree"), None),
    )
    return jax.shard_map(
        on_device,
        mesh=mesh,
        in_specs=placed,
        out_specs=P(("groups", "subtree"), None),
        check_vma=False,
    )
```

```python
import functools

import jax
import jax.numpy as jnp
import ml_dtypes
import numpy as np
from jax import lax
from jax.experimental import pallas as pl
from jax.experimental.pallas import tpu as pltpu
from jax.sharding import PartitionSpec as P

COULOMB_SCALE = 0.15
SOFTENING = 0.25
BF = jnp.bfloat16
F32 = jnp.float32
MIB = 1 << 20


def near_tables(leaf_len):
    cells = np.arange(leaf_len)
    along = (cells // 64).astype(np.float32)
    across = (cells // 8 % 8).astype(np.float32)
    height = (cells % 8).astype(np.float32)
    extent = leaf_len // 64
    tables = []
    for offset in (-1, 0, 1):
        delta_x = along[:, None] - along[None, :] - np.float32(offset * extent)
        delta_y = across[:, None] - across[None, :]
        delta_z = height[:, None] - height[None, :]
        square = delta_x * delta_x + delta_y * delta_y + delta_z * delta_z
        value = np.float32(COULOMB_SCALE) / np.sqrt(square + np.float32(SOFTENING))
        tables.append(value.astype(ml_dtypes.bfloat16))
    return np.concatenate(tables, axis=1)


def send(block, target):
    count = lax.axis_size("subtree")
    return lax.ppermute(block, "subtree", [(d, target(d)) for d in range(count)])


def over_core(block):
    return send(block, lambda d: d ^ 1)


def over_x(block):
    return send(block, lambda d: d ^ 2)


def over_y(block):
    return send(block, lambda d: d ^ 4)


def onward(block):
    return send(block, lambda d: d ^ (2 if d % 2 else 4))


def along_z(block, step):
    layers = lax.axis_size("subtree") // 8
    return send(block, lambda d: (d // 8 + step) % layers * 8 + d % 8)


def params(mib):
    return pltpu.CompilerParams(vmem_limit_bytes=mib * MIB)


def cost(flops, moved):
    return pl.CostEstimate(flops=flops // 64, bytes_accessed=moved // 64, transcendentals=0)


def whole():
    return pl.BlockSpec(memory_space=pltpu.VMEM)


def scalars():
    return pl.BlockSpec(memory_space=pltpu.SMEM)


def dot(a, b):
    return jnp.dot(a, b, preferred_element_type=F32)


def in_hbm(*arrays):
    return [pltpu.with_memory_space_constraint(array, pltpu.HBM) for array in arrays]


def one_hot_leaf(row, leaf_len):
    column = jnp.broadcast_to(row, (128, leaf_len)).astype(jnp.int16).T
    lanes = lax.broadcasted_iota(jnp.int32, (leaf_len, 128), 1)
    one, zero = jnp.ones((), BF), jnp.zeros((), BF)
    return jnp.concatenate(
        [
            jnp.where(column == (lanes + 128 * t).astype(jnp.int16), one, zero)
            for t in range(leaf_len // 128)
        ],
        axis=1,
    )


def one_hot_grid(row, leaf_len):
    cells = lax.broadcasted_iota(jnp.int32, (16, leaf_len), 0).astype(jnp.int16)
    wide = jnp.broadcast_to(row, (16, leaf_len)).astype(jnp.int16)
    one, zero = jnp.ones((), BF), jnp.zeros((), BF)
    return jnp.concatenate(
        [jnp.where(cells + jnp.int16(t) == wide, one, zero) for t in range(0, leaf_len, 16)], axis=0
    )


def owner_tables(me, layers, owners, blocks):
    leaves, entries = owners.shape
    slots = layers * 4
    rows = leaves + 1
    shape = (rows, 2 * slots)
    lane = lax.broadcasted_iota(jnp.int32, shape, 1)
    plane = (lane >= slots).astype(jnp.int32)
    slot = lane - plane * slots
    layer, chip, core = me // 8, (me // 2) & 3, me & 1
    turn = slot >> 2
    shift = jnp.where(turn < 2, turn, jnp.where(turn == 2, layers - 1, turn - 1))
    source = layer - shift
    source = jnp.where(source < 0, source + layers, source)
    owner = source * 8 + (chip ^ (slot & 3)) * 2 + (core ^ plane)
    row = lax.broadcasted_iota(jnp.int32, shape, 0)
    distant = jnp.abs(owner - me) >= 2
    entry = jnp.where((row == 0) & distant, owner, -1)
    block = jnp.zeros(shape, jnp.int32)
    pad = jnp.full((1, entries), -1, jnp.int32)
    named = jnp.concatenate([pad, owners], axis=0)
    chosen = jnp.concatenate([pad, blocks], axis=0)
    for k in range(entries):
        match = named[:, k:k + 1] == owner
        entry = jnp.where(match, k, entry)
        block = jnp.where(match, chosen[:, k:k + 1] + 1, block)
    return entry, block


def skeleton_kernel(per, layers, me_ref, order_ref, comp_ref, basis_ref, transfer_ref,
                    owner_ref, leaf_ref, ordered_ref, shared_ref, cross_ref, inner_ref,
                    entry_ref, block_ref, root_ref):
    step = pl.program_id(0)
    leaf_len = basis_ref.shape[2]

    @pl.when(step == 0)
    def _():
        root_ref[...] = jnp.zeros_like(root_ref)
        entry, block = owner_tables(me_ref[0], layers, owner_ref[...], leaf_ref[...])
        rows, lanes = entry.shape
        entry_ref[:rows, :lanes] = entry
        block_ref[:rows, :lanes] = block

    hots = [one_hot_leaf(order_ref[pl.ds(step * per + i, 1), :], leaf_len) for i in range(per)]
    ordered = [
        dot(hots[i], comp_ref[i * leaf_len:(i + 1) * leaf_len, :]).astype(BF) for i in range(per)
    ]
    skeletons = [dot(basis_ref[i], ordered[i]).astype(BF) for i in range(per)]
    across = jnp.concatenate([transfer_ref[i] for i in range(per)], axis=1)
    root_ref[...] += dot(across, jnp.concatenate(skeletons, axis=0))
    for i in range(per):
        at = pl.multiple_of((step * per + i) * leaf_len, leaf_len)
        ordered_ref[pl.ds(at, leaf_len), :] = ordered[i]
        shared_ref[pl.ds(step * per + i + 1, 1)] = skeletons[i][None]

    even = me_ref[0] % 2 == 0

    @pl.when((step == 0) & even)
    def _():
        cross_ref[...] = ordered[0]

    @pl.when((step == 0) & ~even)
    def _():
        inner_ref[...] = ordered[0]

    last = step == pl.num_programs(0) - 1

    @pl.when(last & even)
    def _():
        inner_ref[...] = ordered[-1]

    @pl.when(last & ~even)
    def _():
        cross_ref[...] = ordered[-1]

    @pl.when(last)
    def _():
        shared_ref[pl.ds(0, 1)] = root_ref[...].astype(BF)[None]


def skeletons_of(me, leaf_order, composition, leaf_basis, transfer, owners, blocks, layers, per=6):
    leaves, rank, leaf_len = leaf_basis.shape
    fields = composition.shape[1]
    entries = owners.shape[1]
    edge = jax.ShapeDtypeStruct((leaf_len, fields), BF)
    return pl.pallas_call(
        functools.partial(skeleton_kernel, per, layers),
        name="order_and_skeleton",
        grid=(leaves // per,),
        in_specs=[
            scalars(),
            pl.BlockSpec((leaves, leaf_len), lambda s: (0, 0)),
            pl.BlockSpec((per * leaf_len, fields), lambda s: (s, 0)),
            pl.BlockSpec((per, rank, leaf_len), lambda s: (s, 0, 0)),
            pl.BlockSpec((per, rank, rank), lambda s: (s, 0, 0)),
            pl.BlockSpec((leaves, entries), lambda s: (0, 0)),
            pl.BlockSpec((leaves, entries), lambda s: (0, 0)),
        ],
        out_specs=[whole()] * 6,
        out_shape=[
            jax.ShapeDtypeStruct((leaves * leaf_len, fields), BF),
            jax.ShapeDtypeStruct((leaves + 1, rank, fields), BF),
            edge,
            edge,
            jax.ShapeDtypeStruct((16, 128), jnp.int32),
            jax.ShapeDtypeStruct((16, 128), jnp.int32),
        ],
        scratch_shapes=[pltpu.VMEM((rank, fields), F32)],
        compiler_params=params(16),
        cost_estimate=cost(leaves * leaf_len * leaf_len * fields * 2, 4 * MIB),
    )(me, *in_hbm(leaf_order, composition, leaf_basis, transfer, owners, blocks))


def join_kernel(*refs):
    out = refs[-1]
    at = 0
    for ref in refs[:-1]:
        out[at:at + ref.shape[0]] = ref[...]
        at += ref.shape[0]


def join(parts):
    if len(parts) == 1:
        return parts[0]
    shape = (sum(part.shape[0] for part in parts),) + parts[0].shape[1:]
    return pl.pallas_call(
        join_kernel,
        name="join",
        in_specs=[whole()] * len(parts),
        out_specs=whole(),
        out_shape=jax.ShapeDtypeStruct(shape, BF),
        compiler_params=params(8 if shape[0] <= 32 else 32),
        cost_estimate=cost(0, MIB // 2),
    )(*parts)


def choose_kernel(me_ref, x_ref, y_ref, out_ref):
    @pl.when(me_ref[0] % 2 == 0)
    def _():
        out_ref[...] = x_ref[...]

    @pl.when(me_ref[0] % 2 == 1)
    def _():
        out_ref[...] = y_ref[...]


def choose(me, from_x, from_y):
    return pl.pallas_call(
        choose_kernel,
        name="choose",
        in_specs=[scalars(), whole(), whole()],
        out_specs=whole(),
        out_shape=jax.ShapeDtypeStruct(from_x.shape, BF),
        compiler_params=params(8),
        cost_estimate=cost(0, MIB // 4),
    )(me, from_x, from_y)


def dense_kernel(per, slots, entry_ref, block_ref, inner_ref, coupling_ref, top_ref,
                 transfer_ref, own_ref, other_ref, turned_ref):
    step = pl.program_id(0)
    rank = coupling_ref.shape[2]
    fields = inner_ref.shape[1]
    leaves = own_ref.shape[0] - 1
    for i in range(per):
        turned_ref[step * per + i] = transfer_ref[i].T

    def fill(out_ref, plane, row, entry_row, block_of):
        for slot in range(0, slots, 2):
            pair = []
            for one in (slot, slot + 1):
                entry = entry_ref[entry_row, plane * slots + one]
                block = block_of(jnp.maximum(entry, 0))
                pair.append(jnp.where(entry >= 0, block, jnp.zeros_like(block)))
            out_ref[row, :, slot * rank:(slot + 2) * rank] = jnp.concatenate(pair, axis=1)

    for plane, out_ref in ((0, own_ref), (1, other_ref)):
        for i in range(per):
            leaf = step * per + i
            fill(out_ref, plane, leaf, leaf + 1, lambda entry, i=i: coupling_ref[i, entry])

        @pl.when(step == pl.num_programs(0) - 1)
        def _(plane=plane, out_ref=out_ref):
            fill(out_ref, plane, leaves, 0, lambda entry: top_ref[0, entry])

    @pl.when(step == 0)
    def _():
        for t in range(inner_ref.shape[0] // rank):
            part = inner_ref[t * rank:(t + 1) * rank, :]
            other_ref[leaves + 1, :, t * fields:(t + 1) * fields] = part
        other_ref[leaves + 2] = jnp.zeros(other_ref.shape[1:], BF)
        blocks = block_ref[...].astype(F32).astype(BF)
        other_ref[leaves + 2, :blocks.shape[0], :blocks.shape[1]] = blocks


def dense_couplings(entry, block, inner, coupling, top_coupling, transfer, slots, per=6):
    leaves, entries, rank, _ = coupling.shape
    own = (leaves + 1, rank, slots * rank)
    other = (leaves + 3, rank, slots * rank)
    return pl.pallas_call(
        functools.partial(dense_kernel, per, slots),
        name="couplings_by_owner",
        grid=(leaves // per,),
        in_specs=[
            scalars(),
            pl.BlockSpec(block.shape, lambda s: (0, 0)),
            pl.BlockSpec(inner.shape, lambda s: (0, 0)),
            pl.BlockSpec((per, entries, rank, rank), lambda s: (s, 0, 0, 0)),
            pl.BlockSpec(top_coupling.shape, lambda s: (0, 0, 0, 0)),
            pl.BlockSpec((per, rank, rank), lambda s: (s, 0, 0)),
        ],
        out_specs=[whole()] * 3,
        out_shape=[
            jax.ShapeDtypeStruct(own, BF),
            jax.ShapeDtypeStruct(other, BF),
            jax.ShapeDtypeStruct(transfer.shape, BF),
        ],
        compiler_params=params(16 if slots <= 16 else 48),
        cost_estimate=cost(0, 8 * MIB),
    )(entry, block, inner, *in_hbm(coupling, top_coupling, transfer))


def round_kernel(planes, steps, slots, counts, *refs):
    number = len(planes)
    tables, refs = refs[:number], refs[number:]
    sides = []
    for length in counts:
        sides.append(refs[:length])
        refs = refs[length:]
    blocks, totals, outs = refs[:number], refs[number:-number], refs[-number:]
    rows, rank, _ = outs[0].shape
    low, high = steps[0] * 4 * rank, (steps[-1] + 1) * 4 * rank

    def block_at(side, base, index):
        for ref in side:
            if base < ref.shape[0]:
                return ref[base + index]
            base -= ref.shape[0]

    for place, plane in enumerate(planes):
        for row in range(rows):
            chosen = [
                block_at(
                    side, at * rows, tables[place][(row + 1) % rows, plane * slots + step * 4 + q]
                )
                for at, step in enumerate(steps)
                for q, side in enumerate(sides)
            ]
            value = dot(blocks[place][row, :, low:high], jnp.concatenate(chosen, axis=0))
            if totals:
                value = value + totals[place][row]
            outs[place][row] = value


def far_rounds(planes, steps, slots, tables, parts, blocks, totals=()):
    rank, fields = parts[0][0].shape[1:]
    rows = parts[0][0].shape[0] // (1 if len(parts[0]) > 1 else len(steps))
    args = [part for side in parts for part in side] + list(blocks) + list(totals)
    shape = jax.ShapeDtypeStruct((rows, rank, fields), F32)
    return pl.pallas_call(
        functools.partial(round_kernel, planes, steps, slots, [len(side) for side in parts]),
        name="far_" + str(planes[-1]) + "_" + str(steps[0]),
        in_specs=[scalars()] * len(planes) + [whole()] * len(args),
        out_specs=[whole()] * len(planes),
        out_shape=[shape] * len(planes),
        compiler_params=params(16 if slots <= 16 else 48),
        cost_estimate=cost(rows * rank * 4 * rank * fields * 2 * len(steps), MIB),
    )(*tables, *args)


def near_kernel(edges, pairs, mask_ref, order_ref, table_ref, basis_ref, ordered_ref, *refs):
    if edges:
        me_ref, cross_ref, inner_ref = refs[:3]
        near_ref, turned_ref, at_ref = refs[-3:]
        even = me_ref[0] % 2 == 0
    else:
        near_ref, turned_ref = refs[-2:]
    leaves, _, leaf_len = basis_ref.shape
    fields = ordered_ref.shape[1]
    if edges:
        rows, rank = at_ref.shape[0], basis_ref.shape[1]
        blocks = inner_ref[leaves + 2, :rows, :at_ref.shape[1]]
        at_ref[...] = blocks.astype(F32).astype(jnp.int32)
        inner = jnp.concatenate(
            [
                inner_ref[leaves + 1, :, t * fields:(t + 1) * fields]
                for t in range(leaf_len // rank)
            ],
            axis=0,
        )

    def leaf_at(leaf):
        if leaf < 0:
            return jnp.where(even, cross_ref[...], inner)
        if leaf >= leaves:
            return jnp.where(even, inner, cross_ref[...])
        return ordered_ref[leaf * leaf_len:(leaf + 1) * leaf_len, :]

    def masked(leaf, side):
        value = leaf_at(leaf - 1 + 2 * side)
        return jnp.where(mask_ref[side, leaf] > 0, value, jnp.zeros_like(value))

    near_leaves = [leaf for pair in pairs for leaf in (2 * pair, 2 * pair + 1)]
    columns = [
        jnp.concatenate([masked(leaf, 0), leaf_at(leaf), masked(leaf, 1)], axis=0)
        for leaf in near_leaves
    ]
    near = dot(table_ref[...], jnp.concatenate(columns, axis=1)).astype(BF)
    moved = []
    for i, leaf in enumerate(near_leaves):
        hot = one_hot_grid(order_ref[leaf:leaf + 1, :], leaf_len)
        both = jnp.concatenate([near[:, i * fields:(i + 1) * fields], basis_ref[leaf].T], axis=1)
        moved.append(dot(hot, both).astype(BF))
        near_ref[leaf * leaf_len:(leaf + 1) * leaf_len, :] = moved[i][:, :fields]
    for i, pair in enumerate(pairs):
        turned = [part[:, fields:] for part in moved[2 * i:2 * i + 2]]
        turned_ref[pair * leaf_len:(pair + 1) * leaf_len, :] = jnp.concatenate(turned, axis=1)


def near_field(pairs, near_list, leaf_order, tables, basis, ordered, halos=None, filled=None):
    leaves, rank, leaf_len = basis.shape
    fields = ordered.shape[1]
    args = [near_list.T, leaf_order, tables, basis, ordered]
    in_specs = [scalars()] + [whole()] * 4
    out_shape = [
        jax.ShapeDtypeStruct((leaves * leaf_len, fields), BF),
        jax.ShapeDtypeStruct((leaves // 2 * leaf_len, 2 * rank), BF),
    ]
    aliases = {}
    if halos is not None:
        in_specs += [scalars(), whole(), whole()]
        args += list(halos)
        out_shape.append(jax.ShapeDtypeStruct((16, 128), jnp.int32))
    if filled is not None:
        aliases = {len(args): 0, len(args) + 1: 1}
        in_specs += [whole()] * 2
        args += list(filled)
    return pl.pallas_call(
        functools.partial(near_kernel, halos is not None, tuple(pairs)),
        name="near_" + str(pairs[0]),
        in_specs=in_specs,
        out_specs=[whole()] * len(out_shape),
        out_shape=out_shape,
        input_output_aliases=aliases,
        compiler_params=params(16),
        cost_estimate=cost(len(pairs) * 2 * leaf_len * leaf_len * fields * 10, len(pairs) * MIB),
    )(*args)


def field_kernel(per, own_ref, other_ref, turned_transfer_ref, near_ref, turned_ref, out_ref):
    step = pl.program_id(0)
    leaf_len = out_ref.shape[0] // per
    root = own_ref.shape[0] - 1
    local = own_ref[root] + other_ref[root]
    coarse = local.astype(BF)
    fine = (local - coarse.astype(F32)).astype(BF)
    both = jnp.concatenate([coarse, fine], axis=1)
    fields = local.shape[1]
    for pair in range(per // 2):
        values = []
        for i in range(2):
            leaf = step * per + 2 * pair + i
            down = dot(turned_transfer_ref[leaf], both)
            value = own_ref[leaf] + other_ref[leaf] + (down[:, :fields] + down[:, fields:])
            values.append(value.astype(BF))
        zero = jnp.zeros_like(values[0])
        corner = jnp.concatenate(
            [
                jnp.concatenate([values[0], zero], axis=1),
                jnp.concatenate([zero, values[1]], axis=1),
            ],
            axis=0,
        )
        at = pl.multiple_of((step * (per // 2) + pair) * leaf_len, leaf_len)
        far = dot(turned_ref[pl.ds(at, leaf_len), :], corner)
        for i in range(2):
            near = near_ref[pl.ds(2 * at + i * leaf_len, leaf_len), :].astype(F32)
            rows = slice((2 * pair + i) * leaf_len, (2 * pair + i + 1) * leaf_len)
            out_ref[rows, :] = (near + far[:, i * fields:(i + 1) * fields]).astype(BF)


def field(own, other, turned_transfer, near, turned, per=6):
    leaves, rank, _ = turned_transfer.shape
    fields = near.shape[1]
    leaf_len = near.shape[0] // leaves
    return pl.pallas_call(
        functools.partial(field_kernel, per),
        name="local_and_field",
        grid=(leaves // per,),
        in_specs=[whole()] * 5,
        out_specs=pl.BlockSpec((per * leaf_len, fields), lambda s: (s, 0)),
        out_shape=jax.ShapeDtypeStruct(near.shape, BF),
        compiler_params=params(16),
        cost_estimate=cost(leaves * leaf_len * rank * fields * 2, 4 * MIB),
    )(own, other, turned_transfer, near, turned)


def after(block, *others):
    return lax.optimization_barrier((block,) + others)[0]


def on_device(
    composition,
    leaf_basis,
    transfer,
    coupling,
    top_coupling,
    admissible_owner,
    admissible_leaf,
    near_list,
    leaf_order,
):
    leaves, rank, leaf_len = leaf_basis.shape
    count = lax.axis_size("subtree")
    layers = count // 8
    slots = layers * 4
    pairs = leaves // 2
    cut = pairs // 2
    me = lax.axis_index("subtree").reshape(1)

    ordered, shared, cross, inner, entry, own_at = skeletons_of(
        me, leaf_order, composition, leaf_basis, transfer, admissible_owner, admissible_leaf, layers
    )
    tables = jnp.asarray(near_tables(leaf_len))
    near_args = (near_list, leaf_order, tables, leaf_basis)

    line = along_z(shared, 1)
    from_x, from_y = over_x(shared), over_y(shared)
    filled = near_field(list(range(1, cut)), *near_args, ordered)
    line = after(line, filled[0])
    lines = [along_z(shared, layers - 1)]
    for _ in range(layers - 3):
        lines.append(along_z(line if len(lines) == 1 else lines[-1], 1))
    ready = after(line, from_x, from_y)
    next_x, next_y = over_x(ready), over_y(ready)
    far = onward(choose(me, after(from_x, ready, lines[0]), from_y))
    cross = lax.ppermute(
        cross,
        "subtree",
        [(d, d + 1) for d in range(1, count - 1, 2)] + [(d, d - 1) for d in range(2, count, 2)],
    )
    own_blocks, my_other, turned_transfer = dense_couplings(
        after(entry, ready), own_at, inner, coupling, top_coupling, transfer, slots
    )

    joined = after(join([after(lines[0], my_other)] + lines[1:]), next_x, next_y, cross)
    last_x, last_y = over_x(joined), over_y(joined)
    chosen = choose(me, after(next_x, joined, far), next_y)
    next_far = onward(chosen)
    other_blocks = over_core(after(my_other, chosen))
    held = after(ordered, joined)
    filled = near_field(list(range(cut, pairs - 1)), *near_args, held, filled=filled)
    next_far = after(next_far, filled[0])
    last_far = [along_z(far, layers - 1)]
    for _ in range(layers - 3):
        last_far.append(along_z(next_far if len(last_far) == 1 else last_far[-1], 1))
    held = after(ordered, filled[0])
    *filled, other_at = near_field(
        [0, pairs - 1], *near_args, held, halos=(me, cross, other_blocks), filled=filled
    )
    round_0 = ((shared, line), (from_x, next_x), (from_y, next_y), (far, next_far))
    own, other = far_rounds(
        (0, 1), [0, 1], slots, (own_at, other_at), round_0, (own_blocks, other_blocks)
    )
    steps = list(range(2, layers))
    round_1 = ((joined,), (last_x,), (last_y,), (after(last_far[0], own), *last_far[1:]))
    (other,) = far_rounds((1,), steps, slots, (other_at,), round_1, (other_blocks,), (other,))
    (own,) = far_rounds((0,), steps, slots, (own_at,), round_1, (own_blocks,), (own,))
    return field(own, over_core(other), turned_transfer, *filled)


def solution(mesh):
    placed = (
        P(("groups", "subtree"), None),
        P("subtree", None, None),
        P("subtree", None, None),
        P("subtree", None, None, None),
        P("subtree", None, None, None),
        P(("groups", "subtree"), None),
        P(("groups", "subtree"), None),
        P(("groups", "subtree"), None),
        P(("groups", "subtree"), None),
    )
    return jax.shard_map(
        on_device,
        mesh=mesh,
        in_specs=placed,
        out_specs=P(("groups", "subtree"), None),
        check_vma=False,
    )
```

```python
import functools

import jax
import jax.numpy as jnp
import ml_dtypes
import numpy as np
from jax import lax
from jax.experimental import pallas as pl
from jax.experimental.pallas import tpu as pltpu
from jax.sharding import PartitionSpec as P

COULOMB_SCALE = 0.15
SOFTENING = 0.25
BF = jnp.bfloat16
F32 = jnp.float32
MIB = 1 << 20


def near_tables(leaf_len):
    cells = np.arange(leaf_len)
    along = (cells // 64).astype(np.float32)
    across = (cells // 8 % 8).astype(np.float32)
    height = (cells % 8).astype(np.float32)
    extent = leaf_len // 64
    tables = []
    for offset in (-1, 0, 1):
        delta_x = along[:, None] - along[None, :] - np.float32(offset * extent)
        delta_y = across[:, None] - across[None, :]
        delta_z = height[:, None] - height[None, :]
        square = delta_x * delta_x + delta_y * delta_y + delta_z * delta_z
        value = np.float32(COULOMB_SCALE) / np.sqrt(square + np.float32(SOFTENING))
        tables.append(value.astype(ml_dtypes.bfloat16))
    return np.concatenate(tables, axis=1)


def send(block, target):
    count = lax.axis_size("subtree")
    return lax.ppermute(block, "subtree", [(d, target(d)) for d in range(count)])


def over_core(block):
    return send(block, lambda d: d ^ 1)


def over_x(block):
    return send(block, lambda d: d ^ 2)


def over_y(block):
    return send(block, lambda d: d ^ 4)


def onward(block):
    return send(block, lambda d: d ^ (2 if d % 2 else 4))


def along_z(block, step):
    layers = lax.axis_size("subtree") // 8
    return send(block, lambda d: (d // 8 + step) % layers * 8 + d % 8)


def params(mib):
    return pltpu.CompilerParams(vmem_limit_bytes=mib * MIB)


def cost(flops, moved):
    return pl.CostEstimate(flops=flops // 64, bytes_accessed=moved // 64, transcendentals=0)


def whole():
    return pl.BlockSpec(memory_space=pltpu.VMEM)


def scalars():
    return pl.BlockSpec(memory_space=pltpu.SMEM)


def dot(a, b):
    return jnp.dot(a, b, preferred_element_type=F32)


def in_hbm(*arrays):
    return [pltpu.with_memory_space_constraint(array, pltpu.HBM) for array in arrays]


def one_hot_leaf(row, leaf_len):
    column = jnp.broadcast_to(row, (128, leaf_len)).astype(jnp.int16).T
    lanes = lax.broadcasted_iota(jnp.int32, (leaf_len, 128), 1)
    one, zero = jnp.ones((), BF), jnp.zeros((), BF)
    return jnp.concatenate(
        [
            jnp.where(column == (lanes + 128 * t).astype(jnp.int16), one, zero)
            for t in range(leaf_len // 128)
        ],
        axis=1,
    )


def one_hot_grid(row, leaf_len):
    cells = lax.broadcasted_iota(jnp.int32, (16, leaf_len), 0).astype(jnp.int16)
    wide = jnp.broadcast_to(row, (16, leaf_len)).astype(jnp.int16)
    one, zero = jnp.ones((), BF), jnp.zeros((), BF)
    return jnp.concatenate(
        [jnp.where(cells + jnp.int16(t) == wide, one, zero) for t in range(0, leaf_len, 16)], axis=0
    )


def owner_tables(me, layers, owners, blocks):
    leaves, entries = owners.shape
    slots = layers * 4
    rows = leaves + 1
    shape = (rows, 2 * slots)
    lane = lax.broadcasted_iota(jnp.int32, shape, 1)
    plane = (lane >= slots).astype(jnp.int32)
    slot = lane - plane * slots
    layer, chip, core = me // 8, (me // 2) & 3, me & 1
    turn = slot >> 2
    shift = jnp.where(turn < 2, turn, jnp.where(turn == 2, layers - 1, turn - 1))
    source = layer - shift
    source = jnp.where(source < 0, source + layers, source)
    owner = source * 8 + (chip ^ (slot & 3)) * 2 + (core ^ plane)
    row = lax.broadcasted_iota(jnp.int32, shape, 0)
    distant = jnp.abs(owner - me) >= 2
    entry = jnp.where((row == 0) & distant, owner, -1)
    block = jnp.zeros(shape, jnp.int32)
    pad = jnp.full((1, entries), -1, jnp.int32)
    named = jnp.concatenate([pad, owners], axis=0)
    chosen = jnp.concatenate([pad, blocks], axis=0)
    for k in range(entries):
        match = named[:, k:k + 1] == owner
        entry = jnp.where(match, k, entry)
        block = jnp.where(match, chosen[:, k:k + 1] + 1, block)
    return entry, block


def skeleton_kernel(per, layers, me_ref, order_ref, comp_ref, basis_ref, transfer_ref,
                    owner_ref, leaf_ref, ordered_ref, shared_ref, cross_ref, inner_ref,
                    entry_ref, block_ref, root_ref):
    step = pl.program_id(0)
    leaf_len = basis_ref.shape[2]

    @pl.when(step == 0)
    def _():
        root_ref[...] = jnp.zeros_like(root_ref)
        entry, block = owner_tables(me_ref[0], layers, owner_ref[...], leaf_ref[...])
        rows, lanes = entry.shape
        entry_ref[:rows, :lanes] = entry
        block_ref[:rows, :lanes] = block

    hots = [one_hot_leaf(order_ref[pl.ds(step * per + i, 1), :], leaf_len) for i in range(per)]
    ordered = [
        dot(hots[i], comp_ref[i * leaf_len:(i + 1) * leaf_len, :]).astype(BF) for i in range(per)
    ]
    skeletons = [dot(basis_ref[i], ordered[i]).astype(BF) for i in range(per)]
    across = jnp.concatenate([transfer_ref[i] for i in range(per)], axis=1)
    root_ref[...] += dot(across, jnp.concatenate(skeletons, axis=0))
    for i in range(per):
        at = pl.multiple_of((step * per + i) * leaf_len, leaf_len)
        ordered_ref[pl.ds(at, leaf_len), :] = ordered[i]
        shared_ref[pl.ds(step * per + i + 1, 1)] = skeletons[i][None]

    even = me_ref[0] % 2 == 0

    @pl.when((step == 0) & even)
    def _():
        cross_ref[...] = ordered[0]

    @pl.when((step == 0) & ~even)
    def _():
        inner_ref[...] = ordered[0]

    last = step == pl.num_programs(0) - 1

    @pl.when(last & even)
    def _():
        inner_ref[...] = ordered[-1]

    @pl.when(last & ~even)
    def _():
        cross_ref[...] = ordered[-1]

    @pl.when(last)
    def _():
        shared_ref[pl.ds(0, 1)] = root_ref[...].astype(BF)[None]


def skeletons_of(me, leaf_order, composition, leaf_basis, transfer, owners, blocks, layers, per=6):
    leaves, rank, leaf_len = leaf_basis.shape
    fields = composition.shape[1]
    entries = owners.shape[1]
    edge = jax.ShapeDtypeStruct((leaf_len, fields), BF)
    return pl.pallas_call(
        functools.partial(skeleton_kernel, per, layers),
        name="order_and_skeleton",
        grid=(leaves // per,),
        in_specs=[
            scalars(),
            pl.BlockSpec((leaves, leaf_len), lambda s: (0, 0)),
            pl.BlockSpec((per * leaf_len, fields), lambda s: (s, 0)),
            pl.BlockSpec((per, rank, leaf_len), lambda s: (s, 0, 0)),
            pl.BlockSpec((per, rank, rank), lambda s: (s, 0, 0)),
            pl.BlockSpec((leaves, entries), lambda s: (0, 0)),
            pl.BlockSpec((leaves, entries), lambda s: (0, 0)),
        ],
        out_specs=[whole()] * 6,
        out_shape=[
            jax.ShapeDtypeStruct((leaves * leaf_len, fields), BF),
            jax.ShapeDtypeStruct((leaves + 1, rank, fields), BF),
            edge,
            edge,
            jax.ShapeDtypeStruct((16, 128), jnp.int32),
            jax.ShapeDtypeStruct((16, 128), jnp.int32),
        ],
        scratch_shapes=[pltpu.VMEM((rank, fields), F32)],
        compiler_params=params(16),
        cost_estimate=cost(leaves * leaf_len * leaf_len * fields * 2, 4 * MIB),
    )(me, *in_hbm(leaf_order, composition, leaf_basis, transfer, owners, blocks))


def join_kernel(*refs):
    out = refs[-1]
    at = 0
    for ref in refs[:-1]:
        out[at:at + ref.shape[0]] = ref[...]
        at += ref.shape[0]


def join(parts):
    if len(parts) == 1:
        return parts[0]
    shape = (sum(part.shape[0] for part in parts),) + parts[0].shape[1:]
    return pl.pallas_call(
        join_kernel,
        name="join",
        in_specs=[whole()] * len(parts),
        out_specs=whole(),
        out_shape=jax.ShapeDtypeStruct(shape, BF),
        compiler_params=params(8 if shape[0] <= 32 else 32),
        cost_estimate=cost(0, MIB // 2),
    )(*parts)


def choose_kernel(me_ref, x_ref, y_ref, out_ref):
    @pl.when(me_ref[0] % 2 == 0)
    def _():
        out_ref[...] = x_ref[...]

    @pl.when(me_ref[0] % 2 == 1)
    def _():
        out_ref[...] = y_ref[...]


def choose(me, from_x, from_y):
    return pl.pallas_call(
        choose_kernel,
        name="choose",
        in_specs=[scalars(), whole(), whole()],
        out_specs=whole(),
        out_shape=jax.ShapeDtypeStruct(from_x.shape, BF),
        compiler_params=params(8),
        cost_estimate=cost(0, MIB // 4),
    )(me, from_x, from_y)


def dense_kernel(per, slots, entry_ref, block_ref, inner_ref, coupling_ref, top_ref,
                 transfer_ref, own_ref, other_ref, turned_ref):
    step = pl.program_id(0)
    rank = coupling_ref.shape[2]
    fields = inner_ref.shape[1]
    leaves = own_ref.shape[0] - 1
    for i in range(per):
        turned_ref[step * per + i] = transfer_ref[i].T

    def fill(out_ref, plane, row, entry_row, block_of):
        for slot in range(0, slots, 2):
            pair = []
            for one in (slot, slot + 1):
                entry = entry_ref[entry_row, plane * slots + one]
                block = block_of(jnp.maximum(entry, 0))
                pair.append(jnp.where(entry >= 0, block, jnp.zeros_like(block)))
            out_ref[row, :, slot * rank:(slot + 2) * rank] = jnp.concatenate(pair, axis=1)

    for plane, out_ref in ((0, own_ref), (1, other_ref)):
        for i in range(per):
            leaf = step * per + i
            fill(out_ref, plane, leaf, leaf + 1, lambda entry, i=i: coupling_ref[i, entry])

        @pl.when(step == pl.num_programs(0) - 1)
        def _(plane=plane, out_ref=out_ref):
            fill(out_ref, plane, leaves, 0, lambda entry: top_ref[0, entry])

    @pl.when(step == 0)
    def _():
        for t in range(inner_ref.shape[0] // rank):
            part = inner_ref[t * rank:(t + 1) * rank, :]
            other_ref[leaves + 1, :, t * fields:(t + 1) * fields] = part
        other_ref[leaves + 2] = jnp.zeros(other_ref.shape[1:], BF)
        blocks = block_ref[...].astype(F32).astype(BF)
        other_ref[leaves + 2, :blocks.shape[0], :blocks.shape[1]] = blocks


def dense_couplings(entry, block, inner, coupling, top_coupling, transfer, slots, per=6):
    leaves, entries, rank, _ = coupling.shape
    own = (leaves + 1, rank, slots * rank)
    other = (leaves + 3, rank, slots * rank)
    return pl.pallas_call(
        functools.partial(dense_kernel, per, slots),
        name="couplings_by_owner",
        grid=(leaves // per,),
        in_specs=[
            scalars(),
            pl.BlockSpec(block.shape, lambda s: (0, 0)),
            pl.BlockSpec(inner.shape, lambda s: (0, 0)),
            pl.BlockSpec((per, entries, rank, rank), lambda s: (s, 0, 0, 0)),
            pl.BlockSpec(top_coupling.shape, lambda s: (0, 0, 0, 0)),
            pl.BlockSpec((per, rank, rank), lambda s: (s, 0, 0)),
        ],
        out_specs=[whole()] * 3,
        out_shape=[
            jax.ShapeDtypeStruct(own, BF),
            jax.ShapeDtypeStruct(other, BF),
            jax.ShapeDtypeStruct(transfer.shape, BF),
        ],
        compiler_params=params(16 if slots <= 16 else 48),
        cost_estimate=cost(0, 8 * MIB),
    )(entry, block, inner, *in_hbm(coupling, top_coupling, transfer))


def round_kernel(planes, steps, slots, counts, *refs):
    number = len(planes)
    tables, refs = refs[:number], refs[number:]
    sides = []
    for length in counts:
        sides.append(refs[:length])
        refs = refs[length:]
    blocks, totals, outs = refs[:number], refs[number:-number], refs[-number:]
    rows, rank, _ = outs[0].shape
    low, high = steps[0] * 4 * rank, (steps[-1] + 1) * 4 * rank

    def block_at(side, base, index):
        for ref in side:
            if base < ref.shape[0]:
                return ref[base + index]
            base -= ref.shape[0]

    for place, plane in enumerate(planes):
        for row in range(rows):
            chosen = [
                block_at(
                    side, at * rows, tables[place][(row + 1) % rows, plane * slots + step * 4 + q]
                )
                for at, step in enumerate(steps)
                for q, side in enumerate(sides)
            ]
            value = dot(blocks[place][row, :, low:high], jnp.concatenate(chosen, axis=0))
            if totals:
                value = value + totals[place][row]
            outs[place][row] = value


def far_rounds(planes, steps, slots, tables, parts, blocks, totals=()):
    rank, fields = parts[0][0].shape[1:]
    rows = parts[0][0].shape[0] // (1 if len(parts[0]) > 1 else len(steps))
    args = [part for side in parts for part in side] + list(blocks) + list(totals)
    shape = jax.ShapeDtypeStruct((rows, rank, fields), F32)
    return pl.pallas_call(
        functools.partial(round_kernel, planes, steps, slots, [len(side) for side in parts]),
        name="far_" + str(planes[-1]) + "_" + str(steps[0]),
        in_specs=[scalars()] * len(planes) + [whole()] * len(args),
        out_specs=[whole()] * len(planes),
        out_shape=[shape] * len(planes),
        compiler_params=params(16 if slots <= 16 else 48),
        cost_estimate=cost(rows * rank * 4 * rank * fields * 2 * len(steps), MIB),
    )(*tables, *args)


def near_kernel(edges, pairs, mask_ref, order_ref, table_ref, basis_ref, ordered_ref, *refs):
    if edges:
        me_ref, cross_ref, inner_ref = refs[:3]
        near_ref, turned_ref, at_ref = refs[-3:]
        even = me_ref[0] % 2 == 0
    else:
        near_ref, turned_ref = refs[-2:]
    leaves, _, leaf_len = basis_ref.shape
    fields = ordered_ref.shape[1]
    if edges:
        rows, rank = at_ref.shape[0], basis_ref.shape[1]
        blocks = inner_ref[leaves + 2, :rows, :at_ref.shape[1]]
        at_ref[...] = blocks.astype(F32).astype(jnp.int32)
        inner = jnp.concatenate(
            [
                inner_ref[leaves + 1, :, t * fields:(t + 1) * fields]
                for t in range(leaf_len // rank)
            ],
            axis=0,
        )

    def leaf_at(leaf):
        if leaf < 0:
            return jnp.where(even, cross_ref[...], inner)
        if leaf >= leaves:
            return jnp.where(even, inner, cross_ref[...])
        return ordered_ref[leaf * leaf_len:(leaf + 1) * leaf_len, :]

    def masked(leaf, side):
        value = leaf_at(leaf - 1 + 2 * side)
        return jnp.where(mask_ref[side, leaf] > 0, value, jnp.zeros_like(value))

    near_leaves = [leaf for pair in pairs for leaf in (2 * pair, 2 * pair + 1)]
    columns = [
        jnp.concatenate([masked(leaf, 0), leaf_at(leaf), masked(leaf, 1)], axis=0)
        for leaf in near_leaves
    ]
    near = dot(table_ref[...], jnp.concatenate(columns, axis=1)).astype(BF)
    moved = []
    for i, leaf in enumerate(near_leaves):
        hot = one_hot_grid(order_ref[leaf:leaf + 1, :], leaf_len)
        both = jnp.concatenate([near[:, i * fields:(i + 1) * fields], basis_ref[leaf].T], axis=1)
        moved.append(dot(hot, both).astype(BF))
        near_ref[leaf * leaf_len:(leaf + 1) * leaf_len, :] = moved[i][:, :fields]
    for i, pair in enumerate(pairs):
        turned = [part[:, fields:] for part in moved[2 * i:2 * i + 2]]
        turned_ref[pair * leaf_len:(pair + 1) * leaf_len, :] = jnp.concatenate(turned, axis=1)


def near_field(pairs, near_list, leaf_order, tables, basis, ordered, halos=None, filled=None):
    leaves, rank, leaf_len = basis.shape
    fields = ordered.shape[1]
    args = [near_list.T, leaf_order, tables, basis, ordered]
    in_specs = [scalars()] + [whole()] * 4
    out_shape = [
        jax.ShapeDtypeStruct((leaves * leaf_len, fields), BF),
        jax.ShapeDtypeStruct((leaves // 2 * leaf_len, 2 * rank), BF),
    ]
    aliases = {}
    if halos is not None:
        in_specs += [scalars(), whole(), whole()]
        args += list(halos)
        out_shape.append(jax.ShapeDtypeStruct((16, 128), jnp.int32))
    if filled is not None:
        aliases = {len(args): 0, len(args) + 1: 1}
        in_specs += [whole()] * 2
        args += list(filled)
    return pl.pallas_call(
        functools.partial(near_kernel, halos is not None, tuple(pairs)),
        name="near_" + str(pairs[0]),
        in_specs=in_specs,
        out_specs=[whole()] * len(out_shape),
        out_shape=out_shape,
        input_output_aliases=aliases,
        compiler_params=params(16),
        cost_estimate=cost(len(pairs) * 2 * leaf_len * leaf_len * fields * 10, len(pairs) * MIB),
    )(*args)


def field_kernel(per, own_ref, other_ref, turned_transfer_ref, near_ref, turned_ref, out_ref):
    step = pl.program_id(0)
    leaf_len = out_ref.shape[0] // per
    root = own_ref.shape[0] - 1
    local = own_ref[root] + other_ref[root]
    coarse = local.astype(BF)
    fine = (local - coarse.astype(F32)).astype(BF)
    both = jnp.concatenate([coarse, fine], axis=1)
    fields = local.shape[1]
    for start in range(0, per, 4):
        size = min(4, per - start)
        rows = []
        for i in range(size):
            leaf = step * per + start + i
            down = dot(turned_transfer_ref[leaf], both)
            value = own_ref[leaf] + other_ref[leaf] + (down[:, :fields] + down[:, fields:])
            parts = [jnp.zeros(value.shape, BF)] * size
            parts[i] = value.astype(BF)
            rows.append(jnp.concatenate(parts, axis=1))
        first = step * per + start
        turned = [
            turned_ref[pl.ds(pl.multiple_of((first // 2 + i) * leaf_len, leaf_len), leaf_len), :]
            for i in range(size // 2)
        ]
        far = dot(jnp.concatenate(turned, axis=1), jnp.concatenate(rows, axis=0))
        for i in range(size):
            at = pl.multiple_of((first + i) * leaf_len, leaf_len)
            near = near_ref[pl.ds(at, leaf_len), :].astype(F32)
            out_ref[(start + i) * leaf_len:(start + i + 1) * leaf_len, :] = (
                near + far[:, i * fields:(i + 1) * fields]
            ).astype(BF)


def field(own, other, turned_transfer, near, turned, per=6):
    leaves, rank, _ = turned_transfer.shape
    fields = near.shape[1]
    leaf_len = near.shape[0] // leaves
    return pl.pallas_call(
        functools.partial(field_kernel, per),
        name="local_and_field",
        grid=(leaves // per,),
        in_specs=[whole()] * 5,
        out_specs=pl.BlockSpec((per * leaf_len, fields), lambda s: (s, 0)),
        out_shape=jax.ShapeDtypeStruct(near.shape, BF),
        compiler_params=params(16),
        cost_estimate=cost(leaves * leaf_len * rank * fields * 2, 4 * MIB),
    )(own, other, turned_transfer, near, turned)


def after(block, *others):
    return lax.optimization_barrier((block,) + others)[0]


def on_device(
    composition,
    leaf_basis,
    transfer,
    coupling,
    top_coupling,
    admissible_owner,
    admissible_leaf,
    near_list,
    leaf_order,
):
    leaves, rank, leaf_len = leaf_basis.shape
    count = lax.axis_size("subtree")
    layers = count // 8
    slots = layers * 4
    pairs = leaves // 2
    cut = pairs // 2
    me = lax.axis_index("subtree").reshape(1)

    ordered, shared, cross, inner, entry, own_at = skeletons_of(
        me, leaf_order, composition, leaf_basis, transfer, admissible_owner, admissible_leaf, layers
    )
    tables = jnp.asarray(near_tables(leaf_len))
    near_args = (near_list, leaf_order, tables, leaf_basis)

    line = along_z(shared, 1)
    from_x, from_y = over_x(shared), over_y(shared)
    filled = near_field(list(range(1, cut)), *near_args, ordered)
    line = after(line, filled[0])
    lines = [along_z(shared, layers - 1)]
    for _ in range(layers - 3):
        lines.append(along_z(line if len(lines) == 1 else lines[-1], 1))
    ready = after(line, from_x, from_y)
    next_x, next_y = over_x(ready), over_y(ready)
    far = onward(choose(me, after(from_x, ready, lines[0]), from_y))
    cross = lax.ppermute(
        cross,
        "subtree",
        [(d, d + 1) for d in range(1, count - 1, 2)] + [(d, d - 1) for d in range(2, count, 2)],
    )
    own_blocks, my_other, turned_transfer = dense_couplings(
        after(entry, ready), own_at, inner, coupling, top_coupling, transfer, slots
    )

    joined = after(join([after(lines[0], my_other)] + lines[1:]), next_x, next_y, cross)
    last_x, last_y = over_x(joined), over_y(joined)
    chosen = choose(me, after(next_x, joined, far), next_y)
    next_far = onward(chosen)
    other_blocks = over_core(after(my_other, chosen))
    held = after(ordered, joined)
    filled = near_field(list(range(cut, pairs - 1)), *near_args, held, filled=filled)
    last_far = [along_z(far, layers - 1)]
    for _ in range(layers - 3):
        last_far.append(along_z(next_far if len(last_far) == 1 else last_far[-1], 1))
    held = after(ordered, filled[0])
    *filled, other_at = near_field(
        [0, pairs - 1], *near_args, held, halos=(me, cross, other_blocks), filled=filled
    )
    round_0 = ((shared, line), (from_x, next_x), (from_y, next_y), (far, next_far))
    own, other = far_rounds(
        (0, 1), [0, 1], slots, (own_at, other_at), round_0, (own_blocks, other_blocks)
    )
    steps = list(range(2, layers))
    round_1 = ((joined,), (last_x,), (last_y,), (after(last_far[0], own), *last_far[1:]))
    (other,) = far_rounds((1,), steps, slots, (other_at,), round_1, (other_blocks,), (other,))
    (own,) = far_rounds((0,), steps, slots, (own_at,), round_1, (own_blocks,), (own,))
    return field(own, over_core(other), turned_transfer, *filled)


def solution(mesh):
    placed = (
        P(("groups", "subtree"), None),
        P("subtree", None, None),
        P("subtree", None, None),
        P("subtree", None, None, None),
        P("subtree", None, None, None),
        P(("groups", "subtree"), None),
        P(("groups", "subtree"), None),
        P(("groups", "subtree"), None),
        P(("groups", "subtree"), None),
    )
    return jax.shard_map(
        on_device,
        mesh=mesh,
        in_specs=placed,
        out_specs=P(("groups", "subtree"), None),
        check_vma=False,
    )
```

```python
import functools

import jax
import jax.numpy as jnp
import ml_dtypes
import numpy as np
from jax import lax
from jax.experimental import pallas as pl
from jax.experimental.pallas import tpu as pltpu
from jax.sharding import PartitionSpec as P

COULOMB_SCALE = 0.15
SOFTENING = 0.25
BF = jnp.bfloat16
F32 = jnp.float32
MIB = 1 << 20


def near_tables(leaf_len):
    cells = np.arange(leaf_len)
    along = (cells // 64).astype(np.float32)
    across = (cells // 8 % 8).astype(np.float32)
    height = (cells % 8).astype(np.float32)
    extent = leaf_len // 64
    tables = []
    for offset in (-1, 0, 1):
        delta_x = along[:, None] - along[None, :] - np.float32(offset * extent)
        delta_y = across[:, None] - across[None, :]
        delta_z = height[:, None] - height[None, :]
        square = delta_x * delta_x + delta_y * delta_y + delta_z * delta_z
        value = np.float32(COULOMB_SCALE) / np.sqrt(square + np.float32(SOFTENING))
        tables.append(value.astype(ml_dtypes.bfloat16))
    return np.concatenate(tables, axis=1)


def send(block, target):
    count = lax.axis_size("subtree")
    return lax.ppermute(block, "subtree", [(d, target(d)) for d in range(count)])


def over_core(block):
    return send(block, lambda d: d ^ 1)


def over_x(block):
    return send(block, lambda d: d ^ 2)


def over_y(block):
    return send(block, lambda d: d ^ 4)


def onward(block):
    return send(block, lambda d: d ^ (2 if d % 2 else 4))


def along_z(block, step):
    layers = lax.axis_size("subtree") // 8
    return send(block, lambda d: (d // 8 + step) % layers * 8 + d % 8)


def params(mib):
    return pltpu.CompilerParams(vmem_limit_bytes=mib * MIB)


def cost(flops, moved):
    return pl.CostEstimate(flops=flops // 64, bytes_accessed=moved // 64, transcendentals=0)


def whole():
    return pl.BlockSpec(memory_space=pltpu.VMEM)


def scalars():
    return pl.BlockSpec(memory_space=pltpu.SMEM)


def dot(a, b):
    return jnp.dot(a, b, preferred_element_type=F32)


def in_hbm(*arrays):
    return [pltpu.with_memory_space_constraint(array, pltpu.HBM) for array in arrays]


def one_hot_leaf(row, leaf_len):
    column = jnp.broadcast_to(row, (128, leaf_len)).astype(jnp.int16).T
    lanes = lax.broadcasted_iota(jnp.int32, (leaf_len, 128), 1)
    one, zero = jnp.ones((), BF), jnp.zeros((), BF)
    return jnp.concatenate(
        [
            jnp.where(column == (lanes + 128 * t).astype(jnp.int16), one, zero)
            for t in range(leaf_len // 128)
        ],
        axis=1,
    )


def one_hot_grid(row, leaf_len):
    cells = lax.broadcasted_iota(jnp.int32, (16, leaf_len), 0).astype(jnp.int16)
    wide = jnp.broadcast_to(row, (16, leaf_len)).astype(jnp.int16)
    one, zero = jnp.ones((), BF), jnp.zeros((), BF)
    return jnp.concatenate(
        [jnp.where(cells + jnp.int16(t) == wide, one, zero) for t in range(0, leaf_len, 16)], axis=0
    )


def owner_tables(me, layers, owners, blocks):
    leaves, entries = owners.shape
    slots = layers * 4
    rows = leaves + 1
    shape = (rows, 2 * slots)
    lane = lax.broadcasted_iota(jnp.int32, shape, 1)
    plane = (lane >= slots).astype(jnp.int32)
    slot = lane - plane * slots
    layer, chip, core = me // 8, (me // 2) & 3, me & 1
    turn = slot >> 2
    shift = jnp.where(turn < 2, turn, jnp.where(turn == 2, layers - 1, turn - 1))
    source = layer - shift
    source = jnp.where(source < 0, source + layers, source)
    owner = source * 8 + (chip ^ (slot & 3)) * 2 + (core ^ plane)
    row = lax.broadcasted_iota(jnp.int32, shape, 0)
    distant = jnp.abs(owner - me) >= 2
    entry = jnp.where((row == 0) & distant, owner, -1)
    block = jnp.zeros(shape, jnp.int32)
    pad = jnp.full((1, entries), -1, jnp.int32)
    named = jnp.concatenate([pad, owners], axis=0)
    chosen = jnp.concatenate([pad, blocks], axis=0)
    for k in range(entries):
        match = named[:, k:k + 1] == owner
        entry = jnp.where(match, k, entry)
        block = jnp.where(match, chosen[:, k:k + 1] + 1, block)
    return entry, block


def skeleton_kernel(per, layers, me_ref, order_ref, comp_ref, basis_ref, transfer_ref,
                    owner_ref, leaf_ref, ordered_ref, shared_ref, cross_ref, inner_ref,
                    entry_ref, block_ref, root_ref):
    step = pl.program_id(0)
    leaf_len = basis_ref.shape[2]

    @pl.when(step == 0)
    def _():
        root_ref[...] = jnp.zeros_like(root_ref)
        entry, block = owner_tables(me_ref[0], layers, owner_ref[...], leaf_ref[...])
        rows, lanes = entry.shape
        entry_ref[:rows, :lanes] = entry
        block_ref[:rows, :lanes] = block

    hots = [one_hot_leaf(order_ref[pl.ds(step * per + i, 1), :], leaf_len) for i in range(per)]
    ordered = [
        dot(hots[i], comp_ref[i * leaf_len:(i + 1) * leaf_len, :]).astype(BF) for i in range(per)
    ]
    skeletons = [dot(basis_ref[i], ordered[i]).astype(BF) for i in range(per)]
    across = jnp.concatenate([transfer_ref[i] for i in range(per)], axis=1)
    root_ref[...] += dot(across, jnp.concatenate(skeletons, axis=0))
    for i in range(per):
        at = pl.multiple_of((step * per + i) * leaf_len, leaf_len)
        ordered_ref[pl.ds(at, leaf_len), :] = ordered[i]
        shared_ref[pl.ds(step * per + i + 1, 1)] = skeletons[i][None]

    even = me_ref[0] % 2 == 0

    @pl.when((step == 0) & even)
    def _():
        cross_ref[...] = ordered[0]

    @pl.when((step == 0) & ~even)
    def _():
        inner_ref[...] = ordered[0]

    last = step == pl.num_programs(0) - 1

    @pl.when(last & even)
    def _():
        inner_ref[...] = ordered[-1]

    @pl.when(last & ~even)
    def _():
        cross_ref[...] = ordered[-1]

    @pl.when(last)
    def _():
        shared_ref[pl.ds(0, 1)] = root_ref[...].astype(BF)[None]


def skeletons_of(me, leaf_order, composition, leaf_basis, transfer, owners, blocks, layers, per=6):
    leaves, rank, leaf_len = leaf_basis.shape
    fields = composition.shape[1]
    entries = owners.shape[1]
    edge = jax.ShapeDtypeStruct((leaf_len, fields), BF)
    return pl.pallas_call(
        functools.partial(skeleton_kernel, per, layers),
        name="order_and_skeleton",
        grid=(leaves // per,),
        in_specs=[
            scalars(),
            pl.BlockSpec((leaves, leaf_len), lambda s: (0, 0)),
            pl.BlockSpec((per * leaf_len, fields), lambda s: (s, 0)),
            pl.BlockSpec((per, rank, leaf_len), lambda s: (s, 0, 0)),
            pl.BlockSpec((per, rank, rank), lambda s: (s, 0, 0)),
            pl.BlockSpec((leaves, entries), lambda s: (0, 0)),
            pl.BlockSpec((leaves, entries), lambda s: (0, 0)),
        ],
        out_specs=[whole()] * 6,
        out_shape=[
            jax.ShapeDtypeStruct((leaves * leaf_len, fields), BF),
            jax.ShapeDtypeStruct((leaves + 1, rank, fields), BF),
            edge,
            edge,
            jax.ShapeDtypeStruct((16, 128), jnp.int32),
            jax.ShapeDtypeStruct((16, 128), jnp.int32),
        ],
        scratch_shapes=[pltpu.VMEM((rank, fields), F32)],
        compiler_params=params(16),
        cost_estimate=cost(leaves * leaf_len * leaf_len * fields * 2, 4 * MIB),
    )(me, *in_hbm(leaf_order, composition, leaf_basis, transfer, owners, blocks))


def join_kernel(*refs):
    out = refs[-1]
    at = 0
    for ref in refs[:-1]:
        out[at:at + ref.shape[0]] = ref[...]
        at += ref.shape[0]


def join(parts):
    if len(parts) == 1:
        return parts[0]
    shape = (sum(part.shape[0] for part in parts),) + parts[0].shape[1:]
    return pl.pallas_call(
        join_kernel,
        name="join",
        in_specs=[whole()] * len(parts),
        out_specs=whole(),
        out_shape=jax.ShapeDtypeStruct(shape, BF),
        compiler_params=params(8 if shape[0] <= 32 else 32),
        cost_estimate=cost(0, MIB // 2),
    )(*parts)


def choose_kernel(me_ref, x_ref, y_ref, out_ref):
    @pl.when(me_ref[0] % 2 == 0)
    def _():
        out_ref[...] = x_ref[...]

    @pl.when(me_ref[0] % 2 == 1)
    def _():
        out_ref[...] = y_ref[...]


def choose(me, from_x, from_y):
    return pl.pallas_call(
        choose_kernel,
        name="choose",
        in_specs=[scalars(), whole(), whole()],
        out_specs=whole(),
        out_shape=jax.ShapeDtypeStruct(from_x.shape, BF),
        compiler_params=params(8),
        cost_estimate=cost(0, MIB // 4),
    )(me, from_x, from_y)


def dense_kernel(per, slots, entry_ref, block_ref, inner_ref, coupling_ref, top_ref,
                 transfer_ref, own_ref, other_ref, turned_ref):
    step = pl.program_id(0)
    rank = coupling_ref.shape[2]
    fields = inner_ref.shape[1]
    leaves = own_ref.shape[0] - 1
    for i in range(per):
        turned_ref[step * per + i] = transfer_ref[i].T

    def fill(out_ref, plane, row, entry_row, block_of):
        for slot in range(0, slots, 2):
            pair = []
            for one in (slot, slot + 1):
                entry = entry_ref[entry_row, plane * slots + one]
                block = block_of(jnp.maximum(entry, 0))
                pair.append(jnp.where(entry >= 0, block, jnp.zeros_like(block)))
            out_ref[row, :, slot * rank:(slot + 2) * rank] = jnp.concatenate(pair, axis=1)

    for plane, out_ref in ((0, own_ref), (1, other_ref)):
        for i in range(per):
            leaf = step * per + i
            fill(out_ref, plane, leaf, leaf + 1, lambda entry, i=i: coupling_ref[i, entry])

        @pl.when(step == pl.num_programs(0) - 1)
        def _(plane=plane, out_ref=out_ref):
            fill(out_ref, plane, leaves, 0, lambda entry: top_ref[0, entry])

    @pl.when(step == 0)
    def _():
        for t in range(inner_ref.shape[0] // rank):
            part = inner_ref[t * rank:(t + 1) * rank, :]
            other_ref[leaves + 1, :, t * fields:(t + 1) * fields] = part
        other_ref[leaves + 2] = jnp.zeros(other_ref.shape[1:], BF)
        blocks = block_ref[...].astype(F32).astype(BF)
        other_ref[leaves + 2, :blocks.shape[0], :blocks.shape[1]] = blocks


def dense_couplings(entry, block, inner, coupling, top_coupling, transfer, slots, per=6):
    leaves, entries, rank, _ = coupling.shape
    own = (leaves + 1, rank, slots * rank)
    other = (leaves + 3, rank, slots * rank)
    return pl.pallas_call(
        functools.partial(dense_kernel, per, slots),
        name="couplings_by_owner",
        grid=(leaves // per,),
        in_specs=[
            scalars(),
            pl.BlockSpec(block.shape, lambda s: (0, 0)),
            pl.BlockSpec(inner.shape, lambda s: (0, 0)),
            pl.BlockSpec((per, entries, rank, rank), lambda s: (s, 0, 0, 0)),
            pl.BlockSpec(top_coupling.shape, lambda s: (0, 0, 0, 0)),
            pl.BlockSpec((per, rank, rank), lambda s: (s, 0, 0)),
        ],
        out_specs=[whole()] * 3,
        out_shape=[
            jax.ShapeDtypeStruct(own, BF),
            jax.ShapeDtypeStruct(other, BF),
            jax.ShapeDtypeStruct(transfer.shape, BF),
        ],
        compiler_params=params(16 if slots <= 16 else 48),
        cost_estimate=cost(0, 8 * MIB),
    )(entry, block, inner, *in_hbm(coupling, top_coupling, transfer))


def round_kernel(planes, steps, slots, counts, *refs):
    number = len(planes)
    tables, refs = refs[:number], refs[number:]
    sides = []
    for length in counts:
        sides.append(refs[:length])
        refs = refs[length:]
    blocks, totals, outs = refs[:number], refs[number:-number], refs[-number:]
    rows, rank, _ = outs[0].shape
    low, high = steps[0] * 4 * rank, (steps[-1] + 1) * 4 * rank

    def block_at(side, base, index):
        for ref in side:
            if base < ref.shape[0]:
                return ref[base + index]
            base -= ref.shape[0]

    for place, plane in enumerate(planes):
        for row in range(rows):
            chosen = [
                block_at(
                    side, at * rows, tables[place][(row + 1) % rows, plane * slots + step * 4 + q]
                )
                for at, step in enumerate(steps)
                for q, side in enumerate(sides)
            ]
            value = dot(blocks[place][row, :, low:high], jnp.concatenate(chosen, axis=0))
            if totals:
                value = value + totals[place][row]
            outs[place][row] = value


def far_rounds(planes, steps, slots, tables, parts, blocks, totals=()):
    rank, fields = parts[0][0].shape[1:]
    rows = parts[0][0].shape[0] // (1 if len(parts[0]) > 1 else len(steps))
    args = [part for side in parts for part in side] + list(blocks) + list(totals)
    shape = jax.ShapeDtypeStruct((rows, rank, fields), F32)
    return pl.pallas_call(
        functools.partial(round_kernel, planes, steps, slots, [len(side) for side in parts]),
        name="far_" + str(planes[-1]) + "_" + str(steps[0]),
        in_specs=[scalars()] * len(planes) + [whole()] * len(args),
        out_specs=[whole()] * len(planes),
        out_shape=[shape] * len(planes),
        compiler_params=params(16 if slots <= 16 else 48),
        cost_estimate=cost(rows * rank * 4 * rank * fields * 2 * len(steps), MIB),
    )(*tables, *args)


def near_kernel(edges, pairs, mask_ref, order_ref, table_ref, basis_ref, ordered_ref, *refs):
    if edges:
        me_ref, cross_ref, inner_ref = refs[:3]
        near_ref, turned_ref, at_ref = refs[-3:]
        even = me_ref[0] % 2 == 0
    else:
        near_ref, turned_ref = refs[-2:]
    leaves, _, leaf_len = basis_ref.shape
    fields = ordered_ref.shape[1]
    if edges:
        rows, rank = at_ref.shape[0], basis_ref.shape[1]
        blocks = inner_ref[leaves + 2, :rows, :at_ref.shape[1]]
        at_ref[...] = blocks.astype(F32).astype(jnp.int32)
        inner = jnp.concatenate(
            [
                inner_ref[leaves + 1, :, t * fields:(t + 1) * fields]
                for t in range(leaf_len // rank)
            ],
            axis=0,
        )

    def leaf_at(leaf):
        if leaf < 0:
            return jnp.where(even, cross_ref[...], inner)
        if leaf >= leaves:
            return jnp.where(even, inner, cross_ref[...])
        return ordered_ref[leaf * leaf_len:(leaf + 1) * leaf_len, :]

    def masked(leaf, side):
        value = leaf_at(leaf - 1 + 2 * side)
        return jnp.where(mask_ref[side, leaf] > 0, value, jnp.zeros_like(value))

    near_leaves = [leaf for pair in pairs for leaf in (2 * pair, 2 * pair + 1)]
    columns = [
        jnp.concatenate([masked(leaf, 0), leaf_at(leaf), masked(leaf, 1)], axis=0)
        for leaf in near_leaves
    ]
    near = dot(table_ref[...], jnp.concatenate(columns, axis=1)).astype(BF)
    moved = []
    for i, leaf in enumerate(near_leaves):
        hot = one_hot_grid(order_ref[leaf:leaf + 1, :], leaf_len)
        both = jnp.concatenate([near[:, i * fields:(i + 1) * fields], basis_ref[leaf].T], axis=1)
        moved.append(dot(hot, both).astype(BF))
        near_ref[leaf * leaf_len:(leaf + 1) * leaf_len, :] = moved[i][:, :fields]
    for i, pair in enumerate(pairs):
        turned = [part[:, fields:] for part in moved[2 * i:2 * i + 2]]
        turned_ref[pair * leaf_len:(pair + 1) * leaf_len, :] = jnp.concatenate(turned, axis=1)


def near_field(pairs, near_list, leaf_order, tables, basis, ordered, halos=None, filled=None):
    leaves, rank, leaf_len = basis.shape
    fields = ordered.shape[1]
    args = [near_list.T, leaf_order, tables, basis, ordered]
    in_specs = [scalars()] + [whole()] * 4
    out_shape = [
        jax.ShapeDtypeStruct((leaves * leaf_len, fields), BF),
        jax.ShapeDtypeStruct((leaves // 2 * leaf_len, 2 * rank), BF),
    ]
    aliases = {}
    if halos is not None:
        in_specs += [scalars(), whole(), whole()]
        args += list(halos)
        out_shape.append(jax.ShapeDtypeStruct((16, 128), jnp.int32))
    if filled is not None:
        aliases = {len(args): 0, len(args) + 1: 1}
        in_specs += [whole()] * 2
        args += list(filled)
    return pl.pallas_call(
        functools.partial(near_kernel, halos is not None, tuple(pairs)),
        name="near_" + str(pairs[0]),
        in_specs=in_specs,
        out_specs=[whole()] * len(out_shape),
        out_shape=out_shape,
        input_output_aliases=aliases,
        compiler_params=params(16),
        cost_estimate=cost(len(pairs) * 2 * leaf_len * leaf_len * fields * 10, len(pairs) * MIB),
    )(*args)


def field_kernel(per, own_ref, other_ref, turned_transfer_ref, near_ref, turned_ref, out_ref):
    step = pl.program_id(0)
    leaf_len = out_ref.shape[0] // per
    root = own_ref.shape[0] - 1
    local = own_ref[root] + other_ref[root]
    coarse = local.astype(BF)
    fine = (local - coarse.astype(F32)).astype(BF)
    both = jnp.concatenate([coarse, fine], axis=1)
    fields = local.shape[1]
    for pair in range(per // 2):
        values = []
        for i in range(2):
            leaf = step * per + 2 * pair + i
            down = dot(turned_transfer_ref[leaf], both)
            value = own_ref[leaf] + other_ref[leaf] + (down[:, :fields] + down[:, fields:])
            values.append(value.astype(BF))
        zero = jnp.zeros_like(values[0])
        corner = jnp.concatenate(
            [
                jnp.concatenate([values[0], zero], axis=1),
                jnp.concatenate([zero, values[1]], axis=1),
            ],
            axis=0,
        )
        at = pl.multiple_of((step * (per // 2) + pair) * leaf_len, leaf_len)
        far = dot(turned_ref[pl.ds(at, leaf_len), :], corner)
        for i in range(2):
            near = near_ref[pl.ds(2 * at + i * leaf_len, leaf_len), :].astype(F32)
            rows = slice((2 * pair + i) * leaf_len, (2 * pair + i + 1) * leaf_len)
            out_ref[rows, :] = (near + far[:, i * fields:(i + 1) * fields]).astype(BF)


def field(own, other, turned_transfer, near, turned, per=6):
    leaves, rank, _ = turned_transfer.shape
    fields = near.shape[1]
    leaf_len = near.shape[0] // leaves
    return pl.pallas_call(
        functools.partial(field_kernel, per),
        name="local_and_field",
        grid=(leaves // per,),
        in_specs=[whole()] * 5,
        out_specs=pl.BlockSpec((per * leaf_len, fields), lambda s: (s, 0)),
        out_shape=jax.ShapeDtypeStruct(near.shape, BF),
        compiler_params=params(16),
        cost_estimate=cost(leaves * leaf_len * rank * fields * 2, 4 * MIB),
    )(own, other, turned_transfer, near, turned)


def after(block, *others):
    return lax.optimization_barrier((block,) + others)[0]


def on_device(
    composition,
    leaf_basis,
    transfer,
    coupling,
    top_coupling,
    admissible_owner,
    admissible_leaf,
    near_list,
    leaf_order,
):
    leaves, rank, leaf_len = leaf_basis.shape
    count = lax.axis_size("subtree")
    layers = count // 8
    slots = layers * 4
    pairs = leaves // 2
    cut = pairs // 2
    me = lax.axis_index("subtree").reshape(1)

    ordered, shared, cross, inner, entry, own_at = skeletons_of(
        me, leaf_order, composition, leaf_basis, transfer, admissible_owner, admissible_leaf, layers
    )
    tables = jnp.asarray(near_tables(leaf_len))
    near_args = (near_list, leaf_order, tables, leaf_basis)

    line = along_z(shared, 1)
    from_x, from_y = over_x(shared), over_y(shared)
    filled = near_field(list(range(1, cut)), *near_args, ordered)
    cross = lax.ppermute(
        cross,
        "subtree",
        [(d, d + 1) for d in range(1, count - 1, 2)] + [(d, d - 1) for d in range(2, count, 2)],
    )
    line = after(line, filled[0], cross)
    lines = [along_z(shared, layers - 1)]
    for _ in range(layers - 3):
        lines.append(along_z(line if len(lines) == 1 else lines[-1], 1))
    ready = after(line, from_x, from_y)
    next_x, next_y = over_x(ready), over_y(ready)
    far = onward(choose(me, after(from_x, ready, lines[0]), from_y))
    own_blocks, my_other, turned_transfer = dense_couplings(
        after(entry, ready), own_at, inner, coupling, top_coupling, transfer, slots
    )

    joined = after(join([after(lines[0], my_other)] + lines[1:]), next_x, next_y)
    last_x, last_y = over_x(joined), over_y(joined)
    chosen = choose(me, after(next_x, joined, far), next_y)
    next_far = onward(chosen)
    other_blocks = over_core(after(my_other, chosen))
    held = after(ordered, joined)
    filled = near_field(list(range(cut, pairs - 1)), *near_args, held, filled=filled)
    last_far = [along_z(far, layers - 1)]
    for _ in range(layers - 3):
        last_far.append(along_z(next_far if len(last_far) == 1 else last_far[-1], 1))
    held = after(ordered, filled[0])
    *filled, other_at = near_field(
        [0, pairs - 1], *near_args, held, halos=(me, cross, other_blocks), filled=filled
    )
    round_0 = ((shared, line), (from_x, next_x), (from_y, next_y), (far, next_far))
    own, other = far_rounds(
        (0, 1), [0, 1], slots, (own_at, other_at), round_0, (own_blocks, other_blocks)
    )
    steps = list(range(2, layers))
    round_1 = ((joined,), (last_x,), (last_y,), (after(last_far[0], own), *last_far[1:]))
    (other,) = far_rounds((1,), steps, slots, (other_at,), round_1, (other_blocks,), (other,))
    (own,) = far_rounds((0,), steps, slots, (own_at,), round_1, (own_blocks,), (own,))
    return field(own, over_core(other), turned_transfer, *filled)


def solution(mesh):
    placed = (
        P(("groups", "subtree"), None),
        P("subtree", None, None),
        P("subtree", None, None),
        P("subtree", None, None, None),
        P("subtree", None, None, None),
        P(("groups", "subtree"), None),
        P(("groups", "subtree"), None),
        P(("groups", "subtree"), None),
        P(("groups", "subtree"), None),
    )
    return jax.shard_map(
        on_device,
        mesh=mesh,
        in_specs=placed,
        out_specs=P(("groups", "subtree"), None),
        check_vma=False,
    )
```
